32 devices in a mesh: dp: 8 (over z, x), rep: 4 (over y, core).
Axes of the slice: x: 2, y: 2, z: 4, core: 2. Of those that a mesh axis runs over, the one named last changes fastest.
Arguments:
- tokens: bfloat16 [4, 4096, 768], P('rep', 'dp'), may hold values from -6 to 6
- cotangent: bfloat16 [4, 4096, 768], P('rep', 'dp'), may hold values from -6 to 6
- padding: int32 [4, 4096], P('rep', 'dp'), may hold values from 0 to 1, as said below
- opening: int32 [4, 4096], P('rep', 'dp'), may hold values from 0 to 1, as said below
- w_in: float32 [768, 4992], P(('dp', 'rep')), may hold values from -0.21875 to 0.21875
- w_out: float32 [2304, 768], P(('dp', 'rep')), may hold values from -0.21875 to 0.21875
- vectors: float32 [2304], replicated, may hold values from -0.5 to 11, as said below
- m_in: float32 [768, 4992], P(('dp', 'rep')), may hold values from -0.0068359375 to 0.0068359375
- v_in: float32 [768, 4992], P(('dp', 'rep')), may hold values from 9.765625e-08 to 3.90625e-07
- m_out: float32 [2304, 768], P(('dp', 'rep')), may hold values from -0.0068359375 to 0.0068359375
- v_out: float32 [2304, 768], P(('dp', 'rep')), may hold values from 9.765625e-08 to 3.90625e-07
- m_vec: float32 [2304], replicated, may hold values from -0.0068359375 to 0.0068359375
- v_vec: float32 [2304], replicated, may hold values from 9.765625e-08 to 3.90625e-07
- counter: int32 [1], replicated, may hold values from 1 to 3
Outputs:
- block_out: bfloat16 [4, 4096, 768], P('rep', 'dp')
- d_tokens: float32 [4, 4096, 768], P('rep', 'dp')
- grad_in: float32 [768, 4992], P(('dp', 'rep'))
- new_in: float32 [768, 4992], P(('dp', 'rep'))
- first_in: float32 [768, 4992], P(('dp', 'rep'))
- second_in: float32 [768, 4992], P(('dp', 'rep'))
- copy_in: bfloat16 [768, 4992], P(('dp', 'rep'))
- grad_out: float32 [2304, 768], P(('dp', 'rep'))
- new_out: float32 [2304, 768], P(('dp', 'rep'))
- first_out: float32 [2304, 768], P(('dp', 'rep'))
- second_out: float32 [2304, 768], P(('dp', 'rep'))
- copy_out: bfloat16 [2304, 768], P(('dp', 'rep'))
- grad_vec: float32 [2304], replicated
- grad_bias: float32 [384], replicated
- update_vec: float32 [2304], replicated
- first_vec: float32 [2304], replicated
- second_vec: float32 [2304], replicated
The draws below stay inside these ranges and needn't reach their ends.
Inputs may be any that keep to these rules, and one draw needn't show every extreme that they name: Each group's slots fall into aligned blocks of 4096; each block holds buckets of 4096, 2048 or 1024 slots, each starting at a multiple of its own length; opening is 1 exactly on each bucket's first slot. In each bucket, padding is 1 on its first slots and 0 after them; at least a quarter of each bucket's slots are 1. `vectors`: the gains and the forget biases are positive.
All inputs are finite; a program needn't handle non-finite values.
Results may differ from the reference program's by a relative error of at most 0.013.
The reference program's roundings to bfloat16 on the way count: a program that leaves them out, or rounds other values in their place, can miss the bound.
Values may be sent and summed in bfloat16 or wider, within the bound.
A program may use at most 320 MiB of HBM per device.

```python
import math
import jax
import jax.numpy as jnp
import numpy as np
from jax import lax

D = 768
CH = 384
FF = 1536
SPAN = 4096
GROUP_TOKENS = 4096
N_REP = 4


OPEN_TABLE = np.array([[1, 0, 0, 0], [1, 0, 1, 0], [1, 0, 1, 1], [1, 1, 1, 1]], np.int32)


LENGTH_TABLE = np.array([[4, 4, 4, 4], [2, 2, 2, 2], [2, 2, 1, 1], [1, 1, 1, 1]], np.int32)


OFFSET_TABLE = np.array([[0, 1, 2, 3], [0, 1, 0, 1], [0, 1, 0, 0], [0, 0, 0, 0]], np.int32)


def bucket_layout(key):
    quarter = SPAN // 4
    blocks = N_REP * GROUP_TOKENS // SPAN
    bucket_key = jax.random.fold_in(key, 7301)
    pattern = jax.random.randint(jax.random.fold_in(bucket_key, 1), (blocks,), 0, 4)
    open_marks = jnp.asarray(OPEN_TABLE)[pattern]
    lengths = jnp.asarray(LENGTH_TABLE)[pattern] * quarter
    offsets = jnp.asarray(OFFSET_TABLE)[pattern]
    random_bits = jax.random.randint(jax.random.fold_in(bucket_key, 2), (blocks, 4), 0, 1 << 20)
    counts = lengths // 4 + random_bits % (lengths - lengths // 4 + 1)
    first_slot = jnp.arange(4, dtype=jnp.int32)[None, :] - offsets
    counts = jnp.take_along_axis(counts, first_slot, axis=1)
    inside = jnp.arange(quarter, dtype=jnp.int32)[None, None, :]
    position = offsets[:, :, None] * quarter + inside
    filled = (position < counts[:, :, None]).astype(jnp.int32).reshape(N_REP, GROUP_TOKENS)
    opening = ((open_marks[:, :, None] == 1) & (inside == 0)).astype(jnp.int32).reshape(N_REP, GROUP_TOKENS)
    return (filled, opening)


def draw_padding(key, part):
    return bucket_layout(key)[0]


def draw_opening(key, part):
    return bucket_layout(key)[1]


def draw_vectors(key, part):
    vector_keys = jax.random.split(jax.random.fold_in(key, 4409), 3)
    gains = jnp.clip(1.0 + 0.15 * jax.random.normal(vector_keys[0], (2 * D,), jnp.float32), 0.6, 1.5)
    angles = jax.random.uniform(vector_keys[1], (CH,), jnp.float32, -0.3, 0.3)
    spread = jax.random.uniform(vector_keys[2], (CH,), jnp.float32, 0.4, 1.3)
    return jnp.concatenate([gains, angles, math.log(SPAN) * spread])


def level_of(own_key, shape, cuts, least, top_value):
    loudness, own = 1.0, jax.random.fold_in(own_key, 6)
    for dim, blocks in cuts:
        heights = jnp.exp(jax.random.uniform(jax.random.fold_in(own, dim), (blocks,), jnp.float32, least / len(cuts), top_value / len(cuts)))
        loudness = loudness * jnp.repeat(heights, shape[dim] // blocks).reshape([-1 if axis == dim else 1 for axis in range(len(shape))])
    return loudness


def normal_values(rng, dims, scale, bound, cuts=(), held_as=jnp.bfloat16):
    result = scale * jax.random.normal(rng, dims, jnp.float32)
    if cuts:
        result = result * level_of(rng, dims, cuts, -0.22, 0.18)
    return jnp.clip(result, -bound, bound).astype(held_as)


def setup_inputs(seed: int = 0) -> dict:
    key_of = jax.random.split(jax.random.key(seed), 15)
    tokens = normal_values(key_of[0], (N_REP, GROUP_TOKENS, D), 1.0, 6.0, ((0, 4), (1, 8)))
    cotangent = normal_values(key_of[1], (N_REP, GROUP_TOKENS, D), 1.0, 6.0, ((0, 4), (1, 8)))
    padding = draw_padding(jax.random.fold_in(key_of[14], 71), 0)
    opening = draw_opening(jax.random.fold_in(key_of[14], 71), 0)
    w_in = normal_values(key_of[4], (D, CH + 2 * D + 2 * FF), D ** -0.5, 0.21875, ((0, 32),), jnp.float32)
    w_out = normal_values(key_of[5], (D + FF, D), D ** -0.5, 0.21875, ((0, 32),), jnp.float32)
    vectors = draw_vectors(jax.random.fold_in(key_of[14], 71), 0)
    m_in = normal_values(key_of[7], (D, CH + 2 * D + 2 * FF), (0.14 * (N_REP * GROUP_TOKENS) ** -0.5), 0.0068359375, ((0, 32),), jnp.float32)
    v_in = jnp.clip(jnp.exp(math.log(3.906249901319825e-07) - 1.3862944 * jax.random.uniform(key_of[8], (D, CH + 2 * D + 2 * FF), jnp.float32) ** level_of(key_of[8], (D, CH + 2 * D + 2 * FF), ((0, 32),), -0.2, 0.2)), 9.765624753299562e-08, 3.906249901319825e-07)
    m_out = normal_values(key_of[9], (D + FF, D), (0.14 * (N_REP * GROUP_TOKENS) ** -0.5), 0.0068359375, ((0, 32),), jnp.float32)
    v_out = jnp.clip(jnp.exp(math.log(3.906249901319825e-07) - 1.3862944 * jax.random.uniform(key_of[10], (D + FF, D), jnp.float32) ** level_of(key_of[10], (D + FF, D), ((0, 32),), -0.2, 0.2)), 9.765624753299562e-08, 3.906249901319825e-07)
    m_vec = normal_values(key_of[11], (2 * D + 2 * CH,), (0.14 * (N_REP * GROUP_TOKENS) ** -0.5), 0.0068359375, (), jnp.float32)
    v_vec = jnp.clip(jnp.exp(jax.random.uniform(key_of[12], (2 * D + 2 * CH,), jnp.float32, math.log(9.765624753299562e-08), math.log(3.906249901319825e-07))), 9.765624753299562e-08, 3.906249901319825e-07)
    counter = jax.random.randint(key_of[13], (1,), 1, 4).astype(jnp.int32)
    return dict(tokens=tokens, cotangent=cotangent, padding=padding, opening=opening, w_in=w_in, w_out=w_out, vectors=vectors, m_in=m_in, v_in=v_in, m_out=m_out, v_out=v_out, m_vec=m_vec, v_vec=v_vec, counter=counter)


NORM_EPSILON = 1e-06
LEARN_RATE = 0.05
BETA_ONE = 0.9
BETA_TWO = 0.999
ADAM_EPSILON = 1e-08
WEIGHT_DECAY = 0.1

@jax.custom_vjp
def low(v):
    return lax.optimization_barrier(v.astype(jnp.bfloat16)).astype(jnp.float32)

@jax.custom_vjp
def low_back(v):
    return v

def low_keep(v):
    return (low(v), None)

def low_pass(kept, grad):
    return (grad,)

def back_keep(v):
    return (v, None)

def back_low(kept, grad):
    return (low(grad),)
low.defvjp(low_keep, low_pass)
low_back.defvjp(back_keep, back_low)

def complex_product(left_real, left_imag, right_real, right_imag):
    return (left_real * right_real - left_imag * right_imag, left_real * right_imag + left_imag * right_real)

def compose(earlier, later):
    product = complex_product(later[0], later[1], earlier[0], earlier[1])
    carried = complex_product(later[0], later[1], earlier[2], earlier[3])
    return (product[0], product[1], carried[0] + later[2], carried[1] + later[3])

def normalize(values, gains):
    return values * lax.rsqrt(lax.optimization_barrier(jnp.mean(values * values, axis=-1, keepdims=True)) + NORM_EPSILON) * gains

def matmul_high(left, right):
    return jnp.dot(left, right, precision=lax.Precision.HIGHEST)

def block(inputs, starting, filled, w_in_low, w_out_low, vectors):
    gains_one = vectors[:D]
    gains_two = vectors[D:2 * D]
    phases = vectors[2 * D:2 * D + CH]
    biases = vectors[2 * D + CH:]
    mixer_cols = CH + 2 * D
    normed = low(normalize(inputs, gains_one))
    pre_mix = low_back(matmul_high(normed, w_in_low[:, :mixer_cols]))
    forget = jax.nn.sigmoid(-(pre_mix[:, :CH] + biases))
    driver = jax.nn.silu(pre_mix[:, CH:CH + D])
    decay_sent = low_back(low(jnp.where(starting[:, None], 1.0, forget)))
    input_sent = low_back(low(jnp.concatenate([forget, forget], axis=1) * driver))
    retain = 1.0 - decay_sent
    step_real = retain * jnp.cos(phases)
    step_imag = retain * jnp.sin(phases)
    scanned = lax.associative_scan(compose, (step_real, step_imag, input_sent[:, :CH], input_sent[:, CH:]), axis=0)
    recurrent = low_back(low(jnp.concatenate([scanned[2], scanned[3]], axis=1)))
    gated_rows = low(recurrent * filled[:, None] * jax.nn.silu(pre_mix[:, CH + D:]))
    middle = inputs + low_back(matmul_high(gated_rows, w_out_low[:D]))
    normed_two = low(normalize(middle, gains_two))
    glu_pre = low_back(matmul_high(normed_two, w_in_low[:, mixer_cols:]))
    hidden = low(jax.nn.silu(glu_pre[:, :FF]) * glu_pre[:, FF:])
    return middle + low_back(matmul_high(hidden, w_out_low[D:]))

def adam_update(master, gradient, first, second, steps, decay):
    first_new = BETA_ONE * first + (1.0 - BETA_ONE) * gradient
    second_new = BETA_TWO * second + (1.0 - BETA_TWO) * gradient * gradient
    corrected = first_new / (1.0 - BETA_ONE ** steps) / (jnp.sqrt(second_new / (1.0 - BETA_TWO ** steps)) + ADAM_EPSILON)
    change = -LEARN_RATE * (corrected + decay * master)
    return (master + change, first_new, second_new, change)

def reference(tokens, cotangent, padding, opening, w_in, w_out, vectors, m_in, v_in, m_out, v_out, m_vec, v_vec, counter):
    blocks = N_REP * GROUP_TOKENS // SPAN
    inputs = tokens.astype(jnp.float32).reshape(blocks, SPAN, D)
    starting = (opening == 1).reshape(blocks, SPAN)
    filled = padding.astype(jnp.float32).reshape(blocks, SPAN)
    upstream = cotangent.astype(jnp.float32).reshape(blocks, SPAN, D) * filled[:, :, None]

    def forward(block_inputs, master_in, master_out, block_vectors):
        w_in_low = low(master_in)
        w_out_low = low(master_out)
        single = jax.checkpoint(lambda rows_now, starts_now, filled_now: block(rows_now, starts_now, filled_now, w_in_low, w_out_low, block_vectors))

        def advance(carried, element):
            return (carried, single(element[0], element[1], element[2]))
        _, outputs = lax.scan(advance, jnp.zeros((), jnp.float32), (block_inputs, starting, filled))
        return outputs
    outputs, pullback = jax.vjp(forward, inputs, w_in, w_out, vectors)
    d_inputs, d_in, d_out, d_vec = pullback(upstream)
    total = jnp.sum(padding).astype(jnp.float32)
    grad_in = d_in / total
    grad_out = d_out / total
    grad_vec = d_vec / total
    steps = counter[0].astype(jnp.float32)
    new_in, first_in, second_in, change_in = adam_update(w_in, grad_in, m_in, v_in, steps, WEIGHT_DECAY)
    new_out, first_out, second_out, change_out = adam_update(w_out, grad_out, m_out, v_out, steps, WEIGHT_DECAY)
    new_vec, first_vec, second_vec, update_vec = adam_update(vectors, grad_vec, m_vec, v_vec, steps, 0.0)
    block_out = outputs.reshape(N_REP, GROUP_TOKENS, D).astype(jnp.bfloat16)
    d_tokens = d_inputs.reshape(N_REP, GROUP_TOKENS, D)
    return (block_out, d_tokens, grad_in, new_in, first_in, second_in, new_in.astype(jnp.bfloat16), grad_out, new_out, first_out, second_out, new_out.astype(jnp.bfloat16), grad_vec, grad_vec[2 * D + CH:], update_vec, first_vec, second_vec)
```

```python
import jax
import jax.numpy as jnp
from jax import lax
from jax.experimental import pallas as pl
from jax.experimental.pallas import tpu as pltpu
from jax.sharding import PartitionSpec as P

D = 768
CH = 384
FF = 1536


NORM_EPSILON = 1e-06
LEARN_RATE = 0.05
BETA_ONE = 0.9
BETA_TWO = 0.999
ADAM_EPSILON = 1e-08
WEIGHT_DECAY = 0.1


LANES = 8


def rotate(real, imag, cosine, sine):
    return cosine * real - sine * imag, sine * real + cosine * imag


def turn_power(cosine, sine, doublings):
    for _ in range(doublings):
        cosine, sine = cosine * cosine - sine * sine, 2.0 * cosine * sine
    return cosine, sine


def local_forward(retain, drive_re, drive_im, turn, summary):
    steps = retain.shape[0] // LANES
    cosine, sine = turn[0:1], turn[1:2]
    zero = jnp.zeros((LANES, retain.shape[1]), jnp.float32)

    def step(i, carry):
        real, imag, product = carry
        rows = pl.ds(pl.multiple_of(LANES * i, LANES), LANES)
        r = retain[rows, :]
        turned_re, turned_im = rotate(real, imag, cosine, sine)
        return r * turned_re + drive_re[rows, :], r * turned_im + drive_im[rows, :], r * product

    real, imag, product = lax.fori_loop(0, steps, step, (zero, zero, zero + 1.0), unroll=4)
    cos_sub, sin_sub = turn_power(cosine, sine, steps.bit_length() - 1)
    total_re, total_im, total = real[0:1], imag[0:1], product[0:1]
    for j in range(1, LANES):
        turned_re, turned_im = rotate(total_re, total_im, cos_sub, sin_sub)
        total_re = product[j : j + 1] * turned_re + real[j : j + 1]
        total_im = product[j : j + 1] * turned_im + imag[j : j + 1]
        total = product[j : j + 1] * total
    summary[0:LANES] = real
    summary[LANES : 2 * LANES] = imag
    summary[2 * LANES : 3 * LANES] = product
    summary[24:25] = total_re
    summary[25:26] = total_im
    summary[26:27] = total


def whole_forward(retain, drive_re, drive_im, turn, summary, start, states):
    steps = retain.shape[0] // LANES
    cosine, sine = turn[0:1], turn[1:2]
    cos_sub, sin_sub = turn_power(cosine, sine, steps.bit_length() - 1)
    now_re, now_im = start[0:1], start[1:2]
    reals, imags = [now_re], [now_im]
    for j in range(LANES - 1):
        turned_re, turned_im = rotate(now_re, now_im, cos_sub, sin_sub)
        product = summary[2 * LANES + j : 2 * LANES + j + 1]
        now_re = product * turned_re + summary[j : j + 1]
        now_im = product * turned_im + summary[LANES + j : LANES + j + 1]
        reals.append(now_re)
        imags.append(now_im)
    carry = (jnp.concatenate(reals, axis=0), jnp.concatenate(imags, axis=0))

    def step(i, carry):
        real, imag = carry
        rows = pl.ds(pl.multiple_of(LANES * i, LANES), LANES)
        states[0, rows, :] = real
        states[1, rows, :] = imag
        r = retain[rows, :]
        turned_re, turned_im = rotate(real, imag, cosine, sine)
        return r * turned_re + drive_re[rows, :], r * turned_im + drive_im[rows, :]

    real, imag = lax.fori_loop(0, steps, step, carry, unroll=4)
    states[0, LANES * steps :, :] = real
    states[1, LANES * steps :, :] = imag


def local_backward(retain, grad_re, grad_im, turn, summary):
    steps = retain.shape[0] // LANES
    cosine, sine = turn[0:1], -turn[1:2]
    zero = jnp.zeros((LANES, retain.shape[1]), jnp.float32)

    def step(k, carry):
        real, imag, product = carry
        rows = pl.ds(pl.multiple_of(LANES * (steps - 1 - k), LANES), LANES)
        r = retain[rows, :]
        turned_re, turned_im = rotate(grad_re[rows, :] + real, grad_im[rows, :] + imag, cosine, sine)
        return r * turned_re, r * turned_im, r * product

    real, imag, product = lax.fori_loop(0, steps, step, (zero, zero, zero + 1.0), unroll=4)
    cos_sub, sin_sub = turn_power(cosine, sine, steps.bit_length() - 1)
    last = LANES - 1
    total_re, total_im, total = real[last:], imag[last:], product[last:]
    for j in range(LANES - 2, -1, -1):
        turned_re, turned_im = rotate(total_re, total_im, cos_sub, sin_sub)
        total_re = product[j : j + 1] * turned_re + real[j : j + 1]
        total_im = product[j : j + 1] * turned_im + imag[j : j + 1]
        total = product[j : j + 1] * total
    summary[0:LANES] = real
    summary[LANES : 2 * LANES] = imag
    summary[2 * LANES : 3 * LANES] = product
    summary[24:25] = total_re
    summary[25:26] = total_im
    summary[26:27] = total


def whole_backward(
    retain, grad_re, grad_im, turn, summary, start, states, d_decay, d_in_re, d_in_im, d_phase
):
    steps = retain.shape[0] // LANES
    cosine, sine = turn[0:1], turn[1:2]
    cos_sub, sin_sub = turn_power(cosine, -sine, steps.bit_length() - 1)
    now_re, now_im = start[0:1], start[1:2]
    reals, imags = [now_re], [now_im]
    for j in range(LANES - 1, 0, -1):
        turned_re, turned_im = rotate(now_re, now_im, cos_sub, sin_sub)
        product = summary[2 * LANES + j : 2 * LANES + j + 1]
        now_re = product * turned_re + summary[j : j + 1]
        now_im = product * turned_im + summary[LANES + j : LANES + j + 1]
        reals.append(now_re)
        imags.append(now_im)
    zero = jnp.zeros((LANES, retain.shape[1]), jnp.float32)
    carry = (jnp.concatenate(reals[::-1], axis=0), jnp.concatenate(imags[::-1], axis=0), zero)

    def step(k, carry):
        real, imag, phase = carry
        rows = pl.ds(pl.multiple_of(LANES * (steps - 1 - k), LANES), LANES)
        r = retain[rows, :]
        real = grad_re[rows, :] + real
        imag = grad_im[rows, :] + imag
        prior_re, prior_im = rotate(states[0, rows, :], states[1, rows, :], cosine, sine)
        d_decay[rows, :] = -(real * prior_re + imag * prior_im)
        d_in_re[rows, :] = real
        d_in_im[rows, :] = imag
        phase = phase + r * (imag * prior_re - real * prior_im)
        turned_re, turned_im = rotate(real, imag, cosine, -sine)
        return r * turned_re, r * turned_im, phase

    _, _, phase = lax.fori_loop(0, steps, step, carry, unroll=4)
    d_phase[...] = jnp.sum(phase, axis=0, keepdims=True)


def stripe(rows):
    count, columns = rows.shape
    return rows.reshape(LANES, count // LANES, columns).swapaxes(0, 1).reshape(count, columns)


def unstripe(rows):
    count, columns = rows.shape
    return rows.reshape(count // LANES, LANES, columns).swapaxes(0, 1).reshape(count, columns)


def local_call(kernel, outs, *args):
    return pl.pallas_call(
        kernel,
        out_shape=[jax.ShapeDtypeStruct(shape, jnp.float32) for shape in outs],
        compiler_params=pltpu.CompilerParams(vmem_limit_bytes=32 * 1024 * 1024),
    )(*args)


def carry_in(summary, turn, length, reverse):
    every = lax.all_gather(summary[24:27], "dp", axis=0)
    cosine, sine = turn_power(
        turn[0], -turn[1] if reverse else turn[1], length.bit_length() - 1
    )
    count = every.shape[0]
    me = lax.axis_index("dp")
    real = jnp.zeros_like(cosine)
    imag = jnp.zeros_like(cosine)
    order = range(count - 1, 0, -1) if reverse else range(count - 1)
    for j in order:
        use = (j > me) if reverse else (j < me)
        turned_re, turned_im = rotate(real, imag, cosine, sine)
        real = jnp.where(use, every[j, 2] * turned_re + every[j, 0], real)
        imag = jnp.where(use, every[j, 2] * turned_im + every[j, 1], imag)
    return jnp.stack([real, imag])


def normalize(values, gains):
    scaling = lax.rsqrt(jnp.mean(values * values, axis=-1, keepdims=True) + NORM_EPSILON)
    return (values * scaling * gains, scaling)


def normalize_back(values, scaling, gains, gradient):
    scaled = gradient * gains
    return scaling * scaled - values * scaling**3 * jnp.mean(
        values * scaled, axis=-1, keepdims=True
    )


def silu_slope(values):
    logistic = jax.nn.sigmoid(values)
    return logistic * (1.0 + values * (1.0 - logistic))


def adam_update(master, gradient, first, second, steps, decay):
    first_new = BETA_ONE * first + (1.0 - BETA_ONE) * gradient
    second_new = BETA_TWO * second + (1.0 - BETA_TWO) * gradient * gradient
    corrected = (
        first_new
        / (1.0 - BETA_ONE**steps)
        / (jnp.sqrt(second_new / (1.0 - BETA_TWO**steps)) + ADAM_EPSILON)
    )
    change = -LEARN_RATE * (corrected + decay * master)
    return (master + change, first_new, second_new, change)


def body(
    tokens,
    cotangent,
    padding,
    opening,
    w_in,
    w_out,
    vectors,
    m_in,
    v_in,
    m_out,
    v_out,
    m_vec,
    v_vec,
    counter,
):
    low = jnp.bfloat16
    wide = jnp.float32
    mixer_cols = CH + 2 * D
    length = tokens.shape[1]
    inputs = stripe(tokens[0]).astype(wide)
    filled = stripe(padding[0][:, None]).astype(wide)
    starting = stripe(opening[0][:, None]) == 1
    gains_one = vectors[:D]
    gains_two = vectors[D : 2 * D]
    phases = vectors[2 * D : 2 * D + CH]
    biases = vectors[2 * D + CH :]
    turn = jnp.stack([jnp.cos(phases), jnp.sin(phases)])
    full_in = lax.all_gather(w_in.astype(low), ("dp", "rep"), axis=0, tiled=True)
    full_out = lax.all_gather(w_out.astype(low), ("dp", "rep"), axis=0, tiled=True)
    normed, scaling_one = normalize(inputs, gains_one)
    normed_low = normed.astype(low)
    pre_mix = jnp.dot(normed_low, full_in[:, :mixer_cols], preferred_element_type=wide)
    forget = jax.nn.sigmoid(-(pre_mix[:, :CH] + biases))
    driver_pre = pre_mix[:, CH : CH + D]
    driver = jax.nn.silu(driver_pre)
    gate_pre = pre_mix[:, CH + D :]
    forget_both = jnp.concatenate([forget, forget], axis=1)
    decay = jnp.where(starting, 1.0, forget).astype(low).astype(wide)
    retain = 1.0 - decay
    drive = (forget_both * driver).astype(low).astype(wide)
    drive_re, drive_im = drive[:, :CH], drive[:, CH:]
    summary = local_call(local_forward, [(32, CH)], retain, drive_re, drive_im, turn)[0]
    start = carry_in(summary, turn, length, False)
    states = local_call(
        whole_forward, [(2, length + 8, CH)], retain, drive_re, drive_im, turn, summary, start
    )[0]
    recurrent = jnp.concatenate([states[0, LANES:], states[1, LANES:]], axis=1)
    recurrent = recurrent.astype(low).astype(wide)
    gate_act = jax.nn.silu(gate_pre)
    masked = recurrent * filled
    gated_rows = (masked * gate_act).astype(low)
    middle = inputs + jnp.dot(gated_rows, full_out[:D], preferred_element_type=wide)
    normed_two, scaling_two = normalize(middle, gains_two)
    normed_two_low = normed_two.astype(low)
    glu_pre = jnp.dot(normed_two_low, full_in[:, mixer_cols:], preferred_element_type=wide)
    gate_glu = glu_pre[:, :FF]
    up_glu = glu_pre[:, FF:]
    hidden = (jax.nn.silu(gate_glu) * up_glu).astype(low)
    block_out = middle + jnp.dot(hidden, full_out[D:], preferred_element_type=wide)
    upstream = stripe(cotangent[0]).astype(wide) * filled
    upstream_low = upstream.astype(low)
    grad_down = jnp.einsum("tf,te->fe", hidden, upstream_low, preferred_element_type=wide)
    d_hidden = jnp.einsum("te,fe->tf", upstream_low, full_out[D:], preferred_element_type=wide)
    d_glu = jnp.concatenate(
        [d_hidden * up_glu * silu_slope(gate_glu), d_hidden * jax.nn.silu(gate_glu)], axis=1
    ).astype(low)
    grad_glu = jnp.einsum("td,tc->dc", normed_two_low, d_glu, preferred_element_type=wide)
    d_normed_two = jnp.einsum(
        "tc,dc->td", d_glu, full_in[:, mixer_cols:], preferred_element_type=wide
    )
    grad_gains_two = jnp.sum(d_normed_two * middle * scaling_two, axis=0)
    d_middle = upstream + normalize_back(middle, scaling_two, gains_two, d_normed_two)
    d_mixed_low = d_middle.astype(low)
    grad_mixer_out = jnp.einsum("td,te->de", gated_rows, d_mixed_low, preferred_element_type=wide)
    d_gated = jnp.einsum("te,de->td", d_mixed_low, full_out[:D], preferred_element_type=wide)
    d_recurrent = (d_gated * gate_act * filled).astype(low).astype(wide)
    d_gate_pre = d_gated * masked * silu_slope(gate_pre)
    grad_re, grad_im = d_recurrent[:, :CH], d_recurrent[:, CH:]
    summary_back = local_call(local_backward, [(32, CH)], retain, grad_re, grad_im, turn)[0]
    start_back = carry_in(summary_back, turn, length, True)
    d_decay, d_in_re, d_in_im, d_phase = local_call(
        whole_backward,
        [(length, CH)] * 3 + [(1, CH)],
        retain,
        grad_re,
        grad_im,
        turn,
        summary_back,
        start_back,
        states,
    )
    d_decay = d_decay.astype(low).astype(wide)
    d_input = jnp.concatenate([d_in_re, d_in_im], axis=1).astype(low).astype(wide)
    pulled = d_input * driver
    d_forget = jnp.where(starting, 0.0, d_decay) + pulled[:, :CH] + pulled[:, CH:]
    d_forget_pre = -forget * (1.0 - forget) * d_forget
    d_driver_pre = d_input * forget_both * silu_slope(driver_pre)
    d_mix = jnp.concatenate([d_forget_pre, d_driver_pre, d_gate_pre], axis=1).astype(low)
    grad_mixer_in = jnp.einsum("td,tc->dc", normed_low, d_mix, preferred_element_type=wide)
    d_normed = jnp.einsum(
        "tc,dc->td", d_mix, full_in[:, :mixer_cols], preferred_element_type=wide
    )
    grad_gains_one = jnp.sum(d_normed * inputs * scaling_one, axis=0)
    d_tokens = d_middle + normalize_back(inputs, scaling_one, gains_one, d_normed)
    grad_biases = jnp.sum(d_forget_pre, axis=0)
    grad_vectors = jnp.concatenate([grad_gains_one, grad_gains_two, d_phase[0], grad_biases])
    grad_in_all = jnp.concatenate([grad_mixer_in, grad_glu], axis=1)
    grad_out_all = jnp.concatenate([grad_mixer_out, grad_down], axis=0)
    summed_in, summed_out = (
        lax.psum_scatter(grad_in_all, ("dp", "rep"), scatter_dimension=0, tiled=True),
        lax.psum_scatter(grad_out_all, ("dp", "rep"), scatter_dimension=0, tiled=True),
    )
    summed_vec, total = lax.psum((grad_vectors, jnp.sum(filled)), ("dp", "rep"))
    steps = counter[0].astype(jnp.float32)
    grad_in = summed_in / total
    grad_out = summed_out / total
    grad_vec = summed_vec / total
    new_in, first_in, second_in, change_in = adam_update(
        w_in, grad_in, m_in, v_in, steps, WEIGHT_DECAY
    )
    new_out, first_out, second_out, change_out = adam_update(
        w_out, grad_out, m_out, v_out, steps, WEIGHT_DECAY
    )
    new_vec, first_vec, second_vec, update_vec = adam_update(
        vectors, grad_vec, m_vec, v_vec, steps, 0.0
    )
    return (
        unstripe(block_out.astype(jnp.bfloat16))[None],
        unstripe(d_tokens)[None],
        grad_in,
        new_in,
        first_in,
        second_in,
        new_in.astype(jnp.bfloat16),
        grad_out,
        new_out,
        first_out,
        second_out,
        new_out.astype(jnp.bfloat16),
        grad_vec,
        grad_vec[2 * D + CH :],
        update_vec,
        first_vec,
        second_vec,
    )


def solution(mesh):
    in_specs = (
        P("rep", "dp", None),
        P("rep", "dp", None),
        P("rep", "dp"),
        P("rep", "dp"),
        P(("dp", "rep"), None),
        P(("dp", "rep"), None),
        P(),
        P(("dp", "rep"), None),
        P(("dp", "rep"), None),
        P(("dp", "rep"), None),
        P(("dp", "rep"), None),
        P(),
        P(),
        P(),
    )
    out_specs = (
        P("rep", "dp", None),
        P("rep", "dp", None),
        P(("dp", "rep"), None),
        P(("dp", "rep"), None),
        P(("dp", "rep"), None),
        P(("dp", "rep"), None),
        P(("dp", "rep"), None),
        P(("dp", "rep"), None),
        P(("dp", "rep"), None),
        P(("dp", "rep"), None),
        P(("dp", "rep"), None),
        P(("dp", "rep"), None),
        P(),
        P(),
        P(),
        P(),
        P(),
    )
    return jax.shard_map(body, mesh=mesh, in_specs=in_specs, out_specs=out_specs, check_vma=False)
```

```python
import functools

import jax
import jax.numpy as jnp
from jax import lax
from jax.experimental import pallas as pl
from jax.experimental.pallas import tpu as pltpu
from jax.sharding import PartitionSpec as P

D = 768
CH = 384
FF = 1536


NORM_EPSILON = 1e-06
LEARN_RATE = 0.05
BETA_ONE = 0.9
BETA_TWO = 0.999
ADAM_EPSILON = 1e-08
WEIGHT_DECAY = 0.1


LANES = 8


def rotate(real, imag, cosine, sine):
    return cosine * real - sine * imag, sine * real + cosine * imag


def turn_power(cosine, sine, doublings):
    for _ in range(doublings):
        cosine, sine = cosine * cosine - sine * sine, 2.0 * cosine * sine
    return cosine, sine


def local_forward(retain, drive_re, drive_im, turn, summary):
    steps = retain.shape[0] // LANES
    cosine, sine = turn[0:1], turn[1:2]
    zero = jnp.zeros((LANES, retain.shape[1]), jnp.float32)

    def step(i, carry):
        real, imag, product = carry
        rows = pl.ds(pl.multiple_of(LANES * i, LANES), LANES)
        r = retain[rows, :]
        turned_re, turned_im = rotate(real, imag, cosine, sine)
        return r * turned_re + drive_re[rows, :], r * turned_im + drive_im[rows, :], r * product

    real, imag, product = lax.fori_loop(0, steps, step, (zero, zero, zero + 1.0), unroll=4)
    cos_sub, sin_sub = turn_power(cosine, sine, steps.bit_length() - 1)
    total_re, total_im, total = real[0:1], imag[0:1], product[0:1]
    for j in range(1, LANES):
        turned_re, turned_im = rotate(total_re, total_im, cos_sub, sin_sub)
        total_re = product[j : j + 1] * turned_re + real[j : j + 1]
        total_im = product[j : j + 1] * turned_im + imag[j : j + 1]
        total = product[j : j + 1] * total
    summary[0:LANES] = real
    summary[LANES : 2 * LANES] = imag
    summary[2 * LANES : 3 * LANES] = product
    summary[24:25] = total_re
    summary[25:26] = total_im
    summary[26:27] = total


def whole_forward(retain, drive_re, drive_im, turn, summary, start, states):
    steps = retain.shape[0] // LANES
    cosine, sine = turn[0:1], turn[1:2]
    cos_sub, sin_sub = turn_power(cosine, sine, steps.bit_length() - 1)
    now_re, now_im = start[0:1], start[1:2]
    reals, imags = [now_re], [now_im]
    for j in range(LANES - 1):
        turned_re, turned_im = rotate(now_re, now_im, cos_sub, sin_sub)
        product = summary[2 * LANES + j : 2 * LANES + j + 1]
        now_re = product * turned_re + summary[j : j + 1]
        now_im = product * turned_im + summary[LANES + j : LANES + j + 1]
        reals.append(now_re)
        imags.append(now_im)
    carry = (jnp.concatenate(reals, axis=0), jnp.concatenate(imags, axis=0))

    def step(i, carry):
        real, imag = carry
        rows = pl.ds(pl.multiple_of(LANES * i, LANES), LANES)
        states[0, rows, :] = real
        states[1, rows, :] = imag
        r = retain[rows, :]
        turned_re, turned_im = rotate(real, imag, cosine, sine)
        return r * turned_re + drive_re[rows, :], r * turned_im + drive_im[rows, :]

    real, imag = lax.fori_loop(0, steps, step, carry, unroll=4)
    states[0, LANES * steps :, :] = real
    states[1, LANES * steps :, :] = imag


def local_backward(retain, grad_re, grad_im, turn, summary):
    steps = retain.shape[0] // LANES
    cosine, sine = turn[0:1], -turn[1:2]
    zero = jnp.zeros((LANES, retain.shape[1]), jnp.float32)

    def step(k, carry):
        real, imag, product = carry
        rows = pl.ds(pl.multiple_of(LANES * (steps - 1 - k), LANES), LANES)
        r = retain[rows, :]
        turned_re, turned_im = rotate(grad_re[rows, :] + real, grad_im[rows, :] + imag, cosine, sine)
        return r * turned_re, r * turned_im, r * product

    real, imag, product = lax.fori_loop(0, steps, step, (zero, zero, zero + 1.0), unroll=4)
    cos_sub, sin_sub = turn_power(cosine, sine, steps.bit_length() - 1)
    last = LANES - 1
    total_re, total_im, total = real[last:], imag[last:], product[last:]
    for j in range(LANES - 2, -1, -1):
        turned_re, turned_im = rotate(total_re, total_im, cos_sub, sin_sub)
        total_re = product[j : j + 1] * turned_re + real[j : j + 1]
        total_im = product[j : j + 1] * turned_im + imag[j : j + 1]
        total = product[j : j + 1] * total
    summary[0:LANES] = real
    summary[LANES : 2 * LANES] = imag
    summary[2 * LANES : 3 * LANES] = product
    summary[24:25] = total_re
    summary[25:26] = total_im
    summary[26:27] = total


def whole_backward(
    retain, grad_re, grad_im, turn, summary, start, states, d_decay, d_in_re, d_in_im, d_phase
):
    steps = retain.shape[0] // LANES
    cosine, sine = turn[0:1], turn[1:2]
    cos_sub, sin_sub = turn_power(cosine, -sine, steps.bit_length() - 1)
    now_re, now_im = start[0:1], start[1:2]
    reals, imags = [now_re], [now_im]
    for j in range(LANES - 1, 0, -1):
        turned_re, turned_im = rotate(now_re, now_im, cos_sub, sin_sub)
        product = summary[2 * LANES + j : 2 * LANES + j + 1]
        now_re = product * turned_re + summary[j : j + 1]
        now_im = product * turned_im + summary[LANES + j : LANES + j + 1]
        reals.append(now_re)
        imags.append(now_im)
    zero = jnp.zeros((LANES, retain.shape[1]), jnp.float32)
    carry = (jnp.concatenate(reals[::-1], axis=0), jnp.concatenate(imags[::-1], axis=0), zero)

    def step(k, carry):
        real, imag, phase = carry
        rows = pl.ds(pl.multiple_of(LANES * (steps - 1 - k), LANES), LANES)
        r = retain[rows, :]
        real = grad_re[rows, :] + real
        imag = grad_im[rows, :] + imag
        prior_re, prior_im = rotate(states[0, rows, :], states[1, rows, :], cosine, sine)
        d_decay[rows, :] = -(real * prior_re + imag * prior_im)
        d_in_re[rows, :] = real
        d_in_im[rows, :] = imag
        phase = phase + r * (imag * prior_re - real * prior_im)
        turned_re, turned_im = rotate(real, imag, cosine, -sine)
        return r * turned_re, r * turned_im, phase

    _, _, phase = lax.fori_loop(0, steps, step, carry, unroll=4)
    d_phase[...] = jnp.sum(phase, axis=0, keepdims=True)


def stripe(rows):
    count, columns = rows.shape
    return rows.reshape(LANES, count // LANES, columns).swapaxes(0, 1).reshape(count, columns)


def unstripe(rows):
    count, columns = rows.shape
    return rows.reshape(count // LANES, LANES, columns).swapaxes(0, 1).reshape(count, columns)


def local_call(kernel, outs, *args):
    return pl.pallas_call(
        kernel,
        out_shape=[jax.ShapeDtypeStruct(shape, jnp.float32) for shape in outs],
        compiler_params=pltpu.CompilerParams(vmem_limit_bytes=32 * 1024 * 1024),
    )(*args)


def carry_in(summary, turn, length, reverse):
    every = lax.all_gather(summary[24:27], "dp", axis=0)
    cosine, sine = turn_power(
        turn[0], -turn[1] if reverse else turn[1], length.bit_length() - 1
    )
    count = every.shape[0]
    me = lax.axis_index("dp")
    real = jnp.zeros_like(cosine)
    imag = jnp.zeros_like(cosine)
    order = range(count - 1, 0, -1) if reverse else range(count - 1)
    for j in order:
        use = (j > me) if reverse else (j < me)
        turned_re, turned_im = rotate(real, imag, cosine, sine)
        real = jnp.where(use, every[j, 2] * turned_re + every[j, 0], real)
        imag = jnp.where(use, every[j, 2] * turned_im + every[j, 1], imag)
    return jnp.stack([real, imag])


def normalize(values, gains):
    scaling = lax.rsqrt(jnp.mean(values * values, axis=-1, keepdims=True) + NORM_EPSILON)
    return (values * scaling * gains, scaling)


def normalize_back(values, scaling, gains, gradient):
    scaled = gradient * gains
    return scaling * scaled - values * scaling**3 * jnp.mean(
        values * scaled, axis=-1, keepdims=True
    )


def silu_slope(values):
    logistic = jax.nn.sigmoid(values)
    return logistic * (1.0 + values * (1.0 - logistic))


def adam_update(master, gradient, first, second, steps, decay):
    first_new = BETA_ONE * first + (1.0 - BETA_ONE) * gradient
    second_new = BETA_TWO * second + (1.0 - BETA_TWO) * gradient * gradient
    corrected = (
        first_new
        / (1.0 - BETA_ONE**steps)
        / (jnp.sqrt(second_new / (1.0 - BETA_TWO**steps)) + ADAM_EPSILON)
    )
    change = -LEARN_RATE * (corrected + decay * master)
    return (master + change, first_new, second_new, change)


MESH = pl.DeviceIdType.MESH
LOW = jnp.bfloat16
WIDE = jnp.float32
PLANES = 4
SIDE = 2
IN_ROWS = 24
OUT_ROWS = 72
MIX = CH + 2 * D
MIX_HALF = 1024
TILE = 128
VMEM_BYTES = 60 * 1024 * 1024


class Piece:
    def __init__(self, matrix, rows, columns, starts, overlap=0):
        self.matrix, self.rows, self.columns = matrix, rows, columns
        self.starts, self.overlap = starts, overlap

    def shape(self):
        return (2, PLANES, SIDE, SIDE, 2 * self.rows, self.columns)


def piece_list():
    half = MIX_HALF // 2
    second = MIX - MIX_HALF
    mix = [
        Piece("in", IN_ROWS, half, (0, second), TILE),
        Piece("in", IN_ROWS, half, (half, second + half)),
    ]
    out = [Piece("out", OUT_ROWS, D // 2, (0, D // 2))]
    wide = FF // 4
    glu = [
        Piece("in", IN_ROWS, wide, (MIX + wide * k, MIX + FF + wide * k)) for k in range(4)
    ]
    return mix + out + glu


PIECES = piece_list()


class Place:
    def __init__(self):
        dp, rep = lax.axis_index("dp"), lax.axis_index("rep")
        self.z, self.x = dp // SIDE, dp % SIDE
        self.y, self.core = rep // 2, rep % 2

    def at(self, z, x, y, core):
        return (z * SIDE + x, y * 2 + core)

    def sibling(self):
        return self.at(self.z, self.x, self.y, 1 - self.core)

    def plane(self, z):
        return self.at(z, self.x, self.y, self.core)

    def near(self, core):
        if core == 0:
            return self.at(self.z, 1 - self.x, self.y, self.core)
        return self.at(self.z, self.x, 1 - self.y, self.core)

    def far(self, core):
        return self.near(1 - core)

    def turn(self, step):
        return lax.rem(self.z + step, PLANES)

    def sides(self, core):
        return (self.x, self.y) if core == 0 else (self.y, self.x)

    def by_core(self, run):
        for core in range(2):
            pl.when(self.core == core)(functools.partial(run, core))

    def greet(self):
        barrier = pltpu.get_barrier_semaphore()
        partners = [self.sibling(), self.near(0), self.near(1)]
        partners += [self.plane(self.turn(step)) for step in (1, 2, 3)]
        for partner in partners:
            pl.semaphore_signal(barrier, inc=1, device_id=partner, device_id_type=MESH)
        return lambda: pl.semaphore_wait(barrier, len(partners))


def block_of(ref, core, z, near, far):
    return ref.at[core, z, near, far] if core == 0 else ref.at[core, z, far, near]


def pair_of(ref, core, z, far):
    return ref.at[core, z, :, far] if core == 0 else ref.at[core, z, far]


def remote(source, target, sent, received, device):
    return pltpu.make_async_remote_copy(
        src_ref=source,
        dst_ref=target,
        send_sem=sent,
        recv_sem=received,
        device_id=device,
        device_id_type=MESH,
    )


GATHER_SEMS = 4 * 2
STEPS_AWAY = (1, 3, 2)


class Gather:
    def __init__(self, place, masters, buffers, staging, sems):
        self.place, self.masters, self.buffers, self.staging = place, masters, buffers, staging
        self.local, self.sent0, self.got0 = sems[:3]
        self.sems = sems[3:]

    @staticmethod
    def scratch():
        n = len(PIECES)
        dma = pltpu.SemaphoreType.DMA
        return (
            [pltpu.VMEM(p.shape(), LOW) for p in PIECES]
            + [pltpu.VMEM((2 * p.rows, p.columns), WIDE) for p in PIECES]
            + [dma((n,))] * 3
            + [dma((n, PLANES))] * GATHER_SEMS
        )

    def part(self, p, half):
        piece = PIECES[p]
        start = piece.starts[0] + half * (piece.starts[1] - piece.starts[0])
        return self.masters[piece.matrix].at[:, pl.ds(pl.multiple_of(start, TILE), piece.columns)]

    def own_rows(self, p):
        rows = PIECES[p].rows
        return self.staging[p].at[pl.ds(pl.multiple_of(self.place.core * rows, 8), rows)]

    def to_sibling(self, p):
        return remote(
            self.part(p, 1 - self.place.core),
            self.own_rows(p),
            self.sent0.at[p],
            self.got0.at[p],
            self.place.sibling(),
        )

    def to_self(self, p):
        return pltpu.make_async_copy(
            self.part(p, self.place.core), self.own_rows(p), self.local.at[p]
        )

    def along_z(self, p, z, target):
        place = self.place
        block = self.buffers[p].at[place.core, z, place.x, place.y]
        return remote(
            block, block, self.sems[0].at[p, target], self.sems[1].at[p, z], place.plane(target)
        )

    def along_near(self, p, z, core):
        block = block_of(self.buffers[p], core, z, *self.place.sides(core))
        return remote(
            block, block, self.sems[2].at[p, z], self.sems[3].at[p, z], self.place.near(core)
        )

    def along_far(self, p, z, core):
        pair = pair_of(self.buffers[p], core, z, self.place.sides(core)[1])
        return remote(
            pair, pair, self.sems[4].at[p, z], self.sems[5].at[p, z], self.place.far(core)
        )

    def in_chip(self, p, z, core):
        plane = self.buffers[p].at[core, z]
        return remote(
            plane, plane, self.sems[6].at[p, z], self.sems[7].at[p, z], self.place.sibling()
        )

    def begin(self):
        for p in range(len(PIECES)):
            self.to_sibling(p).start()
            self.to_self(p).start()

    def stage0(self, p):
        place = self.place
        self.to_self(p).wait()
        self.to_sibling(p).wait_recv()
        self.buffers[p][place.core, place.z, place.x, place.y] = self.staging[p][...].astype(LOW)
        for step in STEPS_AWAY:
            self.along_z(p, place.z, place.turn(step)).start()
        place.by_core(lambda core: self.along_near(p, place.z, core).start())

    def stage1(self, p):
        place = self.place
        for step in STEPS_AWAY:
            z = place.turn(step)
            self.along_z(p, z, place.z).wait_recv()
            place.by_core(lambda core: self.along_near(p, z, core).start())

    def stage2(self, p):
        def run(core):
            for step in (0,) + STEPS_AWAY:
                z = self.place.turn(step)
                self.along_near(p, z, core).wait_recv()
                self.along_far(p, z, core).start()

        self.place.by_core(run)

    def stage3(self, p):
        def run(core):
            for step in (0,) + STEPS_AWAY:
                z = self.place.turn(step)
                self.along_far(p, z, core).wait_recv()
                self.in_chip(p, z, core).start()

        self.place.by_core(run)

    def stage4(self, p):
        for step in (0,) + STEPS_AWAY:
            z = self.place.turn(step)
            self.in_chip(p, z, 1 - self.place.core).wait_recv()

    def drain(self, p):
        self.to_sibling(p).wait_send()
        for step in STEPS_AWAY:
            self.along_z(p, self.place.z, self.place.turn(step)).wait_send()

        def run(core):
            for z in range(PLANES):
                self.along_near(p, z, core).wait_send()
                self.along_far(p, z, core).wait_send()
                self.in_chip(p, z, core).wait_send()

        self.place.by_core(run)


class Reduce:
    ORDER = STEPS_AWAY + (0,)

    def __init__(self, place, grads, refs, results):
        n = len(PIECES)
        self.place, self.grads, self.results = place, grads, results
        self.chip, self.far, self.near, self.planes, self.final = (
            refs[k * n : (k + 1) * n] for k in range(5)
        )
        self.sems = refs[5 * n :]

    @staticmethod
    def scratch():
        n = len(PIECES)
        dma = pltpu.SemaphoreType.DMA
        shapes = [p.shape() for p in PIECES]
        return (
            [pltpu.VMEM(s[1:], LOW) for s in shapes]
            + [pltpu.VMEM((PLANES, SIDE) + s[4:], LOW) for s in shapes]
            + [pltpu.VMEM((PLANES,) + s[4:], LOW) for s in shapes] * 2
            + [pltpu.VMEM(s[4:], WIDE) for s in shapes]
            + [dma((n, PLANES))] * 8
            + [dma((n,))] * 2
        )

    def in_chip(self, p, z, core):
        return remote(
            self.grads[p].at[1 - core, z],
            self.chip[p].at[z],
            self.sems[0].at[p, z],
            self.sems[1].at[p, z],
            self.place.sibling(),
        )

    def along_far(self, p, z, core):
        return remote(
            pair_of(self.grads[p], core, z, 1 - self.place.sides(core)[1]),
            self.far[p].at[z],
            self.sems[2].at[p, z],
            self.sems[3].at[p, z],
            self.place.far(core),
        )

    def along_near(self, p, z, core):
        near, far = self.place.sides(core)
        return remote(
            block_of(self.grads[p], core, z, 1 - near, far),
            self.near[p].at[z],
            self.sems[4].at[p, z],
            self.sems[5].at[p, z],
            self.place.near(core),
        )

    def along_z(self, p, z, sender, core):
        return remote(
            block_of(self.grads[p], core, z, *self.place.sides(core)),
            self.planes[p].at[sender],
            self.sems[6].at[p, z],
            self.sems[7].at[p, sender],
            self.place.plane(z),
        )

    def result(self, p, core):
        piece = PIECES[p]
        skip = piece.overlap * core
        start, width = piece.starts[core] + skip, piece.columns - skip
        return self.results[piece.matrix].at[:, pl.ds(start, width)], pl.ds(skip, width)

    def to_sibling(self, p, core):
        rows = PIECES[p].rows
        target, columns = self.result(p, core)
        return remote(
            self.final[p].at[pl.ds(rows * (1 - core), rows), columns],
            target,
            self.sems[8].at[p],
            self.sems[9].at[p],
            self.place.sibling(),
        )

    @staticmethod
    def add(target, source):
        target[...] = (target[...].astype(WIDE) + source[...].astype(WIDE)).astype(LOW)

    def stage0(self, p):
        def run(core):
            for step in self.ORDER:
                self.in_chip(p, self.place.turn(step), core).start()

        self.place.by_core(run)

    def stage1(self, p):
        def run(core):
            for step in self.ORDER:
                z = self.place.turn(step)
                self.in_chip(p, z, core).wait_recv()
                self.add(self.grads[p].at[core, z], self.chip[p].at[z])
                self.along_far(p, z, core).start()

        self.place.by_core(run)

    def stage2(self, p):
        def run(core):
            for step in self.ORDER:
                z = self.place.turn(step)
                self.along_far(p, z, core).wait_recv()
                own = pair_of(self.grads[p], core, z, self.place.sides(core)[1])
                self.add(own, self.far[p].at[z])
                self.along_near(p, z, core).start()

        self.place.by_core(run)

    def stage3(self, p):
        def run(core):
            for step in self.ORDER:
                z = self.place.turn(step)
                self.along_near(p, z, core).wait_recv()
                own = block_of(self.grads[p], core, z, *self.place.sides(core))
                self.add(own, self.near[p].at[z])
                if step:
                    self.along_z(p, z, self.place.z, core).start()

        self.place.by_core(run)

    def stage4(self, p):
        rows = PIECES[p].rows

        def run(core):
            z = self.place.z
            for step in STEPS_AWAY:
                self.along_z(p, z, self.place.turn(step), core).wait_recv()
            total = block_of(self.grads[p], core, z, *self.place.sides(core))[...].astype(WIDE)
            for step in STEPS_AWAY:
                total = total + self.planes[p][self.place.turn(step)].astype(WIDE)
            self.final[p][...] = total
            self.to_sibling(p, core).start()
            target, columns = self.result(p, core)
            target[...] = self.final[p][pl.ds(rows * core, rows), columns]

        self.place.by_core(run)

    def drain(self, p):
        def run(core):
            self.to_sibling(p, 1 - core).wait_recv()
            self.to_sibling(p, core).wait_send()
            for step in self.ORDER:
                z = self.place.turn(step)
                self.in_chip(p, z, core).wait_send()
                self.along_far(p, z, core).wait_send()
                self.along_near(p, z, core).wait_send()
                if step:
                    self.along_z(p, z, self.place.z, core).wait_send()

        self.place.by_core(run)


def stagger(stages, count):
    for tick in range(count + len(stages) - 1):
        for lag, stage in enumerate(stages):
            if 0 <= tick - lag < count:
                stage(tick - lag)


def gather_kernel(w_in, w_out, *refs):
    n = len(PIECES)
    results, (buffers, staging, rest) = refs[:n], (refs[n : 2 * n], refs[2 * n : 3 * n], refs[3 * n :])
    done, sems = rest[-1], rest[:-1]
    place = Place()
    gather = Gather(place, {"in": w_in, "out": w_out}, buffers, staging, sems)
    place.greet()()
    gather.begin()
    stagger([gather.stage0, gather.stage1, gather.stage2, gather.stage3, gather.stage4], n)
    copies = [pltpu.make_async_copy(buffers[p], results[p], done.at[p]) for p in range(n)]
    for copy in copies:
        copy.start()
    for p in range(n):
        gather.drain(p)
    for copy in copies:
        copy.wait()


def gather_call(w_in, w_out):
    n = len(PIECES)
    anywhere = pl.BlockSpec(memory_space=pl.ANY)
    return pl.pallas_call(
        gather_kernel,
        out_shape=[jax.ShapeDtypeStruct(p.shape(), LOW) for p in PIECES],
        in_specs=[anywhere] * 2,
        out_specs=[anywhere] * n,
        scratch_shapes=Gather.scratch() + [pltpu.SemaphoreType.DMA((n,))],
        compiler_params=pltpu.CompilerParams(
            collective_id=0, has_side_effects=True, vmem_limit_bytes=VMEM_BYTES
        ),
    )(w_in, w_out)


def reduce_kernel(*refs):
    n = len(PIECES)
    sources, results, grads = refs[:n], refs[n : n + 2], refs[n + 2 : 2 * n + 2]
    loaded, rest = refs[2 * n + 2], refs[2 * n + 3 :]
    place = Place()
    reduce = Reduce(place, grads, rest, {"in": results[0], "out": results[1]})
    entered = place.greet()
    copies = [pltpu.make_async_copy(sources[p], grads[p], loaded.at[p]) for p in range(n)]
    for copy in copies:
        copy.start()
    entered()
    for copy in copies:
        copy.wait()
    stagger([reduce.stage0, reduce.stage1, reduce.stage2, reduce.stage3, reduce.stage4], n)
    for p in range(n):
        reduce.drain(p)


def reduce_call(pieces):
    n = len(PIECES)
    return pl.pallas_call(
        reduce_kernel,
        out_shape=[
            jax.ShapeDtypeStruct((IN_ROWS, MIX + 2 * FF), WIDE),
            jax.ShapeDtypeStruct((OUT_ROWS, D), WIDE),
        ],
        in_specs=[pl.BlockSpec(memory_space=pl.ANY)] * n,
        out_specs=[pl.BlockSpec(memory_space=pltpu.VMEM)] * 2,
        scratch_shapes=[pltpu.VMEM(p.shape(), LOW) for p in PIECES]
        + [pltpu.SemaphoreType.DMA((n,))]
        + Reduce.scratch(),
        compiler_params=pltpu.CompilerParams(
            collective_id=1, has_side_effects=True, vmem_limit_bytes=VMEM_BYTES
        ),
    )(*pieces)


def routed(w_in, w_out):
    sizes = (lax.axis_size("dp"), lax.axis_size("rep"))
    return sizes == (PLANES * SIDE, SIDE * 2) and (w_in.shape[0], w_out.shape[0]) == (
        IN_ROWS,
        OUT_ROWS,
    )


def gather_weights(w_in, w_out):
    if not routed(w_in, w_out):
        axes = ("dp", "rep")
        return (
            lax.all_gather(w_in.astype(LOW), axes, axis=0, tiled=True),
            lax.all_gather(w_out.astype(LOW), axes, axis=0, tiled=True),
        )
    got = gather_call(w_in, w_out)
    parts = [[g[half].reshape(-1, g.shape[-1]) for g in got] for half in range(2)]
    mix = parts[0][:2] + [parts[1][0][:, TILE:], parts[1][1]]
    full_in = jnp.concatenate(mix + parts[0][3:] + parts[1][3:], axis=1)
    return full_in, jnp.concatenate([parts[0][2], parts[1][2]], axis=1)


def reduce_grads(grad_in, grad_out, shard_in, shard_out):
    if not routed(shard_in, shard_out):
        axes = ("dp", "rep")
        return (
            lax.psum_scatter(grad_in, axes, scatter_dimension=0, tiled=True),
            lax.psum_scatter(grad_out, axes, scatter_dimension=0, tiled=True),
        )
    whole = {"in": grad_in.astype(LOW), "out": grad_out.astype(LOW)}
    pieces = []
    for piece in PIECES:
        halves = [
            whole[piece.matrix][:, start : start + piece.columns].reshape(piece.shape()[1:])
            for start in piece.starts
        ]
        pieces.append(jnp.stack(halves))
    return reduce_call(pieces)


def body(
    tokens,
    cotangent,
    padding,
    opening,
    w_in,
    w_out,
    vectors,
    m_in,
    v_in,
    m_out,
    v_out,
    m_vec,
    v_vec,
    counter,
):
    low = jnp.bfloat16
    wide = jnp.float32
    mixer_cols = CH + 2 * D
    length = tokens.shape[1]
    inputs = stripe(tokens[0]).astype(wide)
    filled = stripe(padding[0][:, None]).astype(wide)
    starting = stripe(opening[0][:, None]) == 1
    gains_one = vectors[:D]
    gains_two = vectors[D : 2 * D]
    phases = vectors[2 * D : 2 * D + CH]
    biases = vectors[2 * D + CH :]
    turn = jnp.stack([jnp.cos(phases), jnp.sin(phases)])
    full_in, full_out = gather_weights(w_in, w_out)
    normed, scaling_one = normalize(inputs, gains_one)
    normed_low = normed.astype(low)
    pre_mix = jnp.dot(normed_low, full_in[:, :mixer_cols], preferred_element_type=wide)
    forget = jax.nn.sigmoid(-(pre_mix[:, :CH] + biases))
    driver_pre = pre_mix[:, CH : CH + D]
    driver = jax.nn.silu(driver_pre)
    gate_pre = pre_mix[:, CH + D :]
    forget_both = jnp.concatenate([forget, forget], axis=1)
    decay = jnp.where(starting, 1.0, forget).astype(low).astype(wide)
    retain = 1.0 - decay
    drive = (forget_both * driver).astype(low).astype(wide)
    drive_re, drive_im = drive[:, :CH], drive[:, CH:]
    summary = local_call(local_forward, [(32, CH)], retain, drive_re, drive_im, turn)[0]
    start = carry_in(summary, turn, length, False)
    states = local_call(
        whole_forward, [(2, length + 8, CH)], retain, drive_re, drive_im, turn, summary, start
    )[0]
    recurrent = jnp.concatenate([states[0, LANES:], states[1, LANES:]], axis=1)
    recurrent = recurrent.astype(low).astype(wide)
    gate_act = jax.nn.silu(gate_pre)
    masked = recurrent * filled
    gated_rows = (masked * gate_act).astype(low)
    middle = inputs + jnp.dot(gated_rows, full_out[:D], preferred_element_type=wide)
    normed_two, scaling_two = normalize(middle, gains_two)
    normed_two_low = normed_two.astype(low)
    glu_pre = jnp.dot(normed_two_low, full_in[:, mixer_cols:], preferred_element_type=wide)
    gate_glu = glu_pre[:, :FF]
    up_glu = glu_pre[:, FF:]
    hidden = (jax.nn.silu(gate_glu) * up_glu).astype(low)
    block_out = middle + jnp.dot(hidden, full_out[D:], preferred_element_type=wide)
    upstream = stripe(cotangent[0]).astype(wide) * filled
    upstream_low = upstream.astype(low)
    grad_down = jnp.einsum("tf,te->fe", hidden, upstream_low, preferred_element_type=wide)
    d_hidden = jnp.einsum("te,fe->tf", upstream_low, full_out[D:], preferred_element_type=wide)
    d_glu = jnp.concatenate(
        [d_hidden * up_glu * silu_slope(gate_glu), d_hidden * jax.nn.silu(gate_glu)], axis=1
    ).astype(low)
    grad_glu = jnp.einsum("td,tc->dc", normed_two_low, d_glu, preferred_element_type=wide)
    d_normed_two = jnp.einsum(
        "tc,dc->td", d_glu, full_in[:, mixer_cols:], preferred_element_type=wide
    )
    grad_gains_two = jnp.sum(d_normed_two * middle * scaling_two, axis=0)
    d_middle = upstream + normalize_back(middle, scaling_two, gains_two, d_normed_two)
    d_mixed_low = d_middle.astype(low)
    grad_mixer_out = jnp.einsum("td,te->de", gated_rows, d_mixed_low, preferred_element_type=wide)
    d_gated = jnp.einsum("te,de->td", d_mixed_low, full_out[:D], preferred_element_type=wide)
    d_recurrent = (d_gated * gate_act * filled).astype(low).astype(wide)
    d_gate_pre = d_gated * masked * silu_slope(gate_pre)
    grad_re, grad_im = d_recurrent[:, :CH], d_recurrent[:, CH:]
    summary_back = local_call(local_backward, [(32, CH)], retain, grad_re, grad_im, turn)[0]
    start_back = carry_in(summary_back, turn, length, True)
    d_decay, d_in_re, d_in_im, d_phase = local_call(
        whole_backward,
        [(length, CH)] * 3 + [(1, CH)],
        retain,
        grad_re,
        grad_im,
        turn,
        summary_back,
        start_back,
        states,
    )
    d_decay = d_decay.astype(low).astype(wide)
    d_input = jnp.concatenate([d_in_re, d_in_im], axis=1).astype(low).astype(wide)
    pulled = d_input * driver
    d_forget = jnp.where(starting, 0.0, d_decay) + pulled[:, :CH] + pulled[:, CH:]
    d_forget_pre = -forget * (1.0 - forget) * d_forget
    d_driver_pre = d_input * forget_both * silu_slope(driver_pre)
    d_mix = jnp.concatenate([d_forget_pre, d_driver_pre, d_gate_pre], axis=1).astype(low)
    grad_mixer_in = jnp.einsum("td,tc->dc", normed_low, d_mix, preferred_element_type=wide)
    d_normed = jnp.einsum(
        "tc,dc->td", d_mix, full_in[:, :mixer_cols], preferred_element_type=wide
    )
    grad_gains_one = jnp.sum(d_normed * inputs * scaling_one, axis=0)
    d_tokens = d_middle + normalize_back(inputs, scaling_one, gains_one, d_normed)
    grad_biases = jnp.sum(d_forget_pre, axis=0)
    grad_vectors = jnp.concatenate([grad_gains_one, grad_gains_two, d_phase[0], grad_biases])
    grad_in_all = jnp.concatenate([grad_mixer_in, grad_glu], axis=1)
    grad_out_all = jnp.concatenate([grad_mixer_out, grad_down], axis=0)
    summed_in, summed_out = reduce_grads(grad_in_all, grad_out_all, w_in, w_out)
    summed_vec, total = lax.psum((grad_vectors, jnp.sum(filled)), ("dp", "rep"))
    steps = counter[0].astype(jnp.float32)
    grad_in = summed_in / total
    grad_out = summed_out / total
    grad_vec = summed_vec / total
    new_in, first_in, second_in, change_in = adam_update(
        w_in, grad_in, m_in, v_in, steps, WEIGHT_DECAY
    )
    new_out, first_out, second_out, change_out = adam_update(
        w_out, grad_out, m_out, v_out, steps, WEIGHT_DECAY
    )
    new_vec, first_vec, second_vec, update_vec = adam_update(
        vectors, grad_vec, m_vec, v_vec, steps, 0.0
    )
    return (
        unstripe(block_out.astype(jnp.bfloat16))[None],
        unstripe(d_tokens)[None],
        grad_in,
        new_in,
        first_in,
        second_in,
        new_in.astype(jnp.bfloat16),
        grad_out,
        new_out,
        first_out,
        second_out,
        new_out.astype(jnp.bfloat16),
        grad_vec,
        grad_vec[2 * D + CH :],
        update_vec,
        first_vec,
        second_vec,
    )


def solution(mesh):
    in_specs = (
        P("rep", "dp", None),
        P("rep", "dp", None),
        P("rep", "dp"),
        P("rep", "dp"),
        P(("dp", "rep"), None),
        P(("dp", "rep"), None),
        P(),
        P(("dp", "rep"), None),
        P(("dp", "rep"), None),
        P(("dp", "rep"), None),
        P(("dp", "rep"), None),
        P(),
        P(),
        P(),
    )
    out_specs = (
        P("rep", "dp", None),
        P("rep", "dp", None),
        P(("dp", "rep"), None),
        P(("dp", "rep"), None),
        P(("dp", "rep"), None),
        P(("dp", "rep"), None),
        P(("dp", "rep"), None),
        P(("dp", "rep"), None),
        P(("dp", "rep"), None),
        P(("dp", "rep"), None),
        P(("dp", "rep"), None),
        P(("dp", "rep"), None),
        P(),
        P(),
        P(),
        P(),
        P(),
    )
    return jax.shard_map(body, mesh=mesh, in_specs=in_specs, out_specs=out_specs, check_vma=False)
```

```python
import functools

import jax
import jax.numpy as jnp
from jax import lax
from jax.experimental import pallas as pl
from jax.experimental.pallas import tpu as pltpu
from jax.sharding import PartitionSpec as P

D = 768
CH = 384
FF = 1536


NORM_EPSILON = 1e-06
LEARN_RATE = 0.05
BETA_ONE = 0.9
BETA_TWO = 0.999
ADAM_EPSILON = 1e-08
WEIGHT_DECAY = 0.1


LANES = 8


def rotate(real, imag, cosine, sine):
    return cosine * real - sine * imag, sine * real + cosine * imag


def turn_power(cosine, sine, doublings):
    for _ in range(doublings):
        cosine, sine = cosine * cosine - sine * sine, 2.0 * cosine * sine
    return cosine, sine


def local_forward(retain, drive_re, drive_im, turn, summary):
    steps = retain.shape[0] // LANES
    cosine, sine = turn[0:1], turn[1:2]
    zero = jnp.zeros((LANES, retain.shape[1]), jnp.float32)

    def step(i, carry):
        real, imag, product = carry
        rows = pl.ds(pl.multiple_of(LANES * i, LANES), LANES)
        r = retain[rows, :]
        turned_re, turned_im = rotate(real, imag, cosine, sine)
        return r * turned_re + drive_re[rows, :], r * turned_im + drive_im[rows, :], r * product

    real, imag, product = lax.fori_loop(0, steps, step, (zero, zero, zero + 1.0), unroll=4)
    cos_sub, sin_sub = turn_power(cosine, sine, steps.bit_length() - 1)
    total_re, total_im, total = real[0:1], imag[0:1], product[0:1]
    for j in range(1, LANES):
        turned_re, turned_im = rotate(total_re, total_im, cos_sub, sin_sub)
        total_re = product[j : j + 1] * turned_re + real[j : j + 1]
        total_im = product[j : j + 1] * turned_im + imag[j : j + 1]
        total = product[j : j + 1] * total
    summary[0:LANES] = real
    summary[LANES : 2 * LANES] = imag
    summary[2 * LANES : 3 * LANES] = product
    summary[24:32] = jnp.concatenate([total_re, total_im, total, zero[3:]], axis=0)


def whole_forward(retain, drive_re, drive_im, turn, summary, start, states):
    steps = retain.shape[0] // LANES
    cosine, sine = turn[0:1], turn[1:2]
    cos_sub, sin_sub = turn_power(cosine, sine, steps.bit_length() - 1)
    now_re, now_im = start[0:1], start[1:2]
    reals, imags = [now_re], [now_im]
    for j in range(LANES - 1):
        turned_re, turned_im = rotate(now_re, now_im, cos_sub, sin_sub)
        product = summary[2 * LANES + j : 2 * LANES + j + 1]
        now_re = product * turned_re + summary[j : j + 1]
        now_im = product * turned_im + summary[LANES + j : LANES + j + 1]
        reals.append(now_re)
        imags.append(now_im)
    carry = (jnp.concatenate(reals, axis=0), jnp.concatenate(imags, axis=0))

    def step(i, carry):
        real, imag = carry
        rows = pl.ds(pl.multiple_of(LANES * i, LANES), LANES)
        states[0, rows, :] = real
        states[1, rows, :] = imag
        r = retain[rows, :]
        turned_re, turned_im = rotate(real, imag, cosine, sine)
        return r * turned_re + drive_re[rows, :], r * turned_im + drive_im[rows, :]

    real, imag = lax.fori_loop(0, steps, step, carry, unroll=4)
    states[0, LANES * steps :, :] = real
    states[1, LANES * steps :, :] = imag


def local_backward(retain, grad_re, grad_im, turn, summary):
    steps = retain.shape[0] // LANES
    cosine, sine = turn[0:1], -turn[1:2]
    zero = jnp.zeros((LANES, retain.shape[1]), jnp.float32)

    def step(k, carry):
        real, imag, product = carry
        rows = pl.ds(pl.multiple_of(LANES * (steps - 1 - k), LANES), LANES)
        r = retain[rows, :]
        turned_re, turned_im = rotate(grad_re[rows, :] + real, grad_im[rows, :] + imag, cosine, sine)
        return r * turned_re, r * turned_im, r * product

    real, imag, product = lax.fori_loop(0, steps, step, (zero, zero, zero + 1.0), unroll=4)
    cos_sub, sin_sub = turn_power(cosine, sine, steps.bit_length() - 1)
    last = LANES - 1
    total_re, total_im, total = real[last:], imag[last:], product[last:]
    for j in range(LANES - 2, -1, -1):
        turned_re, turned_im = rotate(total_re, total_im, cos_sub, sin_sub)
        total_re = product[j : j + 1] * turned_re + real[j : j + 1]
        total_im = product[j : j + 1] * turned_im + imag[j : j + 1]
        total = product[j : j + 1] * total
    summary[0:LANES] = real
    summary[LANES : 2 * LANES] = imag
    summary[2 * LANES : 3 * LANES] = product
    summary[24:32] = jnp.concatenate([total_re, total_im, total, zero[3:]], axis=0)


def whole_backward(
    retain, grad_re, grad_im, turn, summary, start, states, d_decay, d_in_re, d_in_im, d_phase
):
    steps = retain.shape[0] // LANES
    cosine, sine = turn[0:1], turn[1:2]
    cos_sub, sin_sub = turn_power(cosine, -sine, steps.bit_length() - 1)
    now_re, now_im = start[0:1], start[1:2]
    reals, imags = [now_re], [now_im]
    for j in range(LANES - 1, 0, -1):
        turned_re, turned_im = rotate(now_re, now_im, cos_sub, sin_sub)
        product = summary[2 * LANES + j : 2 * LANES + j + 1]
        now_re = product * turned_re + summary[j : j + 1]
        now_im = product * turned_im + summary[LANES + j : LANES + j + 1]
        reals.append(now_re)
        imags.append(now_im)
    zero = jnp.zeros((LANES, retain.shape[1]), jnp.float32)
    carry = (jnp.concatenate(reals[::-1], axis=0), jnp.concatenate(imags[::-1], axis=0), zero)

    def step(k, carry):
        real, imag, phase = carry
        rows = pl.ds(pl.multiple_of(LANES * (steps - 1 - k), LANES), LANES)
        r = retain[rows, :]
        real = grad_re[rows, :] + real
        imag = grad_im[rows, :] + imag
        prior_re, prior_im = rotate(states[0, rows, :], states[1, rows, :], cosine, sine)
        d_decay[rows, :] = -(real * prior_re + imag * prior_im)
        d_in_re[rows, :] = real
        d_in_im[rows, :] = imag
        phase = phase + r * (imag * prior_re - real * prior_im)
        turned_re, turned_im = rotate(real, imag, cosine, -sine)
        return r * turned_re, r * turned_im, phase

    _, _, phase = lax.fori_loop(0, steps, step, carry, unroll=4)
    d_phase[...] = jnp.sum(phase, axis=0, keepdims=True)


def stripe(rows):
    count, columns = rows.shape
    return rows.reshape(LANES, count // LANES, columns).swapaxes(0, 1).reshape(count, columns)


def unstripe(rows):
    count, columns = rows.shape
    return rows.reshape(count // LANES, LANES, columns).swapaxes(0, 1).reshape(count, columns)


def local_call(kernel, outs, *args):
    return pl.pallas_call(
        kernel,
        out_shape=[jax.ShapeDtypeStruct(shape, jnp.float32) for shape in outs],
        compiler_params=pltpu.CompilerParams(vmem_limit_bytes=32 * 1024 * 1024),
    )(*args)


def carry_chain(every, turn, me, length, reverse):
    sine = -turn[1:2] if reverse else turn[1:2]
    cosine, sine = turn_power(turn[0:1], sine, length.bit_length() - 1)
    count = every.shape[0]
    real = jnp.zeros_like(cosine)
    imag = jnp.zeros_like(cosine)
    for j in range(count - 1, 0, -1) if reverse else range(count - 1):
        use = (j > me) if reverse else (j < me)
        turned_re, turned_im = rotate(real, imag, cosine, sine)
        real = jnp.where(use, every[j, 2:3] * turned_re + every[j, 0:1], real)
        imag = jnp.where(use, every[j, 2:3] * turned_im + every[j, 1:2], imag)
    return jnp.concatenate([real, imag], axis=0)


def carry_in(summary, turn, length, reverse):
    every = lax.all_gather(summary[24:32], "dp", axis=0)
    return carry_chain(every, turn, lax.axis_index("dp"), length, reverse)


def normalize(values, gains):
    scaling = lax.rsqrt(jnp.mean(values * values, axis=-1, keepdims=True) + NORM_EPSILON)
    return (values * scaling * gains, scaling)


def normalize_back(values, scaling, gains, gradient):
    scaled = gradient * gains
    return scaling * scaled - values * scaling**3 * jnp.mean(
        values * scaled, axis=-1, keepdims=True
    )


def silu_slope(values):
    logistic = jax.nn.sigmoid(values)
    return logistic * (1.0 + values * (1.0 - logistic))


def adam_update(master, gradient, first, second, steps, decay):
    first_new = BETA_ONE * first + (1.0 - BETA_ONE) * gradient
    second_new = BETA_TWO * second + (1.0 - BETA_TWO) * gradient * gradient
    corrected = (
        first_new
        / (1.0 - BETA_ONE**steps)
        / (jnp.sqrt(second_new / (1.0 - BETA_TWO**steps)) + ADAM_EPSILON)
    )
    change = -LEARN_RATE * (corrected + decay * master)
    return (master + change, first_new, second_new, change)


MESH = pl.DeviceIdType.MESH
LOW = jnp.bfloat16
WIDE = jnp.float32
PLANES = 4
SIDE = 2
IN_ROWS = 24
OUT_ROWS = 72
MIX = CH + 2 * D
MIX_HALF = 1024
CHUNK = 512
CHUNKS = FF // CHUNK
OUT = 2
TILE = 128
VMEM_BYTES = 63 * 1024 * 1024
SLOTS = 512
ROWS = 64
RUN = SLOTS // LANES


class Piece:
    def __init__(self, matrix, rows, columns, starts, overlap=0):
        self.matrix, self.rows, self.columns = matrix, rows, columns
        self.starts, self.overlap = starts, overlap

    def shape(self):
        return (2, PLANES, SIDE, SIDE, 2 * self.rows, self.columns)


def piece_list():
    half = MIX_HALF // 2
    second = MIX - MIX_HALF
    mix = [
        Piece("in", IN_ROWS, half, (0, second), TILE),
        Piece("in", IN_ROWS, half, (half, second + half)),
    ]
    out = [Piece("out", OUT_ROWS, D // 2, (0, D // 2))]
    glu = [
        Piece("in", IN_ROWS, CHUNK, (MIX + CHUNK * k, MIX + FF + CHUNK * k)) for k in range(CHUNKS)
    ]
    return mix + out + glu


PIECES = piece_list()


class Place:
    def __init__(self):
        dp, rep = lax.axis_index("dp"), lax.axis_index("rep")
        self.z, self.x = dp // SIDE, dp % SIDE
        self.y, self.core = rep // 2, rep % 2

    def at(self, z, x, y, core):
        return (z * SIDE + x, y * 2 + core)

    def sibling(self):
        return self.at(self.z, self.x, self.y, 1 - self.core)

    def plane(self, z):
        return self.at(z, self.x, self.y, self.core)

    def near(self, core):
        if core == 0:
            return self.at(self.z, 1 - self.x, self.y, self.core)
        return self.at(self.z, self.x, 1 - self.y, self.core)

    def far(self, core):
        return self.near(1 - core)

    def turn(self, step):
        return lax.rem(self.z + step, PLANES)

    def sides(self, core):
        return (self.x, self.y) if core == 0 else (self.y, self.x)

    def by_core(self, run):
        for core in range(2):
            pl.when(self.core == core)(functools.partial(run, core))

    def greet(self):
        barrier = pltpu.get_barrier_semaphore()
        partners = [self.sibling(), self.near(0), self.near(1)]
        for step in (1, 2, 3):
            partners.append(self.plane(self.turn(step)))
            partners.append(self.at(self.turn(step), 1 - self.x, self.y, self.core))
        for partner in partners:
            pl.semaphore_signal(barrier, inc=1, device_id=partner, device_id_type=MESH)
        return lambda: pl.semaphore_wait(barrier, len(partners))


def block_of(ref, core, z, near, far):
    return ref.at[core, z, near, far] if core == 0 else ref.at[core, z, far, near]


def pair_of(ref, core, z, far):
    return ref.at[core, z, :, far] if core == 0 else ref.at[core, z, far]


def remote(source, target, sent, received, device):
    return pltpu.make_async_remote_copy(
        src_ref=source,
        dst_ref=target,
        send_sem=sent,
        recv_sem=received,
        device_id=device,
        device_id_type=MESH,
    )


GATHER_SEMS = 4 * 2
STEPS_AWAY = (1, 3, 2)


class Gather:
    def __init__(self, place, masters, buffers, staging, sems):
        self.place, self.masters, self.buffers, self.staging = place, masters, buffers, staging
        self.local, self.sent0, self.got0 = sems[:3]
        self.sems = sems[3:]

    @staticmethod
    def scratch():
        n = len(PIECES)
        dma = pltpu.SemaphoreType.DMA
        return (
            [pltpu.VMEM(p.shape(), LOW) for p in PIECES]
            + [pltpu.VMEM((2 * p.rows, p.columns), WIDE) for p in PIECES]
            + [dma((n,))] * 3
            + [dma((n, PLANES))] * GATHER_SEMS
        )

    def part(self, p, half):
        piece = PIECES[p]
        start = piece.starts[0] + half * (piece.starts[1] - piece.starts[0])
        return self.masters[piece.matrix].at[:, pl.ds(pl.multiple_of(start, TILE), piece.columns)]

    def own_rows(self, p):
        rows = PIECES[p].rows
        return self.staging[p].at[pl.ds(pl.multiple_of(self.place.core * rows, 8), rows)]

    def to_sibling(self, p):
        return remote(
            self.part(p, 1 - self.place.core),
            self.own_rows(p),
            self.sent0.at[p],
            self.got0.at[p],
            self.place.sibling(),
        )

    def to_self(self, p):
        return pltpu.make_async_copy(
            self.part(p, self.place.core), self.own_rows(p), self.local.at[p]
        )

    def along_z(self, p, z, target):
        place = self.place
        block = self.buffers[p].at[place.core, z, place.x, place.y]
        return remote(
            block, block, self.sems[0].at[p, target], self.sems[1].at[p, z], place.plane(target)
        )

    def along_near(self, p, z, core):
        block = block_of(self.buffers[p], core, z, *self.place.sides(core))
        return remote(
            block, block, self.sems[2].at[p, z], self.sems[3].at[p, z], self.place.near(core)
        )

    def along_far(self, p, z, core):
        pair = pair_of(self.buffers[p], core, z, self.place.sides(core)[1])
        return remote(
            pair, pair, self.sems[4].at[p, z], self.sems[5].at[p, z], self.place.far(core)
        )

    def in_chip(self, p, z, core):
        plane = self.buffers[p].at[core, z]
        return remote(
            plane, plane, self.sems[6].at[p, z], self.sems[7].at[p, z], self.place.sibling()
        )

    def begin(self):
        for p in range(len(PIECES)):
            self.to_sibling(p).start()
            self.to_self(p).start()

    def stage0(self, p):
        place = self.place
        self.to_self(p).wait()
        self.to_sibling(p).wait_recv()
        self.buffers[p][place.core, place.z, place.x, place.y] = self.staging[p][...].astype(LOW)
        for step in STEPS_AWAY:
            self.along_z(p, place.z, place.turn(step)).start()
        place.by_core(lambda core: self.along_near(p, place.z, core).start())

    def stage1(self, p):
        place = self.place
        for step in STEPS_AWAY:
            z = place.turn(step)
            self.along_z(p, z, place.z).wait_recv()
            place.by_core(lambda core: self.along_near(p, z, core).start())

    def stage2(self, p):
        def run(core):
            for step in (0,) + STEPS_AWAY:
                z = self.place.turn(step)
                self.along_near(p, z, core).wait_recv()
                self.along_far(p, z, core).start()

        self.place.by_core(run)

    def stage3(self, p):
        def run(core):
            for step in (0,) + STEPS_AWAY:
                z = self.place.turn(step)
                self.along_far(p, z, core).wait_recv()
                self.in_chip(p, z, core).start()

        self.place.by_core(run)

    def stage4(self, p):
        for step in (0,) + STEPS_AWAY:
            z = self.place.turn(step)
            self.in_chip(p, z, 1 - self.place.core).wait_recv()

    def drain(self, p):
        self.to_sibling(p).wait_send()
        for step in STEPS_AWAY:
            self.along_z(p, self.place.z, self.place.turn(step)).wait_send()

        def run(core):
            for z in range(PLANES):
                self.along_near(p, z, core).wait_send()
                self.along_far(p, z, core).wait_send()
                self.in_chip(p, z, core).wait_send()

        self.place.by_core(run)


class Reduce:
    ORDER = STEPS_AWAY + (0,)

    def __init__(self, place, grads, refs, results):
        n = len(PIECES)
        self.place, self.grads, self.results = place, grads, results
        self.far, self.near, self.planes, self.final = (refs[k * n : (k + 1) * n] for k in range(4))
        self.sems = refs[4 * n :]

    @staticmethod
    def scratch():
        n = len(PIECES)
        dma = pltpu.SemaphoreType.DMA
        blocks = [p.shape()[4:] for p in PIECES]
        return (
            [pltpu.VMEM((PLANES, SIDE) + s, LOW) for s in blocks]
            + [pltpu.VMEM((PLANES,) + s, LOW) for s in blocks] * 2
            + [pltpu.VMEM(s, WIDE) for s in blocks]
            + [dma((n, PLANES))] * 6
            + [dma((n,))] * 2
        )

    def block(self, p, z, near, far, core):
        return self.grads[p].at[z, near, far] if core == 0 else self.grads[p].at[z, far, near]

    def pair(self, p, z, far, core):
        return self.grads[p].at[z, :, far] if core == 0 else self.grads[p].at[z, far]

    def along_far(self, p, z, core):
        return remote(
            self.pair(p, z, 1 - self.place.sides(core)[1], core),
            self.far[p].at[z],
            self.sems[0].at[p, z],
            self.sems[1].at[p, z],
            self.place.far(core),
        )

    def along_near(self, p, z, core):
        near, far = self.place.sides(core)
        return remote(
            self.block(p, z, 1 - near, far, core),
            self.near[p].at[z],
            self.sems[2].at[p, z],
            self.sems[3].at[p, z],
            self.place.near(core),
        )

    def along_z(self, p, z, sender, core):
        return remote(
            self.block(p, z, *self.place.sides(core), core),
            self.planes[p].at[sender],
            self.sems[4].at[p, z],
            self.sems[5].at[p, sender],
            self.place.plane(z),
        )

    def result(self, p, core):
        piece = PIECES[p]
        skip = piece.overlap * core
        start, width = piece.starts[core] + skip, piece.columns - skip
        return self.results[piece.matrix].at[:, pl.ds(start, width)], pl.ds(skip, width)

    def to_sibling(self, p, core):
        rows = PIECES[p].rows
        target, columns = self.result(p, core)
        return remote(
            self.final[p].at[pl.ds(rows * (1 - core), rows), columns],
            target,
            self.sems[6].at[p],
            self.sems[7].at[p],
            self.place.sibling(),
        )

    @staticmethod
    def add(target, source):
        target[...] = (target[...].astype(WIDE) + source[...].astype(WIDE)).astype(LOW)

    def stage0(self, p):
        def run(core):
            for step in self.ORDER:
                self.along_far(p, self.place.turn(step), core).start()

        self.place.by_core(run)

    def stage1(self, p):
        def run(core):
            for step in self.ORDER:
                z = self.place.turn(step)
                self.along_far(p, z, core).wait_recv()
                self.add(self.pair(p, z, self.place.sides(core)[1], core), self.far[p].at[z])
                self.along_near(p, z, core).start()

        self.place.by_core(run)

    def stage2(self, p):
        def run(core):
            for step in self.ORDER:
                z = self.place.turn(step)
                self.along_near(p, z, core).wait_recv()
                self.add(self.block(p, z, *self.place.sides(core), core), self.near[p].at[z])
                if step:
                    self.along_z(p, z, self.place.z, core).start()

        self.place.by_core(run)

    def stage3(self, p):
        rows = PIECES[p].rows

        def run(core):
            z = self.place.z
            for step in STEPS_AWAY:
                self.along_z(p, z, self.place.turn(step), core).wait_recv()
            total = self.block(p, z, *self.place.sides(core), core)[...].astype(WIDE)
            for step in STEPS_AWAY:
                total = total + self.planes[p][self.place.turn(step)].astype(WIDE)
            self.final[p][...] = total
            self.to_sibling(p, core).start()
            target, columns = self.result(p, core)
            target[...] = self.final[p][pl.ds(rows * core, rows), columns]

        self.place.by_core(run)

    def drain(self, p):
        def run(core):
            self.to_sibling(p, 1 - core).wait_recv()
            self.to_sibling(p, core).wait_send()
            for step in self.ORDER:
                z = self.place.turn(step)
                self.along_far(p, z, core).wait_send()
                self.along_near(p, z, core).wait_send()
                if step:
                    self.along_z(p, z, self.place.z, core).wait_send()

        self.place.by_core(run)


def tiled(column, count):
    return jnp.concatenate([column] * count, axis=1)


def some(index, size=ROWS):
    return pl.ds(pl.multiple_of(index * size, size), size)


def each_block(run, size=ROWS, count=SLOTS):
    lax.fori_loop(0, count // size, lambda i, _: (run(some(i, size)), 0)[1], 0)


def inner(left, right, dims=((1,), (0,))):
    return lax.dot_general(left, right, (dims, ((), ())), preferred_element_type=WIDE)


def across(left, right):
    return inner(left, right, ((1,), (1,)))


def along(left, right):
    return inner(left, right, ((0,), (0,)))


def out_segments(start, count):
    size, runs, stop = 2 * OUT_ROWS, [], start + count
    while start < stop:
        chip, first = divmod(start, size)
        last = min(size, first + stop - start)
        runs.append((chip // 4, chip // 2 % 2, chip % 2, first, last))
        start += last - first
    return runs


def row_norm(values):
    return lax.rsqrt(jnp.mean(values * values, axis=1, keepdims=True) + NORM_EPSILON)


def eights(values):
    return jnp.sum(values.reshape(values.shape[0] // 8, 8, values.shape[1]), axis=0)


def block_scratch():
    vmem, dma = pltpu.VMEM, pltpu.SemaphoreType.DMA
    rows = (SLOTS, D)
    both = (2 * SLOTS, D)
    return dict(
        arrivals=dma((2,)),
        departures=dma((2,)),
        perm=vmem((SLOTS, SLOTS), LOW),
        live=vmem((SLOTS, TILE), WIDE),
        opens=vmem((SLOTS, TILE), WIDE),
        params=vmem((8, D), WIDE),
        tokens=vmem(rows, LOW),
        upstream=vmem((2, SLOTS, D // 2), LOW),
        upstream_got=vmem((SLOTS, D // 2), LOW),
        normed=vmem(both, LOW),
        normed_two=vmem(both, LOW),
        gated=vmem(both, LOW),
        hidden=vmem((CHUNKS, 2 * SLOTS, CHUNK), LOW),
        d_glu=vmem((CHUNKS, 2, SLOTS, CHUNK), LOW),
        d_glu_got=vmem((CHUNKS, SLOTS, CHUNK), LOW),
        d_out=vmem((2, SLOTS, D // 2), LOW),
        d_out_got=vmem((SLOTS, D // 2), LOW),
        d_mix=vmem((2, 2, SLOTS, MIX_HALF // 2), LOW),
        d_mix_got=vmem((2, SLOTS, MIX_HALF // 2), LOW),
        pre_mix=vmem((SLOTS, MIX), WIDE),
        glu=vmem((3, SLOTS // 2, CHUNK), WIDE),
        retain=vmem((SLOTS, CH), WIDE),
        drive=vmem(rows, WIDE),
        states=vmem((2, SLOTS + LANES, CH), WIDE),
        summaries=vmem((2, 32, CH), WIDE),
        every=vmem((2, PLANES * SIDE, 8, CH), WIDE),
        middle=vmem(rows, WIDE),
        d_normed=vmem(rows, WIDE),
        total=vmem(rows, WIDE),
        block_out=vmem(rows, LOW),
        sums=vmem((3, 8, D), WIDE),
        vector=vmem((8, VEC_ROWS, TILE), WIDE),
        pair_sent=dma((PAIRS,)),
        pair_got=dma((PAIRS,)),
        carry_sent=dma((2, PLANES * SIDE)),
        carry_got=dma((2, PLANES * SIDE)),
        vector_sent=dma((6,)),
        vector_got=dma((6,)),
    )


VEC_ROWS = 24
VEC_COUNT = 18
PAIRS = 16


class Block:
    def __init__(self, place, buffers, grads, refs):
        self.place, self.weights, self.grads = place, buffers, grads
        for name, ref in refs.items():
            setattr(self, name, ref)
        self.me = place.z * SIDE + place.x


    def swaps(self):
        own, got = pl.ds(0, SLOTS), pl.ds(SLOTS, SLOTS)
        other = 1 - self.place.core
        pairs = dict(
            normed=(self.normed.at[own], self.normed.at[got]),
            normed_two=(self.normed_two.at[own], self.normed_two.at[got]),
            gated=(self.gated.at[own], self.gated.at[got]),
            upstream=(self.upstream.at[other], self.upstream_got),
            d_out=(self.d_out.at[other], self.d_out_got),
        )
        for k in range(CHUNKS):
            pairs["hidden", k] = (self.hidden.at[k, own], self.hidden.at[k, got])
            pairs["d_glu", k] = (self.d_glu.at[k, other], self.d_glu_got.at[k])
        for m in range(2):
            pairs["d_mix", m] = (self.d_mix.at[other, m], self.d_mix_got.at[m])
        return pairs

    def swap(self, name):
        pairs = self.swaps()
        slot = list(pairs).index(name)
        sems = self.pair_sent.at[slot], self.pair_got.at[slot]
        return remote(*pairs[name], *sems, self.place.sibling())

    def give(self, *names):
        for name in names:
            self.swap(name).start()

    def take(self, *names):
        for name in names:
            self.swap(name).wait_recv()

    def settle(self):
        for name in self.swaps():
            self.swap(name).wait_send()


    def mix_weight(self, half, m):
        return self.weights[m][half].reshape(D, MIX_HALF // 2)

    def glu_weight(self, k):
        parts = [self.weights[OUT + 1 + k][half].reshape(D, CHUNK) for half in range(2)]
        return jnp.concatenate(parts, axis=1)

    def out_weight(self, start, count):
        halves = []
        for half in range(2):
            ref = self.weights[OUT]
            parts = [
                ref[half, z, x, y, first:last] for z, x, y, first, last in out_segments(start, count)
            ]
            halves.append(jnp.concatenate(parts, axis=0))
        return jnp.concatenate(halves, axis=1)

    def put_in(self, p, value):
        self.grads[p][...] = value.astype(LOW).reshape(self.grads[p].shape)

    def put_out(self, start, value):
        value, done = value.astype(LOW), 0
        for z, x, y, first, last in out_segments(start, value.shape[0]):
            count = last - first
            self.grads[OUT][z, x, y, first:last] = value[done : done + count]
            done += count


    def prepare(self, padding, opening, vectors):
        row = lax.broadcasted_iota(jnp.int32, (SLOTS, SLOTS), 0)
        column = lax.broadcasted_iota(jnp.int32, (SLOTS, SLOTS), 1)
        perm = (column == row % LANES * RUN + row // LANES).astype(WIDE)
        self.perm[...] = perm.astype(LOW)
        ones = jnp.ones((SLOTS, TILE), LOW)
        self.live[...] = inner((perm * padding[...].astype(WIDE)).astype(LOW), ones)
        self.opens[...] = inner((perm * opening[...].astype(WIDE)).astype(LOW), ones)

        def line(first, count):
            return jnp.concatenate([vectors[first + i : first + i + 1] for i in range(count)], axis=1)

        phase = line(12, 3)
        self.params[0:1] = line(0, 6)
        self.params[1:2] = line(6, 6)
        self.params[2:3] = jnp.concatenate([jnp.cos(phase), jnp.sin(phase)], axis=1)
        self.params[3:4] = jnp.concatenate([line(15, 3)] * 2, axis=1)
        self.sums[...] = jnp.zeros_like(self.sums)

    def turn(self):
        return jnp.concatenate([self.params[2:3, :CH], self.params[2:3, CH:]], axis=0)

    def first_norm(self, raw):
        self.tokens[...] = inner(self.perm[...], raw[...]).astype(LOW)

        def run(rows):
            values = self.tokens[rows, :].astype(WIDE)
            self.normed[rows, :] = (values * row_norm(values) * self.params[0:1]).astype(LOW)

        each_block(run)

    def mask_upstream(self, raw):
        striped = inner(self.perm[...], raw[...]) * tiled(self.live[...], D // TILE)
        self.upstream[0] = striped[:, : D // 2].astype(LOW)
        self.upstream[1] = striped[:, D // 2 :].astype(LOW)

    def mix(self, m):
        normed, width = self.normed[0:SLOTS, :], MIX_HALF // 2
        piece = PIECES[m]
        for half in range(2):
            skip = piece.overlap * half
            start = piece.starts[half] + skip
            product = inner(normed, self.mix_weight(half, m))
            self.pre_mix[:, start : start + width - skip] = product[:, skip:]

    def drives(self):
        def run(rows):
            forget = jax.nn.sigmoid(-(self.pre_mix[rows, :CH] + self.params[3:4, :CH]))
            pre = self.pre_mix[rows, CH : CH + D]
            driver = pre * jax.nn.sigmoid(pre)
            opens = tiled(self.opens[rows, :], CH // TILE)
            decay = jnp.where(opens > 0.5, 1.0, forget).astype(LOW).astype(WIDE)
            self.retain[rows, :] = 1.0 - decay
            drive = jnp.concatenate([forget, forget], axis=1) * driver
            self.drive[rows, :] = drive.astype(LOW).astype(WIDE)

        each_block(run)

    def parts(self):
        return self.drive.at[:, pl.ds(0, CH)], self.drive.at[:, pl.ds(CH, CH)]

    def others(self):
        place = self.place
        for step in range(PLANES):
            for flip in range(SIDE):
                if step or flip:
                    z = place.turn(step)
                    x = 1 - place.x if flip else place.x
                    yield z * SIDE + x, place.at(z, x, place.y, place.core)

    def carry_copy(self, way, other, device, sender):
        return remote(
            self.summaries.at[way, pl.ds(24, 8)],
            self.every.at[way, sender],
            self.carry_sent.at[way, other],
            self.carry_got.at[way, sender],
            device,
        )

    def scan_own(self, way):
        run = local_backward if way else local_forward
        run(self.retain, *self.parts(), self.turn(), self.summaries.at[way])
        self.every[way, self.me] = self.summaries[way, 24:32]
        for other, device in self.others():
            self.carry_copy(way, other, device, self.me).start()

    def carried(self, way):
        for other, device in self.others():
            self.carry_copy(way, other, device, other).wait_recv()
        turn = self.turn()
        return carry_chain(self.every.at[way], turn, self.me, SLOTS, way == 1)

    def scan_states(self):
        start = self.carried(0)
        run = whole_forward
        run(self.retain, *self.parts(), self.turn(), self.summaries.at[0], start, self.states)

    def recurrent(self, rows):
        after = pl.ds(pl.multiple_of(rows.start + LANES, LANES), rows.size)
        both = jnp.concatenate([self.states[0, after, :], self.states[1, after, :]], axis=1)
        return both.astype(LOW).astype(WIDE)

    def gate_rows(self):
        def run(rows):
            pre = self.pre_mix[rows, CH + D :]
            masked = self.recurrent(rows) * tiled(self.live[rows, :], D // TILE)
            self.gated[rows, :] = (masked * (pre * jax.nn.sigmoid(pre))).astype(LOW)

        each_block(run)

    def second_norm(self):
        self.middle[...] = inner(self.gated[0:SLOTS, :], self.out_weight(0, D))

        def run(rows):
            middle = self.tokens[rows, :].astype(WIDE) + self.middle[rows, :]
            self.middle[rows, :] = middle
            self.normed_two[rows, :] = (middle * row_norm(middle) * self.params[1:2]).astype(LOW)

        each_block(run)

    def glu_forward(self, k):
        weight = self.glu_weight(k)
        down = self.out_weight(D + CHUNK * k, CHUNK)
        half = SLOTS // 2
        for part in range(2):
            rows = slice(part * half, (part + 1) * half)
            pre = inner(self.normed_two[rows, :], weight)
            self.glu[0] = pre[:, :CHUNK]
            self.glu[1] = pre[:, CHUNK:]
            upstream = jnp.concatenate([self.upstream[0, rows], self.upstream[1, rows]], axis=1)
            self.glu[2] = across(upstream, down)

            def run(block):
                gate, up, d_hidden = (self.glu[i, block, :] for i in range(3))
                own = pl.ds(pl.multiple_of(block.start + part * half, ROWS), ROWS)
                logistic = jax.nn.sigmoid(gate)
                active = gate * logistic
                slope = logistic * (1.0 + gate * (1.0 - logistic))
                self.hidden[k, own, :] = (active * up).astype(LOW)
                self.d_glu[k, 0, own, :] = (d_hidden * up * slope).astype(LOW)
                self.d_glu[k, 1, own, :] = (d_hidden * active).astype(LOW)

            each_block(run, count=half)

    def glu_back(self, k):
        down = self.out_weight(D + CHUNK * k, CHUNK)
        share = inner(self.hidden[k, 0:SLOTS, :], down)
        d_glu = jnp.concatenate([self.d_glu[k, 0], self.d_glu[k, 1]], axis=1)
        d_share = across(d_glu, self.glu_weight(k))
        if k == 0:
            self.total[...] = self.middle[...] + share
            self.d_normed[...] = d_share
        else:
            self.total[...] += share
            self.d_normed[...] += d_share
        if k == CHUNKS - 1:
            self.block_out[...] = self.total[...].astype(LOW)

    def own_half(self, ref, got):
        return jnp.concatenate([ref[self.place.core], got], axis=0)

    def glu_grads(self, k):
        d_glu = jnp.concatenate([self.d_glu[k, self.place.core], self.d_glu_got[k]], axis=0)
        self.put_in(OUT + 1 + k, along(self.normed_two[...], d_glu))
        upstream = self.own_half(self.upstream, self.upstream_got[...])
        self.put_out(D + CHUNK * k, along(self.hidden[k], upstream))

    def add_sum(self, index, values):
        self.sums[index, :, : values.shape[1]] += eights(values)

    def middle_back(self):
        def run(rows):
            middle, d_normed = self.middle[rows, :], self.d_normed[rows, :]
            scaling = row_norm(middle)
            self.add_sum(1, d_normed * middle * scaling)
            scaled = d_normed * self.params[1:2]
            mean = jnp.mean(middle * scaled, axis=1, keepdims=True)
            upstream = jnp.concatenate([self.upstream[0, rows], self.upstream[1, rows]], axis=1)
            d_middle = upstream.astype(WIDE) + scaling * scaled - middle * (scaling**3 * mean)
            self.middle[rows, :] = d_middle
            self.d_out[0, rows] = d_middle[:, : D // 2].astype(LOW)
            self.d_out[1, rows] = d_middle[:, D // 2 :].astype(LOW)

        each_block(run)

    def gate_back(self):
        d_out = jnp.concatenate([self.d_out[0], self.d_out[1]], axis=1)
        self.total[...] = across(d_out, self.out_weight(0, D))

        def run(rows):
            pre, d_gated = self.pre_mix[rows, CH + D :], self.total[rows, :]
            logistic = jax.nn.sigmoid(pre)
            d_live = d_gated * tiled(self.live[rows, :], D // TILE)
            self.drive[rows, :] = (d_live * (pre * logistic)).astype(LOW).astype(WIDE)
            slope = logistic * (1.0 + pre * (1.0 - logistic))
            d_gate = (d_live * self.recurrent(rows) * slope).astype(LOW)
            self.d_mix[1, 0, rows, 2 * TILE :] = d_gate[:, : 2 * TILE]
            self.d_mix[1, 1, rows, :] = d_gate[:, 2 * TILE :]

        each_block(run)

    def mixer_out_grad(self):
        d_out = self.own_half(self.d_out, self.d_out_got[...])
        self.put_out(0, along(self.gated[...], d_out))

    def scan_back(self):
        start = self.carried(1)
        real, imag = self.parts()
        whole_backward(
            self.retain,
            real,
            imag,
            self.turn(),
            self.summaries.at[1],
            start,
            self.states,
            self.retain,
            real,
            imag,
            self.sums.at[2, pl.ds(0, 1), pl.ds(0, CH)],
        )

    def drives_back(self):
        def run(rows):
            forget = jax.nn.sigmoid(-(self.pre_mix[rows, :CH] + self.params[3:4, :CH]))
            pre = self.pre_mix[rows, CH : CH + D]
            logistic = jax.nn.sigmoid(pre)
            d_decay = self.retain[rows, :].astype(LOW).astype(WIDE)
            d_input = self.drive[rows, :].astype(LOW).astype(WIDE)
            pulled = d_input * (pre * logistic)
            opens = tiled(self.opens[rows, :], CH // TILE)
            d_forget = jnp.where(opens > 0.5, 0.0, d_decay) + pulled[:, :CH] + pulled[:, CH:]
            d_first = -forget * (1.0 - forget) * d_forget
            self.sums[2, :, CH:] += eights(d_first)
            slope = logistic * (1.0 + pre * (1.0 - logistic))
            d_driver = d_input * jnp.concatenate([forget, forget], axis=1) * slope
            d_pre = jnp.concatenate([d_first, d_driver], axis=1).astype(LOW)
            half = MIX_HALF // 2
            self.d_mix[0, 0, rows, :] = d_pre[:, :half]
            self.d_mix[0, 1, rows, :] = d_pre[:, half : 2 * half]
            self.d_mix[1, 0, rows, : 2 * TILE] = d_pre[:, MIX_HALF - TILE :]

        each_block(run)

    def mix_grads(self, m):
        d_mix = jnp.concatenate([self.d_mix[self.place.core, m], self.d_mix_got[m]], axis=0)
        self.put_in(m, along(self.normed[...], d_mix))

    def first_back(self):
        lefts, rights = [], []
        for half in range(2):
            for m in range(2):
                skip = PIECES[m].overlap * half
                lefts.append(self.d_mix[half, m][:, skip:])
                rights.append(self.mix_weight(half, m)[:, skip:])
        product = across(jnp.concatenate(lefts, axis=1), jnp.concatenate(rights, axis=1))
        self.d_normed[...] = product

        def run(rows):
            values, d_normed = self.tokens[rows, :].astype(WIDE), self.d_normed[rows, :]
            scaling = row_norm(values)
            self.add_sum(0, d_normed * values * scaling)
            scaled = d_normed * self.params[0:1]
            mean = jnp.mean(values * scaled, axis=1, keepdims=True)
            self.middle[rows, :] += scaling * scaled - values * (scaling**3 * mean)

        each_block(run)


    def gather_vector(self):
        lines = [
            jnp.sum(self.sums[0], axis=0, keepdims=True),
            jnp.sum(self.sums[1], axis=0, keepdims=True),
            jnp.concatenate(
                [self.sums[2, 0:1, :CH], jnp.sum(self.sums[2, :, CH:], axis=0, keepdims=True)], axis=1
            ),
        ]
        for i, line in enumerate(lines):
            for j in range(D // TILE):
                row = i * (D // TILE) + j
                self.vector[0, row : row + 1] = line[:, j * TILE : (j + 1) * TILE]
        filled = jnp.sum(self.live[...], axis=0, keepdims=True)
        rest = jnp.zeros((VEC_ROWS - VEC_COUNT - 1, TILE), WIDE)
        self.vector[0, VEC_COUNT:] = jnp.concatenate([filled, rest], axis=0)

    def vector_copy(self, stage):
        place = self.place
        device = (place.sibling(), place.near(0), place.near(1))[stage]
        source = self.vector.at[stage]
        target = self.vector.at[4 + stage]
        return remote(source, target, self.vector_sent.at[stage], self.vector_got.at[stage], device)

    def vector_step(self, stage):
        if stage:
            self.vector_copy(stage - 1).wait_recv()
            self.vector[stage] = self.vector[stage - 1] + self.vector[3 + stage]
        if stage < 3:
            self.vector_copy(stage).start()

    def vector_plane(self, planes, step, sender):
        place = self.place
        return remote(
            self.vector.at[3],
            planes.at[sender],
            self.vector_sent.at[2 + step],
            self.vector_got.at[2 + step],
            place.plane(place.turn(step)),
        )


def block_kernel(tokens, cotangent, padding, opening, w_in, w_out, vectors, *refs):
    n = len(PIECES)
    block_out, d_tokens, sum_in, sum_out, planes = refs[:5]
    refs = refs[5:]
    count = len(Gather.scratch())
    gather_refs, refs = refs[:count], refs[count:]
    buffers, staging, gather_sems = gather_refs[:n], gather_refs[n : 2 * n], gather_refs[2 * n :]
    grads, refs = refs[:n], refs[n:]
    count = len(Reduce.scratch())
    reduce_refs, refs = refs[:count], refs[count:]
    place = Place()
    gather = Gather(place, {"in": w_in, "out": w_out}, buffers, staging, gather_sems)
    reduce = Reduce(place, grads, reduce_refs, {"in": sum_in, "out": sum_out})
    block = Block(place, buffers, grads, dict(zip(block_scratch(), refs, strict=True)))

    entered = place.greet()
    raw_tokens, raw_upstream = block.gated.at[pl.ds(0, SLOTS)], block.block_out
    loads = [
        pltpu.make_async_copy(tokens.at[0], raw_tokens, block.arrivals.at[0]),
        pltpu.make_async_copy(cotangent.at[0], raw_upstream, block.arrivals.at[1]),
    ]
    for load in loads:
        load.start()
    block.prepare(padding, opening, vectors)
    entered()
    gather.begin()
    loads[0].wait()
    block.first_norm(raw_tokens)
    loads[1].wait()
    block.mask_upstream(raw_upstream)
    block.give("normed", "upstream")

    stages = (gather.stage0, gather.stage1, gather.stage2, gather.stage3, gather.stage4)

    def tick(now):
        for lag, stage in enumerate(stages):
            if 0 <= now - lag < n:
                stage(now - lag)

    for now in range(5):
        tick(now)
    block.mix(0)
    tick(5)
    block.mix(1)
    block.drives()
    block.scan_own(0)
    tick(6)
    block.scan_states()
    block.gate_rows()
    block.give("gated")
    block.second_norm()
    block.give("normed_two")
    block.take("upstream", "normed_two")

    def glu(k):
        block.glu_forward(k)
        block.give(("hidden", k), ("d_glu", k))
        block.glu_back(k)
        block.take(("hidden", k), ("d_glu", k))
        block.glu_grads(k)
        reduce.stage0(OUT + 1 + k)

    tick(7)
    glu(0)
    tick(8)
    reduce.stage1(OUT + 1)
    glu(1)
    tick(9)
    reduce.stage2(OUT + 1)
    reduce.stage1(OUT + 2)
    glu(2)
    leave_out = pltpu.make_async_copy(block.block_out, block_out, block.departures.at[0])
    leave_out.start()
    block.middle_back()
    block.give("d_out")
    reduce.stage3(OUT + 1)
    reduce.stage2(OUT + 2)
    reduce.stage1(OUT + 3)
    block.gate_back()
    block.scan_own(1)
    block.take("gated", "d_out")
    block.mixer_out_grad()
    reduce.stage0(OUT)
    block.scan_back()
    reduce.stage3(OUT + 2)
    reduce.stage2(OUT + 3)
    block.drives_back()
    block.give(("d_mix", 0), ("d_mix", 1))
    reduce.stage1(OUT)
    block.take("normed", ("d_mix", 0), ("d_mix", 1))
    block.mix_grads(0)
    reduce.stage0(0)
    block.mix_grads(1)
    reduce.stage0(1)
    reduce.stage3(OUT + 3)
    block.first_back()
    leave_tokens = pltpu.make_async_copy(block.middle, d_tokens, block.departures.at[1])
    leave_tokens.start()
    block.gather_vector()
    block.vector_step(0)
    reduce.stage2(OUT)
    reduce.stage1(0)
    block.vector_step(1)
    reduce.stage1(1)
    reduce.stage3(OUT)
    block.vector_step(2)
    reduce.stage2(0)
    reduce.stage2(1)
    block.vector_step(3)
    for step in (1, 2, 3):
        block.vector_plane(planes, step, place.z).start()
    planes[place.z] = block.vector[3]
    reduce.stage3(0)
    reduce.stage3(1)

    for step in (1, 2, 3):
        block.vector_plane(planes, step, place.z).wait_send()
        block.vector_plane(planes, step, place.turn(4 - step)).wait_recv()
    for stage in range(3):
        block.vector_copy(stage).wait_send()
    for way in range(2):
        for other, device in block.others():
            block.carry_copy(way, other, device, block.me).wait_send()
    block.settle()
    for p in range(n):
        gather.drain(p)
        reduce.drain(p)
    leave_out.wait()
    leave_tokens.wait()


def block_routed(tokens, cotangent, padding, opening, w_in, w_out, vectors):
    vmem = pl.BlockSpec(memory_space=pltpu.VMEM)
    anywhere = pl.BlockSpec(memory_space=pl.ANY)
    out_shape = [
        jax.ShapeDtypeStruct((SLOTS, D), LOW),
        jax.ShapeDtypeStruct((SLOTS, D), WIDE),
        jax.ShapeDtypeStruct(w_in.shape, WIDE),
        jax.ShapeDtypeStruct(w_out.shape, WIDE),
        jax.ShapeDtypeStruct((PLANES, VEC_ROWS, TILE), WIDE),
    ]
    grads = [pltpu.VMEM(p.shape()[1:], LOW) for p in PIECES]
    block_out, d_tokens, sum_in, sum_out, planes = pl.pallas_call(
        block_kernel,
        out_shape=out_shape,
        in_specs=[anywhere, anywhere, vmem, vmem, anywhere, anywhere, vmem],
        out_specs=[anywhere, anywhere, vmem, vmem, vmem],
        scratch_shapes=Gather.scratch()
        + grads
        + Reduce.scratch()
        + list(block_scratch().values()),
        compiler_params=pltpu.CompilerParams(
            collective_id=0, has_side_effects=True, vmem_limit_bytes=VMEM_BYTES
        ),
    )(tokens, cotangent, padding, opening, w_in, w_out, vectors.reshape(VEC_COUNT, TILE))
    sums = jnp.sum(planes, axis=0)
    return block_out, d_tokens, sum_in, sum_out, sums[:VEC_COUNT].reshape(-1), sums[VEC_COUNT, 0]


def routed(tokens, w_in, w_out):
    sizes = (lax.axis_size("dp"), lax.axis_size("rep"))
    shards = (tokens.shape[1], w_in.shape[0], w_out.shape[0])
    return sizes == (PLANES * SIDE, SIDE * 2) and shards == (SLOTS, IN_ROWS, OUT_ROWS)


def block_anywhere(tokens, cotangent, padding, opening, w_in, w_out, vectors):
    low = jnp.bfloat16
    wide = jnp.float32
    mixer_cols = CH + 2 * D
    length = tokens.shape[1]
    inputs = stripe(tokens[0]).astype(wide)
    filled = stripe(padding[0][:, None]).astype(wide)
    starting = stripe(opening[0][:, None]) == 1
    gains_one = vectors[:D]
    gains_two = vectors[D : 2 * D]
    phases = vectors[2 * D : 2 * D + CH]
    biases = vectors[2 * D + CH :]
    turn = jnp.stack([jnp.cos(phases), jnp.sin(phases)])
    axes = ("dp", "rep")
    full_in = lax.all_gather(w_in.astype(low), axes, axis=0, tiled=True)
    full_out = lax.all_gather(w_out.astype(low), axes, axis=0, tiled=True)
    normed, scaling_one = normalize(inputs, gains_one)
    normed_low = normed.astype(low)
    pre_mix = jnp.dot(normed_low, full_in[:, :mixer_cols], preferred_element_type=wide)
    forget = jax.nn.sigmoid(-(pre_mix[:, :CH] + biases))
    driver_pre = pre_mix[:, CH : CH + D]
    driver = jax.nn.silu(driver_pre)
    gate_pre = pre_mix[:, CH + D :]
    forget_both = jnp.concatenate([forget, forget], axis=1)
    decay = jnp.where(starting, 1.0, forget).astype(low).astype(wide)
    retain = 1.0 - decay
    drive = (forget_both * driver).astype(low).astype(wide)
    drive_re, drive_im = drive[:, :CH], drive[:, CH:]
    summary = local_call(local_forward, [(32, CH)], retain, drive_re, drive_im, turn)[0]
    start = carry_in(summary, turn, length, False)
    states = local_call(
        whole_forward, [(2, length + 8, CH)], retain, drive_re, drive_im, turn, summary, start
    )[0]
    recurrent = jnp.concatenate([states[0, LANES:], states[1, LANES:]], axis=1)
    recurrent = recurrent.astype(low).astype(wide)
    gate_act = jax.nn.silu(gate_pre)
    masked = recurrent * filled
    gated_rows = (masked * gate_act).astype(low)
    middle = inputs + jnp.dot(gated_rows, full_out[:D], preferred_element_type=wide)
    normed_two, scaling_two = normalize(middle, gains_two)
    normed_two_low = normed_two.astype(low)
    glu_pre = jnp.dot(normed_two_low, full_in[:, mixer_cols:], preferred_element_type=wide)
    gate_glu = glu_pre[:, :FF]
    up_glu = glu_pre[:, FF:]
    hidden = (jax.nn.silu(gate_glu) * up_glu).astype(low)
    block_out = middle + jnp.dot(hidden, full_out[D:], preferred_element_type=wide)
    upstream = stripe(cotangent[0]).astype(wide) * filled
    upstream_low = upstream.astype(low)
    grad_down = jnp.einsum("tf,te->fe", hidden, upstream_low, preferred_element_type=wide)
    d_hidden = jnp.einsum("te,fe->tf", upstream_low, full_out[D:], preferred_element_type=wide)
    d_glu = jnp.concatenate(
        [d_hidden * up_glu * silu_slope(gate_glu), d_hidden * jax.nn.silu(gate_glu)], axis=1
    ).astype(low)
    grad_glu = jnp.einsum("td,tc->dc", normed_two_low, d_glu, preferred_element_type=wide)
    d_normed_two = jnp.einsum(
        "tc,dc->td", d_glu, full_in[:, mixer_cols:], preferred_element_type=wide
    )
    grad_gains_two = jnp.sum(d_normed_two * middle * scaling_two, axis=0)
    d_middle = upstream + normalize_back(middle, scaling_two, gains_two, d_normed_two)
    d_mixed_low = d_middle.astype(low)
    grad_mixer_out = jnp.einsum("td,te->de", gated_rows, d_mixed_low, preferred_element_type=wide)
    d_gated = jnp.einsum("te,de->td", d_mixed_low, full_out[:D], preferred_element_type=wide)
    d_recurrent = (d_gated * gate_act * filled).astype(low).astype(wide)
    d_gate_pre = d_gated * masked * silu_slope(gate_pre)
    grad_re, grad_im = d_recurrent[:, :CH], d_recurrent[:, CH:]
    summary_back = local_call(local_backward, [(32, CH)], retain, grad_re, grad_im, turn)[0]
    start_back = carry_in(summary_back, turn, length, True)
    d_decay, d_in_re, d_in_im, d_phase = local_call(
        whole_backward,
        [(length, CH)] * 3 + [(1, CH)],
        retain,
        grad_re,
        grad_im,
        turn,
        summary_back,
        start_back,
        states,
    )
    d_decay = d_decay.astype(low).astype(wide)
    d_input = jnp.concatenate([d_in_re, d_in_im], axis=1).astype(low).astype(wide)
    pulled = d_input * driver
    d_forget = jnp.where(starting, 0.0, d_decay) + pulled[:, :CH] + pulled[:, CH:]
    d_forget_pre = -forget * (1.0 - forget) * d_forget
    d_driver_pre = d_input * forget_both * silu_slope(driver_pre)
    d_mix = jnp.concatenate([d_forget_pre, d_driver_pre, d_gate_pre], axis=1).astype(low)
    grad_mixer_in = jnp.einsum("td,tc->dc", normed_low, d_mix, preferred_element_type=wide)
    d_normed = jnp.einsum(
        "tc,dc->td", d_mix, full_in[:, :mixer_cols], preferred_element_type=wide
    )
    grad_gains_one = jnp.sum(d_normed * inputs * scaling_one, axis=0)
    d_tokens = d_middle + normalize_back(inputs, scaling_one, gains_one, d_normed)
    grad_biases = jnp.sum(d_forget_pre, axis=0)
    grad_vectors = jnp.concatenate([grad_gains_one, grad_gains_two, d_phase[0], grad_biases])
    grad_in_all = jnp.concatenate([grad_mixer_in, grad_glu], axis=1)
    grad_out_all = jnp.concatenate([grad_mixer_out, grad_down], axis=0)
    summed_in = lax.psum_scatter(grad_in_all, axes, scatter_dimension=0, tiled=True)
    summed_out = lax.psum_scatter(grad_out_all, axes, scatter_dimension=0, tiled=True)
    summed_vec, total = lax.psum((grad_vectors, jnp.sum(filled)), axes)
    return block_out.astype(low), d_tokens, summed_in, summed_out, summed_vec, total


def body(
    tokens,
    cotangent,
    padding,
    opening,
    w_in,
    w_out,
    vectors,
    m_in,
    v_in,
    m_out,
    v_out,
    m_vec,
    v_vec,
    counter,
):
    run = block_routed if routed(tokens, w_in, w_out) else block_anywhere
    block_out, d_tokens, summed_in, summed_out, summed_vec, total = run(
        tokens, cotangent, padding, opening, w_in, w_out, vectors
    )
    steps = counter[0].astype(jnp.float32)
    grad_in = summed_in / total
    grad_out = summed_out / total
    grad_vec = summed_vec / total
    new_in, first_in, second_in, change_in = adam_update(
        w_in, grad_in, m_in, v_in, steps, WEIGHT_DECAY
    )
    new_out, first_out, second_out, change_out = adam_update(
        w_out, grad_out, m_out, v_out, steps, WEIGHT_DECAY
    )
    new_vec, first_vec, second_vec, update_vec = adam_update(
        vectors, grad_vec, m_vec, v_vec, steps, 0.0
    )
    return (
        unstripe(block_out)[None],
        unstripe(d_tokens)[None],
        grad_in,
        new_in,
        first_in,
        second_in,
        new_in.astype(jnp.bfloat16),
        grad_out,
        new_out,
        first_out,
        second_out,
        new_out.astype(jnp.bfloat16),
        grad_vec,
        grad_vec[2 * D + CH :],
        update_vec,
        first_vec,
        second_vec,
    )


def solution(mesh):
    in_specs = (
        P("rep", "dp", None),
        P("rep", "dp", None),
        P("rep", "dp"),
        P("rep", "dp"),
        P(("dp", "rep"), None),
        P(("dp", "rep"), None),
        P(),
        P(("dp", "rep"), None),
        P(("dp", "rep"), None),
        P(("dp", "rep"), None),
        P(("dp", "rep"), None),
        P(),
        P(),
        P(),
    )
    out_specs = (
        P("rep", "dp", None),
        P("rep", "dp", None),
        P(("dp", "rep"), None),
        P(("dp", "rep"), None),
        P(("dp", "rep"), None),
        P(("dp", "rep"), None),
        P(("dp", "rep"), None),
        P(("dp", "rep"), None),
        P(("dp", "rep"), None),
        P(("dp", "rep"), None),
        P(("dp", "rep"), None),
        P(("dp", "rep"), None),
        P(),
        P(),
        P(),
        P(),
        P(),
    )
    return jax.shard_map(body, mesh=mesh, in_specs=in_specs, out_specs=out_specs, check_vma=False)
```

```python
import functools

import jax
import jax.numpy as jnp
from jax import lax
from jax.experimental import pallas as pl
from jax.experimental.pallas import tpu as pltpu
from jax.sharding import PartitionSpec as P

D = 768
CH = 384
FF = 1536


NORM_EPSILON = 1e-06
LEARN_RATE = 0.05
BETA_ONE = 0.9
BETA_TWO = 0.999
ADAM_EPSILON = 1e-08
WEIGHT_DECAY = 0.1


LANES = 8


def rotate(real, imag, cosine, sine):
    return cosine * real - sine * imag, sine * real + cosine * imag


def turn_power(cosine, sine, doublings):
    for _ in range(doublings):
        cosine, sine = cosine * cosine - sine * sine, 2.0 * cosine * sine
    return cosine, sine


def local_forward(retain, drive_re, drive_im, turn, summary):
    steps = retain.shape[0] // LANES
    cosine, sine = turn[0:1], turn[1:2]
    zero = jnp.zeros((LANES, retain.shape[1]), jnp.float32)

    def step(i, carry):
        real, imag, product = carry
        rows = pl.ds(pl.multiple_of(LANES * i, LANES), LANES)
        r = retain[rows, :]
        turned_re, turned_im = rotate(real, imag, cosine, sine)
        return r * turned_re + drive_re[rows, :], r * turned_im + drive_im[rows, :], r * product

    real, imag, product = lax.fori_loop(0, steps, step, (zero, zero, zero + 1.0), unroll=4)
    cos_sub, sin_sub = turn_power(cosine, sine, steps.bit_length() - 1)
    total_re, total_im, total = real[0:1], imag[0:1], product[0:1]
    for j in range(1, LANES):
        turned_re, turned_im = rotate(total_re, total_im, cos_sub, sin_sub)
        total_re = product[j : j + 1] * turned_re + real[j : j + 1]
        total_im = product[j : j + 1] * turned_im + imag[j : j + 1]
        total = product[j : j + 1] * total
    summary[0:LANES] = real
    summary[LANES : 2 * LANES] = imag
    summary[2 * LANES : 3 * LANES] = product
    summary[24:32] = jnp.concatenate([total_re, total_im, total, zero[3:]], axis=0)


def whole_forward(retain, drive_re, drive_im, turn, summary, start, states):
    steps = retain.shape[0] // LANES
    cosine, sine = turn[0:1], turn[1:2]
    cos_sub, sin_sub = turn_power(cosine, sine, steps.bit_length() - 1)
    now_re, now_im = start[0:1], start[1:2]
    reals, imags = [now_re], [now_im]
    for j in range(LANES - 1):
        turned_re, turned_im = rotate(now_re, now_im, cos_sub, sin_sub)
        product = summary[2 * LANES + j : 2 * LANES + j + 1]
        now_re = product * turned_re + summary[j : j + 1]
        now_im = product * turned_im + summary[LANES + j : LANES + j + 1]
        reals.append(now_re)
        imags.append(now_im)
    carry = (jnp.concatenate(reals, axis=0), jnp.concatenate(imags, axis=0))

    def step(i, carry):
        real, imag = carry
        rows = pl.ds(pl.multiple_of(LANES * i, LANES), LANES)
        states[0, rows, :] = real
        states[1, rows, :] = imag
        r = retain[rows, :]
        turned_re, turned_im = rotate(real, imag, cosine, sine)
        return r * turned_re + drive_re[rows, :], r * turned_im + drive_im[rows, :]

    real, imag = lax.fori_loop(0, steps, step, carry, unroll=4)
    states[0, LANES * steps :, :] = real
    states[1, LANES * steps :, :] = imag


def local_backward(retain, grad_re, grad_im, turn, summary):
    steps = retain.shape[0] // LANES
    cosine, sine = turn[0:1], -turn[1:2]
    zero = jnp.zeros((LANES, retain.shape[1]), jnp.float32)

    def step(k, carry):
        real, imag, product = carry
        rows = pl.ds(pl.multiple_of(LANES * (steps - 1 - k), LANES), LANES)
        r = retain[rows, :]
        turned_re, turned_im = rotate(grad_re[rows, :] + real, grad_im[rows, :] + imag, cosine, sine)
        return r * turned_re, r * turned_im, r * product

    real, imag, product = lax.fori_loop(0, steps, step, (zero, zero, zero + 1.0), unroll=4)
    cos_sub, sin_sub = turn_power(cosine, sine, steps.bit_length() - 1)
    last = LANES - 1
    total_re, total_im, total = real[last:], imag[last:], product[last:]
    for j in range(LANES - 2, -1, -1):
        turned_re, turned_im = rotate(total_re, total_im, cos_sub, sin_sub)
        total_re = product[j : j + 1] * turned_re + real[j : j + 1]
        total_im = product[j : j + 1] * turned_im + imag[j : j + 1]
        total = product[j : j + 1] * total
    summary[0:LANES] = real
    summary[LANES : 2 * LANES] = imag
    summary[2 * LANES : 3 * LANES] = product
    summary[24:32] = jnp.concatenate([total_re, total_im, total, zero[3:]], axis=0)


def whole_backward(
    retain, grad_re, grad_im, turn, summary, start, states, d_decay, d_in_re, d_in_im, d_phase
):
    steps = retain.shape[0] // LANES
    cosine, sine = turn[0:1], turn[1:2]
    cos_sub, sin_sub = turn_power(cosine, -sine, steps.bit_length() - 1)
    now_re, now_im = start[0:1], start[1:2]
    reals, imags = [now_re], [now_im]
    for j in range(LANES - 1, 0, -1):
        turned_re, turned_im = rotate(now_re, now_im, cos_sub, sin_sub)
        product = summary[2 * LANES + j : 2 * LANES + j + 1]
        now_re = product * turned_re + summary[j : j + 1]
        now_im = product * turned_im + summary[LANES + j : LANES + j + 1]
        reals.append(now_re)
        imags.append(now_im)
    zero = jnp.zeros((LANES, retain.shape[1]), jnp.float32)
    carry = (jnp.concatenate(reals[::-1], axis=0), jnp.concatenate(imags[::-1], axis=0), zero)

    def step(k, carry):
        real, imag, phase = carry
        rows = pl.ds(pl.multiple_of(LANES * (steps - 1 - k), LANES), LANES)
        r = retain[rows, :]
        real = grad_re[rows, :] + real
        imag = grad_im[rows, :] + imag
        prior_re, prior_im = rotate(states[0, rows, :], states[1, rows, :], cosine, sine)
        d_decay[rows, :] = -(real * prior_re + imag * prior_im)
        d_in_re[rows, :] = real
        d_in_im[rows, :] = imag
        phase = phase + r * (imag * prior_re - real * prior_im)
        turned_re, turned_im = rotate(real, imag, cosine, -sine)
        return r * turned_re, r * turned_im, phase

    _, _, phase = lax.fori_loop(0, steps, step, carry, unroll=4)
    d_phase[...] = jnp.sum(phase, axis=0, keepdims=True)


def stripe(rows):
    count, columns = rows.shape
    return rows.reshape(LANES, count // LANES, columns).swapaxes(0, 1).reshape(count, columns)


def unstripe(rows):
    count, columns = rows.shape
    return rows.reshape(count // LANES, LANES, columns).swapaxes(0, 1).reshape(count, columns)


def local_call(kernel, outs, *args):
    return pl.pallas_call(
        kernel,
        out_shape=[jax.ShapeDtypeStruct(shape, jnp.float32) for shape in outs],
        compiler_params=pltpu.CompilerParams(vmem_limit_bytes=32 * 1024 * 1024),
    )(*args)


def carry_chain(every, turn, me, length, reverse):
    sine = -turn[1:2] if reverse else turn[1:2]
    cosine, sine = turn_power(turn[0:1], sine, length.bit_length() - 1)
    count = every.shape[0]
    real = jnp.zeros_like(cosine)
    imag = jnp.zeros_like(cosine)
    for j in range(count - 1, 0, -1) if reverse else range(count - 1):
        use = (j > me) if reverse else (j < me)
        turned_re, turned_im = rotate(real, imag, cosine, sine)
        real = jnp.where(use, every[j, 2:3] * turned_re + every[j, 0:1], real)
        imag = jnp.where(use, every[j, 2:3] * turned_im + every[j, 1:2], imag)
    return jnp.concatenate([real, imag], axis=0)


def carry_in(summary, turn, length, reverse):
    every = lax.all_gather(summary[24:32], "dp", axis=0)
    return carry_chain(every, turn, lax.axis_index("dp"), length, reverse)


def normalize(values, gains):
    scaling = lax.rsqrt(jnp.mean(values * values, axis=-1, keepdims=True) + NORM_EPSILON)
    return (values * scaling * gains, scaling)


def normalize_back(values, scaling, gains, gradient):
    scaled = gradient * gains
    return scaling * scaled - values * scaling**3 * jnp.mean(
        values * scaled, axis=-1, keepdims=True
    )


def silu_slope(values):
    logistic = jax.nn.sigmoid(values)
    return logistic * (1.0 + values * (1.0 - logistic))


def adam_update(master, gradient, first, second, steps, decay):
    first_new = BETA_ONE * first + (1.0 - BETA_ONE) * gradient
    second_new = BETA_TWO * second + (1.0 - BETA_TWO) * gradient * gradient
    corrected = (
        first_new
        / (1.0 - BETA_ONE**steps)
        / (jnp.sqrt(second_new / (1.0 - BETA_TWO**steps)) + ADAM_EPSILON)
    )
    change = -LEARN_RATE * (corrected + decay * master)
    return (master + change, first_new, second_new, change)


MESH = pl.DeviceIdType.MESH
LOW = jnp.bfloat16
WIDE = jnp.float32
PLANES = 4
SIDE = 2
IN_ROWS = 24
OUT_ROWS = 72
MIX = CH + 2 * D
CHUNK = 512
CHUNKS = FF // CHUNK
OUT = 2
TILE = 128
OUTS = D // 2 // TILE
GLU = OUT + OUTS
VMEM_BYTES = 63 * 1024 * 1024
SLOTS = 512
ROWS = 64
RUN = SLOTS // LANES


class Piece:
    def __init__(self, matrix, rows, columns, starts, overlap=0):
        self.matrix, self.rows, self.columns = matrix, rows, columns
        self.starts, self.overlap = starts, overlap

    def shape(self):
        return (2, PLANES, SIDE, SIDE, 2 * self.rows, self.columns)


def piece_list():
    drive = (CH + D) // 2 + TILE // 2
    mix = [
        Piece("in", IN_ROWS, drive, (0, CH + D - drive), TILE),
        Piece("in", IN_ROWS, D // 2, (CH + D, MIX - D // 2)),
    ]
    out = [Piece("out", OUT_ROWS, TILE, (TILE * k, D // 2 + TILE * k)) for k in range(OUTS)]
    glu = [
        Piece("in", IN_ROWS, CHUNK, (MIX + CHUNK * k, MIX + FF + CHUNK * k)) for k in range(CHUNKS)
    ]
    return mix + out + glu


PIECES = piece_list()


class Place:
    def __init__(self):
        dp, rep = lax.axis_index("dp"), lax.axis_index("rep")
        self.z, self.x = dp // SIDE, dp % SIDE
        self.y, self.core = rep // 2, rep % 2

    def at(self, z, x, y, core):
        return (z * SIDE + x, y * 2 + core)

    def sibling(self):
        return self.at(self.z, self.x, self.y, 1 - self.core)

    def plane(self, z):
        return self.at(z, self.x, self.y, self.core)

    def near(self, core):
        if core == 0:
            return self.at(self.z, 1 - self.x, self.y, self.core)
        return self.at(self.z, self.x, 1 - self.y, self.core)

    def far(self, core):
        return self.near(1 - core)

    def turn(self, step):
        return lax.rem(self.z + step, PLANES)

    def sides(self, core):
        return (self.x, self.y) if core == 0 else (self.y, self.x)

    def by_core(self, run):
        for core in range(2):
            pl.when(self.core == core)(functools.partial(run, core))

    def greet(self):
        barrier = pltpu.get_barrier_semaphore()
        partners = [self.sibling(), self.near(0), self.near(1)]
        for step in (1, 2, 3):
            partners.append(self.plane(self.turn(step)))
            partners.append(self.at(self.turn(step), 1 - self.x, self.y, self.core))
        for partner in partners:
            pl.semaphore_signal(barrier, inc=1, device_id=partner, device_id_type=MESH)
        return lambda: pl.semaphore_wait(barrier, len(partners))


def block_of(ref, core, z, near, far):
    return ref.at[core, z, near, far] if core == 0 else ref.at[core, z, far, near]


def pair_of(ref, core, z, far):
    return ref.at[core, z, :, far] if core == 0 else ref.at[core, z, far]


def remote(source, target, sent, received, device):
    return pltpu.make_async_remote_copy(
        src_ref=source,
        dst_ref=target,
        send_sem=sent,
        recv_sem=received,
        device_id=device,
        device_id_type=MESH,
    )


GATHER_SEMS = 4 * 2
STEPS_AWAY = (1, 3, 2)
GATHER_NEAR_FIRST = (GLU + 1, GLU + 2)
REDUCE_NEAR_LAST = (GLU, GLU + 1)


class Gather:
    def __init__(self, place, masters, buffers, staging, sems):
        self.place, self.masters, self.buffers, self.staging = place, masters, buffers, staging
        self.local, self.sent0, self.got0 = sems[:3]
        self.sems = sems[3:]

    @staticmethod
    def scratch():
        n = len(PIECES)
        dma = pltpu.SemaphoreType.DMA
        return (
            [pltpu.VMEM(p.shape(), LOW) for p in PIECES]
            + [pltpu.VMEM((2 * p.rows, p.columns), WIDE) for p in PIECES]
            + [dma((n,))] * 3
            + [dma((n, PLANES))] * GATHER_SEMS
        )

    def part(self, p, half):
        piece = PIECES[p]
        start = piece.starts[0] + half * (piece.starts[1] - piece.starts[0])
        return self.masters[piece.matrix].at[:, pl.ds(pl.multiple_of(start, TILE), piece.columns)]

    def own_rows(self, p):
        rows = PIECES[p].rows
        return self.staging[p].at[pl.ds(pl.multiple_of(self.place.core * rows, 8), rows)]

    def to_sibling(self, p):
        return remote(
            self.part(p, 1 - self.place.core),
            self.own_rows(p),
            self.sent0.at[p],
            self.got0.at[p],
            self.place.sibling(),
        )

    def to_self(self, p):
        return pltpu.make_async_copy(
            self.part(p, self.place.core), self.own_rows(p), self.local.at[p]
        )

    def along_z(self, p, z, target, core):
        place = self.place
        near, far = place.sides(core)
        if p in GATHER_NEAR_FIRST:
            part = pair_of(self.buffers[p], core, z, far)
        else:
            part = block_of(self.buffers[p], core, z, near, far)
        sems = self.sems[0].at[p, target], self.sems[1].at[p, z]
        return remote(part, part, *sems, place.plane(target))

    def along_near(self, p, z, core):
        block = block_of(self.buffers[p], core, z, *self.place.sides(core))
        return remote(
            block, block, self.sems[2].at[p, z], self.sems[3].at[p, z], self.place.near(core)
        )

    def along_far(self, p, z, core):
        pair = pair_of(self.buffers[p], core, z, self.place.sides(core)[1])
        return remote(
            pair, pair, self.sems[4].at[p, z], self.sems[5].at[p, z], self.place.far(core)
        )

    def in_chip(self, p, z, core):
        plane = self.buffers[p].at[core, z]
        return remote(
            plane, plane, self.sems[6].at[p, z], self.sems[7].at[p, z], self.place.sibling()
        )

    def begin(self):
        for p in range(len(PIECES)):
            self.to_sibling(p).start()
            self.to_self(p).start()


    def near_own(self, p):
        place = self.place
        self.to_self(p).wait()
        self.to_sibling(p).wait_recv()
        self.buffers[p][place.core, place.z, place.x, place.y] = self.staging[p][...].astype(LOW)
        place.by_core(lambda core: self.along_near(p, place.z, core).start())

    def z_own(self, p):
        place = self.place

        def run(core):
            for step in STEPS_AWAY:
                self.along_z(p, place.z, place.turn(step), core).start()

        place.by_core(run)

    def far_own(self, p):
        place = self.place

        def run(core):
            self.along_near(p, place.z, core).wait_recv()
            self.along_far(p, place.z, core).start()

        place.by_core(run)

    def near(self, p):
        place = self.place

        def run(core):
            for step in STEPS_AWAY:
                z = place.turn(step)
                self.along_z(p, z, place.z, core).wait_recv()
                self.along_near(p, z, core).start()

        if p not in GATHER_NEAR_FIRST:
            place.by_core(run)

    def far(self, p):
        place = self.place

        def run(core):
            for step in STEPS_AWAY:
                z = place.turn(step)
                if p in GATHER_NEAR_FIRST:
                    self.along_z(p, z, place.z, core).wait_recv()
                else:
                    self.along_near(p, z, core).wait_recv()
                self.along_far(p, z, core).start()

        place.by_core(run)

    def chip(self, p):
        def run(core):
            for step in (0,) + STEPS_AWAY:
                z = self.place.turn(step)
                self.along_far(p, z, core).wait_recv()
                self.in_chip(p, z, core).start()

        self.place.by_core(run)

    def arrive(self, p):
        for step in (0,) + STEPS_AWAY:
            z = self.place.turn(step)
            self.in_chip(p, z, 1 - self.place.core).wait_recv()

    def drain(self, p):
        self.to_sibling(p).wait_send()

        def run(core):
            for step in (0,) + STEPS_AWAY:
                z = self.place.turn(step)
                if step:
                    self.along_z(p, self.place.z, z, core).wait_send()
                if p not in GATHER_NEAR_FIRST or step == 0:
                    self.along_near(p, z, core).wait_send()
                self.along_far(p, z, core).wait_send()
                self.in_chip(p, z, core).wait_send()

        self.place.by_core(run)


class Reduce:
    ORDER = STEPS_AWAY + (0,)

    def __init__(self, place, grads, refs, results):
        n = len(PIECES)
        self.place, self.grads, self.results = place, grads, results
        self.far_got, self.near_got, self.planes, self.final = (refs[k * n : (k + 1) * n] for k in range(4))
        self.sems = refs[4 * n :]

    @staticmethod
    def scratch():
        n = len(PIECES)
        dma = pltpu.SemaphoreType.DMA
        blocks = [p.shape()[4:] for p in PIECES]
        return (
            [pltpu.VMEM((PLANES, SIDE) + s, LOW) for s in blocks]
            + [pltpu.VMEM((PLANES,) + s, LOW) for s in blocks]
            + [
                pltpu.VMEM((PLANES,) + (SIDE,) * (p in REDUCE_NEAR_LAST) + s, LOW)
                for p, s in enumerate(blocks)
            ]
            + [pltpu.VMEM(s, WIDE) for s in blocks]
            + [dma((n, PLANES))] * 6
            + [dma((n,))] * 2
        )

    def block(self, p, z, near, far, core):
        return self.grads[p].at[z, near, far] if core == 0 else self.grads[p].at[z, far, near]

    def pair(self, p, z, far, core):
        return self.grads[p].at[z, :, far] if core == 0 else self.grads[p].at[z, far]

    def along_far(self, p, z, core):
        return remote(
            self.pair(p, z, 1 - self.place.sides(core)[1], core),
            self.far_got[p].at[z],
            self.sems[0].at[p, z],
            self.sems[1].at[p, z],
            self.place.far(core),
        )

    def along_near(self, p, z, core):
        near, far = self.place.sides(core)
        return remote(
            self.block(p, z, 1 - near, far, core),
            self.near_got[p].at[z],
            self.sems[2].at[p, z],
            self.sems[3].at[p, z],
            self.place.near(core),
        )

    def along_z(self, p, z, sender, core):
        near, far = self.place.sides(core)
        if p in REDUCE_NEAR_LAST:
            part = self.pair(p, z, far, core)
        else:
            part = self.block(p, z, near, far, core)
        sems = self.sems[4].at[p, z], self.sems[5].at[p, sender]
        return remote(part, self.planes[p].at[sender], *sems, self.place.plane(z))

    def result(self, p, core):
        piece = PIECES[p]
        skip = piece.overlap * core
        start, width = piece.starts[core] + skip, piece.columns - skip
        return self.results[piece.matrix].at[:, pl.ds(start, width)], pl.ds(skip, width)

    def to_sibling(self, p, core):
        rows = PIECES[p].rows
        target, columns = self.result(p, core)
        return remote(
            self.final[p].at[pl.ds(rows * (1 - core), rows), columns],
            target,
            self.sems[6].at[p],
            self.sems[7].at[p],
            self.place.sibling(),
        )

    @staticmethod
    def add(target, source):
        target[...] = (target[...].astype(WIDE) + source[...].astype(WIDE)).astype(LOW)

    def far(self, p):
        def run(core):
            for step in self.ORDER:
                self.along_far(p, self.place.turn(step), core).start()

        self.place.by_core(run)

    def after_far(self, p):
        def run(core):
            for step in self.ORDER:
                z = self.place.turn(step)
                self.along_far(p, z, core).wait_recv()
                self.add(self.pair(p, z, self.place.sides(core)[1], core), self.far_got[p].at[z])
                if p not in REDUCE_NEAR_LAST:
                    self.along_near(p, z, core).start()
                elif step:
                    self.along_z(p, z, self.place.z, core).start()

        self.place.by_core(run)

    def after_near(self, p):
        place = self.place

        def run(core):
            near, far = place.sides(core)
            if p in REDUCE_NEAR_LAST:
                self.along_z_waits(p, core)
                total = self.pair(p, place.z, far, core)[...].astype(WIDE)
                for step in STEPS_AWAY:
                    total = total + self.planes[p][place.turn(step)].astype(WIDE)
                self.pair(p, place.z, far, core)[...] = total.astype(LOW)
                self.along_near(p, place.z, core).start()
                return
            for step in self.ORDER:
                z = place.turn(step)
                self.along_near(p, z, core).wait_recv()
                self.add(self.block(p, z, near, far, core), self.near_got[p].at[z])
                if step:
                    self.along_z(p, z, place.z, core).start()

        place.by_core(run)

    def along_z_waits(self, p, core):
        for step in STEPS_AWAY:
            self.along_z(p, self.place.z, self.place.turn(step), core).wait_recv()

    def finish(self, p):
        rows, place = PIECES[p].rows, self.place

        def run(core):
            near, far = place.sides(core)
            if p in REDUCE_NEAR_LAST:
                self.along_near(p, place.z, core).wait_recv()
                others = [self.near_got[p].at[place.z]]
            else:
                self.along_z_waits(p, core)
                others = [self.planes[p].at[place.turn(step)] for step in STEPS_AWAY]
            total = self.block(p, place.z, near, far, core)[...].astype(WIDE)
            for other in others:
                total = total + other[...].astype(WIDE)
            self.final[p][...] = total
            self.to_sibling(p, core).start()
            target, columns = self.result(p, core)
            target[...] = self.final[p][pl.ds(rows * core, rows), columns]

        place.by_core(run)

    def drain(self, p):
        def run(core):
            self.to_sibling(p, 1 - core).wait_recv()
            self.to_sibling(p, core).wait_send()
            for step in self.ORDER:
                z = self.place.turn(step)
                self.along_far(p, z, core).wait_send()
                if p not in REDUCE_NEAR_LAST or step == 0:
                    self.along_near(p, z, core).wait_send()
                if step:
                    self.along_z(p, z, self.place.z, core).wait_send()

        self.place.by_core(run)


def tiled(column, count):
    return jnp.concatenate([column] * count, axis=1)


def some(index, size=ROWS):
    return pl.ds(pl.multiple_of(index * size, size), size)


def each_block(run, size=ROWS, count=SLOTS):
    lax.fori_loop(0, count // size, lambda i, _: (run(some(i, size)), 0)[1], 0)


def inner(left, right, dims=((1,), (0,))):
    return lax.dot_general(left, right, (dims, ((), ())), preferred_element_type=WIDE)


def across(left, right):
    return inner(left, right, ((1,), (1,)))


def along(left, right):
    return inner(left, right, ((0,), (0,)))


def out_segments(start, count):
    size, runs, stop = 2 * OUT_ROWS, [], start + count
    while start < stop:
        chip, first = divmod(start, size)
        last = min(size, first + stop - start)
        runs.append((chip // 4, chip // 2 % 2, chip % 2, first, last))
        start += last - first
    return runs


def row_norm(values):
    return lax.rsqrt(jnp.mean(values * values, axis=1, keepdims=True) + NORM_EPSILON)


def eights(values):
    return jnp.sum(values.reshape(values.shape[0] // 8, 8, values.shape[1]), axis=0)


def block_scratch():
    vmem, dma = pltpu.VMEM, pltpu.SemaphoreType.DMA
    rows = (SLOTS, D)
    both = (2 * SLOTS, D)
    return dict(
        arrivals=dma((2,)),
        departures=dma((2,)),
        perm=vmem((SLOTS, SLOTS), LOW),
        live=vmem((SLOTS, TILE), WIDE),
        opens=vmem((SLOTS, TILE), WIDE),
        params=vmem((8, D), WIDE),
        tokens=vmem(rows, LOW),
        upstream=vmem((2, SLOTS, D // 2), LOW),
        upstream_got=vmem((SLOTS, D // 2), LOW),
        normed=vmem(both, LOW),
        normed_two=vmem(both, LOW),
        gated=vmem(both, LOW),
        hidden=vmem((CHUNKS, 2 * SLOTS, CHUNK), LOW),
        d_glu=vmem((CHUNKS, 2, SLOTS, CHUNK), LOW),
        d_glu_got=vmem((CHUNKS, SLOTS, CHUNK), LOW),
        d_out=vmem((2, SLOTS, D // 2), LOW),
        d_out_got=vmem((SLOTS, D // 2), LOW),
        d_drive=vmem((2, SLOTS, PIECES[0].columns), LOW),
        d_drive_got=vmem((SLOTS, PIECES[0].columns), LOW),
        d_gate=vmem((2, SLOTS, PIECES[1].columns), LOW),
        d_gate_got=vmem((SLOTS, PIECES[1].columns), LOW),
        pre_mix=vmem((SLOTS, MIX), WIDE),
        glu=vmem((3, SLOTS // 2, CHUNK), WIDE),
        retain=vmem((SLOTS, CH), WIDE),
        drive=vmem(rows, WIDE),
        states=vmem((2, SLOTS + LANES, CH), WIDE),
        summaries=vmem((2, 32, CH), WIDE),
        every=vmem((2, PLANES * SIDE, 8, CH), WIDE),
        middle=vmem(rows, WIDE),
        d_normed=vmem(rows, WIDE),
        total=vmem(rows, WIDE),
        block_out=vmem(rows, LOW),
        sums=vmem((3, 8, D), WIDE),
        vector=vmem((8, VEC_ROWS, TILE), WIDE),
        pair_sent=dma((PAIRS,)),
        pair_got=dma((PAIRS,)),
        carry_sent=dma((2, PLANES * SIDE)),
        carry_got=dma((2, PLANES * SIDE)),
        vector_sent=dma((6,)),
        vector_got=dma((6,)),
    )


VEC_ROWS = 24
VEC_COUNT = 18
PAIRS = 16


class Block:
    def __init__(self, place, buffers, grads, refs):
        self.place, self.weights, self.grads = place, buffers, grads
        for name, ref in refs.items():
            setattr(self, name, ref)
        self.me = place.z * SIDE + place.x


    def swaps(self):
        own, got = pl.ds(0, SLOTS), pl.ds(SLOTS, SLOTS)
        other = 1 - self.place.core
        pairs = dict(
            normed=(self.normed.at[own], self.normed.at[got]),
            normed_two=(self.normed_two.at[own], self.normed_two.at[got]),
            gated=(self.gated.at[own], self.gated.at[got]),
            upstream=(self.upstream.at[other], self.upstream_got),
            d_out=(self.d_out.at[other], self.d_out_got),
            d_drive=(self.d_drive.at[other], self.d_drive_got),
            d_gate=(self.d_gate.at[other], self.d_gate_got),
        )
        for k in range(CHUNKS):
            pairs["hidden", k] = (self.hidden.at[k, own], self.hidden.at[k, got])
            pairs["d_glu", k] = (self.d_glu.at[k, other], self.d_glu_got.at[k])
        return pairs

    def swap(self, name):
        pairs = self.swaps()
        slot = list(pairs).index(name)
        sems = self.pair_sent.at[slot], self.pair_got.at[slot]
        return remote(*pairs[name], *sems, self.place.sibling())

    def give(self, *names):
        for name in names:
            self.swap(name).start()

    def take(self, *names):
        for name in names:
            self.swap(name).wait_recv()

    def settle(self):
        for name in self.swaps():
            self.swap(name).wait_send()


    def mix_weight(self, half, m):
        return self.weights[m][half].reshape(D, PIECES[m].columns)

    def glu_weight(self, k):
        parts = [self.weights[GLU + k][half].reshape(D, CHUNK) for half in range(2)]
        return jnp.concatenate(parts, axis=1)

    def out_weight(self, start, count):
        columns = []
        for half in range(2):
            for p in range(OUT, GLU):
                ref = self.weights[p]
                runs = out_segments(start, count)
                parts = [ref[half, z, x, y, first:last] for z, x, y, first, last in runs]
                columns.append(jnp.concatenate(parts, axis=0))
        return jnp.concatenate(columns, axis=1)

    def put_in(self, p, value):
        self.grads[p][...] = value.astype(LOW).reshape(self.grads[p].shape)

    def put_out(self, start, value):
        value, done = value.astype(LOW), 0
        for z, x, y, first, last in out_segments(start, value.shape[0]):
            count = last - first
            for k in range(OUTS):
                part = value[done : done + count, k * TILE : (k + 1) * TILE]
                self.grads[OUT + k][z, x, y, first:last] = part
            done += count


    def prepare(self, padding, opening, vectors):
        row = lax.broadcasted_iota(jnp.int32, (SLOTS, SLOTS), 0)
        column = lax.broadcasted_iota(jnp.int32, (SLOTS, SLOTS), 1)
        perm = (column == row % LANES * RUN + row // LANES).astype(WIDE)
        self.perm[...] = perm.astype(LOW)
        ones = jnp.ones((SLOTS, TILE), LOW)
        self.live[...] = inner((perm * padding[...].astype(WIDE)).astype(LOW), ones)
        self.opens[...] = inner((perm * opening[...].astype(WIDE)).astype(LOW), ones)

        def line(first, count):
            return jnp.concatenate([vectors[first + i : first + i + 1] for i in range(count)], axis=1)

        phase = line(12, 3)
        self.params[0:1] = line(0, 6)
        self.params[1:2] = line(6, 6)
        self.params[2:3] = jnp.concatenate([jnp.cos(phase), jnp.sin(phase)], axis=1)
        self.params[3:4] = jnp.concatenate([line(15, 3)] * 2, axis=1)
        self.sums[...] = jnp.zeros_like(self.sums)

    def turn(self):
        return jnp.concatenate([self.params[2:3, :CH], self.params[2:3, CH:]], axis=0)

    def first_norm(self, raw):
        self.tokens[...] = inner(self.perm[...], raw[...]).astype(LOW)

        def run(rows):
            values = self.tokens[rows, :].astype(WIDE)
            self.normed[rows, :] = (values * row_norm(values) * self.params[0:1]).astype(LOW)

        each_block(run)

    def mask_upstream(self, raw):
        striped = inner(self.perm[...], raw[...]) * tiled(self.live[...], D // TILE)
        self.upstream[0] = striped[:, : D // 2].astype(LOW)
        self.upstream[1] = striped[:, D // 2 :].astype(LOW)

    def mix(self, m):
        normed, piece = self.normed[0:SLOTS, :], PIECES[m]
        for half in range(2):
            skip = piece.overlap * half
            start = piece.starts[half] + skip
            product = inner(normed, self.mix_weight(half, m))
            self.pre_mix[:, start : start + piece.columns - skip] = product[:, skip:]

    def drives(self):
        def run(rows):
            forget = jax.nn.sigmoid(-(self.pre_mix[rows, :CH] + self.params[3:4, :CH]))
            pre = self.pre_mix[rows, CH : CH + D]
            driver = pre * jax.nn.sigmoid(pre)
            opens = tiled(self.opens[rows, :], CH // TILE)
            decay = jnp.where(opens > 0.5, 1.0, forget).astype(LOW).astype(WIDE)
            self.retain[rows, :] = 1.0 - decay
            drive = jnp.concatenate([forget, forget], axis=1) * driver
            self.drive[rows, :] = drive.astype(LOW).astype(WIDE)

        each_block(run)

    def parts(self):
        return self.drive.at[:, pl.ds(0, CH)], self.drive.at[:, pl.ds(CH, CH)]

    def others(self):
        place = self.place
        for step in range(PLANES):
            for flip in range(SIDE):
                if step or flip:
                    z = place.turn(step)
                    x = 1 - place.x if flip else place.x
                    yield z * SIDE + x, place.at(z, x, place.y, place.core)

    def carry_copy(self, way, other, device, sender):
        return remote(
            self.summaries.at[way, pl.ds(24, 8)],
            self.every.at[way, sender],
            self.carry_sent.at[way, other],
            self.carry_got.at[way, sender],
            device,
        )

    def scan_own(self, way):
        run = local_backward if way else local_forward
        run(self.retain, *self.parts(), self.turn(), self.summaries.at[way])
        self.every[way, self.me] = self.summaries[way, 24:32]
        for other, device in self.others():
            self.carry_copy(way, other, device, self.me).start()

    def carried(self, way):
        for other, device in self.others():
            self.carry_copy(way, other, device, other).wait_recv()
        turn = self.turn()
        return carry_chain(self.every.at[way], turn, self.me, SLOTS, way == 1)

    def scan_states(self):
        start = self.carried(0)
        run = whole_forward
        run(self.retain, *self.parts(), self.turn(), self.summaries.at[0], start, self.states)

    def recurrent(self, rows):
        after = pl.ds(pl.multiple_of(rows.start + LANES, LANES), rows.size)
        both = jnp.concatenate([self.states[0, after, :], self.states[1, after, :]], axis=1)
        return both.astype(LOW).astype(WIDE)

    def gate_rows(self):
        def run(rows):
            pre = self.pre_mix[rows, CH + D :]
            masked = self.recurrent(rows) * tiled(self.live[rows, :], D // TILE)
            self.gated[rows, :] = (masked * (pre * jax.nn.sigmoid(pre))).astype(LOW)

        each_block(run)

    def second_norm(self):
        self.middle[...] = inner(self.gated[0:SLOTS, :], self.out_weight(0, D))

        def run(rows):
            middle = self.tokens[rows, :].astype(WIDE) + self.middle[rows, :]
            self.middle[rows, :] = middle
            self.normed_two[rows, :] = (middle * row_norm(middle) * self.params[1:2]).astype(LOW)

        each_block(run)

    def glu_forward(self, k):
        weight = self.glu_weight(k)
        down = self.out_weight(D + CHUNK * k, CHUNK)
        half = SLOTS // 2
        for part in range(2):
            rows = slice(part * half, (part + 1) * half)
            pre = inner(self.normed_two[rows, :], weight)
            self.glu[0] = pre[:, :CHUNK]
            self.glu[1] = pre[:, CHUNK:]
            upstream = jnp.concatenate([self.upstream[0, rows], self.upstream[1, rows]], axis=1)
            self.glu[2] = across(upstream, down)

            def run(block):
                gate, up, d_hidden = (self.glu[i, block, :] for i in range(3))
                own = pl.ds(pl.multiple_of(block.start + part * half, ROWS), ROWS)
                logistic = jax.nn.sigmoid(gate)
                active = gate * logistic
                slope = logistic * (1.0 + gate * (1.0 - logistic))
                self.hidden[k, own, :] = (active * up).astype(LOW)
                self.d_glu[k, 0, own, :] = (d_hidden * up * slope).astype(LOW)
                self.d_glu[k, 1, own, :] = (d_hidden * active).astype(LOW)

            each_block(run, count=half)

    def glu_back(self, k):
        down = self.out_weight(D + CHUNK * k, CHUNK)
        share = inner(self.hidden[k, 0:SLOTS, :], down)
        d_glu = jnp.concatenate([self.d_glu[k, 0], self.d_glu[k, 1]], axis=1)
        d_share = across(d_glu, self.glu_weight(k))
        if k == 0:
            self.total[...] = self.middle[...] + share
            self.d_normed[...] = d_share
        else:
            self.total[...] += share
            self.d_normed[...] += d_share
        if k == CHUNKS - 1:
            self.block_out[...] = self.total[...].astype(LOW)

    def own_half(self, ref, got):
        return jnp.concatenate([ref[self.place.core], got], axis=0)

    def glu_grads(self, k):
        d_glu = jnp.concatenate([self.d_glu[k, self.place.core], self.d_glu_got[k]], axis=0)
        self.put_in(GLU + k, along(self.normed_two[...], d_glu))
        upstream = self.own_half(self.upstream, self.upstream_got[...])
        self.put_out(D + CHUNK * k, along(self.hidden[k], upstream))

    def add_sum(self, index, values):
        self.sums[index, :, : values.shape[1]] += eights(values)

    def middle_back(self):
        def run(rows):
            middle, d_normed = self.middle[rows, :], self.d_normed[rows, :]
            scaling = row_norm(middle)
            self.add_sum(1, d_normed * middle * scaling)
            scaled = d_normed * self.params[1:2]
            mean = jnp.mean(middle * scaled, axis=1, keepdims=True)
            upstream = jnp.concatenate([self.upstream[0, rows], self.upstream[1, rows]], axis=1)
            d_middle = upstream.astype(WIDE) + scaling * scaled - middle * (scaling**3 * mean)
            self.middle[rows, :] = d_middle
            self.d_out[0, rows] = d_middle[:, : D // 2].astype(LOW)
            self.d_out[1, rows] = d_middle[:, D // 2 :].astype(LOW)

        each_block(run)

    def gate_back(self):
        d_out = jnp.concatenate([self.d_out[0], self.d_out[1]], axis=1)
        self.total[...] = across(d_out, self.out_weight(0, D))

        def run(rows):
            pre, d_gated = self.pre_mix[rows, CH + D :], self.total[rows, :]
            logistic = jax.nn.sigmoid(pre)
            d_live = d_gated * tiled(self.live[rows, :], D // TILE)
            self.drive[rows, :] = (d_live * (pre * logistic)).astype(LOW).astype(WIDE)
            slope = logistic * (1.0 + pre * (1.0 - logistic))
            d_gate = (d_live * self.recurrent(rows) * slope).astype(LOW)
            self.d_gate[0, rows, :] = d_gate[:, : D // 2]
            self.d_gate[1, rows, :] = d_gate[:, D // 2 :]

        each_block(run)

    def mixer_out_grad(self):
        d_out = self.own_half(self.d_out, self.d_out_got[...])
        self.put_out(0, along(self.gated[...], d_out))

    def scan_back(self):
        start = self.carried(1)
        real, imag = self.parts()
        whole_backward(
            self.retain,
            real,
            imag,
            self.turn(),
            self.summaries.at[1],
            start,
            self.states,
            self.retain,
            real,
            imag,
            self.sums.at[2, pl.ds(0, 1), pl.ds(0, CH)],
        )

    def drives_back(self):
        def run(rows):
            forget = jax.nn.sigmoid(-(self.pre_mix[rows, :CH] + self.params[3:4, :CH]))
            pre = self.pre_mix[rows, CH : CH + D]
            logistic = jax.nn.sigmoid(pre)
            d_decay = self.retain[rows, :].astype(LOW).astype(WIDE)
            d_input = self.drive[rows, :].astype(LOW).astype(WIDE)
            pulled = d_input * (pre * logistic)
            opens = tiled(self.opens[rows, :], CH // TILE)
            d_forget = jnp.where(opens > 0.5, 0.0, d_decay) + pulled[:, :CH] + pulled[:, CH:]
            d_first = -forget * (1.0 - forget) * d_forget
            self.sums[2, :, CH:] += eights(d_first)
            slope = logistic * (1.0 + pre * (1.0 - logistic))
            d_driver = d_input * jnp.concatenate([forget, forget], axis=1) * slope
            d_pre = jnp.concatenate([d_first, d_driver], axis=1).astype(LOW)
            piece = PIECES[0]
            for half, start in enumerate(piece.starts):
                self.d_drive[half, rows, :] = d_pre[:, start : start + piece.columns]

        each_block(run)

    def mix_grads(self, m):
        own, got = ((self.d_drive, self.d_drive_got), (self.d_gate, self.d_gate_got))[m]
        self.put_in(m, along(self.normed[...], self.own_half(own, got[...])))

    def gate_normed(self):
        left = jnp.concatenate([self.d_gate[0], self.d_gate[1]], axis=1)
        right = jnp.concatenate([self.mix_weight(0, 1), self.mix_weight(1, 1)], axis=1)
        self.d_normed[...] = across(left, right)

    def first_back(self):
        skip = PIECES[0].overlap
        left = jnp.concatenate([self.d_drive[0], self.d_drive[1][:, skip:]], axis=1)
        right = jnp.concatenate([self.mix_weight(0, 0), self.mix_weight(1, 0)[:, skip:]], axis=1)
        self.d_normed[...] += across(left, right)

        def run(rows):
            values, d_normed = self.tokens[rows, :].astype(WIDE), self.d_normed[rows, :]
            scaling = row_norm(values)
            self.add_sum(0, d_normed * values * scaling)
            scaled = d_normed * self.params[0:1]
            mean = jnp.mean(values * scaled, axis=1, keepdims=True)
            self.middle[rows, :] += scaling * scaled - values * (scaling**3 * mean)

        each_block(run)

    def natural_out(self):
        self.block_out[...] = along(self.perm[...], self.block_out[...]).astype(LOW)

    def natural_tokens(self):
        rest = self.middle[...]
        total = jnp.zeros_like(rest)
        for _ in range(3):
            part = rest.astype(LOW)
            total = total + along(self.perm[...], part)
            rest = rest - part.astype(WIDE)
        self.d_normed[...] = total


    def gather_vector(self):
        lines = [
            jnp.sum(self.sums[0], axis=0, keepdims=True),
            jnp.sum(self.sums[1], axis=0, keepdims=True),
            jnp.concatenate(
                [self.sums[2, 0:1, :CH], jnp.sum(self.sums[2, :, CH:], axis=0, keepdims=True)], axis=1
            ),
        ]
        for i, line in enumerate(lines):
            for j in range(D // TILE):
                row = i * (D // TILE) + j
                self.vector[0, row : row + 1] = line[:, j * TILE : (j + 1) * TILE]
        filled = jnp.sum(self.live[...], axis=0, keepdims=True)
        rest = jnp.zeros((VEC_ROWS - VEC_COUNT - 1, TILE), WIDE)
        self.vector[0, VEC_COUNT:] = jnp.concatenate([filled, rest], axis=0)

    def vector_copy(self, stage):
        place = self.place
        device = (place.sibling(), place.near(0), place.near(1))[stage]
        source = self.vector.at[stage]
        target = self.vector.at[4 + stage]
        return remote(source, target, self.vector_sent.at[stage], self.vector_got.at[stage], device)

    def vector_step(self, stage):
        if stage:
            self.vector_copy(stage - 1).wait_recv()
            self.vector[stage] = self.vector[stage - 1] + self.vector[3 + stage]
        if stage < 3:
            self.vector_copy(stage).start()

    def vector_plane(self, planes, step, sender):
        place = self.place
        return remote(
            self.vector.at[3],
            planes.at[sender],
            self.vector_sent.at[2 + step],
            self.vector_got.at[2 + step],
            place.plane(place.turn(step)),
        )


def block_kernel(tokens, cotangent, padding, opening, w_in, w_out, vectors, *refs):
    n = len(PIECES)
    block_out, d_tokens, sum_in, sum_out, planes = refs[:5]
    refs = refs[5:]
    count = len(Gather.scratch())
    gather_refs, refs = refs[:count], refs[count:]
    buffers, staging, gather_sems = gather_refs[:n], gather_refs[n : 2 * n], gather_refs[2 * n :]
    grads, refs = refs[:n], refs[n:]
    count = len(Reduce.scratch())
    reduce_refs, refs = refs[:count], refs[count:]
    place = Place()
    gather = Gather(place, {"in": w_in, "out": w_out}, buffers, staging, gather_sems)
    reduce = Reduce(place, grads, reduce_refs, {"in": sum_in, "out": sum_out})
    block = Block(place, buffers, grads, dict(zip(block_scratch(), refs, strict=True)))

    entered = place.greet()
    raw_tokens, raw_upstream = block.gated.at[pl.ds(0, SLOTS)], block.block_out
    loads = [
        pltpu.make_async_copy(tokens.at[0], raw_tokens, block.arrivals.at[0]),
        pltpu.make_async_copy(cotangent.at[0], raw_upstream, block.arrivals.at[1]),
    ]
    for load in loads:
        load.start()
    block.prepare(padding, opening, vectors)
    entered()
    gather.begin()
    loads[0].wait()
    block.first_norm(raw_tokens)

    out = range(OUT, GLU)
    for p in (0, 1):
        gather.near_own(p)
        gather.z_own(p)
    for p in range(2, n):
        gather.near_own(p)
    loads[1].wait()
    block.mask_upstream(raw_upstream)
    block.give("normed", "upstream")
    gather.far_own(0)
    gather.far_own(1)
    gather.near(0)
    gather.z_own(2)
    gather.far_own(2)
    gather.far(0)
    gather.near(1)
    gather.z_own(3)
    gather.far_own(3)
    gather.chip(0)
    gather.far(1)
    gather.near(2)
    gather.z_own(4)
    gather.far_own(4)
    gather.arrive(0)
    block.mix(0)
    block.drives()
    block.scan_own(0)
    gather.chip(1)
    gather.far(2)
    gather.near(3)
    gather.z_own(5)
    gather.far_own(5)
    gather.arrive(1)
    block.mix(1)
    gather.chip(2)
    gather.far(3)
    gather.near(4)
    gather.far_own(6)
    gather.z_own(6)
    block.scan_states()
    block.gate_rows()
    block.give("gated")
    gather.chip(3)
    gather.far(4)
    gather.near(5)
    gather.far_own(7)
    gather.z_own(7)
    gather.chip(4)
    gather.far(5)
    for p in out:
        gather.arrive(p)
    block.second_norm()
    block.give("normed_two")
    gather.chip(5)
    gather.far(6)

    def glu_chunk(k, beside):
        gather.arrive(GLU + k)
        block.glu_forward(k)
        block.give(("hidden", k), ("d_glu", k))
        for run, p in beside:
            run(p)
        block.glu_back(k)
        if k == 0:
            block.take("upstream", "normed_two")
        block.take(("hidden", k), ("d_glu", k))
        block.glu_grads(k)

    glu_chunk(0, ((gather.chip, 6), (gather.far, 7)))
    reduce.far(GLU)
    glu_chunk(1, ((gather.chip, 7),))
    reduce.far(GLU + 1)
    glu_chunk(2, ((reduce.after_far, GLU),))
    block.middle_back()
    block.give("d_out")
    block.gate_back()
    block.scan_own(1)
    reduce.far(GLU + 2)
    block.give("d_gate")
    block.take("gated", "d_out")
    block.mixer_out_grad()
    reduce.after_far(GLU + 1)
    for p in out:
        reduce.far(p)
    block.take("normed", "d_gate")
    block.mix_grads(1)
    reduce.far(1)
    block.gate_normed()
    reduce.after_near(GLU)
    reduce.after_far(GLU + 2)
    block.scan_back()
    block.drives_back()
    block.give("d_drive")
    reduce.after_far(OUT)
    reduce.after_near(GLU + 1)
    block.take("d_drive")
    block.mix_grads(0)
    reduce.far(0)
    block.natural_out()
    leave_out = pltpu.make_async_copy(block.block_out, block_out, block.departures.at[0])
    leave_out.start()
    reduce.after_far(OUT + 1)
    reduce.after_near(GLU + 2)
    reduce.finish(GLU)
    block.first_back()
    reduce.after_far(OUT + 2)
    reduce.after_near(OUT)
    block.gather_vector()
    block.vector_step(0)
    block.natural_tokens()
    leave_tokens = pltpu.make_async_copy(block.d_normed, d_tokens, block.departures.at[1])
    leave_tokens.start()
    reduce.after_far(1)
    reduce.after_near(OUT + 1)
    block.vector_step(1)
    reduce.finish(GLU + 1)
    reduce.after_near(OUT + 2)
    reduce.after_far(0)
    reduce.finish(GLU + 2)
    reduce.after_near(1)
    block.vector_step(2)
    reduce.finish(OUT)
    reduce.after_near(0)
    block.vector_step(3)
    for step in (1, 2, 3):
        block.vector_plane(planes, step, place.z).start()
    planes[place.z] = block.vector[3]
    reduce.finish(OUT + 1)
    reduce.finish(OUT + 2)
    reduce.finish(1)
    reduce.finish(0)

    for step in (1, 2, 3):
        block.vector_plane(planes, step, place.z).wait_send()
        block.vector_plane(planes, step, place.turn(4 - step)).wait_recv()
    for stage in range(3):
        block.vector_copy(stage).wait_send()
    for way in range(2):
        for other, device in block.others():
            block.carry_copy(way, other, device, block.me).wait_send()
    block.settle()
    for p in range(n):
        gather.drain(p)
        reduce.drain(p)
    leave_out.wait()
    leave_tokens.wait()


def block_routed(tokens, cotangent, padding, opening, w_in, w_out, vectors):
    vmem = pl.BlockSpec(memory_space=pltpu.VMEM)
    anywhere = pl.BlockSpec(memory_space=pl.ANY)
    out_shape = [
        jax.ShapeDtypeStruct((SLOTS, D), LOW),
        jax.ShapeDtypeStruct((SLOTS, D), WIDE),
        jax.ShapeDtypeStruct(w_in.shape, WIDE),
        jax.ShapeDtypeStruct(w_out.shape, WIDE),
        jax.ShapeDtypeStruct((PLANES, VEC_ROWS, TILE), WIDE),
    ]
    grads = [pltpu.VMEM(p.shape()[1:], LOW) for p in PIECES]
    block_out, d_tokens, sum_in, sum_out, planes = pl.pallas_call(
        block_kernel,
        out_shape=out_shape,
        in_specs=[anywhere, anywhere, vmem, vmem, anywhere, anywhere, vmem],
        out_specs=[anywhere, anywhere, vmem, vmem, vmem],
        scratch_shapes=Gather.scratch()
        + grads
        + Reduce.scratch()
        + list(block_scratch().values()),
        compiler_params=pltpu.CompilerParams(
            collective_id=0, has_side_effects=True, vmem_limit_bytes=VMEM_BYTES
        ),
    )(tokens, cotangent, padding, opening, w_in, w_out, vectors.reshape(VEC_COUNT, TILE))
    return block_out, d_tokens, sum_in, sum_out, planes


def power(base, count):
    return lax.fori_loop(0, count, lambda _, value: value * base, jnp.float32(1.0))


def update_kernel(counter, planes, block_from, tokens_from, *refs):
    ins, outs = refs[:11], refs[11:]
    outs[0][...] = block_from[...]
    outs[1][...] = tokens_from[...]
    first_scale = 1.0 - power(BETA_ONE, counter[0])
    second_scale = 1.0 - power(BETA_TWO, counter[0])
    vectors = (planes[0] + planes[1]) + (planes[2] + planes[3])
    total = vectors[VEC_COUNT : VEC_COUNT + 1, 0:1]

    def step(summed, master, first, second, decay):
        gradient = summed / total
        first = BETA_ONE * first + (1.0 - BETA_ONE) * gradient
        second = BETA_TWO * second + (1.0 - BETA_TWO) * gradient * gradient
        corrected = first / first_scale / (jnp.sqrt(second / second_scale) + ADAM_EPSILON)
        return gradient, -LEARN_RATE * (corrected + decay * master), first, second

    for k in range(2):
        summed, master, first, second = (ref[...] for ref in ins[4 * k : 4 * k + 4])
        gradient, change, first, second = step(summed, master, first, second, WEIGHT_DECAY)
        new = master + change
        results = (gradient, new, first, second, new.astype(LOW))
        for ref, value in zip(outs[2 + 5 * k : 7 + 5 * k], results, strict=True):
            ref[...] = value
    master, first, second = (ref[...] for ref in ins[8:])
    results = step(vectors[:VEC_COUNT], master, first, second, 0.0)
    for ref, value in zip(outs[12:], results, strict=True):
        ref[...] = value


UPDATE_BLOCKS = 3


def update(counter, planes, block_out, d_tokens, sums, masters, moments, vector_state):
    shapes = [x.shape for x in sums]

    def by_columns(shape):
        return pl.BlockSpec((shape[0], shape[1] // UPDATE_BLOCKS), lambda i: (0, i))

    def whole(shape):
        return pl.BlockSpec(shape, lambda i: (0,) * len(shape))

    vector = whole((VEC_COUNT, TILE))
    columns = [by_columns(shape) for shape in shapes]
    types = (WIDE, WIDE, WIDE, WIDE, LOW)
    out_shape = [
        jax.ShapeDtypeStruct(block_out.shape, block_out.dtype),
        jax.ShapeDtypeStruct(d_tokens.shape, d_tokens.dtype),
    ]
    out_shape += [jax.ShapeDtypeStruct(shape, kind) for shape in shapes for kind in types]
    out_shape += [jax.ShapeDtypeStruct((VEC_COUNT, TILE), WIDE)] * 4
    operands = []
    for k in range(2):
        operands += [sums[k], masters[k], *moments[k]]
    return pl.pallas_call(
        update_kernel,
        grid=(UPDATE_BLOCKS,),
        out_shape=out_shape,
        in_specs=[pl.BlockSpec(memory_space=pltpu.SMEM), whole(planes.shape)]
        + [by_columns(block_out.shape)] * 2
        + [columns[0]] * 4
        + [columns[1]] * 4
        + [vector] * 3,
        out_specs=[by_columns(block_out.shape)] * 2 + [columns[0]] * 5 + [columns[1]] * 5 + [vector] * 4,
        compiler_params=pltpu.CompilerParams(vmem_limit_bytes=VMEM_BYTES),
    )(counter, planes, block_out, d_tokens, *operands, *vector_state)


def routed(tokens, w_in, w_out):
    sizes = (lax.axis_size("dp"), lax.axis_size("rep"))
    shards = (tokens.shape[1], w_in.shape[0], w_out.shape[0])
    return sizes == (PLANES * SIDE, SIDE * 2) and shards == (SLOTS, IN_ROWS, OUT_ROWS)


def block_anywhere(tokens, cotangent, padding, opening, w_in, w_out, vectors):
    low = jnp.bfloat16
    wide = jnp.float32
    mixer_cols = CH + 2 * D
    length = tokens.shape[1]
    inputs = stripe(tokens[0]).astype(wide)
    filled = stripe(padding[0][:, None]).astype(wide)
    starting = stripe(opening[0][:, None]) == 1
    gains_one = vectors[:D]
    gains_two = vectors[D : 2 * D]
    phases = vectors[2 * D : 2 * D + CH]
    biases = vectors[2 * D + CH :]
    turn = jnp.stack([jnp.cos(phases), jnp.sin(phases)])
    axes = ("dp", "rep")
    full_in = lax.all_gather(w_in.astype(low), axes, axis=0, tiled=True)
    full_out = lax.all_gather(w_out.astype(low), axes, axis=0, tiled=True)
    normed, scaling_one = normalize(inputs, gains_one)
    normed_low = normed.astype(low)
    pre_mix = jnp.dot(normed_low, full_in[:, :mixer_cols], preferred_element_type=wide)
    forget = jax.nn.sigmoid(-(pre_mix[:, :CH] + biases))
    driver_pre = pre_mix[:, CH : CH + D]
    driver = jax.nn.silu(driver_pre)
    gate_pre = pre_mix[:, CH + D :]
    forget_both = jnp.concatenate([forget, forget], axis=1)
    decay = jnp.where(starting, 1.0, forget).astype(low).astype(wide)
    retain = 1.0 - decay
    drive = (forget_both * driver).astype(low).astype(wide)
    drive_re, drive_im = drive[:, :CH], drive[:, CH:]
    summary = local_call(local_forward, [(32, CH)], retain, drive_re, drive_im, turn)[0]
    start = carry_in(summary, turn, length, False)
    states = local_call(
        whole_forward, [(2, length + 8, CH)], retain, drive_re, drive_im, turn, summary, start
    )[0]
    recurrent = jnp.concatenate([states[0, LANES:], states[1, LANES:]], axis=1)
    recurrent = recurrent.astype(low).astype(wide)
    gate_act = jax.nn.silu(gate_pre)
    masked = recurrent * filled
    gated_rows = (masked * gate_act).astype(low)
    middle = inputs + jnp.dot(gated_rows, full_out[:D], preferred_element_type=wide)
    normed_two, scaling_two = normalize(middle, gains_two)
    normed_two_low = normed_two.astype(low)
    glu_pre = jnp.dot(normed_two_low, full_in[:, mixer_cols:], preferred_element_type=wide)
    gate_glu = glu_pre[:, :FF]
    up_glu = glu_pre[:, FF:]
    hidden = (jax.nn.silu(gate_glu) * up_glu).astype(low)
    block_out = middle + jnp.dot(hidden, full_out[D:], preferred_element_type=wide)
    upstream = stripe(cotangent[0]).astype(wide) * filled
    upstream_low = upstream.astype(low)
    grad_down = jnp.einsum("tf,te->fe", hidden, upstream_low, preferred_element_type=wide)
    d_hidden = jnp.einsum("te,fe->tf", upstream_low, full_out[D:], preferred_element_type=wide)
    d_glu = jnp.concatenate(
        [d_hidden * up_glu * silu_slope(gate_glu), d_hidden * jax.nn.silu(gate_glu)], axis=1
    ).astype(low)
    grad_glu = jnp.einsum("td,tc->dc", normed_two_low, d_glu, preferred_element_type=wide)
    d_normed_two = jnp.einsum(
        "tc,dc->td", d_glu, full_in[:, mixer_cols:], preferred_element_type=wide
    )
    grad_gains_two = jnp.sum(d_normed_two * middle * scaling_two, axis=0)
    d_middle = upstream + normalize_back(middle, scaling_two, gains_two, d_normed_two)
    d_mixed_low = d_middle.astype(low)
    grad_mixer_out = jnp.einsum("td,te->de", gated_rows, d_mixed_low, preferred_element_type=wide)
    d_gated = jnp.einsum("te,de->td", d_mixed_low, full_out[:D], preferred_element_type=wide)
    d_recurrent = (d_gated * gate_act * filled).astype(low).astype(wide)
    d_gate_pre = d_gated * masked * silu_slope(gate_pre)
    grad_re, grad_im = d_recurrent[:, :CH], d_recurrent[:, CH:]
    summary_back = local_call(local_backward, [(32, CH)], retain, grad_re, grad_im, turn)[0]
    start_back = carry_in(summary_back, turn, length, True)
    d_decay, d_in_re, d_in_im, d_phase = local_call(
        whole_backward,
        [(length, CH)] * 3 + [(1, CH)],
        retain,
        grad_re,
        grad_im,
        turn,
        summary_back,
        start_back,
        states,
    )
    d_decay = d_decay.astype(low).astype(wide)
    d_input = jnp.concatenate([d_in_re, d_in_im], axis=1).astype(low).astype(wide)
    pulled = d_input * driver
    d_forget = jnp.where(starting, 0.0, d_decay) + pulled[:, :CH] + pulled[:, CH:]
    d_forget_pre = -forget * (1.0 - forget) * d_forget
    d_driver_pre = d_input * forget_both * silu_slope(driver_pre)
    d_mix = jnp.concatenate([d_forget_pre, d_driver_pre, d_gate_pre], axis=1).astype(low)
    grad_mixer_in = jnp.einsum("td,tc->dc", normed_low, d_mix, preferred_element_type=wide)
    d_normed = jnp.einsum(
        "tc,dc->td", d_mix, full_in[:, :mixer_cols], preferred_element_type=wide
    )
    grad_gains_one = jnp.sum(d_normed * inputs * scaling_one, axis=0)
    d_tokens = d_middle + normalize_back(inputs, scaling_one, gains_one, d_normed)
    grad_biases = jnp.sum(d_forget_pre, axis=0)
    grad_vectors = jnp.concatenate([grad_gains_one, grad_gains_two, d_phase[0], grad_biases])
    grad_in_all = jnp.concatenate([grad_mixer_in, grad_glu], axis=1)
    grad_out_all = jnp.concatenate([grad_mixer_out, grad_down], axis=0)
    summed_in = lax.psum_scatter(grad_in_all, axes, scatter_dimension=0, tiled=True)
    summed_out = lax.psum_scatter(grad_out_all, axes, scatter_dimension=0, tiled=True)
    summed_vec, total = lax.psum((grad_vectors, jnp.sum(filled)), axes)
    return unstripe(block_out.astype(low)), unstripe(d_tokens), summed_in, summed_out, summed_vec, total


def body(
    tokens,
    cotangent,
    padding,
    opening,
    w_in,
    w_out,
    vectors,
    m_in,
    v_in,
    m_out,
    v_out,
    m_vec,
    v_vec,
    counter,
):
    if routed(tokens, w_in, w_out):
        block_out, d_tokens, sum_in, sum_out, planes = block_routed(
            tokens, cotangent, padding, opening, w_in, w_out, vectors
        )
        sums, masters = (sum_in, sum_out), (w_in, w_out)
        moments = ((m_in, v_in), (m_out, v_out))
        lines = [x.reshape(VEC_COUNT, TILE) for x in (vectors, m_vec, v_vec)]
        results = update(
            counter, planes, block_out, d_tokens, sums, masters, moments, lines
        )
        block_out, d_tokens = results[:2]
        grad_vec, update_vec, first_vec, second_vec = (x.reshape(-1) for x in results[12:])
        return (
            block_out[None],
            d_tokens[None],
            *results[2:12],
            grad_vec,
            grad_vec[2 * D + CH :],
            update_vec,
            first_vec,
            second_vec,
        )
    block_out, d_tokens, summed_in, summed_out, summed_vec, total = block_anywhere(
        tokens, cotangent, padding, opening, w_in, w_out, vectors
    )
    steps = counter[0].astype(jnp.float32)
    grad_in = summed_in / total
    grad_out = summed_out / total
    grad_vec = summed_vec / total
    new_in, first_in, second_in, change_in = adam_update(
        w_in, grad_in, m_in, v_in, steps, WEIGHT_DECAY
    )
    new_out, first_out, second_out, change_out = adam_update(
        w_out, grad_out, m_out, v_out, steps, WEIGHT_DECAY
    )
    new_vec, first_vec, second_vec, update_vec = adam_update(
        vectors, grad_vec, m_vec, v_vec, steps, 0.0
    )
    return (
        block_out[None],
        d_tokens[None],
        grad_in,
        new_in,
        first_in,
        second_in,
        new_in.astype(jnp.bfloat16),
        grad_out,
        new_out,
        first_out,
        second_out,
        new_out.astype(jnp.bfloat16),
        grad_vec,
        grad_vec[2 * D + CH :],
        update_vec,
        first_vec,
        second_vec,
    )


def solution(mesh):
    in_specs = (
        P("rep", "dp", None),
        P("rep", "dp", None),
        P("rep", "dp"),
        P("rep", "dp"),
        P(("dp", "rep"), None),
        P(("dp", "rep"), None),
        P(),
        P(("dp", "rep"), None),
        P(("dp", "rep"), None),
        P(("dp", "rep"), None),
        P(("dp", "rep"), None),
        P(),
        P(),
        P(),
    )
    out_specs = (
        P("rep", "dp", None),
        P("rep", "dp", None),
        P(("dp", "rep"), None),
        P(("dp", "rep"), None),
        P(("dp", "rep"), None),
        P(("dp", "rep"), None),
        P(("dp", "rep"), None),
        P(("dp", "rep"), None),
        P(("dp", "rep"), None),
        P(("dp", "rep"), None),
        P(("dp", "rep"), None),
        P(("dp", "rep"), None),
        P(),
        P(),
        P(),
        P(),
        P(),
    )
    return jax.shard_map(body, mesh=mesh, in_specs=in_specs, out_specs=out_specs, check_vma=False)
```

```python
import functools

import jax
import jax.numpy as jnp
from jax import lax
from jax.experimental import pallas as pl
from jax.experimental.pallas import tpu as pltpu
from jax.sharding import PartitionSpec as P

D = 768
CH = 384
FF = 1536


NORM_EPSILON = 1e-06
LEARN_RATE = 0.05
BETA_ONE = 0.9
BETA_TWO = 0.999
ADAM_EPSILON = 1e-08
WEIGHT_DECAY = 0.1


LANES = 8


def rotate(real, imag, cosine, sine):
    return cosine * real - sine * imag, sine * real + cosine * imag


def turn_power(cosine, sine, doublings):
    for _ in range(doublings):
        cosine, sine = cosine * cosine - sine * sine, 2.0 * cosine * sine
    return cosine, sine


def local_forward(retain, drive_re, drive_im, turn, summary):
    steps = retain.shape[0] // LANES
    cosine, sine = turn[0:1], turn[1:2]
    zero = jnp.zeros((LANES, retain.shape[1]), jnp.float32)

    def step(i, carry):
        real, imag, product = carry
        rows = pl.ds(pl.multiple_of(LANES * i, LANES), LANES)
        r = retain[rows, :]
        turned_re, turned_im = rotate(real, imag, cosine, sine)
        return r * turned_re + drive_re[rows, :], r * turned_im + drive_im[rows, :], r * product

    real, imag, product = lax.fori_loop(0, steps, step, (zero, zero, zero + 1.0), unroll=4)
    cos_sub, sin_sub = turn_power(cosine, sine, steps.bit_length() - 1)
    total_re, total_im, total = real[0:1], imag[0:1], product[0:1]
    for j in range(1, LANES):
        turned_re, turned_im = rotate(total_re, total_im, cos_sub, sin_sub)
        total_re = product[j : j + 1] * turned_re + real[j : j + 1]
        total_im = product[j : j + 1] * turned_im + imag[j : j + 1]
        total = product[j : j + 1] * total
    summary[0:LANES] = real
    summary[LANES : 2 * LANES] = imag
    summary[2 * LANES : 3 * LANES] = product
    summary[24:32] = jnp.concatenate([total_re, total_im, total, zero[3:]], axis=0)


def whole_forward(retain, drive_re, drive_im, turn, summary, start, states):
    steps = retain.shape[0] // LANES
    cosine, sine = turn[0:1], turn[1:2]
    cos_sub, sin_sub = turn_power(cosine, sine, steps.bit_length() - 1)
    now_re, now_im = start[0:1], start[1:2]
    reals, imags = [now_re], [now_im]
    for j in range(LANES - 1):
        turned_re, turned_im = rotate(now_re, now_im, cos_sub, sin_sub)
        product = summary[2 * LANES + j : 2 * LANES + j + 1]
        now_re = product * turned_re + summary[j : j + 1]
        now_im = product * turned_im + summary[LANES + j : LANES + j + 1]
        reals.append(now_re)
        imags.append(now_im)
    carry = (jnp.concatenate(reals, axis=0), jnp.concatenate(imags, axis=0))

    def step(i, carry):
        real, imag = carry
        rows = pl.ds(pl.multiple_of(LANES * i, LANES), LANES)
        states[0, rows, :] = real
        states[1, rows, :] = imag
        r = retain[rows, :]
        turned_re, turned_im = rotate(real, imag, cosine, sine)
        return r * turned_re + drive_re[rows, :], r * turned_im + drive_im[rows, :]

    real, imag = lax.fori_loop(0, steps, step, carry, unroll=4)
    states[0, LANES * steps :, :] = real
    states[1, LANES * steps :, :] = imag


def local_backward(retain, grad_re, grad_im, turn, summary):
    steps = retain.shape[0] // LANES
    cosine, sine = turn[0:1], -turn[1:2]
    zero = jnp.zeros((LANES, retain.shape[1]), jnp.float32)

    def step(k, carry):
        real, imag, product = carry
        rows = pl.ds(pl.multiple_of(LANES * (steps - 1 - k), LANES), LANES)
        r = retain[rows, :]
        turned_re, turned_im = rotate(grad_re[rows, :] + real, grad_im[rows, :] + imag, cosine, sine)
        return r * turned_re, r * turned_im, r * product

    real, imag, product = lax.fori_loop(0, steps, step, (zero, zero, zero + 1.0), unroll=4)
    cos_sub, sin_sub = turn_power(cosine, sine, steps.bit_length() - 1)
    last = LANES - 1
    total_re, total_im, total = real[last:], imag[last:], product[last:]
    for j in range(LANES - 2, -1, -1):
        turned_re, turned_im = rotate(total_re, total_im, cos_sub, sin_sub)
        total_re = product[j : j + 1] * turned_re + real[j : j + 1]
        total_im = product[j : j + 1] * turned_im + imag[j : j + 1]
        total = product[j : j + 1] * total
    summary[0:LANES] = real
    summary[LANES : 2 * LANES] = imag
    summary[2 * LANES : 3 * LANES] = product
    summary[24:32] = jnp.concatenate([total_re, total_im, total, zero[3:]], axis=0)


def whole_backward(
    retain, grad_re, grad_im, turn, summary, start, states, d_decay, d_in_re, d_in_im, d_phase
):
    steps = retain.shape[0] // LANES
    cosine, sine = turn[0:1], turn[1:2]
    cos_sub, sin_sub = turn_power(cosine, -sine, steps.bit_length() - 1)
    now_re, now_im = start[0:1], start[1:2]
    reals, imags = [now_re], [now_im]
    for j in range(LANES - 1, 0, -1):
        turned_re, turned_im = rotate(now_re, now_im, cos_sub, sin_sub)
        product = summary[2 * LANES + j : 2 * LANES + j + 1]
        now_re = product * turned_re + summary[j : j + 1]
        now_im = product * turned_im + summary[LANES + j : LANES + j + 1]
        reals.append(now_re)
        imags.append(now_im)
    zero = jnp.zeros((LANES, retain.shape[1]), jnp.float32)
    carry = (jnp.concatenate(reals[::-1], axis=0), jnp.concatenate(imags[::-1], axis=0), zero)

    def step(k, carry):
        real, imag, phase = carry
        rows = pl.ds(pl.multiple_of(LANES * (steps - 1 - k), LANES), LANES)
        r = retain[rows, :]
        real = grad_re[rows, :] + real
        imag = grad_im[rows, :] + imag
        prior_re, prior_im = rotate(states[0, rows, :], states[1, rows, :], cosine, sine)
        d_decay[rows, :] = -(real * prior_re + imag * prior_im)
        d_in_re[rows, :] = real
        d_in_im[rows, :] = imag
        phase = phase + r * (imag * prior_re - real * prior_im)
        turned_re, turned_im = rotate(real, imag, cosine, -sine)
        return r * turned_re, r * turned_im, phase

    _, _, phase = lax.fori_loop(0, steps, step, carry, unroll=4)
    d_phase[...] = jnp.sum(phase, axis=0, keepdims=True)


def stripe(rows):
    count, columns = rows.shape
    return rows.reshape(LANES, count // LANES, columns).swapaxes(0, 1).reshape(count, columns)


def unstripe(rows):
    count, columns = rows.shape
    return rows.reshape(count // LANES, LANES, columns).swapaxes(0, 1).reshape(count, columns)


def local_call(kernel, outs, *args):
    return pl.pallas_call(
        kernel,
        out_shape=[jax.ShapeDtypeStruct(shape, jnp.float32) for shape in outs],
        compiler_params=pltpu.CompilerParams(vmem_limit_bytes=32 * 1024 * 1024),
    )(*args)


def carry_chain(every, turn, me, length, reverse):
    sine = -turn[1:2] if reverse else turn[1:2]
    cosine, sine = turn_power(turn[0:1], sine, length.bit_length() - 1)
    count = every.shape[0]
    real = jnp.zeros_like(cosine)
    imag = jnp.zeros_like(cosine)
    for j in range(count - 1, 0, -1) if reverse else range(count - 1):
        use = (j > me) if reverse else (j < me)
        turned_re, turned_im = rotate(real, imag, cosine, sine)
        real = jnp.where(use, every[j, 2:3] * turned_re + every[j, 0:1], real)
        imag = jnp.where(use, every[j, 2:3] * turned_im + every[j, 1:2], imag)
    return jnp.concatenate([real, imag], axis=0)


def carry_in(summary, turn, length, reverse):
    every = lax.all_gather(summary[24:32], "dp", axis=0)
    return carry_chain(every, turn, lax.axis_index("dp"), length, reverse)


def normalize(values, gains):
    scaling = lax.rsqrt(jnp.mean(values * values, axis=-1, keepdims=True) + NORM_EPSILON)
    return (values * scaling * gains, scaling)


def normalize_back(values, scaling, gains, gradient):
    scaled = gradient * gains
    return scaling * scaled - values * scaling**3 * jnp.mean(
        values * scaled, axis=-1, keepdims=True
    )


def silu_slope(values):
    logistic = jax.nn.sigmoid(values)
    return logistic * (1.0 + values * (1.0 - logistic))


def adam_update(master, gradient, first, second, steps, decay):
    first_new = BETA_ONE * first + (1.0 - BETA_ONE) * gradient
    second_new = BETA_TWO * second + (1.0 - BETA_TWO) * gradient * gradient
    corrected = (
        first_new
        / (1.0 - BETA_ONE**steps)
        / (jnp.sqrt(second_new / (1.0 - BETA_TWO**steps)) + ADAM_EPSILON)
    )
    change = -LEARN_RATE * (corrected + decay * master)
    return (master + change, first_new, second_new, change)


MESH = pl.DeviceIdType.MESH
LOW = jnp.bfloat16
WIDE = jnp.float32
PLANES = 4
SIDE = 2
IN_ROWS = 24
OUT_ROWS = 72
MIX = CH + 2 * D
CHUNK = 512
CHUNKS = FF // CHUNK
OUT = 2
TILE = 128
OUTS = D // 2 // TILE
GLU = OUT + OUTS
VMEM_BYTES = 63 * 1024 * 1024
SLOTS = 512
ROWS = 64
RUN = SLOTS // LANES


class Piece:
    def __init__(self, matrix, rows, columns, starts, overlap=0):
        self.matrix, self.rows, self.columns = matrix, rows, columns
        self.starts, self.overlap = starts, overlap

    def shape(self):
        return (2, PLANES, SIDE, SIDE, 2 * self.rows, self.columns)


def piece_list():
    drive = (CH + D) // 2 + TILE // 2
    mix = [
        Piece("in", IN_ROWS, drive, (0, CH + D - drive), TILE),
        Piece("in", IN_ROWS, D // 2, (CH + D, MIX - D // 2)),
    ]
    out = [Piece("out", OUT_ROWS, TILE, (TILE * k, D // 2 + TILE * k)) for k in range(OUTS)]
    glu = [
        Piece("in", IN_ROWS, CHUNK, (MIX + CHUNK * k, MIX + FF + CHUNK * k)) for k in range(CHUNKS)
    ]
    return mix + out + glu


PIECES = piece_list()


class Place:
    def __init__(self):
        dp, rep = lax.axis_index("dp"), lax.axis_index("rep")
        self.z, self.x = dp // SIDE, dp % SIDE
        self.y, self.core = rep // 2, rep % 2

    def at(self, z, x, y, core):
        return (z * SIDE + x, y * 2 + core)

    def sibling(self):
        return self.at(self.z, self.x, self.y, 1 - self.core)

    def plane(self, z):
        return self.at(z, self.x, self.y, self.core)

    def near(self, core):
        if core == 0:
            return self.at(self.z, 1 - self.x, self.y, self.core)
        return self.at(self.z, self.x, 1 - self.y, self.core)

    def far(self, core):
        return self.near(1 - core)

    def away(self):
        return self.z % 2 + 1, (3 * self.z + 2) % 5, 3 - 3 * (self.z // 2)

    def when_inner(self, run):
        pl.when((self.z + 1) // 2 == 1)(run)

    def when_end(self, run):
        pl.when((self.z + 1) // 2 != 1)(run)

    def turn(self, step):
        return lax.rem(self.z + step, PLANES)

    def sides(self, core):
        return (self.x, self.y) if core == 0 else (self.y, self.x)

    def by_core(self, run):
        for core in range(2):
            pl.when(self.core == core)(functools.partial(run, core))

    def greet(self):
        barrier = pltpu.get_barrier_semaphore()
        partners = [self.sibling(), self.near(0), self.near(1)]
        for step in (1, 2, 3):
            partners.append(self.plane(self.turn(step)))
            partners.append(self.at(self.turn(step), 1 - self.x, self.y, self.core))
        for partner in partners:
            pl.semaphore_signal(barrier, inc=1, device_id=partner, device_id_type=MESH)
        return lambda: pl.semaphore_wait(barrier, len(partners))


def always(run):
    run()


def block_of(ref, core, z, near, far):
    return ref.at[core, z, near, far] if core == 0 else ref.at[core, z, far, near]


def pair_of(ref, core, z, far):
    return ref.at[core, z, :, far] if core == 0 else ref.at[core, z, far]


def remote(source, target, sent, received, device):
    return pltpu.make_async_remote_copy(
        src_ref=source,
        dst_ref=target,
        send_sem=sent,
        recv_sem=received,
        device_id=device,
        device_id_type=MESH,
    )


GATHER_SEMS = 4 * 2
GATHER_NEAR_FIRST = (1, 6, 7)
REDUCE_NEAR_LAST = (2, 4, 5, 7)
GATHER_RELAYED = (0, 1, 2, 3, 4, 5)
REDUCE_RELAYED = (0, 1, 2, 3, 4, 5, 6, 7)


class Gather:
    def __init__(self, place, masters, buffers, staging, sems):
        self.place, self.masters, self.buffers, self.staging = place, masters, buffers, staging
        self.local, self.sent0, self.got0 = sems[:3]
        self.sems = sems[3:]

    @staticmethod
    def scratch():
        n = len(PIECES)
        dma = pltpu.SemaphoreType.DMA
        return (
            [pltpu.VMEM(p.shape(), LOW) for p in PIECES]
            + [pltpu.VMEM((2 * p.rows, p.columns), WIDE) for p in PIECES]
            + [dma((n,))] * 3
            + [dma((n, PLANES))] * GATHER_SEMS
        )

    def part(self, p, half):
        piece = PIECES[p]
        start = piece.starts[0] + half * (piece.starts[1] - piece.starts[0])
        return self.masters[piece.matrix].at[:, pl.ds(pl.multiple_of(start, TILE), piece.columns)]

    def own_rows(self, p):
        rows = PIECES[p].rows
        return self.staging[p].at[pl.ds(pl.multiple_of(self.place.core * rows, 8), rows)]

    def to_sibling(self, p):
        return remote(
            self.part(p, 1 - self.place.core),
            self.own_rows(p),
            self.sent0.at[p],
            self.got0.at[p],
            self.place.sibling(),
        )

    def to_self(self, p):
        return pltpu.make_async_copy(
            self.part(p, self.place.core), self.own_rows(p), self.local.at[p]
        )

    def along_z(self, p, z, target, core, sent=None):
        place = self.place
        near, far = place.sides(core)
        if p in GATHER_NEAR_FIRST:
            part = pair_of(self.buffers[p], core, z, far)
        else:
            part = block_of(self.buffers[p], core, z, near, far)
        sems = self.sems[0].at[p, target if sent is None else sent], self.sems[1].at[p, z]
        return remote(part, part, *sems, place.plane(target))

    def relay(self, p, core):
        place = self.place
        last = place.away()[2]
        return self.along_z(p, last, 3 - last, core, sent=place.z)

    def along_near(self, p, z, core):
        block = block_of(self.buffers[p], core, z, *self.place.sides(core))
        return remote(
            block, block, self.sems[2].at[p, z], self.sems[3].at[p, z], self.place.near(core)
        )

    def along_far(self, p, z, core):
        pair = pair_of(self.buffers[p], core, z, self.place.sides(core)[1])
        return remote(
            pair, pair, self.sems[4].at[p, z], self.sems[5].at[p, z], self.place.far(core)
        )

    def in_chip(self, p, z, core):
        plane = self.buffers[p].at[core, z]
        return remote(
            plane, plane, self.sems[6].at[p, z], self.sems[7].at[p, z], self.place.sibling()
        )

    def begin(self):
        for p in range(len(PIECES)):
            self.to_sibling(p).start()
            self.to_self(p).start()


    def near_own(self, p):
        place = self.place
        self.to_self(p).wait()
        self.to_sibling(p).wait_recv()
        self.buffers[p][place.core, place.z, place.x, place.y] = self.staging[p][...].astype(LOW)
        place.by_core(lambda core: self.along_near(p, place.z, core).start())

    def z_targets(self, p):
        first, second, third = self.place.away()
        relayed = self.place.when_inner if p in GATHER_RELAYED else always
        return (first, always), (second, always), (third, relayed)

    def z_own(self, p):
        place = self.place

        def run(core):
            for z, when in self.z_targets(p):
                when(lambda: self.along_z(p, place.z, z, core).start())

        place.by_core(run)

    def from_z(self, p, index, core):
        place = self.place
        z = place.away()[index]
        self.along_z(p, z, place.z, core).wait_recv()
        if index == 2 and p in GATHER_RELAYED:
            place.when_inner(lambda: self.relay(p, core).start())
        return z

    def far_own(self, p):
        place = self.place

        def run(core):
            self.along_near(p, place.z, core).wait_recv()
            self.along_far(p, place.z, core).start()

        place.by_core(run)

    def near(self, p, *indices):
        place = self.place

        def run(core):
            for index in indices or range(3):
                z = self.from_z(p, index, core)
                self.along_near(p, z, core).start()

        if p not in GATHER_NEAR_FIRST:
            place.by_core(run)

    def far(self, p, *indices):
        place = self.place

        def run(core):
            for index in indices or range(3):
                z = place.away()[index]
                if p in GATHER_NEAR_FIRST:
                    self.from_z(p, index, core)
                else:
                    self.along_near(p, z, core).wait_recv()
                self.along_far(p, z, core).start()

        place.by_core(run)

    def chip(self, p, *indices):
        def run(core):
            for index in indices or range(4):
                z = (self.place.z, *self.place.away())[index]
                self.along_far(p, z, core).wait_recv()
                self.in_chip(p, z, core).start()

        self.place.by_core(run)

    def arrive(self, p):
        for z in (self.place.z, *self.place.away()):
            self.in_chip(p, z, 1 - self.place.core).wait_recv()

    def drain(self, p):
        self.to_sibling(p).wait_send()

        def run(core):
            place = self.place
            for z, when in self.z_targets(p):
                when(lambda: self.along_z(p, place.z, z, core).wait_send())
            if p in GATHER_RELAYED:
                place.when_inner(lambda: self.relay(p, core).wait_send())
            for index, z in enumerate((place.z, *place.away())):
                if p not in GATHER_NEAR_FIRST or index == 0:
                    self.along_near(p, z, core).wait_send()
                self.along_far(p, z, core).wait_send()
                self.in_chip(p, z, core).wait_send()

        self.place.by_core(run)


class Reduce:
    def __init__(self, place, grads, refs, results):
        n = len(PIECES)
        self.place, self.grads, self.results = place, grads, results
        self.far_got, self.near_got, self.planes, self.final = (refs[k * n : (k + 1) * n] for k in range(4))
        self.sems = refs[4 * n :]

    @staticmethod
    def scratch():
        n = len(PIECES)
        dma = pltpu.SemaphoreType.DMA
        blocks = [p.shape()[4:] for p in PIECES]
        return (
            [pltpu.VMEM((PLANES, SIDE) + s, LOW) for s in blocks]
            + [pltpu.VMEM((PLANES,) + s, LOW) for s in blocks]
            + [
                pltpu.VMEM((PLANES,) + (SIDE,) * (p in REDUCE_NEAR_LAST) + s, LOW)
                for p, s in enumerate(blocks)
            ]
            + [pltpu.VMEM(s, WIDE) for s in blocks]
            + [dma((n, PLANES))] * 6
            + [dma((n,))] * 2
        )

    def block(self, p, z, near, far, core):
        return self.grads[p].at[z, near, far] if core == 0 else self.grads[p].at[z, far, near]

    def pair(self, p, z, far, core):
        return self.grads[p].at[z, :, far] if core == 0 else self.grads[p].at[z, far]

    def along_far(self, p, z, core):
        return remote(
            self.pair(p, z, 1 - self.place.sides(core)[1], core),
            self.far_got[p].at[z],
            self.sems[0].at[p, z],
            self.sems[1].at[p, z],
            self.place.far(core),
        )

    def along_near(self, p, z, core):
        near, far = self.place.sides(core)
        return remote(
            self.block(p, z, 1 - near, far, core),
            self.near_got[p].at[z],
            self.sems[2].at[p, z],
            self.sems[3].at[p, z],
            self.place.near(core),
        )

    def order(self):
        first, second, third = self.place.away()
        inner = (self.place.z + 1) // 2 % 2
        return (
            inner * first + (1 - inner) * third,
            second,
            inner * third + (1 - inner) * first,
            self.place.z,
        )

    def z_part(self, p, z, core):
        near, far = self.place.sides(core)
        if p in REDUCE_NEAR_LAST:
            return self.pair(p, z, far, core)
        return self.block(p, z, near, far, core)

    def along_z(self, p, z, sender, core):
        sems = self.sems[4].at[p, z], self.sems[5].at[p, sender]
        target = self.planes[p].at[sender]
        return remote(self.z_part(p, z, core), target, *sems, self.place.plane(z))

    def to_relay(self, p, core, slot):
        first, _, third = self.place.away()
        sems = self.sems[4].at[p, third], self.sems[5].at[p, slot]
        target = self.planes[p].at[slot]
        return remote(self.z_part(p, third, core), target, *sems, self.place.plane(first))

    def send_z(self, p, core, index):
        place = self.place
        z = self.order()[index]
        if index == 1:
            self.along_z(p, z, place.z, core).start()
        elif p not in REDUCE_RELAYED:
            if index != 3:
                self.along_z(p, z, place.z, core).start()
        elif index == 0:
            place.when_inner(lambda: self.along_z(p, z, place.z, core).start())
            place.when_end(lambda: self.to_relay(p, core, place.away()[0]).start())
        elif index == 2:

            def pass_on():
                self.to_relay(p, core, place.z).wait_recv()
                self.add(self.z_part(p, z, core), self.planes[p].at[place.z])

            place.when_inner(pass_on)
            self.along_z(p, z, place.z, core).start()

    def sum_planes(self, p, core, result):
        place = self.place
        first, second, third = place.away()
        for z in (first, second):
            self.along_z(p, place.z, z, core).wait_recv()
        total = self.z_part(p, place.z, core)[...].astype(WIDE)
        total = total + self.planes[p][first].astype(WIDE) + self.planes[p][second].astype(WIDE)

        def inner():
            self.along_z(p, place.z, third, core).wait_recv()
            result[...] = (total + self.planes[p][third].astype(WIDE)).astype(result.dtype)

        def end():
            result[...] = total.astype(result.dtype)

        if p in REDUCE_RELAYED:
            place.when_inner(inner)
            place.when_end(end)
        else:
            inner()

    def result(self, p, core):
        piece = PIECES[p]
        skip = piece.overlap * core
        start, width = piece.starts[core] + skip, piece.columns - skip
        return self.results[piece.matrix].at[:, pl.ds(start, width)], pl.ds(skip, width)

    def to_sibling(self, p, core):
        rows = PIECES[p].rows
        target, columns = self.result(p, core)
        return remote(
            self.final[p].at[pl.ds(rows * (1 - core), rows), columns],
            target,
            self.sems[6].at[p],
            self.sems[7].at[p],
            self.place.sibling(),
        )

    @staticmethod
    def add(target, source):
        target[...] = (target[...].astype(WIDE) + source[...].astype(WIDE)).astype(LOW)

    def far(self, p):
        def run(core):
            for z in self.order():
                self.along_far(p, z, core).start()

        self.place.by_core(run)

    def after_far(self, p, *indices):
        def run(core):
            for index in indices or range(4):
                z = self.order()[index]
                self.along_far(p, z, core).wait_recv()
                self.add(self.pair(p, z, self.place.sides(core)[1], core), self.far_got[p].at[z])
                if p in REDUCE_NEAR_LAST:
                    self.send_z(p, core, index)
                else:
                    self.along_near(p, z, core).start()

        self.place.by_core(run)

    def after_near(self, p, *indices):
        place = self.place

        def run(core):
            near, far = place.sides(core)
            if p in REDUCE_NEAR_LAST:
                self.sum_planes(p, core, self.pair(p, place.z, far, core))
                self.along_near(p, place.z, core).start()
                return
            for index in indices or range(4):
                z = self.order()[index]
                self.along_near(p, z, core).wait_recv()
                self.add(self.block(p, z, near, far, core), self.near_got[p].at[z])
                self.send_z(p, core, index)

        place.by_core(run)

    def finish(self, p):
        rows, place = PIECES[p].rows, self.place

        def run(core):
            near, far = place.sides(core)
            if p in REDUCE_NEAR_LAST:
                self.along_near(p, place.z, core).wait_recv()
                own = self.block(p, place.z, near, far, core)[...].astype(WIDE)
                self.final[p][...] = own + self.near_got[p][place.z].astype(WIDE)
            else:
                self.sum_planes(p, core, self.final[p])
            self.to_sibling(p, core).start()
            target, columns = self.result(p, core)
            target[...] = self.final[p][pl.ds(rows * core, rows), columns]

        place.by_core(run)

    def drain(self, p):
        place = self.place

        def run(core):
            self.to_sibling(p, 1 - core).wait_recv()
            self.to_sibling(p, core).wait_send()
            first, second, third = place.away()
            for z in (first, second):
                self.along_z(p, z, place.z, core).wait_send()
            if p in REDUCE_RELAYED:
                place.when_inner(lambda: self.along_z(p, third, place.z, core).wait_send())
                place.when_end(lambda: self.to_relay(p, core, first).wait_send())
            else:
                self.along_z(p, third, place.z, core).wait_send()
            for index, z in enumerate((place.z, first, second, third)):
                self.along_far(p, z, core).wait_send()
                if p not in REDUCE_NEAR_LAST or index == 0:
                    self.along_near(p, z, core).wait_send()

        place.by_core(run)


def tiled(column, count):
    return jnp.concatenate([column] * count, axis=1)


def each_block(run, size=ROWS):
    def block(i, carry):
        run(pl.ds(pl.multiple_of(i * size, size), size))
        return carry

    lax.fori_loop(0, SLOTS // size, block, 0)


def inner(left, right, dims=((1,), (0,))):
    return lax.dot_general(left, right, (dims, ((), ())), preferred_element_type=WIDE)


def across(left, right):
    return inner(left, right, ((1,), (1,)))


def along(left, right):
    return inner(left, right, ((0,), (0,)))


def out_segments(start, count):
    size, runs, stop = 2 * OUT_ROWS, [], start + count
    while start < stop:
        chip, first = divmod(start, size)
        last = min(size, first + stop - start)
        runs.append((chip // 4, chip // 2 % 2, chip % 2, first, last))
        start += last - first
    return runs


def row_norm(values):
    return lax.rsqrt(jnp.mean(values * values, axis=1, keepdims=True) + NORM_EPSILON)


def eights(values):
    return jnp.sum(values.reshape(values.shape[0] // 8, 8, values.shape[1]), axis=0)


def block_scratch():
    vmem, dma = pltpu.VMEM, pltpu.SemaphoreType.DMA
    rows = (SLOTS, D)
    both = (2 * SLOTS, D)
    return dict(
        arrivals=dma((2,)),
        departures=dma((2,)),
        perm=vmem((SLOTS, SLOTS), LOW),
        live=vmem((SLOTS, TILE), WIDE),
        opens=vmem((SLOTS, TILE), WIDE),
        params=vmem((8, D), WIDE),
        tokens=vmem(rows, LOW),
        upstream=vmem((2, SLOTS, D // 2), LOW),
        upstream_got=vmem((SLOTS, D // 2), LOW),
        normed=vmem(both, LOW),
        normed_two=vmem(both, LOW),
        gated=vmem(both, LOW),
        hidden=vmem((CHUNKS, 2 * SLOTS, CHUNK), LOW),
        d_glu=vmem((CHUNKS, 2, SLOTS, CHUNK), LOW),
        d_glu_got=vmem((CHUNKS, SLOTS, CHUNK), LOW),
        d_out=vmem((2, SLOTS, D // 2), LOW),
        d_out_got=vmem((SLOTS, D // 2), LOW),
        d_drive=vmem((2, SLOTS, PIECES[0].columns), LOW),
        d_drive_got=vmem((SLOTS, PIECES[0].columns), LOW),
        d_gate=vmem((2, SLOTS, PIECES[1].columns), LOW),
        d_gate_got=vmem((SLOTS, PIECES[1].columns), LOW),
        pre_mix=vmem((SLOTS, MIX), WIDE),
        retain=vmem((SLOTS, CH), WIDE),
        drive=vmem(rows, WIDE),
        states=vmem((2, SLOTS + LANES, CH), WIDE),
        summaries=vmem((2, 32, CH), WIDE),
        every=vmem((2, PLANES * SIDE, 8, CH), WIDE),
        middle=vmem(rows, WIDE),
        d_normed=vmem(rows, WIDE),
        total=vmem(rows, WIDE),
        block_out=vmem(rows, LOW),
        sums=vmem((3, 8, D), WIDE),
        vector=vmem((8, VEC_ROWS, TILE), WIDE),
        pair_sent=dma((PAIRS,)),
        pair_got=dma((PAIRS,)),
        carry_sent=dma((2, PLANES * SIDE)),
        carry_got=dma((2, PLANES * SIDE)),
        vector_sent=dma((6,)),
        vector_got=dma((6,)),
    )


VEC_ROWS = 24
VEC_COUNT = 18
PAIRS = 16


class Block:
    def __init__(self, place, buffers, grads, refs):
        self.place, self.weights, self.grads = place, buffers, grads
        for name, ref in refs.items():
            setattr(self, name, ref)
        self.me = place.z * SIDE + place.x


    def swaps(self):
        own, got = pl.ds(0, SLOTS), pl.ds(SLOTS, SLOTS)
        other = 1 - self.place.core
        pairs = dict(
            normed=(self.normed.at[own], self.normed.at[got]),
            normed_two=(self.normed_two.at[own], self.normed_two.at[got]),
            gated=(self.gated.at[own], self.gated.at[got]),
            upstream=(self.upstream.at[other], self.upstream_got),
            d_out=(self.d_out.at[other], self.d_out_got),
            d_drive=(self.d_drive.at[other], self.d_drive_got),
            d_gate=(self.d_gate.at[other], self.d_gate_got),
        )
        for k in range(CHUNKS):
            pairs["hidden", k] = (self.hidden.at[k, own], self.hidden.at[k, got])
            pairs["d_glu", k] = (self.d_glu.at[k, other], self.d_glu_got.at[k])
        return pairs

    def swap(self, name):
        pairs = self.swaps()
        slot = list(pairs).index(name)
        sems = self.pair_sent.at[slot], self.pair_got.at[slot]
        return remote(*pairs[name], *sems, self.place.sibling())

    def give(self, *names):
        for name in names:
            self.swap(name).start()

    def take(self, *names):
        for name in names:
            self.swap(name).wait_recv()

    def settle(self):
        for name in self.swaps():
            self.swap(name).wait_send()


    def mix_weight(self, half, m):
        return self.weights[m][half].reshape(D, PIECES[m].columns)

    def glu_weight(self, k):
        parts = [self.weights[GLU + k][half].reshape(D, CHUNK) for half in range(2)]
        return jnp.concatenate(parts, axis=1)

    def out_weight(self, start, count):
        columns = []
        for half in range(2):
            for p in range(OUT, GLU):
                ref = self.weights[p]
                runs = out_segments(start, count)
                parts = [ref[half, z, x, y, first:last] for z, x, y, first, last in runs]
                columns.append(jnp.concatenate(parts, axis=0))
        return jnp.concatenate(columns, axis=1)

    def put_in(self, p, value):
        self.grads[p][...] = value.astype(LOW).reshape(self.grads[p].shape)

    def put_out(self, start, value):
        value, done = value.astype(LOW), 0
        for z, x, y, first, last in out_segments(start, value.shape[0]):
            count = last - first
            for k in range(OUTS):
                part = value[done : done + count, k * TILE : (k + 1) * TILE]
                self.grads[OUT + k][z, x, y, first:last] = part
            done += count


    def prepare(self, padding, opening, vectors):
        row = lax.broadcasted_iota(jnp.int32, (SLOTS, SLOTS), 0)
        column = lax.broadcasted_iota(jnp.int32, (SLOTS, SLOTS), 1)
        perm = (column == row % LANES * RUN + row // LANES).astype(WIDE)
        self.perm[...] = perm.astype(LOW)
        ones = jnp.ones((SLOTS, TILE), LOW)
        self.live[...] = inner((perm * padding[...].astype(WIDE)).astype(LOW), ones)
        self.opens[...] = inner((perm * opening[...].astype(WIDE)).astype(LOW), ones)

        def line(first, count):
            return jnp.concatenate([vectors[first + i : first + i + 1] for i in range(count)], axis=1)

        phase = line(12, 3)
        self.params[0:1] = line(0, 6)
        self.params[1:2] = line(6, 6)
        self.params[2:3] = jnp.concatenate([jnp.cos(phase), jnp.sin(phase)], axis=1)
        self.params[3:4] = jnp.concatenate([line(15, 3)] * 2, axis=1)
        self.sums[...] = jnp.zeros_like(self.sums)

    def turn(self):
        return jnp.concatenate([self.params[2:3, :CH], self.params[2:3, CH:]], axis=0)

    def first_norm(self, raw):
        values = inner(self.perm[...], raw[...])
        self.tokens[...] = values.astype(LOW)
        self.normed[0:SLOTS] = (values * row_norm(values) * self.params[0:1]).astype(LOW)

    def mask_upstream(self, raw):
        striped = inner(self.perm[...], raw[...]) * tiled(self.live[...], D // TILE)
        self.upstream[0] = striped[:, : D // 2].astype(LOW)
        self.upstream[1] = striped[:, D // 2 :].astype(LOW)

    def mix(self, m):
        piece = PIECES[m]
        weight = (self.mix_weight(0, m), self.mix_weight(1, m)[:, piece.overlap :])
        weight = jnp.concatenate(weight, axis=1)
        start = piece.starts[0]
        self.pre_mix[:, start : start + weight.shape[1]] = inner(self.normed[0:SLOTS], weight)

    def drives(self):
        forget = jax.nn.sigmoid(-(self.pre_mix[:, :CH] + self.params[3:4, :CH]))
        pre = self.pre_mix[:, CH : CH + D]
        driver = pre * jax.nn.sigmoid(pre)
        opens = tiled(self.opens[...], CH // TILE)
        decay = jnp.where(opens > 0.5, 1.0, forget).astype(LOW).astype(WIDE)
        self.retain[...] = 1.0 - decay
        drive = jnp.concatenate([forget, forget], axis=1) * driver
        self.drive[...] = drive.astype(LOW).astype(WIDE)

    def parts(self):
        return self.drive.at[:, pl.ds(0, CH)], self.drive.at[:, pl.ds(CH, CH)]

    def others(self):
        place = self.place
        for step in range(PLANES):
            for flip in range(SIDE):
                if step or flip:
                    z = place.turn(step)
                    x = 1 - place.x if flip else place.x
                    yield z * SIDE + x, place.at(z, x, place.y, place.core)

    def carry_copy(self, way, other, device, sender):
        return remote(
            self.summaries.at[way, pl.ds(24, 8)],
            self.every.at[way, sender],
            self.carry_sent.at[way, other],
            self.carry_got.at[way, sender],
            device,
        )

    def scan_own(self, way):
        run = local_backward if way else local_forward
        run(self.retain, *self.parts(), self.turn(), self.summaries.at[way])
        self.every[way, self.me] = self.summaries[way, 24:32]
        for other, device in self.others():
            self.carry_copy(way, other, device, self.me).start()

    def carried(self, way):
        for other, device in self.others():
            self.carry_copy(way, other, device, other).wait_recv()
        turn = self.turn()
        return carry_chain(self.every.at[way], turn, self.me, SLOTS, way == 1)

    def scan_states(self):
        start = self.carried(0)
        run = whole_forward
        run(self.retain, *self.parts(), self.turn(), self.summaries.at[0], start, self.states)

    def recurrent(self):
        both = jnp.concatenate([self.states[0, LANES:], self.states[1, LANES:]], axis=1)
        return both.astype(LOW).astype(WIDE)

    def gate_rows(self):
        pre = self.pre_mix[:, CH + D :]
        masked = self.recurrent() * tiled(self.live[...], D // TILE)
        self.gated[0:SLOTS] = (masked * (pre * jax.nn.sigmoid(pre))).astype(LOW)

    def second_norm(self):
        mixed = inner(self.gated[0:SLOTS], self.out_weight(0, D))
        middle = self.tokens[...].astype(WIDE) + mixed
        self.middle[...] = middle
        self.total[...] = middle
        self.normed_two[0:SLOTS] = (middle * row_norm(middle) * self.params[1:2]).astype(LOW)

    def whole_upstream(self):
        return jnp.concatenate([self.upstream[0], self.upstream[1]], axis=1)

    def glu_forward(self, k):
        pre = inner(self.normed_two[0:SLOTS], self.glu_weight(k))
        gate, up = pre[:, :CHUNK], pre[:, CHUNK:]
        d_hidden = across(self.whole_upstream(), self.out_weight(D + CHUNK * k, CHUNK))
        logistic = jax.nn.sigmoid(gate)
        active = gate * logistic
        slope = logistic * (1.0 + gate * (1.0 - logistic))
        self.hidden[k, 0:SLOTS] = (active * up).astype(LOW)
        self.d_glu[k, 0] = (d_hidden * up * slope).astype(LOW)
        self.d_glu[k, 1] = (d_hidden * active).astype(LOW)

    def glu_back(self, k):
        d_glu = jnp.concatenate([self.d_glu[k, 0], self.d_glu[k, 1]], axis=1)
        d_share = across(d_glu, self.glu_weight(k))
        self.d_normed[...] = d_share if k == 0 else self.d_normed[...] + d_share

    def own_half(self, ref, got):
        return jnp.concatenate([ref[self.place.core], got], axis=0)

    def glu_grads(self, k):
        d_glu = jnp.concatenate([self.d_glu[k, self.place.core], self.d_glu_got[k]], axis=0)
        self.put_in(GLU + k, along(self.normed_two[...], d_glu))
        upstream = self.own_half(self.upstream, self.upstream_got[...])
        self.put_out(D + CHUNK * k, along(self.hidden[k], upstream))

    def add_sum(self, index, values):
        self.sums[index] += eights(values)

    def middle_back(self):
        middle, d_normed = self.middle[...], self.d_normed[...]
        scaling = row_norm(middle)
        self.add_sum(1, d_normed * middle * scaling)
        scaled = d_normed * self.params[1:2]
        mean = jnp.mean(middle * scaled, axis=1, keepdims=True)
        upstream = self.whole_upstream().astype(WIDE)
        d_middle = upstream + scaling * scaled - middle * (scaling**3 * mean)
        self.middle[...] = d_middle
        self.d_out[0] = d_middle[:, : D // 2].astype(LOW)
        self.d_out[1] = d_middle[:, D // 2 :].astype(LOW)

    def gate_back(self):
        d_out = jnp.concatenate([self.d_out[0], self.d_out[1]], axis=1)
        d_gated = across(d_out, self.out_weight(0, D))
        pre = self.pre_mix[:, CH + D :]
        logistic = jax.nn.sigmoid(pre)
        d_live = d_gated * tiled(self.live[...], D // TILE)
        self.drive[...] = (d_live * (pre * logistic)).astype(LOW).astype(WIDE)
        slope = logistic * (1.0 + pre * (1.0 - logistic))
        d_gate = (d_live * self.recurrent() * slope).astype(LOW)
        self.d_gate[0] = d_gate[:, : D // 2]
        self.d_gate[1] = d_gate[:, D // 2 :]

    def mixer_out_grad(self):
        d_out = self.own_half(self.d_out, self.d_out_got[...])
        self.put_out(0, along(self.gated[...], d_out))

    def scan_back(self):
        start = self.carried(1)
        real, imag = self.parts()
        whole_backward(
            self.retain,
            real,
            imag,
            self.turn(),
            self.summaries.at[1],
            start,
            self.states,
            self.retain,
            real,
            imag,
            self.sums.at[2, pl.ds(0, 1), pl.ds(0, CH)],
        )

    def drives_back(self):
        def run(rows):
            forget = jax.nn.sigmoid(-(self.pre_mix[rows, :CH] + self.params[3:4, :CH]))
            pre = self.pre_mix[rows, CH : CH + D]
            logistic = jax.nn.sigmoid(pre)
            d_decay = self.retain[rows, :].astype(LOW).astype(WIDE)
            d_input = self.drive[rows, :].astype(LOW).astype(WIDE)
            pulled = d_input * (pre * logistic)
            opens = tiled(self.opens[rows, :], CH // TILE)
            d_forget = jnp.where(opens > 0.5, 0.0, d_decay) + pulled[:, :CH] + pulled[:, CH:]
            d_first = -forget * (1.0 - forget) * d_forget
            self.sums[2, :, CH:] += eights(d_first)
            slope = logistic * (1.0 + pre * (1.0 - logistic))
            d_driver = d_input * jnp.concatenate([forget, forget], axis=1) * slope
            d_pre = jnp.concatenate([d_first, d_driver], axis=1).astype(LOW)
            piece = PIECES[0]
            for half, start in enumerate(piece.starts):
                self.d_drive[half, rows, :] = d_pre[:, start : start + piece.columns]

        each_block(run)

    def mix_grads(self, m):
        own, got = ((self.d_drive, self.d_drive_got), (self.d_gate, self.d_gate_got))[m]
        self.put_in(m, along(self.normed[...], self.own_half(own, got[...])))

    def gate_normed(self):
        left = jnp.concatenate([self.d_gate[0], self.d_gate[1]], axis=1)
        right = jnp.concatenate([self.mix_weight(0, 1), self.mix_weight(1, 1)], axis=1)
        self.d_normed[...] = across(left, right)

    def first_back(self):
        skip = PIECES[0].overlap
        left = jnp.concatenate([self.d_drive[0], self.d_drive[1][:, skip:]], axis=1)
        right = jnp.concatenate([self.mix_weight(0, 0), self.mix_weight(1, 0)[:, skip:]], axis=1)
        d_normed = self.d_normed[...] + across(left, right)
        values = self.tokens[...].astype(WIDE)
        scaling = row_norm(values)
        self.add_sum(0, d_normed * values * scaling)
        scaled = d_normed * self.params[0:1]
        mean = jnp.mean(values * scaled, axis=1, keepdims=True)
        self.middle[...] += scaling * scaled - values * (scaling**3 * mean)

    def natural_out(self):
        hidden = jnp.concatenate([self.hidden[k, 0:SLOTS] for k in range(CHUNKS)], axis=1)
        total = self.total[...] + inner(hidden, self.out_weight(D, FF))
        self.block_out[...] = along(self.perm[...], total.astype(LOW)).astype(LOW)

    def natural_tokens(self):
        rest = self.middle[...]
        total = jnp.zeros_like(rest)
        for _ in range(3):
            part = rest.astype(LOW)
            total = total + along(self.perm[...], part)
            rest = rest - part.astype(WIDE)
        self.d_normed[...] = total


    def gather_vector(self):
        lines = [
            jnp.sum(self.sums[0], axis=0, keepdims=True),
            jnp.sum(self.sums[1], axis=0, keepdims=True),
            jnp.concatenate(
                [self.sums[2, 0:1, :CH], jnp.sum(self.sums[2, :, CH:], axis=0, keepdims=True)], axis=1
            ),
        ]
        for i, line in enumerate(lines):
            for j in range(D // TILE):
                row = i * (D // TILE) + j
                self.vector[0, row : row + 1] = line[:, j * TILE : (j + 1) * TILE]
        filled = jnp.sum(self.live[...], axis=0, keepdims=True)
        rest = jnp.zeros((VEC_ROWS - VEC_COUNT - 1, TILE), WIDE)
        self.vector[0, VEC_COUNT:] = jnp.concatenate([filled, rest], axis=0)

    def vector_copy(self, stage):
        place = self.place
        device = (place.sibling(), place.near(0), place.near(1))[stage]
        source = self.vector.at[stage]
        target = self.vector.at[4 + stage]
        return remote(source, target, self.vector_sent.at[stage], self.vector_got.at[stage], device)

    def vector_step(self, stage):
        if stage:
            self.vector_copy(stage - 1).wait_recv()
            self.vector[stage] = self.vector[stage - 1] + self.vector[3 + stage]
        if stage < 3:
            self.vector_copy(stage).start()

    def vector_plane(self, planes, step, sender):
        place = self.place
        return remote(
            self.vector.at[3],
            planes.at[sender],
            self.vector_sent.at[2 + step],
            self.vector_got.at[2 + step],
            place.plane(place.turn(step)),
        )


def block_kernel(tokens, cotangent, padding, opening, w_in, w_out, vectors, *refs):
    n = len(PIECES)
    block_out, d_tokens, sum_in, sum_out, planes = refs[:5]
    refs = refs[5:]
    count = len(Gather.scratch())
    gather_refs, refs = refs[:count], refs[count:]
    buffers, staging, gather_sems = gather_refs[:n], gather_refs[n : 2 * n], gather_refs[2 * n :]
    grads, refs = refs[:n], refs[n:]
    count = len(Reduce.scratch())
    reduce_refs, refs = refs[:count], refs[count:]
    place = Place()
    gather = Gather(place, {"in": w_in, "out": w_out}, buffers, staging, gather_sems)
    reduce = Reduce(place, grads, reduce_refs, {"in": sum_in, "out": sum_out})
    block = Block(place, buffers, grads, dict(zip(block_scratch(), refs, strict=True)))

    entered = place.greet()
    raw_tokens, raw_upstream = block.gated.at[pl.ds(0, SLOTS)], block.block_out
    loads = [
        pltpu.make_async_copy(tokens.at[0], raw_tokens, block.arrivals.at[0]),
        pltpu.make_async_copy(cotangent.at[0], raw_upstream, block.arrivals.at[1]),
    ]
    leave_out = pltpu.make_async_copy(block.block_out, block_out, block.departures.at[0])
    leave_tokens = pltpu.make_async_copy(block.d_normed, d_tokens, block.departures.at[1])
    for load in loads:
        load.start()
    block.prepare(padding, opening, vectors)
    entered()
    gather.begin()
    gather.near_own(0)
    gather.z_own(0)
    gather.near_own(2)
    gather.near_own(5)
    gather.near_own(3)
    gather.z_own(3)
    gather.near_own(4)
    gather.near_own(1)
    gather.near_own(6)
    gather.z_own(2)
    gather.far_own(0)
    gather.near(0, 0)
    gather.far_own(5)
    gather.near_own(7)
    gather.far_own(4)
    gather.far_own(2)
    gather.far_own(1)
    gather.far_own(3)
    gather.z_own(1)
    gather.far_own(6)
    gather.near(0, 1)
    gather.near(3, 0)
    gather.near(0, 2)
    gather.z_own(4)
    gather.near(3, 1)
    gather.far(0, 1)
    gather.far_own(7)
    loads[0].wait()
    block.first_norm(raw_tokens)
    gather.near(3, 2)
    gather.near(2, 0)
    gather.z_own(5)
    gather.far(0, 0)
    gather.near(2, 1)
    gather.far(1, 0)
    gather.z_own(6)
    loads[1].wait()
    block.mask_upstream(raw_upstream)
    gather.chip(1, 0)
    gather.near(4, 1)
    gather.far(3, 0, 1)
    gather.far(2, 1)
    gather.near(2, 2)
    gather.near(5, 1, 0)
    block.give("normed")
    gather.near(4, 2)
    gather.far(3, 2)
    gather.far(1, 1)
    gather.far(2, 0)
    gather.z_own(7)
    gather.chip(5, 0)
    gather.chip(6, 0)
    gather.far(0, 2)
    gather.chip(0, 2)
    gather.chip(3, 0)
    gather.chip(0, 0)
    gather.far(4, 1)
    gather.near(4, 0)
    gather.far(2, 2)
    gather.near(5, 2)
    gather.far(4, 2)
    gather.chip(7, 0)
    gather.far(6, 1)
    gather.chip(0, 1)
    gather.far(1, 2)
    gather.chip(4, 0)
    gather.chip(0, 3)
    gather.chip(2, 1)
    gather.chip(3, 2)
    gather.chip(1, 2)
    gather.far(4, 0)
    gather.chip(3, 1)
    gather.chip(2, 3)
    gather.far(5, 0)
    gather.chip(4, 3)
    gather.far(5, 1)
    gather.arrive(0)
    gather.chip(2, 0)
    block.give("upstream")
    gather.chip(1, 1)
    gather.chip(4, 2)
    block.mix(0)
    gather.far(6, 0)
    gather.chip(1, 3)
    gather.chip(3, 3)
    block.drives()
    block.scan_own(0)
    gather.chip(5, 1)
    gather.far(5, 2)
    gather.chip(2, 2)
    gather.chip(6, 2)
    gather.chip(4, 1)
    gather.far(6, 2)
    gather.far(7, 1)
    gather.chip(6, 1)
    gather.far(7, 0)
    gather.arrive(2)
    gather.chip(5, 2)
    gather.far(7, 2)
    gather.arrive(1)
    gather.arrive(3)
    block.mix(1)
    gather.chip(5, 3)
    block.scan_states()
    gather.arrive(4)
    block.gate_rows()
    gather.chip(6, 3)
    block.give("gated")
    block.second_norm()
    gather.arrive(5)
    gather.chip(7, 2)
    block.give("normed_two")
    block.glu_forward(0)
    gather.arrive(6)
    gather.chip(7, 3)
    block.take("gated")
    gather.chip(7, 1)
    block.give(("d_glu", 0))
    block.glu_forward(1)
    block.give(("hidden", 0))
    gather.arrive(7)
    block.give(("d_glu", 1))
    block.glu_forward(2)
    block.give(("hidden", 2))
    block.take("normed", "upstream", ("hidden", 0), "normed_two")
    block.give(("d_glu", 2))
    block.take(("d_glu", 0))
    block.glu_grads(0)
    reduce.far(5)
    block.glu_back(0)
    block.take(("d_glu", 2))
    block.give(("hidden", 1))
    block.take(("hidden", 2))
    block.glu_grads(2)
    reduce.far(7)
    block.take(("d_glu", 1))
    block.glu_back(1)
    block.take(("hidden", 1))
    reduce.after_far(5, 0)
    block.glu_grads(1)
    reduce.after_far(5, 1)
    block.glu_back(2)
    reduce.far(6)
    block.middle_back()
    reduce.after_far(7, 0)
    block.give("d_out")
    reduce.after_far(5, 2)
    block.gate_back()
    block.take("d_out")
    block.mixer_out_grad()
    reduce.far(4)
    reduce.far(2)
    block.give("d_gate")
    reduce.after_far(6, 0)
    block.scan_own(1)
    block.take("d_gate")
    block.mix_grads(1)
    reduce.after_far(7, 2)
    reduce.after_far(4, 0)
    reduce.far(1)
    reduce.far(3)
    block.scan_back()
    reduce.after_far(7, 1)
    reduce.after_far(4, 1)
    block.drives_back()
    reduce.after_far(2, 1)
    block.give("d_drive")
    block.take("d_drive")
    block.mix_grads(0)
    reduce.after_far(2, 0)
    reduce.after_far(1, 0)
    reduce.after_far(4, 2)
    reduce.far(0)
    reduce.after_near(6, 0)
    reduce.after_far(1, 2)
    block.gate_normed()
    reduce.after_far(7, 3)
    reduce.after_far(3, 0)
    reduce.after_far(2, 3)
    block.first_back()
    reduce.after_far(1, 1)
    reduce.after_far(2, 2)
    reduce.after_far(5, 3)
    reduce.after_near(1, 0)
    reduce.after_near(3, 0)
    reduce.after_far(3, 1)
    reduce.after_far(0, 0)
    block.natural_out()
    leave_out.start()
    block.gather_vector()
    reduce.after_near(1, 1)
    reduce.after_far(6, 1)
    reduce.after_near(3, 1)
    block.vector_step(0)
    reduce.after_far(0, 1)
    reduce.after_near(1, 2)
    block.vector_step(1)
    reduce.after_near(0, 0)
    reduce.after_far(0, 2)
    reduce.after_far(3, 2)
    reduce.after_near(6, 1)
    reduce.after_far(4, 3)
    reduce.after_near(5)
    reduce.after_far(6, 2)
    reduce.after_far(1, 3)
    reduce.after_far(3, 3)
    reduce.after_near(0, 1)
    reduce.after_near(2)
    block.vector_step(2)
    reduce.after_near(0, 2)
    reduce.after_far(0, 3)
    reduce.after_near(7)
    reduce.after_far(6, 3)
    reduce.after_near(4)
    reduce.after_near(3, 2)
    reduce.after_near(6, 2)
    block.natural_tokens()
    leave_tokens.start()
    block.vector_step(3)
    for step in (1, 2, 3):
        block.vector_plane(planes, step, place.z).start()
    planes[place.z] = block.vector[3]
    reduce.after_near(0, 3)
    reduce.finish(5)
    reduce.after_near(1, 3)
    reduce.finish(2)
    reduce.finish(1)
    reduce.finish(7)
    reduce.after_near(6, 3)
    reduce.finish(4)
    reduce.after_near(3, 3)
    reduce.finish(0)
    reduce.finish(3)
    reduce.finish(6)

    for step in (1, 2, 3):
        block.vector_plane(planes, step, place.z).wait_send()
        block.vector_plane(planes, step, place.turn(4 - step)).wait_recv()
    for stage in range(3):
        block.vector_copy(stage).wait_send()
    for way in range(2):
        for other, device in block.others():
            block.carry_copy(way, other, device, block.me).wait_send()
    block.settle()
    for p in range(n):
        gather.drain(p)
        reduce.drain(p)
    leave_out.wait()
    leave_tokens.wait()


def block_routed(tokens, cotangent, padding, opening, w_in, w_out, vectors):
    vmem = pl.BlockSpec(memory_space=pltpu.VMEM)
    anywhere = pl.BlockSpec(memory_space=pl.ANY)
    out_shape = [
        jax.ShapeDtypeStruct((SLOTS, D), LOW),
        jax.ShapeDtypeStruct((SLOTS, D), WIDE),
        jax.ShapeDtypeStruct(w_in.shape, WIDE),
        jax.ShapeDtypeStruct(w_out.shape, WIDE),
        jax.ShapeDtypeStruct((PLANES, VEC_ROWS, TILE), WIDE),
    ]
    grads = [pltpu.VMEM(p.shape()[1:], LOW) for p in PIECES]
    block_out, d_tokens, sum_in, sum_out, planes = pl.pallas_call(
        block_kernel,
        out_shape=out_shape,
        in_specs=[anywhere, anywhere, vmem, vmem, anywhere, anywhere, vmem],
        out_specs=[anywhere, anywhere, vmem, vmem, vmem],
        scratch_shapes=Gather.scratch()
        + grads
        + Reduce.scratch()
        + list(block_scratch().values()),
        compiler_params=pltpu.CompilerParams(
            collective_id=0, has_side_effects=True, vmem_limit_bytes=VMEM_BYTES
        ),
    )(tokens, cotangent, padding, opening, w_in, w_out, vectors.reshape(VEC_COUNT, TILE))
    return block_out, d_tokens, sum_in, sum_out, planes


def power(base, count):
    return lax.fori_loop(0, count, lambda _, value: value * base, jnp.float32(1.0))


def update_kernel(counter, planes, block_from, tokens_from, *refs):
    ins, outs = refs[:11], refs[11:]
    outs[0][...] = block_from[...]
    outs[1][...] = tokens_from[...]
    first_scale = 1.0 - power(BETA_ONE, counter[0])
    second_scale = 1.0 - power(BETA_TWO, counter[0])
    vectors = (planes[0] + planes[1]) + (planes[2] + planes[3])
    total = vectors[VEC_COUNT : VEC_COUNT + 1, 0:1]

    def step(summed, master, first, second, decay):
        gradient = summed / total
        first = BETA_ONE * first + (1.0 - BETA_ONE) * gradient
        second = BETA_TWO * second + (1.0 - BETA_TWO) * gradient * gradient
        corrected = first / first_scale / (jnp.sqrt(second / second_scale) + ADAM_EPSILON)
        return gradient, -LEARN_RATE * (corrected + decay * master), first, second

    for k in range(2):
        summed, master, first, second = (ref[...] for ref in ins[4 * k : 4 * k + 4])
        gradient, change, first, second = step(summed, master, first, second, WEIGHT_DECAY)
        new = master + change
        results = (gradient, new, first, second, new.astype(LOW))
        for ref, value in zip(outs[2 + 5 * k : 7 + 5 * k], results, strict=True):
            ref[...] = value
    master, first, second = (ref[...] for ref in ins[8:])
    results = step(vectors[:VEC_COUNT], master, first, second, 0.0)
    for ref, value in zip(outs[12:], results, strict=True):
        ref[...] = value


UPDATE_BLOCKS = 3


def update(counter, planes, block_out, d_tokens, sums, masters, moments, vector_state):
    shapes = [x.shape for x in sums]

    def by_columns(shape):
        return pl.BlockSpec((shape[0], shape[1] // UPDATE_BLOCKS), lambda i: (0, i))

    def whole(shape):
        return pl.BlockSpec(shape, lambda i: (0,) * len(shape))

    vector = whole((VEC_COUNT, TILE))
    columns = [by_columns(shape) for shape in shapes]
    types = (WIDE, WIDE, WIDE, WIDE, LOW)
    out_shape = [
        jax.ShapeDtypeStruct(block_out.shape, block_out.dtype),
        jax.ShapeDtypeStruct(d_tokens.shape, d_tokens.dtype),
    ]
    out_shape += [jax.ShapeDtypeStruct(shape, kind) for shape in shapes for kind in types]
    out_shape += [jax.ShapeDtypeStruct((VEC_COUNT, TILE), WIDE)] * 4
    operands = []
    for k in range(2):
        operands += [sums[k], masters[k], *moments[k]]
    return pl.pallas_call(
        update_kernel,
        grid=(UPDATE_BLOCKS,),
        out_shape=out_shape,
        in_specs=[pl.BlockSpec(memory_space=pltpu.SMEM), whole(planes.shape)]
        + [by_columns(block_out.shape)] * 2
        + [columns[0]] * 4
        + [columns[1]] * 4
        + [vector] * 3,
        out_specs=[by_columns(block_out.shape)] * 2 + [columns[0]] * 5 + [columns[1]] * 5 + [vector] * 4,
        compiler_params=pltpu.CompilerParams(vmem_limit_bytes=VMEM_BYTES),
    )(counter, planes, block_out, d_tokens, *operands, *vector_state)


def routed(tokens, w_in, w_out):
    sizes = (lax.axis_size("dp"), lax.axis_size("rep"))
    shards = (tokens.shape[1], w_in.shape[0], w_out.shape[0])
    return sizes == (PLANES * SIDE, SIDE * 2) and shards == (SLOTS, IN_ROWS, OUT_ROWS)


def block_anywhere(tokens, cotangent, padding, opening, w_in, w_out, vectors):
    low = jnp.bfloat16
    wide = jnp.float32
    mixer_cols = CH + 2 * D
    length = tokens.shape[1]
    inputs = stripe(tokens[0]).astype(wide)
    filled = stripe(padding[0][:, None]).astype(wide)
    starting = stripe(opening[0][:, None]) == 1
    gains_one = vectors[:D]
    gains_two = vectors[D : 2 * D]
    phases = vectors[2 * D : 2 * D + CH]
    biases = vectors[2 * D + CH :]
    turn = jnp.stack([jnp.cos(phases), jnp.sin(phases)])
    axes = ("dp", "rep")
    full_in = lax.all_gather(w_in.astype(low), axes, axis=0, tiled=True)
    full_out = lax.all_gather(w_out.astype(low), axes, axis=0, tiled=True)
    normed, scaling_one = normalize(inputs, gains_one)
    normed_low = normed.astype(low)
    pre_mix = jnp.dot(normed_low, full_in[:, :mixer_cols], preferred_element_type=wide)
    forget = jax.nn.sigmoid(-(pre_mix[:, :CH] + biases))
    driver_pre = pre_mix[:, CH : CH + D]
    driver = jax.nn.silu(driver_pre)
    gate_pre = pre_mix[:, CH + D :]
    forget_both = jnp.concatenate([forget, forget], axis=1)
    decay = jnp.where(starting, 1.0, forget).astype(low).astype(wide)
    retain = 1.0 - decay
    drive = (forget_both * driver).astype(low).astype(wide)
    drive_re, drive_im = drive[:, :CH], drive[:, CH:]
    summary = local_call(local_forward, [(32, CH)], retain, drive_re, drive_im, turn)[0]
    start = carry_in(summary, turn, length, False)
    states = local_call(
        whole_forward, [(2, length + 8, CH)], retain, drive_re, drive_im, turn, summary, start
    )[0]
    recurrent = jnp.concatenate([states[0, LANES:], states[1, LANES:]], axis=1)
    recurrent = recurrent.astype(low).astype(wide)
    gate_act = jax.nn.silu(gate_pre)
    masked = recurrent * filled
    gated_rows = (masked * gate_act).astype(low)
    middle = inputs + jnp.dot(gated_rows, full_out[:D], preferred_element_type=wide)
    normed_two, scaling_two = normalize(middle, gains_two)
    normed_two_low = normed_two.astype(low)
    glu_pre = jnp.dot(normed_two_low, full_in[:, mixer_cols:], preferred_element_type=wide)
    gate_glu = glu_pre[:, :FF]
    up_glu = glu_pre[:, FF:]
    hidden = (jax.nn.silu(gate_glu) * up_glu).astype(low)
    block_out = middle + jnp.dot(hidden, full_out[D:], preferred_element_type=wide)
    upstream = stripe(cotangent[0]).astype(wide) * filled
    upstream_low = upstream.astype(low)
    grad_down = jnp.einsum("tf,te->fe", hidden, upstream_low, preferred_element_type=wide)
    d_hidden = jnp.einsum("te,fe->tf", upstream_low, full_out[D:], preferred_element_type=wide)
    d_glu = jnp.concatenate(
        [d_hidden * up_glu * silu_slope(gate_glu), d_hidden * jax.nn.silu(gate_glu)], axis=1
    ).astype(low)
    grad_glu = jnp.einsum("td,tc->dc", normed_two_low, d_glu, preferred_element_type=wide)
    d_normed_two = jnp.einsum(
        "tc,dc->td", d_glu, full_in[:, mixer_cols:], preferred_element_type=wide
    )
    grad_gains_two = jnp.sum(d_normed_two * middle * scaling_two, axis=0)
    d_middle = upstream + normalize_back(middle, scaling_two, gains_two, d_normed_two)
    d_mixed_low = d_middle.astype(low)
    grad_mixer_out = jnp.einsum("td,te->de", gated_rows, d_mixed_low, preferred_element_type=wide)
    d_gated = jnp.einsum("te,de->td", d_mixed_low, full_out[:D], preferred_element_type=wide)
    d_recurrent = (d_gated * gate_act * filled).astype(low).astype(wide)
    d_gate_pre = d_gated * masked * silu_slope(gate_pre)
    grad_re, grad_im = d_recurrent[:, :CH], d_recurrent[:, CH:]
    summary_back = local_call(local_backward, [(32, CH)], retain, grad_re, grad_im, turn)[0]
    start_back = carry_in(summary_back, turn, length, True)
    d_decay, d_in_re, d_in_im, d_phase = local_call(
        whole_backward,
        [(length, CH)] * 3 + [(1, CH)],
        retain,
        grad_re,
        grad_im,
        turn,
        summary_back,
        start_back,
        states,
    )
    d_decay = d_decay.astype(low).astype(wide)
    d_input = jnp.concatenate([d_in_re, d_in_im], axis=1).astype(low).astype(wide)
    pulled = d_input * driver
    d_forget = jnp.where(starting, 0.0, d_decay) + pulled[:, :CH] + pulled[:, CH:]
    d_forget_pre = -forget * (1.0 - forget) * d_forget
    d_driver_pre = d_input * forget_both * silu_slope(driver_pre)
    d_mix = jnp.concatenate([d_forget_pre, d_driver_pre, d_gate_pre], axis=1).astype(low)
    grad_mixer_in = jnp.einsum("td,tc->dc", normed_low, d_mix, preferred_element_type=wide)
    d_normed = jnp.einsum(
        "tc,dc->td", d_mix, full_in[:, :mixer_cols], preferred_element_type=wide
    )
    grad_gains_one = jnp.sum(d_normed * inputs * scaling_one, axis=0)
    d_tokens = d_middle + normalize_back(inputs, scaling_one, gains_one, d_normed)
    grad_biases = jnp.sum(d_forget_pre, axis=0)
    grad_vectors = jnp.concatenate([grad_gains_one, grad_gains_two, d_phase[0], grad_biases])
    grad_in_all = jnp.concatenate([grad_mixer_in, grad_glu], axis=1)
    grad_out_all = jnp.concatenate([grad_mixer_out, grad_down], axis=0)
    summed_in = lax.psum_scatter(grad_in_all, axes, scatter_dimension=0, tiled=True)
    summed_out = lax.psum_scatter(grad_out_all, axes, scatter_dimension=0, tiled=True)
    summed_vec, total = lax.psum((grad_vectors, jnp.sum(filled)), axes)
    return unstripe(block_out.astype(low)), unstripe(d_tokens), summed_in, summed_out, summed_vec, total


def body(
    tokens,
    cotangent,
    padding,
    opening,
    w_in,
    w_out,
    vectors,
    m_in,
    v_in,
    m_out,
    v_out,
    m_vec,
    v_vec,
    counter,
):
    if routed(tokens, w_in, w_out):
        block_out, d_tokens, sum_in, sum_out, planes = block_routed(
            tokens, cotangent, padding, opening, w_in, w_out, vectors
        )
        sums, masters = (sum_in, sum_out), (w_in, w_out)
        moments = ((m_in, v_in), (m_out, v_out))
        lines = [x.reshape(VEC_COUNT, TILE) for x in (vectors, m_vec, v_vec)]
        results = update(
            counter, planes, block_out, d_tokens, sums, masters, moments, lines
        )
        block_out, d_tokens = results[:2]
        grad_vec, update_vec, first_vec, second_vec = (x.reshape(-1) for x in results[12:])
        return (
            block_out[None],
            d_tokens[None],
            *results[2:12],
            grad_vec,
            grad_vec[2 * D + CH :],
            update_vec,
            first_vec,
            second_vec,
        )
    block_out, d_tokens, summed_in, summed_out, summed_vec, total = block_anywhere(
        tokens, cotangent, padding, opening, w_in, w_out, vectors
    )
    steps = counter[0].astype(jnp.float32)
    grad_in = summed_in / total
    grad_out = summed_out / total
    grad_vec = summed_vec / total
    new_in, first_in, second_in, change_in = adam_update(
        w_in, grad_in, m_in, v_in, steps, WEIGHT_DECAY
    )
    new_out, first_out, second_out, change_out = adam_update(
        w_out, grad_out, m_out, v_out, steps, WEIGHT_DECAY
    )
    new_vec, first_vec, second_vec, update_vec = adam_update(
        vectors, grad_vec, m_vec, v_vec, steps, 0.0
    )
    return (
        block_out[None],
        d_tokens[None],
        grad_in,
        new_in,
        first_in,
        second_in,
        new_in.astype(jnp.bfloat16),
        grad_out,
        new_out,
        first_out,
        second_out,
        new_out.astype(jnp.bfloat16),
        grad_vec,
        grad_vec[2 * D + CH :],
        update_vec,
        first_vec,
        second_vec,
    )


def solution(mesh):
    in_specs = (
        P("rep", "dp", None),
        P("rep", "dp", None),
        P("rep", "dp"),
        P("rep", "dp"),
        P(("dp", "rep"), None),
        P(("dp", "rep"), None),
        P(),
        P(("dp", "rep"), None),
        P(("dp", "rep"), None),
        P(("dp", "rep"), None),
        P(("dp", "rep"), None),
        P(),
        P(),
        P(),
    )
    out_specs = (
        P("rep", "dp", None),
        P("rep", "dp", None),
        P(("dp", "rep"), None),
        P(("dp", "rep"), None),
        P(("dp", "rep"), None),
        P(("dp", "rep"), None),
        P(("dp", "rep"), None),
        P(("dp", "rep"), None),
        P(("dp", "rep"), None),
        P(("dp", "rep"), None),
        P(("dp", "rep"), None),
        P(("dp", "rep"), None),
        P(),
        P(),
        P(),
        P(),
        P(),
    )
    return jax.shard_map(body, mesh=mesh, in_specs=in_specs, out_specs=out_specs, check_vma=False)
```

```python
import functools

import jax
import jax.numpy as jnp
from jax import lax
from jax.experimental import pallas as pl
from jax.experimental.pallas import tpu as pltpu
from jax.sharding import PartitionSpec as P

D = 768
CH = 384
FF = 1536


NORM_EPSILON = 1e-06
LEARN_RATE = 0.05
BETA_ONE = 0.9
BETA_TWO = 0.999
ADAM_EPSILON = 1e-08
WEIGHT_DECAY = 0.1


LANES = 8


def rotate(real, imag, cosine, sine):
    return cosine * real - sine * imag, sine * real + cosine * imag


def turn_power(cosine, sine, doublings):
    for _ in range(doublings):
        cosine, sine = cosine * cosine - sine * sine, 2.0 * cosine * sine
    return cosine, sine


def local_forward(retain, drive_re, drive_im, turn, summary):
    steps = retain.shape[0] // LANES
    cosine, sine = turn[0:1], turn[1:2]
    zero = jnp.zeros((LANES, retain.shape[1]), jnp.float32)

    def step(i, carry):
        real, imag, product = carry
        rows = pl.ds(pl.multiple_of(LANES * i, LANES), LANES)
        r = retain[rows, :]
        turned_re, turned_im = rotate(real, imag, cosine, sine)
        return r * turned_re + drive_re[rows, :], r * turned_im + drive_im[rows, :], r * product

    real, imag, product = lax.fori_loop(0, steps, step, (zero, zero, zero + 1.0), unroll=4)
    cos_sub, sin_sub = turn_power(cosine, sine, steps.bit_length() - 1)
    total_re, total_im, total = real[0:1], imag[0:1], product[0:1]
    for j in range(1, LANES):
        turned_re, turned_im = rotate(total_re, total_im, cos_sub, sin_sub)
        total_re = product[j : j + 1] * turned_re + real[j : j + 1]
        total_im = product[j : j + 1] * turned_im + imag[j : j + 1]
        total = product[j : j + 1] * total
    summary[0:LANES] = real
    summary[LANES : 2 * LANES] = imag
    summary[2 * LANES : 3 * LANES] = product
    summary[24:32] = jnp.concatenate([total_re, total_im, total, zero[3:]], axis=0)


def whole_forward(retain, drive_re, drive_im, turn, summary, start, states):
    steps = retain.shape[0] // LANES
    cosine, sine = turn[0:1], turn[1:2]
    cos_sub, sin_sub = turn_power(cosine, sine, steps.bit_length() - 1)
    now_re, now_im = start[0:1], start[1:2]
    reals, imags = [now_re], [now_im]
    for j in range(LANES - 1):
        turned_re, turned_im = rotate(now_re, now_im, cos_sub, sin_sub)
        product = summary[2 * LANES + j : 2 * LANES + j + 1]
        now_re = product * turned_re + summary[j : j + 1]
        now_im = product * turned_im + summary[LANES + j : LANES + j + 1]
        reals.append(now_re)
        imags.append(now_im)
    carry = (jnp.concatenate(reals, axis=0), jnp.concatenate(imags, axis=0))

    def step(i, carry):
        real, imag = carry
        rows = pl.ds(pl.multiple_of(LANES * i, LANES), LANES)
        states[0, rows, :] = real
        states[1, rows, :] = imag
        r = retain[rows, :]
        turned_re, turned_im = rotate(real, imag, cosine, sine)
        return r * turned_re + drive_re[rows, :], r * turned_im + drive_im[rows, :]

    real, imag = lax.fori_loop(0, steps, step, carry, unroll=4)
    states[0, LANES * steps :, :] = real
    states[1, LANES * steps :, :] = imag


def local_backward(retain, grad_re, grad_im, turn, summary):
    steps = retain.shape[0] // LANES
    cosine, sine = turn[0:1], -turn[1:2]
    zero = jnp.zeros((LANES, retain.shape[1]), jnp.float32)

    def step(k, carry):
        real, imag, product = carry
        rows = pl.ds(pl.multiple_of(LANES * (steps - 1 - k), LANES), LANES)
        r = retain[rows, :]
        turned_re, turned_im = rotate(grad_re[rows, :] + real, grad_im[rows, :] + imag, cosine, sine)
        return r * turned_re, r * turned_im, r * product

    real, imag, product = lax.fori_loop(0, steps, step, (zero, zero, zero + 1.0), unroll=4)
    cos_sub, sin_sub = turn_power(cosine, sine, steps.bit_length() - 1)
    last = LANES - 1
    total_re, total_im, total = real[last:], imag[last:], product[last:]
    for j in range(LANES - 2, -1, -1):
        turned_re, turned_im = rotate(total_re, total_im, cos_sub, sin_sub)
        total_re = product[j : j + 1] * turned_re + real[j : j + 1]
        total_im = product[j : j + 1] * turned_im + imag[j : j + 1]
        total = product[j : j + 1] * total
    summary[0:LANES] = real
    summary[LANES : 2 * LANES] = imag
    summary[2 * LANES : 3 * LANES] = product
    summary[24:32] = jnp.concatenate([total_re, total_im, total, zero[3:]], axis=0)


def whole_backward(
    retain, grad_re, grad_im, turn, summary, start, states, d_decay, d_in_re, d_in_im, d_phase
):
    steps = retain.shape[0] // LANES
    cosine, sine = turn[0:1], turn[1:2]
    cos_sub, sin_sub = turn_power(cosine, -sine, steps.bit_length() - 1)
    now_re, now_im = start[0:1], start[1:2]
    reals, imags = [now_re], [now_im]
    for j in range(LANES - 1, 0, -1):
        turned_re, turned_im = rotate(now_re, now_im, cos_sub, sin_sub)
        product = summary[2 * LANES + j : 2 * LANES + j + 1]
        now_re = product * turned_re + summary[j : j + 1]
        now_im = product * turned_im + summary[LANES + j : LANES + j + 1]
        reals.append(now_re)
        imags.append(now_im)
    zero = jnp.zeros((LANES, retain.shape[1]), jnp.float32)
    carry = (jnp.concatenate(reals[::-1], axis=0), jnp.concatenate(imags[::-1], axis=0), zero)

    def step(k, carry):
        real, imag, phase = carry
        rows = pl.ds(pl.multiple_of(LANES * (steps - 1 - k), LANES), LANES)
        r = retain[rows, :]
        real = grad_re[rows, :] + real
        imag = grad_im[rows, :] + imag
        prior_re, prior_im = rotate(states[0, rows, :], states[1, rows, :], cosine, sine)
        d_decay[rows, :] = -(real * prior_re + imag * prior_im)
        d_in_re[rows, :] = real
        d_in_im[rows, :] = imag
        phase = phase + r * (imag * prior_re - real * prior_im)
        turned_re, turned_im = rotate(real, imag, cosine, -sine)
        return r * turned_re, r * turned_im, phase

    _, _, phase = lax.fori_loop(0, steps, step, carry, unroll=4)
    d_phase[...] = jnp.sum(phase, axis=0, keepdims=True)


def stripe(rows):
    count, columns = rows.shape
    return rows.reshape(LANES, count // LANES, columns).swapaxes(0, 1).reshape(count, columns)


def unstripe(rows):
    count, columns = rows.shape
    return rows.reshape(count // LANES, LANES, columns).swapaxes(0, 1).reshape(count, columns)


def local_call(kernel, outs, *args):
    return pl.pallas_call(
        kernel,
        out_shape=[jax.ShapeDtypeStruct(shape, jnp.float32) for shape in outs],
        compiler_params=pltpu.CompilerParams(vmem_limit_bytes=32 * 1024 * 1024),
    )(*args)


def carry_chain(every, turn, me, length, reverse):
    sine = -turn[1:2] if reverse else turn[1:2]
    cosine, sine = turn_power(turn[0:1], sine, length.bit_length() - 1)
    count = every.shape[0]
    real = jnp.zeros_like(cosine)
    imag = jnp.zeros_like(cosine)
    for j in range(count - 1, 0, -1) if reverse else range(count - 1):
        use = (j > me) if reverse else (j < me)
        turned_re, turned_im = rotate(real, imag, cosine, sine)
        real = jnp.where(use, every[j, 2:3] * turned_re + every[j, 0:1], real)
        imag = jnp.where(use, every[j, 2:3] * turned_im + every[j, 1:2], imag)
    return jnp.concatenate([real, imag], axis=0)


def carry_in(summary, turn, length, reverse):
    every = lax.all_gather(summary[24:32], "dp", axis=0)
    return carry_chain(every, turn, lax.axis_index("dp"), length, reverse)


def normalize(values, gains):
    scaling = lax.rsqrt(jnp.mean(values * values, axis=-1, keepdims=True) + NORM_EPSILON)
    return (values * scaling * gains, scaling)


def normalize_back(values, scaling, gains, gradient):
    scaled = gradient * gains
    return scaling * scaled - values * scaling**3 * jnp.mean(
        values * scaled, axis=-1, keepdims=True
    )


def silu_slope(values):
    logistic = jax.nn.sigmoid(values)
    return logistic * (1.0 + values * (1.0 - logistic))


def adam_update(master, gradient, first, second, steps, decay):
    first_new = BETA_ONE * first + (1.0 - BETA_ONE) * gradient
    second_new = BETA_TWO * second + (1.0 - BETA_TWO) * gradient * gradient
    corrected = (
        first_new
        / (1.0 - BETA_ONE**steps)
        / (jnp.sqrt(second_new / (1.0 - BETA_TWO**steps)) + ADAM_EPSILON)
    )
    change = -LEARN_RATE * (corrected + decay * master)
    return (master + change, first_new, second_new, change)


MESH = pl.DeviceIdType.MESH
LOW = jnp.bfloat16
WIDE = jnp.float32
PLANES = 4
SIDE = 2
IN_ROWS = 24
OUT_ROWS = 72
MIX = CH + 2 * D
CHUNK = 512
CHUNKS = FF // CHUNK
OUT = 2
TILE = 128
OUTS = D // 2 // TILE
GLU = OUT + OUTS
VMEM_BYTES = 63 * 1024 * 1024
SLOTS = 512
ROWS = 64
RUN = SLOTS // LANES


class Piece:
    def __init__(self, matrix, rows, columns, starts, overlap=0):
        self.matrix, self.rows, self.columns = matrix, rows, columns
        self.starts, self.overlap = starts, overlap

    def shape(self):
        return (2, PLANES, SIDE, SIDE, 2 * self.rows, self.columns)


def piece_list():
    drive = (CH + D) // 2 + TILE // 2
    mix = [
        Piece("in", IN_ROWS, drive, (0, CH + D - drive), TILE),
        Piece("in", IN_ROWS, D // 2, (CH + D, MIX - D // 2)),
    ]
    out = [Piece("out", OUT_ROWS, TILE, (TILE * k, D // 2 + TILE * k)) for k in range(OUTS)]
    glu = [
        Piece("in", IN_ROWS, CHUNK, (MIX + CHUNK * k, MIX + FF + CHUNK * k)) for k in range(CHUNKS)
    ]
    return mix + out + glu


PIECES = piece_list()


class Place:
    def __init__(self):
        dp, rep = lax.axis_index("dp"), lax.axis_index("rep")
        self.z, self.x = dp // SIDE, dp % SIDE
        self.y, self.core = rep // 2, rep % 2

    def at(self, z, x, y, core):
        return (z * SIDE + x, y * 2 + core)

    def sibling(self):
        return self.at(self.z, self.x, self.y, 1 - self.core)

    def plane(self, z):
        return self.at(z, self.x, self.y, self.core)

    def near(self, core):
        if core == 0:
            return self.at(self.z, 1 - self.x, self.y, self.core)
        return self.at(self.z, self.x, 1 - self.y, self.core)

    def far(self, core):
        return self.near(1 - core)

    def away(self):
        return self.z % 2 + 1, (3 * self.z + 2) % 5, 3 - 3 * (self.z // 2)

    def when_inner(self, run):
        pl.when((self.z + 1) // 2 == 1)(run)

    def when_end(self, run):
        pl.when((self.z + 1) // 2 != 1)(run)

    def turn(self, step):
        return lax.rem(self.z + step, PLANES)

    def sides(self, core):
        return (self.x, self.y) if core == 0 else (self.y, self.x)

    def by_core(self, run):
        for core in range(2):
            pl.when(self.core == core)(functools.partial(run, core))

    def greet(self):
        barrier = pltpu.get_barrier_semaphore()
        partners = [self.sibling(), self.near(0), self.near(1)]
        for step in (1, 2, 3):
            partners.append(self.plane(self.turn(step)))
            partners.append(self.at(self.turn(step), 1 - self.x, self.y, self.core))
        for partner in partners:
            pl.semaphore_signal(barrier, inc=1, device_id=partner, device_id_type=MESH)
        return lambda: pl.semaphore_wait(barrier, len(partners))


def always(run):
    run()


def block_of(ref, core, z, near, far):
    return ref.at[core, z, near, far] if core == 0 else ref.at[core, z, far, near]


def pair_of(ref, core, z, far):
    return ref.at[core, z, :, far] if core == 0 else ref.at[core, z, far]


def remote(source, target, sent, received, device):
    return pltpu.make_async_remote_copy(
        src_ref=source,
        dst_ref=target,
        send_sem=sent,
        recv_sem=received,
        device_id=device,
        device_id_type=MESH,
    )


GATHER_NEAR_FIRST = (4, 6, 7)
REDUCE_NEAR_LAST = (2, 3, 6, 7)
GATHER_RELAYED = (0, 2, 4, 5, 6)
REDUCE_RELAYED = (0, 2, 3, 4, 5, 7)


class Gather:
    def __init__(self, place, masters, buffers, staging, sems):
        self.place, self.masters, self.buffers, self.staging = place, masters, buffers, staging
        self.local, self.sent0, self.got0 = sems[:3]
        self.z_sent, self.near_sent, self.far_sent, self.chip_sent, self.chip_got = sems[3:8]
        self.z_got, self.near_got, self.far_got = sems[8:]

    @staticmethod
    def scratch():
        n = len(PIECES)
        dma = pltpu.SemaphoreType.DMA
        return (
            [pltpu.VMEM(p.shape(), LOW) for p in PIECES]
            + [pltpu.VMEM((2 * p.rows, p.columns), WIDE) for p in PIECES]
            + [dma((n,))] * 8
            + [dma((n, PLANES))] * 3
        )

    def part(self, p, half):
        piece = PIECES[p]
        start = piece.starts[0] + half * (piece.starts[1] - piece.starts[0])
        return self.masters[piece.matrix].at[:, pl.ds(pl.multiple_of(start, TILE), piece.columns)]

    def own_rows(self, p):
        rows = PIECES[p].rows
        return self.staging[p].at[pl.ds(pl.multiple_of(self.place.core * rows, 8), rows)]

    def to_sibling(self, p):
        return remote(
            self.part(p, 1 - self.place.core),
            self.own_rows(p),
            self.sent0.at[p],
            self.got0.at[p],
            self.place.sibling(),
        )

    def to_self(self, p):
        return pltpu.make_async_copy(
            self.part(p, self.place.core), self.own_rows(p), self.local.at[p]
        )

    def along_z(self, p, z, target, core):
        place = self.place
        near, far = place.sides(core)
        if p in GATHER_NEAR_FIRST:
            part = pair_of(self.buffers[p], core, z, far)
        else:
            part = block_of(self.buffers[p], core, z, near, far)
        sems = self.z_sent.at[p], self.z_got.at[p, z]
        return remote(part, part, *sems, place.plane(target))

    def relay(self, p, core):
        place = self.place
        last = place.away()[2]
        return self.along_z(p, last, 3 - last, core)

    def along_near(self, p, z, core):
        block = block_of(self.buffers[p], core, z, *self.place.sides(core))
        return remote(
            block, block, self.near_sent.at[p], self.near_got.at[p, z], self.place.near(core)
        )

    def along_far(self, p, z, core):
        pair = pair_of(self.buffers[p], core, z, self.place.sides(core)[1])
        return remote(
            pair, pair, self.far_sent.at[p], self.far_got.at[p, z], self.place.far(core)
        )

    def in_chip(self, p, planes, core):
        part = self.buffers[p].at[core, planes]
        return remote(
            part, part, self.chip_sent.at[p], self.chip_got.at[p], self.place.sibling()
        )

    def begin(self):
        for p in range(len(PIECES)):
            self.to_sibling(p).start()
            self.to_self(p).start()


    def near_own(self, p):
        place = self.place
        self.to_self(p).wait()
        self.to_sibling(p).wait_recv()
        self.buffers[p][place.core, place.z, place.x, place.y] = self.staging[p][...].astype(LOW)
        place.by_core(lambda core: self.along_near(p, place.z, core).start())

    def z_targets(self, p):
        first, second, third = self.place.away()
        relayed = self.place.when_inner if p in GATHER_RELAYED else always
        return (first, always), (second, always), (third, relayed)

    def z_own(self, p):
        place = self.place

        def run(core):
            for z, when in self.z_targets(p):
                when(lambda: self.along_z(p, place.z, z, core).start())

        place.by_core(run)

    def from_z(self, p, index, core):
        place = self.place
        z = place.away()[index]
        self.along_z(p, z, place.z, core).wait_recv()
        if index == 2 and p in GATHER_RELAYED:
            place.when_inner(lambda: self.relay(p, core).start())
        return z

    def far_own(self, p):
        place = self.place

        def run(core):
            self.along_near(p, place.z, core).wait_recv()
            self.along_far(p, place.z, core).start()

        place.by_core(run)

    def near(self, p, *indices):
        place = self.place

        def run(core):
            for index in indices or range(3):
                z = self.from_z(p, index, core)
                self.along_near(p, z, core).start()

        if p not in GATHER_NEAR_FIRST:
            place.by_core(run)

    def far(self, p, *indices):
        place = self.place

        def run(core):
            for index in indices or range(3):
                z = place.away()[index]
                if p in GATHER_NEAR_FIRST:
                    self.from_z(p, index, core)
                else:
                    self.along_near(p, z, core).wait_recv()
                self.along_far(p, z, core).start()

        place.by_core(run)

    def chip(self, p, *indices):
        def run(core):
            for index in indices or range(4):
                z = (self.place.z, *self.place.away())[index]
                self.along_far(p, z, core).wait_recv()
                self.in_chip(p, z, core).start()

        self.place.by_core(run)

    def arrive(self, p):
        self.in_chip(p, pl.ds(0, PLANES), 1 - self.place.core).wait_recv()

    def drain(self, p):
        place, ref = self.place, self.buffers[p]
        self.to_sibling(p).wait_send()

        def sent(part, sem):
            remote(part, part, sem.at[p], sem.at[p], place.sibling()).wait_send()

        def run(core):
            def sent_z(count):
                planes = pl.ds(0, count)
                near_first = p in GATHER_NEAR_FIRST
                part = ref.at[core, planes, :, 0] if near_first else ref.at[core, planes, 0, 0]
                sent(part, self.z_sent)

            if p in GATHER_RELAYED:
                place.when_inner(lambda: sent_z(4))
                place.when_end(lambda: sent_z(2))
            else:
                sent_z(3)
            sent(ref.at[core, pl.ds(0, 1 if p in GATHER_NEAR_FIRST else 4), 0, 0], self.near_sent)
            sent(ref.at[core, :, :, 0], self.far_sent)
            sent(ref.at[core], self.chip_sent)

        place.by_core(run)


class Reduce:
    def __init__(self, place, grads, refs, results):
        n = len(PIECES)
        self.place, self.grads, self.results = place, grads, results
        self.far_got, self.near_got, self.planes, self.final = (refs[k * n : (k + 1) * n] for k in range(4))
        self.far_sem, self.near_sem, self.z_sem = refs[4 * n : 4 * n + 3]
        self.far_sent, self.near_sent, self.z_sent = refs[4 * n + 3 : 4 * n + 6]
        self.chip_sent, self.chip_got = refs[4 * n + 6 :]

    @staticmethod
    def scratch():
        n = len(PIECES)
        dma = pltpu.SemaphoreType.DMA
        blocks = [p.shape()[4:] for p in PIECES]
        return (
            [pltpu.VMEM((PLANES, SIDE) + s, LOW) for s in blocks]
            + [pltpu.VMEM((PLANES,) + s, LOW) for s in blocks]
            + [
                pltpu.VMEM((PLANES,) + (SIDE,) * (p in REDUCE_NEAR_LAST) + s, LOW)
                for p, s in enumerate(blocks)
            ]
            + [pltpu.VMEM(s, WIDE) for s in blocks]
            + [dma((n, PLANES))] * 3
            + [dma((n,))] * 5
        )

    def block(self, p, z, near, far, core):
        return self.grads[p].at[z, near, far] if core == 0 else self.grads[p].at[z, far, near]

    def pair(self, p, z, far, core):
        return self.grads[p].at[z, :, far] if core == 0 else self.grads[p].at[z, far]

    def along_far(self, p, z, core):
        return remote(
            self.pair(p, z, 1 - self.place.sides(core)[1], core),
            self.far_got[p].at[z],
            self.far_sent.at[p],
            self.far_sem.at[p, z],
            self.place.far(core),
        )

    def along_near(self, p, z, core):
        near, far = self.place.sides(core)
        return remote(
            self.block(p, z, 1 - near, far, core),
            self.near_got[p].at[z],
            self.near_sent.at[p],
            self.near_sem.at[p, z],
            self.place.near(core),
        )

    def order(self):
        first, second, third = self.place.away()
        inner = (self.place.z + 1) // 2 % 2
        return (
            inner * first + (1 - inner) * third,
            second,
            inner * third + (1 - inner) * first,
            self.place.z,
        )

    def z_part(self, p, z, core):
        near, far = self.place.sides(core)
        if p in REDUCE_NEAR_LAST:
            return self.pair(p, z, far, core)
        return self.block(p, z, near, far, core)

    def along_z(self, p, z, sender, core):
        sems = self.z_sent.at[p], self.z_sem.at[p, sender]
        target = self.planes[p].at[sender]
        return remote(self.z_part(p, z, core), target, *sems, self.place.plane(z))

    def to_relay(self, p, core, slot):
        first, _, third = self.place.away()
        sems = self.z_sent.at[p], self.z_sem.at[p, slot]
        target = self.planes[p].at[slot]
        return remote(self.z_part(p, third, core), target, *sems, self.place.plane(first))

    def send_z(self, p, core, index):
        place = self.place
        z = self.order()[index]
        if index == 1:
            self.along_z(p, z, place.z, core).start()
        elif p not in REDUCE_RELAYED:
            if index != 3:
                self.along_z(p, z, place.z, core).start()
        elif index == 0:
            place.when_inner(lambda: self.along_z(p, z, place.z, core).start())
            place.when_end(lambda: self.to_relay(p, core, place.away()[0]).start())
        elif index == 2:

            def pass_on():
                self.to_relay(p, core, place.z).wait_recv()
                self.add(self.z_part(p, z, core), self.planes[p].at[place.z])

            place.when_inner(pass_on)
            self.along_z(p, z, place.z, core).start()

    def sum_planes(self, p, core, result):
        place = self.place
        first, second, third = place.away()
        for z in (first, second):
            self.along_z(p, place.z, z, core).wait_recv()
        total = self.z_part(p, place.z, core)[...].astype(WIDE)
        total = total + self.planes[p][first].astype(WIDE) + self.planes[p][second].astype(WIDE)

        def inner():
            self.along_z(p, place.z, third, core).wait_recv()
            result[...] = (total + self.planes[p][third].astype(WIDE)).astype(result.dtype)

        def end():
            result[...] = total.astype(result.dtype)

        if p in REDUCE_RELAYED:
            place.when_inner(inner)
            place.when_end(end)
        else:
            inner()

    def result(self, p, core):
        piece = PIECES[p]
        skip = piece.overlap * core
        start, width = piece.starts[core] + skip, piece.columns - skip
        return self.results[piece.matrix].at[:, pl.ds(start, width)], pl.ds(skip, width)

    def to_sibling(self, p, core):
        rows = PIECES[p].rows
        target, columns = self.result(p, core)
        return remote(
            self.final[p].at[pl.ds(rows * (1 - core), rows), columns],
            target,
            self.chip_sent.at[p],
            self.chip_got.at[p],
            self.place.sibling(),
        )

    @staticmethod
    def add(target, source):
        target[...] = (target[...].astype(WIDE) + source[...].astype(WIDE)).astype(LOW)

    def far(self, p):
        def run(core):
            for z in self.order():
                self.along_far(p, z, core).start()

        self.place.by_core(run)

    def after_far(self, p, *indices):
        def run(core):
            for index in indices or range(4):
                z = self.order()[index]
                self.along_far(p, z, core).wait_recv()
                self.add(self.pair(p, z, self.place.sides(core)[1], core), self.far_got[p].at[z])
                if p in REDUCE_NEAR_LAST:
                    self.send_z(p, core, index)
                else:
                    self.along_near(p, z, core).start()

        self.place.by_core(run)

    def after_near(self, p, *indices):
        place = self.place

        def run(core):
            near, far = place.sides(core)
            if p in REDUCE_NEAR_LAST:
                self.sum_planes(p, core, self.pair(p, place.z, far, core))
                self.along_near(p, place.z, core).start()
                return
            for index in indices or range(4):
                z = self.order()[index]
                self.along_near(p, z, core).wait_recv()
                self.add(self.block(p, z, near, far, core), self.near_got[p].at[z])
                self.send_z(p, core, index)

        place.by_core(run)

    def finish(self, p):
        rows, place = PIECES[p].rows, self.place

        def run(core):
            near, far = place.sides(core)
            if p in REDUCE_NEAR_LAST:
                self.along_near(p, place.z, core).wait_recv()
                own = self.block(p, place.z, near, far, core)[...].astype(WIDE)
                self.final[p][...] = own + self.near_got[p][place.z].astype(WIDE)
            else:
                self.sum_planes(p, core, self.final[p])
            self.to_sibling(p, core).start()
            target, columns = self.result(p, core)
            target[...] = self.final[p][pl.ds(rows * core, rows), columns]

        place.by_core(run)

    def drain(self, p):
        place = self.place

        def sent(part, sem):
            remote(part, part, sem.at[p], sem.at[p], place.sibling()).wait_send()

        def run(core):
            self.to_sibling(p, 1 - core).wait_recv()
            self.to_sibling(p, core).wait_send()

        place.by_core(run)
        sent(self.far_got[p], self.far_sent)
        sent(self.near_got[p].at[pl.ds(0, 1 if p in REDUCE_NEAR_LAST else 4)], self.near_sent)
        sent(self.planes[p].at[pl.ds(0, 3)], self.z_sent)


def tiled(column, count):
    return jnp.concatenate([column] * count, axis=1)


def each_block(run, size=ROWS):
    def block(i, carry):
        run(pl.ds(pl.multiple_of(i * size, size), size))
        return carry

    lax.fori_loop(0, SLOTS // size, block, 0)


def inner(left, right, dims=((1,), (0,))):
    return lax.dot_general(left, right, (dims, ((), ())), preferred_element_type=WIDE)


def across(left, right):
    return inner(left, right, ((1,), (1,)))


def along(left, right):
    return inner(left, right, ((0,), (0,)))


def out_segments(start, count):
    size, runs, stop = 2 * OUT_ROWS, [], start + count
    while start < stop:
        chip, first = divmod(start, size)
        last = min(size, first + stop - start)
        runs.append((chip // 4, chip // 2 % 2, chip % 2, first, last))
        start += last - first
    return runs


def row_norm(values):
    return lax.rsqrt(jnp.mean(values * values, axis=1, keepdims=True) + NORM_EPSILON)


def eights(values):
    return jnp.sum(values.reshape(values.shape[0] // 8, 8, values.shape[1]), axis=0)


def block_scratch():
    vmem, dma = pltpu.VMEM, pltpu.SemaphoreType.DMA
    rows = (SLOTS, D)
    both = (2 * SLOTS, D)
    return dict(
        arrivals=dma((2,)),
        departures=dma((2,)),
        perm=vmem((SLOTS, SLOTS), LOW),
        live=vmem((SLOTS, TILE), WIDE),
        opens=vmem((SLOTS, TILE), WIDE),
        params=vmem((8, D), WIDE),
        tokens=vmem(rows, LOW),
        upstream=vmem((2, SLOTS, D // 2), LOW),
        upstream_got=vmem((SLOTS, D // 2), LOW),
        normed=vmem(both, LOW),
        normed_two=vmem(both, LOW),
        gated=vmem(both, LOW),
        hidden=vmem((CHUNKS, 2 * SLOTS, CHUNK), LOW),
        d_glu=vmem((CHUNKS, 2, SLOTS, CHUNK), LOW),
        d_glu_got=vmem((CHUNKS, SLOTS, CHUNK), LOW),
        d_out=vmem((2, SLOTS, D // 2), LOW),
        d_out_got=vmem((SLOTS, D // 2), LOW),
        d_drive=vmem((2, SLOTS, PIECES[0].columns), LOW),
        d_drive_got=vmem((SLOTS, PIECES[0].columns), LOW),
        d_gate=vmem((2, SLOTS, PIECES[1].columns), LOW),
        d_gate_got=vmem((SLOTS, PIECES[1].columns), LOW),
        pre_mix=vmem((SLOTS, MIX), WIDE),
        retain=vmem((SLOTS, CH), WIDE),
        drive=vmem(rows, WIDE),
        states=vmem((2, SLOTS + LANES, CH), WIDE),
        summaries=vmem((2, 32, CH), WIDE),
        every=vmem((2, PLANES * SIDE, 8, CH), WIDE),
        middle=vmem(rows, WIDE),
        d_normed=vmem(rows, WIDE),
        total=vmem(rows, WIDE),
        block_out=vmem(rows, LOW),
        sums=vmem((3, 8, D), WIDE),
        vector=vmem((8, VEC_ROWS, TILE), WIDE),
        pair_sent=dma((PAIRS,)),
        pair_got=dma((PAIRS,)),
        carry_sent=dma((2,)),
        carry_got=dma((2,)),
        vector_sent=dma((6,)),
        vector_got=dma((6,)),
    )


VEC_ROWS = 24
VEC_COUNT = 18
PAIRS = 13


class Block:
    def __init__(self, place, buffers, grads, refs):
        self.place, self.weights, self.grads = place, buffers, grads
        for name, ref in refs.items():
            setattr(self, name, ref)
        self.me = place.z * SIDE + place.x


    def swaps(self):
        own, got = pl.ds(0, SLOTS), pl.ds(SLOTS, SLOTS)
        other = 1 - self.place.core
        pairs = dict(
            normed=(self.normed.at[own], self.normed.at[got]),
            normed_two=(self.normed_two.at[own], self.normed_two.at[got]),
            gated=(self.gated.at[own], self.gated.at[got]),
            upstream=(self.upstream.at[other], self.upstream_got),
            d_out=(self.d_out.at[other], self.d_out_got),
            d_drive=(self.d_drive.at[other], self.d_drive_got),
            d_gate=(self.d_gate.at[other], self.d_gate_got),
        )
        for k in range(CHUNKS):
            pairs["hidden", k] = (self.hidden.at[k, own], self.hidden.at[k, got])
            pairs["d_glu", k] = (self.d_glu.at[k, other], self.d_glu_got.at[k])
        return pairs

    def swap(self, name):
        pairs = self.swaps()
        slot = list(pairs).index(name)
        sems = self.pair_sent.at[slot], self.pair_got.at[slot]
        return remote(*pairs[name], *sems, self.place.sibling())

    def give(self, *names):
        for name in names:
            self.swap(name).start()

    def take(self, *names):
        for name in names:
            self.swap(name).wait_recv()

    def settle(self):
        for name in self.swaps():
            self.swap(name).wait_send()


    def mix_weight(self, half, m):
        return self.weights[m][half].reshape(D, PIECES[m].columns)

    def glu_weight(self, k):
        parts = [self.weights[GLU + k][half].reshape(D, CHUNK) for half in range(2)]
        return jnp.concatenate(parts, axis=1)

    def out_weight(self, start, count):
        columns = []
        for half in range(2):
            for p in range(OUT, GLU):
                ref = self.weights[p]
                runs = out_segments(start, count)
                parts = [ref[half, z, x, y, first:last] for z, x, y, first, last in runs]
                columns.append(jnp.concatenate(parts, axis=0))
        return jnp.concatenate(columns, axis=1)

    def put_in(self, p, value):
        self.grads[p][...] = value.astype(LOW).reshape(self.grads[p].shape)

    def put_out(self, start, value):
        value, done = value.astype(LOW), 0
        for z, x, y, first, last in out_segments(start, value.shape[0]):
            count = last - first
            for k in range(OUTS):
                part = value[done : done + count, k * TILE : (k + 1) * TILE]
                self.grads[OUT + k][z, x, y, first:last] = part
            done += count


    def prepare(self, padding, opening, vectors):
        row = lax.broadcasted_iota(jnp.int32, (SLOTS, SLOTS), 0)
        column = lax.broadcasted_iota(jnp.int32, (SLOTS, SLOTS), 1)
        perm = (column == row % LANES * RUN + row // LANES).astype(WIDE)
        self.perm[...] = perm.astype(LOW)
        ones = jnp.ones((SLOTS, TILE), LOW)
        self.live[...] = inner((perm * padding[...].astype(WIDE)).astype(LOW), ones)
        self.opens[...] = inner((perm * opening[...].astype(WIDE)).astype(LOW), ones)

        def line(first, count):
            return jnp.concatenate([vectors[first + i : first + i + 1] for i in range(count)], axis=1)

        phase = line(12, 3)
        self.params[0:1] = line(0, 6)
        self.params[1:2] = line(6, 6)
        self.params[2:3] = jnp.concatenate([jnp.cos(phase), jnp.sin(phase)], axis=1)
        self.params[3:4] = jnp.concatenate([line(15, 3)] * 2, axis=1)
        self.sums[...] = jnp.zeros_like(self.sums)

    def turn(self):
        return jnp.concatenate([self.params[2:3, :CH], self.params[2:3, CH:]], axis=0)

    def first_norm(self, raw):
        values = inner(self.perm[...], raw[...])
        self.tokens[...] = values.astype(LOW)
        self.normed[0:SLOTS] = (values * row_norm(values) * self.params[0:1]).astype(LOW)

    def mask_upstream(self, raw):
        striped = inner(self.perm[...], raw[...]) * tiled(self.live[...], D // TILE)
        self.upstream[0] = striped[:, : D // 2].astype(LOW)
        self.upstream[1] = striped[:, D // 2 :].astype(LOW)

    def mix(self, m):
        piece = PIECES[m]
        weight = (self.mix_weight(0, m), self.mix_weight(1, m)[:, piece.overlap :])
        weight = jnp.concatenate(weight, axis=1)
        start = piece.starts[0]
        self.pre_mix[:, start : start + weight.shape[1]] = inner(self.normed[0:SLOTS], weight)

    def drives(self):
        forget = jax.nn.sigmoid(-(self.pre_mix[:, :CH] + self.params[3:4, :CH]))
        pre = self.pre_mix[:, CH : CH + D]
        driver = pre * jax.nn.sigmoid(pre)
        opens = tiled(self.opens[...], CH // TILE)
        decay = jnp.where(opens > 0.5, 1.0, forget).astype(LOW).astype(WIDE)
        self.retain[...] = 1.0 - decay
        drive = jnp.concatenate([forget, forget], axis=1) * driver
        self.drive[...] = drive.astype(LOW).astype(WIDE)

    def parts(self):
        return self.drive.at[:, pl.ds(0, CH)], self.drive.at[:, pl.ds(CH, CH)]

    def others(self):
        place = self.place
        for step in range(PLANES):
            for flip in range(SIDE):
                if step or flip:
                    z = place.turn(step)
                    x = 1 - place.x if flip else place.x
                    yield place.at(z, x, place.y, place.core)

    def carry_copy(self, way, device):
        return remote(
            self.summaries.at[way, pl.ds(24, 8)],
            self.every.at[way, self.me],
            self.carry_sent.at[way],
            self.carry_got.at[way],
            device,
        )

    def all_carries(self, way):
        part = self.every.at[way, pl.ds(0, PLANES * SIDE - 1)]
        sems = self.carry_sent.at[way], self.carry_got.at[way]
        return remote(part, part, *sems, self.place.sibling())

    def scan_own(self, way):
        run = local_backward if way else local_forward
        run(self.retain, *self.parts(), self.turn(), self.summaries.at[way])
        self.every[way, self.me] = self.summaries[way, 24:32]
        for device in self.others():
            self.carry_copy(way, device).start()

    def carried(self, way):
        self.all_carries(way).wait_recv()
        turn = self.turn()
        return carry_chain(self.every.at[way], turn, self.me, SLOTS, way == 1)

    def scan_states(self):
        start = self.carried(0)
        run = whole_forward
        run(self.retain, *self.parts(), self.turn(), self.summaries.at[0], start, self.states)

    def recurrent(self):
        both = jnp.concatenate([self.states[0, LANES:], self.states[1, LANES:]], axis=1)
        return both.astype(LOW).astype(WIDE)

    def gate_rows(self):
        pre = self.pre_mix[:, CH + D :]
        masked = self.recurrent() * tiled(self.live[...], D // TILE)
        self.gated[0:SLOTS] = (masked * (pre * jax.nn.sigmoid(pre))).astype(LOW)

    def second_norm(self):
        mixed = inner(self.gated[0:SLOTS], self.out_weight(0, D))
        middle = self.tokens[...].astype(WIDE) + mixed
        self.middle[...] = middle
        self.total[...] = middle
        self.normed_two[0:SLOTS] = (middle * row_norm(middle) * self.params[1:2]).astype(LOW)

    def whole_upstream(self):
        return jnp.concatenate([self.upstream[0], self.upstream[1]], axis=1)

    def glu_forward(self, k):
        pre = inner(self.normed_two[0:SLOTS], self.glu_weight(k))
        gate, up = pre[:, :CHUNK], pre[:, CHUNK:]
        d_hidden = across(self.whole_upstream(), self.out_weight(D + CHUNK * k, CHUNK))
        logistic = jax.nn.sigmoid(gate)
        active = gate * logistic
        slope = logistic * (1.0 + gate * (1.0 - logistic))
        self.hidden[k, 0:SLOTS] = (active * up).astype(LOW)
        self.d_glu[k, 0] = (d_hidden * up * slope).astype(LOW)
        self.d_glu[k, 1] = (d_hidden * active).astype(LOW)

    def glu_back(self, k):
        d_glu = jnp.concatenate([self.d_glu[k, 0], self.d_glu[k, 1]], axis=1)
        d_share = across(d_glu, self.glu_weight(k))
        self.d_normed[...] = d_share if k == 0 else self.d_normed[...] + d_share

    def own_half(self, ref, got):
        return jnp.concatenate([ref[self.place.core], got], axis=0)

    def glu_grads(self, k):
        d_glu = jnp.concatenate([self.d_glu[k, self.place.core], self.d_glu_got[k]], axis=0)
        self.put_in(GLU + k, along(self.normed_two[...], d_glu))
        upstream = self.own_half(self.upstream, self.upstream_got[...])
        self.put_out(D + CHUNK * k, along(self.hidden[k], upstream))

    def add_sum(self, index, values):
        self.sums[index] += eights(values)

    def middle_back(self):
        middle, d_normed = self.middle[...], self.d_normed[...]
        scaling = row_norm(middle)
        self.add_sum(1, d_normed * middle * scaling)
        scaled = d_normed * self.params[1:2]
        mean = jnp.mean(middle * scaled, axis=1, keepdims=True)
        upstream = self.whole_upstream().astype(WIDE)
        d_middle = upstream + scaling * scaled - middle * (scaling**3 * mean)
        self.middle[...] = d_middle
        self.d_out[0] = d_middle[:, : D // 2].astype(LOW)
        self.d_out[1] = d_middle[:, D // 2 :].astype(LOW)

    def gate_back(self):
        d_out = jnp.concatenate([self.d_out[0], self.d_out[1]], axis=1)
        d_gated = across(d_out, self.out_weight(0, D))
        pre = self.pre_mix[:, CH + D :]
        logistic = jax.nn.sigmoid(pre)
        d_live = d_gated * tiled(self.live[...], D // TILE)
        self.drive[...] = (d_live * (pre * logistic)).astype(LOW).astype(WIDE)
        slope = logistic * (1.0 + pre * (1.0 - logistic))
        d_gate = (d_live * self.recurrent() * slope).astype(LOW)
        self.d_gate[0] = d_gate[:, : D // 2]
        self.d_gate[1] = d_gate[:, D // 2 :]

    def mixer_out_grad(self):
        d_out = self.own_half(self.d_out, self.d_out_got[...])
        self.put_out(0, along(self.gated[...], d_out))

    def scan_back(self):
        start = self.carried(1)
        real, imag = self.parts()
        whole_backward(
            self.retain,
            real,
            imag,
            self.turn(),
            self.summaries.at[1],
            start,
            self.states,
            self.retain,
            real,
            imag,
            self.sums.at[2, pl.ds(0, 1), pl.ds(0, CH)],
        )

    def drives_back(self):
        def run(rows):
            forget = jax.nn.sigmoid(-(self.pre_mix[rows, :CH] + self.params[3:4, :CH]))
            pre = self.pre_mix[rows, CH : CH + D]
            logistic = jax.nn.sigmoid(pre)
            d_decay = self.retain[rows, :].astype(LOW).astype(WIDE)
            d_input = self.drive[rows, :].astype(LOW).astype(WIDE)
            pulled = d_input * (pre * logistic)
            opens = tiled(self.opens[rows, :], CH // TILE)
            d_forget = jnp.where(opens > 0.5, 0.0, d_decay) + pulled[:, :CH] + pulled[:, CH:]
            d_first = -forget * (1.0 - forget) * d_forget
            self.sums[2, :, CH:] += eights(d_first)
            slope = logistic * (1.0 + pre * (1.0 - logistic))
            d_driver = d_input * jnp.concatenate([forget, forget], axis=1) * slope
            d_pre = jnp.concatenate([d_first, d_driver], axis=1).astype(LOW)
            piece = PIECES[0]
            for half, start in enumerate(piece.starts):
                self.d_drive[half, rows, :] = d_pre[:, start : start + piece.columns]

        each_block(run)

    def mix_grads(self, m):
        own, got = ((self.d_drive, self.d_drive_got), (self.d_gate, self.d_gate_got))[m]
        self.put_in(m, along(self.normed[...], self.own_half(own, got[...])))

    def gate_normed(self):
        left = jnp.concatenate([self.d_gate[0], self.d_gate[1]], axis=1)
        right = jnp.concatenate([self.mix_weight(0, 1), self.mix_weight(1, 1)], axis=1)
        self.d_normed[...] = across(left, right)

    def first_back(self):
        skip = PIECES[0].overlap
        left = jnp.concatenate([self.d_drive[0], self.d_drive[1][:, skip:]], axis=1)
        right = jnp.concatenate([self.mix_weight(0, 0), self.mix_weight(1, 0)[:, skip:]], axis=1)
        d_normed = self.d_normed[...] + across(left, right)
        values = self.tokens[...].astype(WIDE)
        scaling = row_norm(values)
        self.add_sum(0, d_normed * values * scaling)
        scaled = d_normed * self.params[0:1]
        mean = jnp.mean(values * scaled, axis=1, keepdims=True)
        self.middle[...] += scaling * scaled - values * (scaling**3 * mean)

    def natural_out(self):
        hidden = jnp.concatenate([self.hidden[k, 0:SLOTS] for k in range(CHUNKS)], axis=1)
        total = self.total[...] + inner(hidden, self.out_weight(D, FF))
        self.block_out[...] = along(self.perm[...], total.astype(LOW)).astype(LOW)

    def natural_tokens(self):
        rest = self.middle[...]
        total = jnp.zeros_like(rest)
        for _ in range(3):
            part = rest.astype(LOW)
            total = total + along(self.perm[...], part)
            rest = rest - part.astype(WIDE)
        self.d_normed[...] = total


    def gather_vector(self):
        lines = [
            jnp.sum(self.sums[0], axis=0, keepdims=True),
            jnp.sum(self.sums[1], axis=0, keepdims=True),
            jnp.concatenate(
                [self.sums[2, 0:1, :CH], jnp.sum(self.sums[2, :, CH:], axis=0, keepdims=True)], axis=1
            ),
        ]
        for i, line in enumerate(lines):
            for j in range(D // TILE):
                row = i * (D // TILE) + j
                self.vector[0, row : row + 1] = line[:, j * TILE : (j + 1) * TILE]
        filled = jnp.sum(self.live[...], axis=0, keepdims=True)
        rest = jnp.zeros((VEC_ROWS - VEC_COUNT - 1, TILE), WIDE)
        self.vector[0, VEC_COUNT:] = jnp.concatenate([filled, rest], axis=0)

    def vector_copy(self, stage):
        place = self.place
        device = (place.sibling(), place.near(0), place.near(1))[stage]
        source = self.vector.at[stage]
        target = self.vector.at[4 + stage]
        return remote(source, target, self.vector_sent.at[stage], self.vector_got.at[stage], device)

    def vector_step(self, stage):
        if stage:
            self.vector_copy(stage - 1).wait_recv()
            self.vector[stage] = self.vector[stage - 1] + self.vector[3 + stage]
        if stage < 3:
            self.vector_copy(stage).start()

    def vector_plane(self, planes, step, sender):
        place = self.place
        return remote(
            self.vector.at[3],
            planes.at[sender],
            self.vector_sent.at[2 + step],
            self.vector_got.at[2 + step],
            place.plane(place.turn(step)),
        )


def block_kernel(tokens, cotangent, padding, opening, w_in, w_out, vectors, *refs):
    n = len(PIECES)
    block_out, d_tokens, sum_in, sum_out, planes = refs[:5]
    refs = refs[5:]
    count = len(Gather.scratch())
    gather_refs, refs = refs[:count], refs[count:]
    buffers, staging, gather_sems = gather_refs[:n], gather_refs[n : 2 * n], gather_refs[2 * n :]
    grads, refs = refs[:n], refs[n:]
    count = len(Reduce.scratch())
    reduce_refs, refs = refs[:count], refs[count:]
    place = Place()
    gather = Gather(place, {"in": w_in, "out": w_out}, buffers, staging, gather_sems)
    reduce = Reduce(place, grads, reduce_refs, {"in": sum_in, "out": sum_out})
    block = Block(place, buffers, grads, dict(zip(block_scratch(), refs, strict=True)))

    entered = place.greet()
    raw_tokens, raw_upstream = block.gated.at[pl.ds(0, SLOTS)], block.block_out
    loads = [
        pltpu.make_async_copy(tokens.at[0], raw_tokens, block.arrivals.at[0]),
        pltpu.make_async_copy(cotangent.at[0], raw_upstream, block.arrivals.at[1]),
    ]
    leave_out = pltpu.make_async_copy(block.block_out, block_out, block.departures.at[0])
    leave_tokens = pltpu.make_async_copy(block.d_normed, d_tokens, block.departures.at[1])
    for load in loads:
        load.start()
    block.prepare(padding, opening, vectors)
    entered()
    gather.begin()
    gather.near_own(0)
    gather.z_own(0)
    gather.near_own(4)
    gather.near_own(3)
    gather.z_own(3)
    gather.near_own(1)
    gather.near_own(5)
    gather.near_own(7)
    gather.near_own(6)
    gather.z_own(1)
    gather.near_own(2)
    gather.far_own(0)
    gather.z_own(5)
    gather.z_own(2)
    gather.far_own(4)
    gather.far_own(5)
    gather.near(0, 1, 0)
    gather.far_own(6)
    gather.far_own(3)
    gather.far_own(1)
    gather.near(3, 2, 1)
    gather.far(0, 1)
    gather.near(0, 2)
    gather.far(0, 0)
    gather.near(1, 0, 2)
    gather.z_own(4)
    loads[0].wait()
    block.first_norm(raw_tokens)
    gather.near(1, 1)
    gather.near(5, 1)
    gather.z_own(6)
    gather.near(5, 0)
    gather.near(2, 0)
    gather.far(0, 2)
    gather.far(1, 2)
    gather.far(3, 1)
    gather.chip(0, 1)
    gather.far(1, 0)
    gather.near(2, 1)
    gather.far_own(2)
    gather.near(3, 0)
    gather.far(5, 1)
    gather.chip(0, 0)
    gather.far(1, 1)
    gather.near(2, 2)
    gather.far(2, 0)
    gather.far_own(7)
    gather.chip(0, 2, 3)
    gather.chip(6, 0)
    gather.near(5, 2)
    loads[1].wait()
    block.mask_upstream(raw_upstream)
    gather.chip(1, 3)
    gather.arrive(0)
    gather.far(3, 2)
    block.mix(0)
    gather.far(3, 0)
    block.drives()
    gather.chip(3, 2)
    block.scan_own(0)
    gather.chip(4, 0)
    gather.far(5, 0)
    gather.chip(2, 0)
    gather.far(4, 2, 1)
    gather.z_own(7)
    gather.far(2, 2)
    gather.chip(5, 0)
    block.give("upstream")
    gather.far(6, 1)
    gather.chip(3, 0)
    gather.far(5, 2)
    gather.chip(1, 2)
    gather.chip(2, 1)
    gather.chip(1, 1, 0)
    gather.chip(5, 2)
    gather.far(4, 0)
    gather.chip(7, 0)
    gather.far(2, 1)
    gather.chip(3, 3)
    gather.arrive(1)
    block.give("normed")
    gather.chip(3, 1)
    gather.far(6, 0)
    block.mix(1)
    gather.far(6, 2)
    block.take("upstream")
    gather.chip(5, 3)
    gather.chip(2, 3)
    gather.chip(4, 3)
    gather.far(7, 0)
    block.scan_states()
    gather.chip(4, 2, 1)
    gather.chip(2, 2)
    gather.arrive(3)
    gather.far(7, 2)
    block.take("normed")
    gather.chip(6, 2)
    gather.chip(5, 1)
    block.gate_rows()
    gather.arrive(4)
    gather.chip(6, 1)
    gather.far(7, 1)
    gather.arrive(2)
    block.second_norm()
    gather.chip(6, 3)
    gather.arrive(5)
    block.give("normed_two")
    block.glu_forward(0)
    gather.chip(7, 1)
    gather.arrive(6)
    block.give(("d_glu", 0))
    block.glu_back(0)
    gather.chip(7, 3, 2)
    block.glu_forward(1)
    block.give(("d_glu", 1), ("hidden", 1))
    block.take("normed_two")
    block.glu_back(1)
    gather.arrive(7)
    block.glu_forward(2)
    block.give(("d_glu", 2), "gated")
    block.take(("d_glu", 1))
    block.give(("hidden", 2))
    block.take(("hidden", 1), ("d_glu", 0))
    block.glu_grads(1)
    reduce.far(6)
    block.take(("d_glu", 2))
    block.glu_back(2)
    block.middle_back()
    block.gate_back()
    block.scan_own(1)
    block.give(("hidden", 0))
    block.take("gated", ("hidden", 2))
    block.glu_grads(2)
    reduce.far(7)
    block.give("d_out")
    reduce.after_far(6, 1)
    block.take(("hidden", 0))
    block.glu_grads(0)
    reduce.after_far(6, 2)
    block.take("d_out")
    block.mixer_out_grad()
    reduce.far(4)
    reduce.after_far(7, 0)
    reduce.far(3)
    block.scan_back()
    block.drives_back()
    reduce.after_far(6, 0)
    reduce.after_far(4, 0)
    block.give("d_gate")
    reduce.far(2)
    reduce.after_far(7, 2)
    block.gate_normed()
    block.take("d_gate")
    block.give("d_drive")
    block.take("d_drive")
    reduce.far(5)
    reduce.after_far(3, 0)
    reduce.after_far(6, 3)
    reduce.after_far(4, 2)
    block.mix_grads(0)
    block.mix_grads(1)
    reduce.after_far(7, 1)
    reduce.after_far(2, 1)
    block.natural_out()
    leave_out.start()
    reduce.far(1)
    reduce.after_far(3, 1)
    block.first_back()
    reduce.after_far(2, 0)
    block.gather_vector()
    reduce.after_far(5, 0)
    reduce.after_near(4, 0)
    block.natural_tokens()
    leave_tokens.start()
    reduce.after_far(3, 3)
    reduce.far(0)
    reduce.after_far(3, 2)
    reduce.after_far(7, 3)
    reduce.after_far(1, 0)
    reduce.after_near(5, 0)
    reduce.after_far(1, 2)
    reduce.after_far(2, 2)
    reduce.after_far(4, 1)
    reduce.after_far(0, 0)
    reduce.after_near(4, 2)
    reduce.after_near(1, 2)
    reduce.after_far(5, 1)
    reduce.after_near(4, 1)
    reduce.after_far(1, 1)
    reduce.after_far(0, 1)
    reduce.after_far(2, 3)
    reduce.after_near(1, 0)
    reduce.after_far(4, 3)
    reduce.after_near(0, 0)
    reduce.after_near(7)
    block.vector_step(0)
    reduce.after_far(0, 2)
    block.vector_step(1)
    reduce.after_near(5, 1)
    reduce.after_near(3)
    reduce.after_near(1, 1)
    reduce.after_far(5, 2)
    reduce.after_far(1, 3)
    reduce.after_far(0, 3)
    reduce.after_near(0, 1)
    reduce.after_near(2)
    reduce.after_near(4, 3)
    block.vector_step(2)
    reduce.after_near(0, 2)
    reduce.after_far(5, 3)
    reduce.after_near(6)
    reduce.after_near(5, 2)
    reduce.after_near(1, 3)
    reduce.after_near(0, 3)
    reduce.finish(7)
    reduce.finish(1)
    block.vector_step(3)
    for step in (1, 2, 3):
        block.vector_plane(planes, step, place.z).start()
    planes[place.z] = block.vector[3]
    reduce.finish(2)
    reduce.finish(4)
    reduce.finish(6)
    reduce.after_near(5, 3)
    reduce.finish(0)
    reduce.finish(3)
    reduce.finish(5)

    for step in (1, 2, 3):
        block.vector_plane(planes, step, place.z).wait_send()
        block.vector_plane(planes, step, place.turn(4 - step)).wait_recv()
    for stage in range(3):
        block.vector_copy(stage).wait_send()
    for way in range(2):
        block.all_carries(way).wait_send()
    block.settle()
    for p in range(n):
        gather.drain(p)
        reduce.drain(p)
    leave_out.wait()
    leave_tokens.wait()


def block_routed(tokens, cotangent, padding, opening, w_in, w_out, vectors):
    vmem = pl.BlockSpec(memory_space=pltpu.VMEM)
    anywhere = pl.BlockSpec(memory_space=pl.ANY)
    out_shape = [
        jax.ShapeDtypeStruct((SLOTS, D), LOW),
        jax.ShapeDtypeStruct((SLOTS, D), WIDE),
        jax.ShapeDtypeStruct(w_in.shape, WIDE),
        jax.ShapeDtypeStruct(w_out.shape, WIDE),
        jax.ShapeDtypeStruct((PLANES, VEC_ROWS, TILE), WIDE),
    ]
    grads = [pltpu.VMEM(p.shape()[1:], LOW) for p in PIECES]
    block_out, d_tokens, sum_in, sum_out, planes = pl.pallas_call(
        block_kernel,
        out_shape=out_shape,
        in_specs=[anywhere, anywhere, vmem, vmem, anywhere, anywhere, vmem],
        out_specs=[anywhere, anywhere, vmem, vmem, vmem],
        scratch_shapes=Gather.scratch()
        + grads
        + Reduce.scratch()
        + list(block_scratch().values()),
        compiler_params=pltpu.CompilerParams(
            collective_id=0, has_side_effects=True, vmem_limit_bytes=VMEM_BYTES
        ),
    )(tokens, cotangent, padding, opening, w_in, w_out, vectors.reshape(VEC_COUNT, TILE))
    return block_out, d_tokens, sum_in, sum_out, planes


def power(base, count):
    return lax.fori_loop(0, count, lambda _, value: value * base, jnp.float32(1.0))


def update_kernel(counter, planes, block_from, tokens_from, *refs):
    ins, outs = refs[:11], refs[11:]
    outs[0][...] = block_from[...]
    outs[1][...] = tokens_from[...]
    first_scale = 1.0 - power(BETA_ONE, counter[0])
    second_scale = 1.0 - power(BETA_TWO, counter[0])
    vectors = (planes[0] + planes[1]) + (planes[2] + planes[3])
    total = vectors[VEC_COUNT : VEC_COUNT + 1, 0:1]

    def step(summed, master, first, second, decay):
        gradient = summed / total
        first = BETA_ONE * first + (1.0 - BETA_ONE) * gradient
        second = BETA_TWO * second + (1.0 - BETA_TWO) * gradient * gradient
        corrected = first / first_scale / (jnp.sqrt(second / second_scale) + ADAM_EPSILON)
        return gradient, -LEARN_RATE * (corrected + decay * master), first, second

    for k in range(2):
        summed, master, first, second = (ref[...] for ref in ins[4 * k : 4 * k + 4])
        gradient, change, first, second = step(summed, master, first, second, WEIGHT_DECAY)
        new = master + change
        results = (gradient, new, first, second, new.astype(LOW))
        for ref, value in zip(outs[2 + 5 * k : 7 + 5 * k], results, strict=True):
            ref[...] = value
    master, first, second = (ref[...] for ref in ins[8:])
    results = step(vectors[:VEC_COUNT], master, first, second, 0.0)
    for ref, value in zip(outs[12:16], results, strict=True):
        for i in range(VEC_COUNT):
            ref[pl.ds(i * TILE, TILE)] = value[i]
    for i in range(CH // TILE):
        outs[16][pl.ds(i * TILE, TILE)] = results[0][VEC_COUNT - CH // TILE + i]


UPDATE_BLOCKS = 1


def update(counter, planes, block_out, d_tokens, sums, masters, moments, vector_state):
    shapes = [x.shape for x in sums]

    def by_columns(shape):
        return pl.BlockSpec((shape[0], shape[1] // UPDATE_BLOCKS), lambda i: (0, i))

    def whole(shape):
        return pl.BlockSpec(shape, lambda i: (0,) * len(shape))

    vector = whole((VEC_COUNT, TILE))
    columns = [by_columns(shape) for shape in shapes]
    types = (WIDE, WIDE, WIDE, WIDE, LOW)
    out_shape = [
        jax.ShapeDtypeStruct(block_out.shape, block_out.dtype),
        jax.ShapeDtypeStruct(d_tokens.shape, d_tokens.dtype),
    ]
    out_shape += [jax.ShapeDtypeStruct(shape, kind) for shape in shapes for kind in types]
    lines = [(VEC_COUNT * TILE,)] * 4 + [(CH,)]
    out_shape += [jax.ShapeDtypeStruct(line, WIDE) for line in lines]
    operands = []
    for k in range(2):
        operands += [sums[k], masters[k], *moments[k]]
    return pl.pallas_call(
        update_kernel,
        grid=(UPDATE_BLOCKS,),
        out_shape=out_shape,
        in_specs=[pl.BlockSpec(memory_space=pltpu.SMEM), whole(planes.shape)]
        + [by_columns(block_out.shape)] * 2
        + [columns[0]] * 4
        + [columns[1]] * 4
        + [vector] * 3,
        out_specs=[by_columns(block_out.shape)] * 2 + [columns[0]] * 5 + [columns[1]] * 5 + [whole(line) for line in lines],
        compiler_params=pltpu.CompilerParams(vmem_limit_bytes=VMEM_BYTES),
    )(counter, planes, block_out, d_tokens, *operands, *vector_state)


def routed(tokens, w_in, w_out):
    sizes = (lax.axis_size("dp"), lax.axis_size("rep"))
    shards = (tokens.shape[1], w_in.shape[0], w_out.shape[0])
    return sizes == (PLANES * SIDE, SIDE * 2) and shards == (SLOTS, IN_ROWS, OUT_ROWS)


def block_anywhere(tokens, cotangent, padding, opening, w_in, w_out, vectors):
    low = jnp.bfloat16
    wide = jnp.float32
    mixer_cols = CH + 2 * D
    length = tokens.shape[1]
    inputs = stripe(tokens[0]).astype(wide)
    filled = stripe(padding[0][:, None]).astype(wide)
    starting = stripe(opening[0][:, None]) == 1
    gains_one = vectors[:D]
    gains_two = vectors[D : 2 * D]
    phases = vectors[2 * D : 2 * D + CH]
    biases = vectors[2 * D + CH :]
    turn = jnp.stack([jnp.cos(phases), jnp.sin(phases)])
    axes = ("dp", "rep")
    full_in = lax.all_gather(w_in.astype(low), axes, axis=0, tiled=True)
    full_out = lax.all_gather(w_out.astype(low), axes, axis=0, tiled=True)
    normed, scaling_one = normalize(inputs, gains_one)
    normed_low = normed.astype(low)
    pre_mix = jnp.dot(normed_low, full_in[:, :mixer_cols], preferred_element_type=wide)
    forget = jax.nn.sigmoid(-(pre_mix[:, :CH] + biases))
    driver_pre = pre_mix[:, CH : CH + D]
    driver = jax.nn.silu(driver_pre)
    gate_pre = pre_mix[:, CH + D :]
    forget_both = jnp.concatenate([forget, forget], axis=1)
    decay = jnp.where(starting, 1.0, forget).astype(low).astype(wide)
    retain = 1.0 - decay
    drive = (forget_both * driver).astype(low).astype(wide)
    drive_re, drive_im = drive[:, :CH], drive[:, CH:]
    summary = local_call(local_forward, [(32, CH)], retain, drive_re, drive_im, turn)[0]
    start = carry_in(summary, turn, length, False)
    states = local_call(
        whole_forward, [(2, length + 8, CH)], retain, drive_re, drive_im, turn, summary, start
    )[0]
    recurrent = jnp.concatenate([states[0, LANES:], states[1, LANES:]], axis=1)
    recurrent = recurrent.astype(low).astype(wide)
    gate_act = jax.nn.silu(gate_pre)
    masked = recurrent * filled
    gated_rows = (masked * gate_act).astype(low)
    middle = inputs + jnp.dot(gated_rows, full_out[:D], preferred_element_type=wide)
    normed_two, scaling_two = normalize(middle, gains_two)
    normed_two_low = normed_two.astype(low)
    glu_pre = jnp.dot(normed_two_low, full_in[:, mixer_cols:], preferred_element_type=wide)
    gate_glu = glu_pre[:, :FF]
    up_glu = glu_pre[:, FF:]
    hidden = (jax.nn.silu(gate_glu) * up_glu).astype(low)
    block_out = middle + jnp.dot(hidden, full_out[D:], preferred_element_type=wide)
    upstream = stripe(cotangent[0]).astype(wide) * filled
    upstream_low = upstream.astype(low)
    grad_down = jnp.einsum("tf,te->fe", hidden, upstream_low, preferred_element_type=wide)
    d_hidden = jnp.einsum("te,fe->tf", upstream_low, full_out[D:], preferred_element_type=wide)
    d_glu = jnp.concatenate(
        [d_hidden * up_glu * silu_slope(gate_glu), d_hidden * jax.nn.silu(gate_glu)], axis=1
    ).astype(low)
    grad_glu = jnp.einsum("td,tc->dc", normed_two_low, d_glu, preferred_element_type=wide)
    d_normed_two = jnp.einsum(
        "tc,dc->td", d_glu, full_in[:, mixer_cols:], preferred_element_type=wide
    )
    grad_gains_two = jnp.sum(d_normed_two * middle * scaling_two, axis=0)
    d_middle = upstream + normalize_back(middle, scaling_two, gains_two, d_normed_two)
    d_mixed_low = d_middle.astype(low)
    grad_mixer_out = jnp.einsum("td,te->de", gated_rows, d_mixed_low, preferred_element_type=wide)
    d_gated = jnp.einsum("te,de->td", d_mixed_low, full_out[:D], preferred_element_type=wide)
    d_recurrent = (d_gated * gate_act * filled).astype(low).astype(wide)
    d_gate_pre = d_gated * masked * silu_slope(gate_pre)
    grad_re, grad_im = d_recurrent[:, :CH], d_recurrent[:, CH:]
    summary_back = local_call(local_backward, [(32, CH)], retain, grad_re, grad_im, turn)[0]
    start_back = carry_in(summary_back, turn, length, True)
    d_decay, d_in_re, d_in_im, d_phase = local_call(
        whole_backward,
        [(length, CH)] * 3 + [(1, CH)],
        retain,
        grad_re,
        grad_im,
        turn,
        summary_back,
        start_back,
        states,
    )
    d_decay = d_decay.astype(low).astype(wide)
    d_input = jnp.concatenate([d_in_re, d_in_im], axis=1).astype(low).astype(wide)
    pulled = d_input * driver
    d_forget = jnp.where(starting, 0.0, d_decay) + pulled[:, :CH] + pulled[:, CH:]
    d_forget_pre = -forget * (1.0 - forget) * d_forget
    d_driver_pre = d_input * forget_both * silu_slope(driver_pre)
    d_mix = jnp.concatenate([d_forget_pre, d_driver_pre, d_gate_pre], axis=1).astype(low)
    grad_mixer_in = jnp.einsum("td,tc->dc", normed_low, d_mix, preferred_element_type=wide)
    d_normed = jnp.einsum(
        "tc,dc->td", d_mix, full_in[:, :mixer_cols], preferred_element_type=wide
    )
    grad_gains_one = jnp.sum(d_normed * inputs * scaling_one, axis=0)
    d_tokens = d_middle + normalize_back(inputs, scaling_one, gains_one, d_normed)
    grad_biases = jnp.sum(d_forget_pre, axis=0)
    grad_vectors = jnp.concatenate([grad_gains_one, grad_gains_two, d_phase[0], grad_biases])
    grad_in_all = jnp.concatenate([grad_mixer_in, grad_glu], axis=1)
    grad_out_all = jnp.concatenate([grad_mixer_out, grad_down], axis=0)
    summed_in = lax.psum_scatter(grad_in_all, axes, scatter_dimension=0, tiled=True)
    summed_out = lax.psum_scatter(grad_out_all, axes, scatter_dimension=0, tiled=True)
    summed_vec, total = lax.psum((grad_vectors, jnp.sum(filled)), axes)
    return unstripe(block_out.astype(low)), unstripe(d_tokens), summed_in, summed_out, summed_vec, total


def body(
    tokens,
    cotangent,
    padding,
    opening,
    w_in,
    w_out,
    vectors,
    m_in,
    v_in,
    m_out,
    v_out,
    m_vec,
    v_vec,
    counter,
):
    if routed(tokens, w_in, w_out):
        block_out, d_tokens, sum_in, sum_out, planes = block_routed(
            tokens, cotangent, padding, opening, w_in, w_out, vectors
        )
        sums, masters = (sum_in, sum_out), (w_in, w_out)
        moments = ((m_in, v_in), (m_out, v_out))
        lines = [x.reshape(VEC_COUNT, TILE) for x in (vectors, m_vec, v_vec)]
        results = update(
            counter, planes, block_out, d_tokens, sums, masters, moments, lines
        )
        block_out, d_tokens = results[:2]
        grad_vec, update_vec, first_vec, second_vec, grad_bias = results[12:]
        return (
            block_out[None],
            d_tokens[None],
            *results[2:12],
            grad_vec,
            grad_bias,
            update_vec,
            first_vec,
            second_vec,
        )
    block_out, d_tokens, summed_in, summed_out, summed_vec, total = block_anywhere(
        tokens, cotangent, padding, opening, w_in, w_out, vectors
    )
    steps = counter[0].astype(jnp.float32)
    grad_in = summed_in / total
    grad_out = summed_out / total
    grad_vec = summed_vec / total
    new_in, first_in, second_in, change_in = adam_update(
        w_in, grad_in, m_in, v_in, steps, WEIGHT_DECAY
    )
    new_out, first_out, second_out, change_out = adam_update(
        w_out, grad_out, m_out, v_out, steps, WEIGHT_DECAY
    )
    new_vec, first_vec, second_vec, update_vec = adam_update(
        vectors, grad_vec, m_vec, v_vec, steps, 0.0
    )
    return (
        block_out[None],
        d_tokens[None],
        grad_in,
        new_in,
        first_in,
        second_in,
        new_in.astype(jnp.bfloat16),
        grad_out,
        new_out,
        first_out,
        second_out,
        new_out.astype(jnp.bfloat16),
        grad_vec,
        grad_vec[2 * D + CH :],
        update_vec,
        first_vec,
        second_vec,
    )


def solution(mesh):
    in_specs = (
        P("rep", "dp", None),
        P("rep", "dp", None),
        P("rep", "dp"),
        P("rep", "dp"),
        P(("dp", "rep"), None),
        P(("dp", "rep"), None),
        P(),
        P(("dp", "rep"), None),
        P(("dp", "rep"), None),
        P(("dp", "rep"), None),
        P(("dp", "rep"), None),
        P(),
        P(),
        P(),
    )
    out_specs = (
        P("rep", "dp", None),
        P("rep", "dp", None),
        P(("dp", "rep"), None),
        P(("dp", "rep"), None),
        P(("dp", "rep"), None),
        P(("dp", "rep"), None),
        P(("dp", "rep"), None),
        P(("dp", "rep"), None),
        P(("dp", "rep"), None),
        P(("dp", "rep"), None),
        P(("dp", "rep"), None),
        P(("dp", "rep"), None),
        P(),
        P(),
        P(),
        P(),
        P(),
    )
    return jax.shard_map(body, mesh=mesh, in_specs=in_specs, out_specs=out_specs, check_vma=False)
```

```python
import functools

import jax
import jax.numpy as jnp
from jax import lax
from jax.experimental import pallas as pl
from jax.experimental.pallas import tpu as pltpu
from jax.sharding import PartitionSpec as P

D = 768
CH = 384
FF = 1536


NORM_EPSILON = 1e-06
LEARN_RATE = 0.05
BETA_ONE = 0.9
BETA_TWO = 0.999
ADAM_EPSILON = 1e-08
WEIGHT_DECAY = 0.1


LANES = 8


def rotate(real, imag, cosine, sine):
    return cosine * real - sine * imag, sine * real + cosine * imag


def turn_power(cosine, sine, doublings):
    for _ in range(doublings):
        cosine, sine = cosine * cosine - sine * sine, 2.0 * cosine * sine
    return cosine, sine


def local_forward(retain, drive_re, drive_im, turn, summary):
    steps = retain.shape[0] // LANES
    cosine, sine = turn[0:1], turn[1:2]
    zero = jnp.zeros((LANES, retain.shape[1]), jnp.float32)

    def step(i, carry):
        real, imag, product = carry
        rows = pl.ds(pl.multiple_of(LANES * i, LANES), LANES)
        r = retain[rows, :]
        turned_re, turned_im = rotate(real, imag, cosine, sine)
        return r * turned_re + drive_re[rows, :], r * turned_im + drive_im[rows, :], r * product

    real, imag, product = lax.fori_loop(0, steps, step, (zero, zero, zero + 1.0), unroll=4)
    cos_sub, sin_sub = turn_power(cosine, sine, steps.bit_length() - 1)
    total_re, total_im, total = real[0:1], imag[0:1], product[0:1]
    for j in range(1, LANES):
        turned_re, turned_im = rotate(total_re, total_im, cos_sub, sin_sub)
        total_re = product[j : j + 1] * turned_re + real[j : j + 1]
        total_im = product[j : j + 1] * turned_im + imag[j : j + 1]
        total = product[j : j + 1] * total
    summary[0:LANES] = real
    summary[LANES : 2 * LANES] = imag
    summary[2 * LANES : 3 * LANES] = product
    summary[24:32] = jnp.concatenate([total_re, total_im, total, zero[3:]], axis=0)


def whole_forward(retain, drive_re, drive_im, turn, summary, start, states):
    steps = retain.shape[0] // LANES
    cosine, sine = turn[0:1], turn[1:2]
    cos_sub, sin_sub = turn_power(cosine, sine, steps.bit_length() - 1)
    now_re, now_im = start[0:1], start[1:2]
    reals, imags = [now_re], [now_im]
    for j in range(LANES - 1):
        turned_re, turned_im = rotate(now_re, now_im, cos_sub, sin_sub)
        product = summary[2 * LANES + j : 2 * LANES + j + 1]
        now_re = product * turned_re + summary[j : j + 1]
        now_im = product * turned_im + summary[LANES + j : LANES + j + 1]
        reals.append(now_re)
        imags.append(now_im)
    carry = (jnp.concatenate(reals, axis=0), jnp.concatenate(imags, axis=0))

    def step(i, carry):
        real, imag = carry
        rows = pl.ds(pl.multiple_of(LANES * i, LANES), LANES)
        states[0, rows, :] = real
        states[1, rows, :] = imag
        r = retain[rows, :]
        turned_re, turned_im = rotate(real, imag, cosine, sine)
        return r * turned_re + drive_re[rows, :], r * turned_im + drive_im[rows, :]

    real, imag = lax.fori_loop(0, steps, step, carry, unroll=4)
    states[0, LANES * steps :, :] = real
    states[1, LANES * steps :, :] = imag


def local_backward(retain, grad_re, grad_im, turn, summary):
    steps = retain.shape[0] // LANES
    cosine, sine = turn[0:1], -turn[1:2]
    zero = jnp.zeros((LANES, retain.shape[1]), jnp.float32)

    def step(k, carry):
        real, imag, product = carry
        rows = pl.ds(pl.multiple_of(LANES * (steps - 1 - k), LANES), LANES)
        r = retain[rows, :]
        turned_re, turned_im = rotate(grad_re[rows, :] + real, grad_im[rows, :] + imag, cosine, sine)
        return r * turned_re, r * turned_im, r * product

    real, imag, product = lax.fori_loop(0, steps, step, (zero, zero, zero + 1.0), unroll=4)
    cos_sub, sin_sub = turn_power(cosine, sine, steps.bit_length() - 1)
    last = LANES - 1
    total_re, total_im, total = real[last:], imag[last:], product[last:]
    for j in range(LANES - 2, -1, -1):
        turned_re, turned_im = rotate(total_re, total_im, cos_sub, sin_sub)
        total_re = product[j : j + 1] * turned_re + real[j : j + 1]
        total_im = product[j : j + 1] * turned_im + imag[j : j + 1]
        total = product[j : j + 1] * total
    summary[0:LANES] = real
    summary[LANES : 2 * LANES] = imag
    summary[2 * LANES : 3 * LANES] = product
    summary[24:32] = jnp.concatenate([total_re, total_im, total, zero[3:]], axis=0)


def whole_backward(
    retain, grad_re, grad_im, turn, summary, start, states, d_decay, d_in_re, d_in_im, d_phase
):
    steps = retain.shape[0] // LANES
    cosine, sine = turn[0:1], turn[1:2]
    cos_sub, sin_sub = turn_power(cosine, -sine, steps.bit_length() - 1)
    now_re, now_im = start[0:1], start[1:2]
    reals, imags = [now_re], [now_im]
    for j in range(LANES - 1, 0, -1):
        turned_re, turned_im = rotate(now_re, now_im, cos_sub, sin_sub)
        product = summary[2 * LANES + j : 2 * LANES + j + 1]
        now_re = product * turned_re + summary[j : j + 1]
        now_im = product * turned_im + summary[LANES + j : LANES + j + 1]
        reals.append(now_re)
        imags.append(now_im)
    zero = jnp.zeros((LANES, retain.shape[1]), jnp.float32)
    carry = (jnp.concatenate(reals[::-1], axis=0), jnp.concatenate(imags[::-1], axis=0), zero)

    def step(k, carry):
        real, imag, phase = carry
        rows = pl.ds(pl.multiple_of(LANES * (steps - 1 - k), LANES), LANES)
        r = retain[rows, :]
        real = grad_re[rows, :] + real
        imag = grad_im[rows, :] + imag
        prior_re, prior_im = rotate(states[0, rows, :], states[1, rows, :], cosine, sine)
        d_decay[rows, :] = -(real * prior_re + imag * prior_im)
        d_in_re[rows, :] = real
        d_in_im[rows, :] = imag
        phase = phase + r * (imag * prior_re - real * prior_im)
        turned_re, turned_im = rotate(real, imag, cosine, -sine)
        return r * turned_re, r * turned_im, phase

    _, _, phase = lax.fori_loop(0, steps, step, carry, unroll=4)
    d_phase[...] = jnp.sum(phase, axis=0, keepdims=True)


def stripe(rows):
    count, columns = rows.shape
    return rows.reshape(LANES, count // LANES, columns).swapaxes(0, 1).reshape(count, columns)


def unstripe(rows):
    count, columns = rows.shape
    return rows.reshape(count // LANES, LANES, columns).swapaxes(0, 1).reshape(count, columns)


def local_call(kernel, outs, *args):
    return pl.pallas_call(
        kernel,
        out_shape=[jax.ShapeDtypeStruct(shape, jnp.float32) for shape in outs],
        compiler_params=pltpu.CompilerParams(vmem_limit_bytes=32 * 1024 * 1024),
    )(*args)


def carry_chain(every, turn, me, length, reverse):
    sine = -turn[1:2] if reverse else turn[1:2]
    cosine, sine = turn_power(turn[0:1], sine, length.bit_length() - 1)
    count = every.shape[0]
    real = jnp.zeros_like(cosine)
    imag = jnp.zeros_like(cosine)
    for j in range(count - 1, 0, -1) if reverse else range(count - 1):
        use = (j > me) if reverse else (j < me)
        turned_re, turned_im = rotate(real, imag, cosine, sine)
        real = jnp.where(use, every[j, 2:3] * turned_re + every[j, 0:1], real)
        imag = jnp.where(use, every[j, 2:3] * turned_im + every[j, 1:2], imag)
    return jnp.concatenate([real, imag], axis=0)


def carry_in(summary, turn, length, reverse):
    every = lax.all_gather(summary[24:32], "dp", axis=0)
    return carry_chain(every, turn, lax.axis_index("dp"), length, reverse)


def normalize(values, gains):
    scaling = lax.rsqrt(jnp.mean(values * values, axis=-1, keepdims=True) + NORM_EPSILON)
    return (values * scaling * gains, scaling)


def normalize_back(values, scaling, gains, gradient):
    scaled = gradient * gains
    return scaling * scaled - values * scaling**3 * jnp.mean(
        values * scaled, axis=-1, keepdims=True
    )


def silu_slope(values):
    logistic = jax.nn.sigmoid(values)
    return logistic * (1.0 + values * (1.0 - logistic))


def adam_update(master, gradient, first, second, steps, decay):
    first_new = BETA_ONE * first + (1.0 - BETA_ONE) * gradient
    second_new = BETA_TWO * second + (1.0 - BETA_TWO) * gradient * gradient
    corrected = (
        first_new
        / (1.0 - BETA_ONE**steps)
        / (jnp.sqrt(second_new / (1.0 - BETA_TWO**steps)) + ADAM_EPSILON)
    )
    change = -LEARN_RATE * (corrected + decay * master)
    return (master + change, first_new, second_new, change)


MESH = pl.DeviceIdType.MESH
LOW = jnp.bfloat16
WIDE = jnp.float32
PLANES = 4
SIDE = 2
IN_ROWS = 24
OUT_ROWS = 72
MIX = CH + 2 * D
CHUNK = 512
CHUNKS = FF // CHUNK
OUT = 2
TILE = 128
OUTS = D // 2 // TILE
GLU = OUT + OUTS
VMEM_BYTES = 63 * 1024 * 1024
SLOTS = 512
ROWS = 64
RUN = SLOTS // LANES


class Piece:
    def __init__(self, matrix, rows, columns, starts, overlap=0):
        self.matrix, self.rows, self.columns = matrix, rows, columns
        self.starts, self.overlap = starts, overlap

    def shape(self):
        return (2, PLANES, SIDE, SIDE, 2 * self.rows, self.columns)


def piece_list():
    drive = (CH + D) // 2 + TILE // 2
    mix = [
        Piece("in", IN_ROWS, drive, (0, CH + D - drive), TILE),
        Piece("in", IN_ROWS, D // 2, (CH + D, MIX - D // 2)),
    ]
    out = [Piece("out", OUT_ROWS, TILE, (TILE * k, D // 2 + TILE * k)) for k in range(OUTS)]
    glu = [
        Piece("in", IN_ROWS, CHUNK, (MIX + CHUNK * k, MIX + FF + CHUNK * k)) for k in range(CHUNKS)
    ]
    return mix + out + glu


PIECES = piece_list()


class Place:
    def __init__(self):
        dp, rep = lax.axis_index("dp"), lax.axis_index("rep")
        self.z, self.x = dp // SIDE, dp % SIDE
        self.y, self.core = rep // 2, rep % 2

    def at(self, z, x, y, core):
        return (z * SIDE + x, y * 2 + core)

    def sibling(self):
        return self.at(self.z, self.x, self.y, 1 - self.core)

    def plane(self, z):
        return self.at(z, self.x, self.y, self.core)

    def near(self, core):
        if core == 0:
            return self.at(self.z, 1 - self.x, self.y, self.core)
        return self.at(self.z, self.x, 1 - self.y, self.core)

    def far(self, core):
        return self.near(1 - core)

    def away(self):
        return self.z % 2 + 1, (3 * self.z + 2) % 5, 3 - 3 * (self.z // 2)

    def when_inner(self, run):
        pl.when((self.z + 1) // 2 == 1)(run)

    def when_end(self, run):
        pl.when((self.z + 1) // 2 != 1)(run)

    def turn(self, step):
        return lax.rem(self.z + step, PLANES)

    def sides(self, core):
        return (self.x, self.y) if core == 0 else (self.y, self.x)

    def by_core(self, run):
        for core in range(2):
            pl.when(self.core == core)(functools.partial(run, core))

    def greet(self):
        barrier = pltpu.get_barrier_semaphore()
        partners = [self.sibling(), self.near(0), self.near(1)]
        for step in (1, 2, 3):
            partners.append(self.plane(self.turn(step)))
            partners.append(self.at(self.turn(step), 1 - self.x, self.y, self.core))
        for partner in partners:
            pl.semaphore_signal(barrier, inc=1, device_id=partner, device_id_type=MESH)
        return lambda: pl.semaphore_wait(barrier, len(partners))


def always(run):
    run()


def block_of(ref, core, z, near, far):
    return ref.at[core, z, near, far] if core == 0 else ref.at[core, z, far, near]


def pair_of(ref, core, z, far):
    return ref.at[core, z, :, far] if core == 0 else ref.at[core, z, far]


def remote(source, target, sent, received, device):
    return pltpu.make_async_remote_copy(
        src_ref=source,
        dst_ref=target,
        send_sem=sent,
        recv_sem=received,
        device_id=device,
        device_id_type=MESH,
    )


GATHER_NEAR_FIRST = (4, 6, 7)
REDUCE_NEAR_LAST = (2, 3, 6, 7)
GATHER_RELAYED = (0, 1, 2, 3, 4, 5)
REDUCE_RELAYED = (0, 1, 3, 4, 5, 6, 7)


class Gather:
    def __init__(self, place, masters, buffers, staging, sems):
        self.place, self.masters, self.buffers, self.staging = place, masters, buffers, staging
        self.local, self.sent0, self.got0 = sems[:3]
        self.z_sent, self.near_sent, self.far_sent, self.chip_sent, self.chip_got = sems[3:8]
        self.z_got, self.near_got, self.far_got = sems[8:]

    @staticmethod
    def scratch():
        n = len(PIECES)
        dma = pltpu.SemaphoreType.DMA
        return (
            [pltpu.VMEM(p.shape(), LOW) for p in PIECES]
            + [pltpu.VMEM((2 * p.rows, p.columns), WIDE) for p in PIECES]
            + [dma((n,))] * 8
            + [dma((n, PLANES))] * 3
        )

    def part(self, p, half):
        piece = PIECES[p]
        start = piece.starts[0] + half * (piece.starts[1] - piece.starts[0])
        return self.masters[piece.matrix].at[:, pl.ds(pl.multiple_of(start, TILE), piece.columns)]

    def own_rows(self, p):
        rows = PIECES[p].rows
        return self.staging[p].at[pl.ds(pl.multiple_of(self.place.core * rows, 8), rows)]

    def to_sibling(self, p):
        return remote(
            self.part(p, 1 - self.place.core),
            self.own_rows(p),
            self.sent0.at[p],
            self.got0.at[p],
            self.place.sibling(),
        )

    def to_self(self, p):
        return pltpu.make_async_copy(
            self.part(p, self.place.core), self.own_rows(p), self.local.at[p]
        )

    def along_z(self, p, z, target, core):
        place = self.place
        near, far = place.sides(core)
        if p in GATHER_NEAR_FIRST:
            part = pair_of(self.buffers[p], core, z, far)
        else:
            part = block_of(self.buffers[p], core, z, near, far)
        sems = self.z_sent.at[p], self.z_got.at[p, z]
        return remote(part, part, *sems, place.plane(target))

    def relay(self, p, core):
        place = self.place
        last = place.away()[2]
        return self.along_z(p, last, 3 - last, core)

    def along_near(self, p, z, core):
        block = block_of(self.buffers[p], core, z, *self.place.sides(core))
        return remote(
            block, block, self.near_sent.at[p], self.near_got.at[p, z], self.place.near(core)
        )

    def along_far(self, p, z, core):
        pair = pair_of(self.buffers[p], core, z, self.place.sides(core)[1])
        return remote(
            pair, pair, self.far_sent.at[p], self.far_got.at[p, z], self.place.far(core)
        )

    def in_chip(self, p, planes, core):
        part = self.buffers[p].at[core, planes]
        return remote(
            part, part, self.chip_sent.at[p], self.chip_got.at[p], self.place.sibling()
        )

    def begin(self):
        for p in range(len(PIECES)):
            self.to_sibling(p).start()
            self.to_self(p).start()


    def near_own(self, p):
        place = self.place
        self.to_self(p).wait()
        self.to_sibling(p).wait_recv()
        self.buffers[p][place.core, place.z, place.x, place.y] = self.staging[p][...].astype(LOW)
        place.by_core(lambda core: self.along_near(p, place.z, core).start())

    def z_targets(self, p):
        first, second, third = self.place.away()
        relayed = self.place.when_inner if p in GATHER_RELAYED else always
        return (first, always), (second, always), (third, relayed)

    def z_own(self, p):
        place = self.place

        def run(core):
            for z, when in self.z_targets(p):
                when(lambda: self.along_z(p, place.z, z, core).start())

        place.by_core(run)

    def from_z(self, p, index, core):
        place = self.place
        z = place.away()[index]
        self.along_z(p, z, place.z, core).wait_recv()
        if index == 2 and p in GATHER_RELAYED:
            place.when_inner(lambda: self.relay(p, core).start())
        return z

    def far_own(self, p):
        place = self.place

        def run(core):
            self.along_near(p, place.z, core).wait_recv()
            self.along_far(p, place.z, core).start()

        place.by_core(run)

    def near(self, p, *indices):
        place = self.place

        def run(core):
            for index in indices or range(3):
                z = self.from_z(p, index, core)
                self.along_near(p, z, core).start()

        if p not in GATHER_NEAR_FIRST:
            place.by_core(run)

    def far(self, p, *indices):
        place = self.place

        def run(core):
            for index in indices or range(3):
                z = place.away()[index]
                if p in GATHER_NEAR_FIRST:
                    self.from_z(p, index, core)
                else:
                    self.along_near(p, z, core).wait_recv()
                self.along_far(p, z, core).start()

        place.by_core(run)

    def chip(self, p, *indices):
        def run(core):
            for index in indices or range(4):
                z = (self.place.z, *self.place.away())[index]
                self.along_far(p, z, core).wait_recv()
                self.in_chip(p, z, core).start()

        self.place.by_core(run)

    def arrive(self, p):
        self.in_chip(p, pl.ds(0, PLANES), 1 - self.place.core).wait_recv()

    def drain(self, p):
        place, ref = self.place, self.buffers[p]
        self.to_sibling(p).wait_send()

        def sent(part, sem):
            remote(part, part, sem.at[p], sem.at[p], place.sibling()).wait_send()

        def run(core):
            def sent_z(count):
                planes = pl.ds(0, count)
                near_first = p in GATHER_NEAR_FIRST
                part = ref.at[core, planes, :, 0] if near_first else ref.at[core, planes, 0, 0]
                sent(part, self.z_sent)

            if p in GATHER_RELAYED:
                place.when_inner(lambda: sent_z(4))
                place.when_end(lambda: sent_z(2))
            else:
                sent_z(3)
            sent(ref.at[core, pl.ds(0, 1 if p in GATHER_NEAR_FIRST else 4), 0, 0], self.near_sent)
            sent(ref.at[core, :, :, 0], self.far_sent)
            sent(ref.at[core], self.chip_sent)

        place.by_core(run)


class Reduce:
    def __init__(self, place, grads, refs, results):
        n = len(PIECES)
        self.place, self.grads, self.results = place, grads, results
        self.far_got, self.near_got, self.planes, self.final = (refs[k * n : (k + 1) * n] for k in range(4))
        self.far_sem, self.near_sem, self.z_sem = refs[4 * n : 4 * n + 3]
        self.far_sent, self.near_sent, self.z_sent = refs[4 * n + 3 : 4 * n + 6]
        self.chip_sent, self.chip_got = refs[4 * n + 6 :]

    @staticmethod
    def scratch():
        n = len(PIECES)
        dma = pltpu.SemaphoreType.DMA
        blocks = [p.shape()[4:] for p in PIECES]
        return (
            [pltpu.VMEM((PLANES, SIDE) + s, LOW) for s in blocks]
            + [pltpu.VMEM((PLANES,) + s, LOW) for s in blocks]
            + [
                pltpu.VMEM((PLANES,) + (SIDE,) * (p in REDUCE_NEAR_LAST) + s, LOW)
                for p, s in enumerate(blocks)
            ]
            + [pltpu.VMEM(s, WIDE) for s in blocks]
            + [dma((n, PLANES))] * 3
            + [dma((n,))] * 5
        )

    def block(self, p, z, near, far, core):
        return self.grads[p].at[z, near, far] if core == 0 else self.grads[p].at[z, far, near]

    def pair(self, p, z, far, core):
        return self.grads[p].at[z, :, far] if core == 0 else self.grads[p].at[z, far]

    def along_far(self, p, z, core):
        return remote(
            self.pair(p, z, 1 - self.place.sides(core)[1], core),
            self.far_got[p].at[z],
            self.far_sent.at[p],
            self.far_sem.at[p, z],
            self.place.far(core),
        )

    def along_near(self, p, z, core):
        near, far = self.place.sides(core)
        return remote(
            self.block(p, z, 1 - near, far, core),
            self.near_got[p].at[z],
            self.near_sent.at[p],
            self.near_sem.at[p, z],
            self.place.near(core),
        )

    def order(self):
        first, second, third = self.place.away()
        inner = (self.place.z + 1) // 2 % 2
        return (
            inner * first + (1 - inner) * third,
            second,
            inner * third + (1 - inner) * first,
            self.place.z,
        )

    def z_part(self, p, z, core):
        near, far = self.place.sides(core)
        if p in REDUCE_NEAR_LAST:
            return self.pair(p, z, far, core)
        return self.block(p, z, near, far, core)

    def along_z(self, p, z, sender, core):
        sems = self.z_sent.at[p], self.z_sem.at[p, sender]
        target = self.planes[p].at[sender]
        return remote(self.z_part(p, z, core), target, *sems, self.place.plane(z))

    def to_relay(self, p, core, slot):
        first, _, third = self.place.away()
        sems = self.z_sent.at[p], self.z_sem.at[p, slot]
        target = self.planes[p].at[slot]
        return remote(self.z_part(p, third, core), target, *sems, self.place.plane(first))

    def send_z(self, p, core, index):
        place = self.place
        z = self.order()[index]
        if index == 1:
            self.along_z(p, z, place.z, core).start()
        elif p not in REDUCE_RELAYED:
            if index != 3:
                self.along_z(p, z, place.z, core).start()
        elif index == 0:
            place.when_inner(lambda: self.along_z(p, z, place.z, core).start())
            place.when_end(lambda: self.to_relay(p, core, place.away()[0]).start())
        elif index == 2:

            def pass_on():
                self.to_relay(p, core, place.z).wait_recv()
                self.add(self.z_part(p, z, core), self.planes[p].at[place.z])

            place.when_inner(pass_on)
            self.along_z(p, z, place.z, core).start()

    def sum_planes(self, p, core, result):
        place = self.place
        first, second, third = place.away()
        for z in (first, second):
            self.along_z(p, place.z, z, core).wait_recv()
        total = self.z_part(p, place.z, core)[...].astype(WIDE)
        total = total + self.planes[p][first].astype(WIDE) + self.planes[p][second].astype(WIDE)

        def inner():
            self.along_z(p, place.z, third, core).wait_recv()
            result[...] = (total + self.planes[p][third].astype(WIDE)).astype(result.dtype)

        def end():
            result[...] = total.astype(result.dtype)

        if p in REDUCE_RELAYED:
            place.when_inner(inner)
            place.when_end(end)
        else:
            inner()

    def result(self, p, core):
        piece = PIECES[p]
        skip = piece.overlap * core
        start, width = piece.starts[core] + skip, piece.columns - skip
        return self.results[piece.matrix].at[:, pl.ds(start, width)], pl.ds(skip, width)

    def to_sibling(self, p, core):
        rows = PIECES[p].rows
        target, columns = self.result(p, core)
        return remote(
            self.final[p].at[pl.ds(rows * (1 - core), rows), columns],
            target,
            self.chip_sent.at[p],
            self.chip_got.at[p],
            self.place.sibling(),
        )

    @staticmethod
    def add(target, source):
        target[...] = (target[...].astype(WIDE) + source[...].astype(WIDE)).astype(LOW)

    def far(self, p):
        def run(core):
            for z in self.order():
                self.along_far(p, z, core).start()

        self.place.by_core(run)

    def after_far(self, p, *indices):
        def run(core):
            for index in indices or range(4):
                z = self.order()[index]
                self.along_far(p, z, core).wait_recv()
                self.add(self.pair(p, z, self.place.sides(core)[1], core), self.far_got[p].at[z])
                if p in REDUCE_NEAR_LAST:
                    self.send_z(p, core, index)
                else:
                    self.along_near(p, z, core).start()

        self.place.by_core(run)

    def after_near(self, p, *indices):
        place = self.place

        def run(core):
            near, far = place.sides(core)
            if p in REDUCE_NEAR_LAST:
                self.sum_planes(p, core, self.pair(p, place.z, far, core))
                self.along_near(p, place.z, core).start()
                return
            for index in indices or range(4):
                z = self.order()[index]
                self.along_near(p, z, core).wait_recv()
                self.add(self.block(p, z, near, far, core), self.near_got[p].at[z])
                self.send_z(p, core, index)

        place.by_core(run)

    def finish(self, p):
        rows, place = PIECES[p].rows, self.place

        def run(core):
            near, far = place.sides(core)
            if p in REDUCE_NEAR_LAST:
                self.along_near(p, place.z, core).wait_recv()
                own = self.block(p, place.z, near, far, core)[...].astype(WIDE)
                self.final[p][...] = own + self.near_got[p][place.z].astype(WIDE)
            else:
                self.sum_planes(p, core, self.final[p])
            self.to_sibling(p, core).start()
            target, columns = self.result(p, core)
            target[...] = self.final[p][pl.ds(rows * core, rows), columns]

        place.by_core(run)

    def drain(self, p):
        place = self.place

        def sent(part, sem):
            remote(part, part, sem.at[p], sem.at[p], place.sibling()).wait_send()

        def run(core):
            self.to_sibling(p, 1 - core).wait_recv()
            self.to_sibling(p, core).wait_send()

        place.by_core(run)
        sent(self.far_got[p], self.far_sent)
        sent(self.near_got[p].at[pl.ds(0, 1 if p in REDUCE_NEAR_LAST else 4)], self.near_sent)
        sent(self.planes[p].at[pl.ds(0, 3)], self.z_sent)


def tiled(column, count):
    return jnp.concatenate([column] * count, axis=1)


def each_block(run, size=ROWS):
    def block(i, carry):
        run(pl.ds(pl.multiple_of(i * size, size), size))
        return carry

    lax.fori_loop(0, SLOTS // size, block, 0)


def inner(left, right, dims=((1,), (0,))):
    return lax.dot_general(left, right, (dims, ((), ())), preferred_element_type=WIDE)


def across(left, right):
    return inner(left, right, ((1,), (1,)))


def along(left, right):
    return inner(left, right, ((0,), (0,)))


def out_segments(start, count):
    size, runs, stop = 2 * OUT_ROWS, [], start + count
    while start < stop:
        chip, first = divmod(start, size)
        last = min(size, first + stop - start)
        runs.append((chip // 4, chip // 2 % 2, chip % 2, first, last))
        start += last - first
    return runs


def row_norm(values):
    return lax.rsqrt(jnp.mean(values * values, axis=1, keepdims=True) + NORM_EPSILON)


def eights(values):
    return jnp.sum(values.reshape(values.shape[0] // 8, 8, values.shape[1]), axis=0)


def block_scratch():
    vmem, dma = pltpu.VMEM, pltpu.SemaphoreType.DMA
    rows = (SLOTS, D)
    both = (2 * SLOTS, D)
    return dict(
        arrivals=dma((2,)),
        departures=dma((2,)),
        perm=vmem((SLOTS, SLOTS), LOW),
        live=vmem((SLOTS, TILE), WIDE),
        opens=vmem((SLOTS, TILE), WIDE),
        params=vmem((8, D), WIDE),
        tokens=vmem(rows, LOW),
        upstream=vmem((2, SLOTS, D // 2), LOW),
        upstream_got=vmem((SLOTS, D // 2), LOW),
        normed=vmem(both, LOW),
        normed_two=vmem(both, LOW),
        gated=vmem(both, LOW),
        hidden=vmem((CHUNKS, 2 * SLOTS, CHUNK), LOW),
        d_glu=vmem((CHUNKS, 2, SLOTS, CHUNK), LOW),
        d_glu_got=vmem((CHUNKS, SLOTS, CHUNK), LOW),
        d_out=vmem((2, SLOTS, D // 2), LOW),
        d_out_got=vmem((SLOTS, D // 2), LOW),
        d_drive=vmem((2, SLOTS, PIECES[0].columns), LOW),
        d_drive_got=vmem((SLOTS, PIECES[0].columns), LOW),
        d_gate=vmem((2, SLOTS, PIECES[1].columns), LOW),
        d_gate_got=vmem((SLOTS, PIECES[1].columns), LOW),
        pre_mix=vmem((SLOTS, MIX), WIDE),
        retain=vmem((SLOTS, CH), WIDE),
        drive=vmem(rows, WIDE),
        states=vmem((2, SLOTS + LANES, CH), WIDE),
        summaries=vmem((2, 32, CH), WIDE),
        every=vmem((2, PLANES * SIDE, 8, CH), WIDE),
        middle=vmem(rows, WIDE),
        d_normed=vmem(rows, WIDE),
        total=vmem(rows, WIDE),
        block_out=vmem(rows, LOW),
        sums=vmem((3, 8, D), WIDE),
        vector=vmem((8, VEC_ROWS, TILE), WIDE),
        pair_sent=dma((PAIRS,)),
        pair_got=dma((PAIRS,)),
        carry_sent=dma((2,)),
        carry_got=dma((2,)),
        vector_sent=dma((6,)),
        vector_got=dma((6,)),
    )


VEC_ROWS = 24
VEC_COUNT = 18
PAIRS = 13


class Block:
    def __init__(self, place, buffers, grads, refs):
        self.place, self.weights, self.grads = place, buffers, grads
        for name, ref in refs.items():
            setattr(self, name, ref)
        self.me = place.z * SIDE + place.x


    def swaps(self):
        own, got = pl.ds(0, SLOTS), pl.ds(SLOTS, SLOTS)
        other = 1 - self.place.core
        pairs = dict(
            normed=(self.normed.at[own], self.normed.at[got]),
            normed_two=(self.normed_two.at[own], self.normed_two.at[got]),
            gated=(self.gated.at[own], self.gated.at[got]),
            upstream=(self.upstream.at[other], self.upstream_got),
            d_out=(self.d_out.at[other], self.d_out_got),
            d_drive=(self.d_drive.at[other], self.d_drive_got),
            d_gate=(self.d_gate.at[other], self.d_gate_got),
        )
        for k in range(CHUNKS):
            pairs["hidden", k] = (self.hidden.at[k, own], self.hidden.at[k, got])
            pairs["d_glu", k] = (self.d_glu.at[k, other], self.d_glu_got.at[k])
        return pairs

    def swap(self, name):
        pairs = self.swaps()
        slot = list(pairs).index(name)
        sems = self.pair_sent.at[slot], self.pair_got.at[slot]
        return remote(*pairs[name], *sems, self.place.sibling())

    def give(self, *names):
        for name in names:
            self.swap(name).start()

    def take(self, *names):
        for name in names:
            self.swap(name).wait_recv()

    def settle(self):
        for name in self.swaps():
            self.swap(name).wait_send()


    def mix_weight(self, half, m):
        return self.weights[m][half].reshape(D, PIECES[m].columns)

    def glu_weight(self, k):
        parts = [self.weights[GLU + k][half].reshape(D, CHUNK) for half in range(2)]
        return jnp.concatenate(parts, axis=1)

    def out_weight(self, start, count):
        columns = []
        for half in range(2):
            for p in range(OUT, GLU):
                ref = self.weights[p]
                runs = out_segments(start, count)
                parts = [ref[half, z, x, y, first:last] for z, x, y, first, last in runs]
                columns.append(jnp.concatenate(parts, axis=0))
        return jnp.concatenate(columns, axis=1)

    def put_in(self, p, value):
        self.grads[p][...] = value.astype(LOW).reshape(self.grads[p].shape)

    def put_out(self, start, value):
        value, done = value.astype(LOW), 0
        for z, x, y, first, last in out_segments(start, value.shape[0]):
            count = last - first
            for k in range(OUTS):
                part = value[done : done + count, k * TILE : (k + 1) * TILE]
                self.grads[OUT + k][z, x, y, first:last] = part
            done += count


    def prepare(self, padding, opening, vectors):
        row = lax.broadcasted_iota(jnp.int32, (SLOTS, SLOTS), 0)
        column = lax.broadcasted_iota(jnp.int32, (SLOTS, SLOTS), 1)
        perm = (column == row % LANES * RUN + row // LANES).astype(WIDE)
        self.perm[...] = perm.astype(LOW)
        ones = jnp.ones((SLOTS, TILE), LOW)
        self.live[...] = inner((perm * padding[...].astype(WIDE)).astype(LOW), ones)
        self.opens[...] = inner((perm * opening[...].astype(WIDE)).astype(LOW), ones)

        def line(first, count):
            return jnp.concatenate([vectors[first + i : first + i + 1] for i in range(count)], axis=1)

        phase = line(12, 3)
        self.params[0:1] = line(0, 6)
        self.params[1:2] = line(6, 6)
        self.params[2:3] = jnp.concatenate([jnp.cos(phase), jnp.sin(phase)], axis=1)
        self.params[3:4] = jnp.concatenate([line(15, 3)] * 2, axis=1)
        self.sums[...] = jnp.zeros_like(self.sums)

    def turn(self):
        return jnp.concatenate([self.params[2:3, :CH], self.params[2:3, CH:]], axis=0)

    def first_norm(self, raw):
        values = inner(self.perm[...], raw[...])
        self.tokens[...] = values.astype(LOW)
        self.normed[0:SLOTS] = (values * row_norm(values) * self.params[0:1]).astype(LOW)

    def mask_upstream(self, raw):
        striped = inner(self.perm[...], raw[...]) * tiled(self.live[...], D // TILE)
        self.upstream[0] = striped[:, : D // 2].astype(LOW)
        self.upstream[1] = striped[:, D // 2 :].astype(LOW)

    def mix(self, m):
        piece = PIECES[m]
        weight = (self.mix_weight(0, m), self.mix_weight(1, m)[:, piece.overlap :])
        weight = jnp.concatenate(weight, axis=1)
        start = piece.starts[0]
        self.pre_mix[:, start : start + weight.shape[1]] = inner(self.normed[0:SLOTS], weight)

    def drives(self):
        forget = jax.nn.sigmoid(-(self.pre_mix[:, :CH] + self.params[3:4, :CH]))
        pre = self.pre_mix[:, CH : CH + D]
        driver = pre * jax.nn.sigmoid(pre)
        opens = tiled(self.opens[...], CH // TILE)
        decay = jnp.where(opens > 0.5, 1.0, forget).astype(LOW).astype(WIDE)
        self.retain[...] = 1.0 - decay
        drive = jnp.concatenate([forget, forget], axis=1) * driver
        self.drive[...] = drive.astype(LOW).astype(WIDE)

    def parts(self):
        return self.drive.at[:, pl.ds(0, CH)], self.drive.at[:, pl.ds(CH, CH)]

    def others(self):
        place = self.place
        for step in range(PLANES):
            for flip in range(SIDE):
                if step or flip:
                    z = place.turn(step)
                    x = 1 - place.x if flip else place.x
                    yield place.at(z, x, place.y, place.core)

    def carry_copy(self, way, device):
        return remote(
            self.summaries.at[way, pl.ds(24, 8)],
            self.every.at[way, self.me],
            self.carry_sent.at[way],
            self.carry_got.at[way],
            device,
        )

    def all_carries(self, way):
        part = self.every.at[way, pl.ds(0, PLANES * SIDE - 1)]
        sems = self.carry_sent.at[way], self.carry_got.at[way]
        return remote(part, part, *sems, self.place.sibling())

    def scan_own(self, way):
        run = local_backward if way else local_forward
        run(self.retain, *self.parts(), self.turn(), self.summaries.at[way])
        self.every[way, self.me] = self.summaries[way, 24:32]
        for device in self.others():
            self.carry_copy(way, device).start()

    def carried(self, way):
        self.all_carries(way).wait_recv()
        turn = self.turn()
        return carry_chain(self.every.at[way], turn, self.me, SLOTS, way == 1)

    def scan_states(self):
        start = self.carried(0)
        run = whole_forward
        run(self.retain, *self.parts(), self.turn(), self.summaries.at[0], start, self.states)

    def recurrent(self):
        both = jnp.concatenate([self.states[0, LANES:], self.states[1, LANES:]], axis=1)
        return both.astype(LOW).astype(WIDE)

    def gate_rows(self):
        pre = self.pre_mix[:, CH + D :]
        masked = self.recurrent() * tiled(self.live[...], D // TILE)
        self.gated[0:SLOTS] = (masked * (pre * jax.nn.sigmoid(pre))).astype(LOW)

    def second_norm(self):
        mixed = inner(self.gated[0:SLOTS], self.out_weight(0, D))
        middle = self.tokens[...].astype(WIDE) + mixed
        self.middle[...] = middle
        self.total[...] = middle
        self.normed_two[0:SLOTS] = (middle * row_norm(middle) * self.params[1:2]).astype(LOW)

    def whole_upstream(self):
        return jnp.concatenate([self.upstream[0], self.upstream[1]], axis=1)

    def glu_forward(self, k):
        pre = inner(self.normed_two[0:SLOTS], self.glu_weight(k))
        gate, up = pre[:, :CHUNK], pre[:, CHUNK:]
        d_hidden = across(self.whole_upstream(), self.out_weight(D + CHUNK * k, CHUNK))
        logistic = jax.nn.sigmoid(gate)
        active = gate * logistic
        slope = logistic * (1.0 + gate * (1.0 - logistic))
        self.hidden[k, 0:SLOTS] = (active * up).astype(LOW)
        self.d_glu[k, 0] = (d_hidden * up * slope).astype(LOW)
        self.d_glu[k, 1] = (d_hidden * active).astype(LOW)

    def glu_back(self, k):
        d_glu = jnp.concatenate([self.d_glu[k, 0], self.d_glu[k, 1]], axis=1)
        d_share = across(d_glu, self.glu_weight(k))
        self.d_normed[...] = d_share if k == 0 else self.d_normed[...] + d_share

    def own_half(self, ref, got):
        return jnp.concatenate([ref[self.place.core], got], axis=0)

    def glu_grads(self, k):
        d_glu = jnp.concatenate([self.d_glu[k, self.place.core], self.d_glu_got[k]], axis=0)
        self.put_in(GLU + k, along(self.normed_two[...], d_glu))
        upstream = self.own_half(self.upstream, self.upstream_got[...])
        self.put_out(D + CHUNK * k, along(self.hidden[k], upstream))

    def add_sum(self, index, values):
        self.sums[index] += eights(values)

    def middle_back(self):
        middle, d_normed = self.middle[...], self.d_normed[...]
        scaling = row_norm(middle)
        self.add_sum(1, d_normed * middle * scaling)
        scaled = d_normed * self.params[1:2]
        mean = jnp.mean(middle * scaled, axis=1, keepdims=True)
        upstream = self.whole_upstream().astype(WIDE)
        d_middle = upstream + scaling * scaled - middle * (scaling**3 * mean)
        self.middle[...] = d_middle
        self.d_out[0] = d_middle[:, : D // 2].astype(LOW)
        self.d_out[1] = d_middle[:, D // 2 :].astype(LOW)

    def gate_back(self):
        d_out = jnp.concatenate([self.d_out[0], self.d_out[1]], axis=1)
        d_gated = across(d_out, self.out_weight(0, D))
        pre = self.pre_mix[:, CH + D :]
        logistic = jax.nn.sigmoid(pre)
        d_live = d_gated * tiled(self.live[...], D // TILE)
        self.drive[...] = (d_live * (pre * logistic)).astype(LOW).astype(WIDE)
        slope = logistic * (1.0 + pre * (1.0 - logistic))
        d_gate = (d_live * self.recurrent() * slope).astype(LOW)
        self.d_gate[0] = d_gate[:, : D // 2]
        self.d_gate[1] = d_gate[:, D // 2 :]

    def mixer_out_grad(self):
        d_out = self.own_half(self.d_out, self.d_out_got[...])
        self.put_out(0, along(self.gated[...], d_out))

    def scan_back(self):
        start = self.carried(1)
        real, imag = self.parts()
        whole_backward(
            self.retain,
            real,
            imag,
            self.turn(),
            self.summaries.at[1],
            start,
            self.states,
            self.retain,
            real,
            imag,
            self.sums.at[2, pl.ds(0, 1), pl.ds(0, CH)],
        )

    def drives_back(self):
        def run(rows):
            forget = jax.nn.sigmoid(-(self.pre_mix[rows, :CH] + self.params[3:4, :CH]))
            pre = self.pre_mix[rows, CH : CH + D]
            logistic = jax.nn.sigmoid(pre)
            d_decay = self.retain[rows, :].astype(LOW).astype(WIDE)
            d_input = self.drive[rows, :].astype(LOW).astype(WIDE)
            pulled = d_input * (pre * logistic)
            opens = tiled(self.opens[rows, :], CH // TILE)
            d_forget = jnp.where(opens > 0.5, 0.0, d_decay) + pulled[:, :CH] + pulled[:, CH:]
            d_first = -forget * (1.0 - forget) * d_forget
            self.sums[2, :, CH:] += eights(d_first)
            slope = logistic * (1.0 + pre * (1.0 - logistic))
            d_driver = d_input * jnp.concatenate([forget, forget], axis=1) * slope
            d_pre = jnp.concatenate([d_first, d_driver], axis=1).astype(LOW)
            piece = PIECES[0]
            for half, start in enumerate(piece.starts):
                self.d_drive[half, rows, :] = d_pre[:, start : start + piece.columns]

        each_block(run)

    def mix_grads(self, m):
        own, got = ((self.d_drive, self.d_drive_got), (self.d_gate, self.d_gate_got))[m]
        self.put_in(m, along(self.normed[...], self.own_half(own, got[...])))

    def gate_normed(self):
        left = jnp.concatenate([self.d_gate[0], self.d_gate[1]], axis=1)
        right = jnp.concatenate([self.mix_weight(0, 1), self.mix_weight(1, 1)], axis=1)
        self.d_normed[...] = across(left, right)

    def first_back(self):
        skip = PIECES[0].overlap
        left = jnp.concatenate([self.d_drive[0], self.d_drive[1][:, skip:]], axis=1)
        right = jnp.concatenate([self.mix_weight(0, 0), self.mix_weight(1, 0)[:, skip:]], axis=1)
        d_normed = self.d_normed[...] + across(left, right)
        values = self.tokens[...].astype(WIDE)
        scaling = row_norm(values)
        self.add_sum(0, d_normed * values * scaling)
        scaled = d_normed * self.params[0:1]
        mean = jnp.mean(values * scaled, axis=1, keepdims=True)
        self.middle[...] += scaling * scaled - values * (scaling**3 * mean)

    def natural_out(self):
        hidden = jnp.concatenate([self.hidden[k, 0:SLOTS] for k in range(CHUNKS)], axis=1)
        total = self.total[...] + inner(hidden, self.out_weight(D, FF))
        self.block_out[...] = along(self.perm[...], total.astype(LOW)).astype(LOW)

    def natural_tokens(self):
        rest = self.middle[...]
        total = jnp.zeros_like(rest)
        for _ in range(3):
            part = rest.astype(LOW)
            total = total + along(self.perm[...], part)
            rest = rest - part.astype(WIDE)
        self.d_normed[...] = total


    def gather_vector(self):
        lines = [
            jnp.sum(self.sums[0], axis=0, keepdims=True),
            jnp.sum(self.sums[1], axis=0, keepdims=True),
            jnp.concatenate(
                [self.sums[2, 0:1, :CH], jnp.sum(self.sums[2, :, CH:], axis=0, keepdims=True)], axis=1
            ),
        ]
        for i, line in enumerate(lines):
            for j in range(D // TILE):
                row = i * (D // TILE) + j
                self.vector[0, row : row + 1] = line[:, j * TILE : (j + 1) * TILE]
        filled = jnp.sum(self.live[...], axis=0, keepdims=True)
        rest = jnp.zeros((VEC_ROWS - VEC_COUNT - 1, TILE), WIDE)
        self.vector[0, VEC_COUNT:] = jnp.concatenate([filled, rest], axis=0)

    def vector_copy(self, stage):
        place = self.place
        device = (place.sibling(), place.near(0), place.near(1))[stage]
        source = self.vector.at[stage]
        target = self.vector.at[4 + stage]
        return remote(source, target, self.vector_sent.at[stage], self.vector_got.at[stage], device)

    def vector_step(self, stage):
        if stage:
            self.vector_copy(stage - 1).wait_recv()
            self.vector[stage] = self.vector[stage - 1] + self.vector[3 + stage]
        if stage < 3:
            self.vector_copy(stage).start()

    def vector_plane(self, planes, step, sender):
        place = self.place
        return remote(
            self.vector.at[3],
            planes.at[sender],
            self.vector_sent.at[2 + step],
            self.vector_got.at[2 + step],
            place.plane(place.turn(step)),
        )


def block_kernel(tokens, cotangent, padding, opening, w_in, w_out, vectors, *refs):
    n = len(PIECES)
    block_out, d_tokens, sum_in, sum_out, planes = refs[:5]
    refs = refs[5:]
    count = len(Gather.scratch())
    gather_refs, refs = refs[:count], refs[count:]
    buffers, staging, gather_sems = gather_refs[:n], gather_refs[n : 2 * n], gather_refs[2 * n :]
    grads, refs = refs[:n], refs[n:]
    count = len(Reduce.scratch())
    reduce_refs, refs = refs[:count], refs[count:]
    place = Place()
    gather = Gather(place, {"in": w_in, "out": w_out}, buffers, staging, gather_sems)
    reduce = Reduce(place, grads, reduce_refs, {"in": sum_in, "out": sum_out})
    block = Block(place, buffers, grads, dict(zip(block_scratch(), refs, strict=True)))

    entered = place.greet()
    raw_tokens, raw_upstream = block.gated.at[pl.ds(0, SLOTS)], block.block_out
    loads = [
        pltpu.make_async_copy(tokens.at[0], raw_tokens, block.arrivals.at[0]),
        pltpu.make_async_copy(cotangent.at[0], raw_upstream, block.arrivals.at[1]),
    ]
    leave_out = pltpu.make_async_copy(block.block_out, block_out, block.departures.at[0])
    leave_tokens = pltpu.make_async_copy(block.d_normed, d_tokens, block.departures.at[1])
    for load in loads:
        load.start()
    block.prepare(padding, opening, vectors)
    entered()
    gather.begin()
    gather.near_own(0)
    gather.z_own(0)
    gather.near_own(3)
    gather.near_own(1)
    gather.near_own(2)
    gather.near_own(6)
    gather.near_own(4)
    gather.z_own(1)
    gather.z_own(2)
    loads[0].wait()
    block.first_norm(raw_tokens)
    gather.near_own(7)
    gather.near_own(5)
    gather.far_own(0)
    gather.far_own(3)
    gather.z_own(3)
    gather.far_own(2)
    gather.near(0, 1)
    gather.z_own(5)
    loads[1].wait()
    block.mask_upstream(raw_upstream)
    gather.near(1, 0)
    gather.near(0, 0)
    block.give("normed")
    gather.far_own(7)
    gather.far_own(5)
    gather.far_own(4)
    gather.far_own(6)
    gather.near(0, 2)
    gather.far(0, 1)
    gather.near(1, 2)
    gather.near(2, 0)
    gather.z_own(4)
    gather.near(3, 0)
    gather.far(0, 0)
    gather.far(1, 0)
    gather.near(3, 1)
    gather.near(5, 0)
    gather.near(2, 1)
    gather.chip(2, 0)
    gather.far(0, 2)
    gather.far(1, 2)
    gather.near(3, 2)
    gather.z_own(6)
    gather.chip(6, 0)
    gather.far(5, 0)
    gather.near(1, 1)
    gather.near(2, 2)
    gather.far(3, 2)
    gather.chip(0, 0)
    gather.far_own(1)
    gather.far(2, 0)
    gather.near(5, 2)
    gather.far(4, 1)
    gather.far(1, 1)
    gather.far(4, 2)
    gather.chip(7, 0)
    gather.chip(0, 3)
    gather.z_own(7)
    gather.chip(1, 0)
    gather.near(5, 1)
    gather.chip(0, 1)
    gather.far(3, 0)
    gather.chip(4, 0)
    gather.far(2, 1)
    gather.chip(0, 2)
    gather.far(3, 1)
    gather.chip(1, 3)
    gather.far(6, 1)
    gather.arrive(0)
    gather.far(2, 2)
    gather.chip(4, 2)
    gather.chip(1, 2)
    block.take("normed")
    block.give("upstream")
    gather.far(5, 1, 2)
    block.mix(0)
    gather.chip(5, 1)
    gather.chip(3, 2)
    gather.chip(2, 1)
    gather.chip(3, 0, 1)
    gather.far(4, 0)
    gather.chip(2, 2)
    block.drives()
    gather.chip(1, 1)
    block.scan_own(0)
    gather.chip(2, 3)
    gather.chip(4, 3)
    gather.far(6, 2)
    gather.chip(3, 3)
    gather.far(6, 0)
    gather.chip(5, 0, 2)
    gather.chip(4, 1)
    gather.far(7, 1, 2)
    gather.arrive(3)
    gather.chip(5, 3)
    gather.far(7, 0)
    gather.arrive(1)
    block.mix(1)
    gather.chip(6, 2)
    block.take("upstream")
    gather.arrive(2)
    gather.arrive(4)
    block.scan_states()
    gather.arrive(5)
    block.gate_rows()
    block.second_norm()
    gather.chip(6, 1, 3)
    block.give("normed_two")
    block.glu_forward(0)
    gather.chip(7, 3)
    gather.arrive(6)
    gather.chip(7, 2)
    block.glu_forward(1)
    gather.chip(7, 1)
    block.give(("d_glu", 1), ("hidden", 1))
    block.glu_back(0)
    block.give(("hidden", 0))
    gather.arrive(7)
    block.glu_forward(2)
    block.give(("hidden", 2))
    block.take(("d_glu", 1))
    block.give(("d_glu", 2), ("d_glu", 0))
    block.take(("hidden", 1), "normed_two")
    block.glu_grads(1)
    reduce.far(6)
    block.glu_back(1)
    block.take(("hidden", 2), ("d_glu", 2))
    block.glu_grads(2)
    block.take(("hidden", 0))
    reduce.far(7)
    block.glu_back(2)
    reduce.after_far(6, 0)
    block.take(("d_glu", 0))
    block.middle_back()
    block.gate_back()
    block.scan_own(1)
    block.give("gated")
    block.glu_grads(0)
    reduce.far(5)
    block.give("d_out")
    reduce.after_far(6, 1)
    block.give("d_gate")
    block.take("gated")
    block.gate_normed()
    block.take("d_out")
    reduce.after_far(7, 1)
    block.mixer_out_grad()
    block.scan_back()
    reduce.after_far(7, 3)
    reduce.after_far(5, 0)
    reduce.far(3)
    reduce.far(2)
    reduce.after_far(7, 0)
    block.drives_back()
    block.take("d_gate")
    reduce.after_far(6, 2)
    block.first_back()
    block.mix_grads(1)
    reduce.after_far(3, 0)
    reduce.after_far(7, 2)
    reduce.after_far(5, 1)
    block.give("d_drive")
    block.natural_tokens()
    leave_tokens.start()
    block.gather_vector()
    block.vector_step(0)
    reduce.far(1)
    block.take("d_drive")
    reduce.after_far(5, 2)
    reduce.after_far(2, 0)
    reduce.after_near(5, 0)
    block.mix_grads(0)
    reduce.far(4)
    reduce.after_far(2, 2)
    reduce.after_far(3, 2, 1)
    reduce.far(0)
    block.natural_out()
    leave_out.start()
    reduce.after_far(1, 1)
    block.vector_step(1)
    reduce.after_far(1, 0)
    reduce.after_near(1, 0)
    reduce.after_far(1, 2)
    reduce.after_near(5, 1)
    reduce.after_far(2, 1, 3)
    reduce.after_near(1, 1)
    reduce.after_far(6, 3)
    reduce.after_far(4, 0)
    reduce.after_far(5, 3)
    reduce.after_far(0, 0)
    reduce.after_far(4, 1)
    reduce.after_near(4, 0)
    reduce.after_far(0, 1)
    reduce.after_far(3, 3)
    reduce.after_near(5, 2)
    reduce.after_near(1, 2)
    reduce.after_near(0, 0)
    reduce.after_far(4, 2)
    reduce.after_far(1, 3)
    reduce.after_near(4, 1)
    reduce.after_far(0, 2)
    reduce.after_near(2)
    reduce.after_near(0, 1)
    reduce.after_near(5, 3)
    reduce.finish(5)
    reduce.after_near(6)
    reduce.after_far(4, 3)
    block.vector_step(2)
    reduce.after_near(3)
    reduce.after_near(1, 3)
    reduce.after_far(0, 3)
    reduce.after_near(4, 2)
    reduce.after_near(0, 2)
    reduce.after_near(7)
    reduce.finish(6)
    block.vector_step(3)
    for step in (1, 2, 3):
        block.vector_plane(planes, step, place.z).start()
    planes[place.z] = block.vector[3]
    reduce.finish(1)
    reduce.finish(2)
    reduce.after_near(0, 3)
    reduce.after_near(4, 3)
    reduce.finish(4)
    reduce.finish(7)
    reduce.finish(3)
    reduce.finish(0)

    for step in (1, 2, 3):
        block.vector_plane(planes, step, place.z).wait_send()
        block.vector_plane(planes, step, place.turn(4 - step)).wait_recv()
    for stage in range(3):
        block.vector_copy(stage).wait_send()
    for way in range(2):
        block.all_carries(way).wait_send()
    block.settle()
    for p in range(n):
        gather.drain(p)
        reduce.drain(p)
    leave_out.wait()
    leave_tokens.wait()


def block_routed(tokens, cotangent, padding, opening, w_in, w_out, vectors):
    vmem = pl.BlockSpec(memory_space=pltpu.VMEM)
    anywhere = pl.BlockSpec(memory_space=pl.ANY)
    out_shape = [
        jax.ShapeDtypeStruct((SLOTS, D), LOW),
        jax.ShapeDtypeStruct((SLOTS, D), WIDE),
        jax.ShapeDtypeStruct(w_in.shape, WIDE),
        jax.ShapeDtypeStruct(w_out.shape, WIDE),
        jax.ShapeDtypeStruct((PLANES, VEC_ROWS, TILE), WIDE),
    ]
    grads = [pltpu.VMEM(p.shape()[1:], LOW) for p in PIECES]
    block_out, d_tokens, sum_in, sum_out, planes = pl.pallas_call(
        block_kernel,
        out_shape=out_shape,
        in_specs=[anywhere, anywhere, vmem, vmem, anywhere, anywhere, vmem],
        out_specs=[anywhere, anywhere, vmem, vmem, vmem],
        scratch_shapes=Gather.scratch()
        + grads
        + Reduce.scratch()
        + list(block_scratch().values()),
        compiler_params=pltpu.CompilerParams(
            collective_id=0, has_side_effects=True, vmem_limit_bytes=VMEM_BYTES
        ),
    )(tokens, cotangent, padding, opening, w_in, w_out, vectors.reshape(VEC_COUNT, TILE))
    return block_out, d_tokens, sum_in, sum_out, planes


def power(base, count):
    return lax.fori_loop(0, count, lambda _, value: value * base, jnp.float32(1.0))


def update_kernel(counter, planes, block_from, tokens_from, *refs):
    ins, outs = refs[:11], refs[11:]
    outs[0][...] = block_from[...]
    outs[1][...] = tokens_from[...]
    first_scale = 1.0 - power(BETA_ONE, counter[0])
    second_scale = 1.0 - power(BETA_TWO, counter[0])
    vectors = (planes[0] + planes[1]) + (planes[2] + planes[3])
    total = vectors[VEC_COUNT : VEC_COUNT + 1, 0:1]

    def step(summed, master, first, second, decay):
        gradient = summed / total
        first = BETA_ONE * first + (1.0 - BETA_ONE) * gradient
        second = BETA_TWO * second + (1.0 - BETA_TWO) * gradient * gradient
        corrected = first / first_scale / (jnp.sqrt(second / second_scale) + ADAM_EPSILON)
        return gradient, -LEARN_RATE * (corrected + decay * master), first, second

    for k in range(2):
        summed, master, first, second = (ref[...] for ref in ins[4 * k : 4 * k + 4])
        gradient, change, first, second = step(summed, master, first, second, WEIGHT_DECAY)
        new = master + change
        results = (gradient, new, first, second, new.astype(LOW))
        for ref, value in zip(outs[2 + 5 * k : 7 + 5 * k], results, strict=True):
            ref[...] = value
    master, first, second = (ref[...] for ref in ins[8:])
    results = step(vectors[:VEC_COUNT], master, first, second, 0.0)
    for ref, value in zip(outs[12:16], results, strict=True):
        for i in range(VEC_COUNT):
            ref[pl.ds(i * TILE, TILE)] = value[i]
    for i in range(CH // TILE):
        outs[16][pl.ds(i * TILE, TILE)] = results[0][VEC_COUNT - CH // TILE + i]


UPDATE_BLOCKS = 1


def update(counter, planes, block_out, d_tokens, sums, masters, moments, vector_state):
    shapes = [x.shape for x in sums]

    def by_columns(shape):
        return pl.BlockSpec((shape[0], shape[1] // UPDATE_BLOCKS), lambda i: (0, i))

    def whole(shape):
        return pl.BlockSpec(shape, lambda i: (0,) * len(shape))

    vector = whole((VEC_COUNT, TILE))
    columns = [by_columns(shape) for shape in shapes]
    types = (WIDE, WIDE, WIDE, WIDE, LOW)
    out_shape = [
        jax.ShapeDtypeStruct(block_out.shape, block_out.dtype),
        jax.ShapeDtypeStruct(d_tokens.shape, d_tokens.dtype),
    ]
    out_shape += [jax.ShapeDtypeStruct(shape, kind) for shape in shapes for kind in types]
    lines = [(VEC_COUNT * TILE,)] * 4 + [(CH,)]
    out_shape += [jax.ShapeDtypeStruct(line, WIDE) for line in lines]
    operands = []
    for k in range(2):
        operands += [sums[k], masters[k], *moments[k]]
    return pl.pallas_call(
        update_kernel,
        grid=(UPDATE_BLOCKS,),
        out_shape=out_shape,
        in_specs=[pl.BlockSpec(memory_space=pltpu.SMEM), whole(planes.shape)]
        + [by_columns(block_out.shape)] * 2
        + [columns[0]] * 4
        + [columns[1]] * 4
        + [vector] * 3,
        out_specs=[by_columns(block_out.shape)] * 2 + [columns[0]] * 5 + [columns[1]] * 5 + [whole(line) for line in lines],
        compiler_params=pltpu.CompilerParams(vmem_limit_bytes=VMEM_BYTES),
    )(counter, planes, block_out, d_tokens, *operands, *vector_state)


def routed(tokens, w_in, w_out):
    sizes = (lax.axis_size("dp"), lax.axis_size("rep"))
    shards = (tokens.shape[1], w_in.shape[0], w_out.shape[0])
    return sizes == (PLANES * SIDE, SIDE * 2) and shards == (SLOTS, IN_ROWS, OUT_ROWS)


def block_anywhere(tokens, cotangent, padding, opening, w_in, w_out, vectors):
    low = jnp.bfloat16
    wide = jnp.float32
    mixer_cols = CH + 2 * D
    length = tokens.shape[1]
    inputs = stripe(tokens[0]).astype(wide)
    filled = stripe(padding[0][:, None]).astype(wide)
    starting = stripe(opening[0][:, None]) == 1
    gains_one = vectors[:D]
    gains_two = vectors[D : 2 * D]
    phases = vectors[2 * D : 2 * D + CH]
    biases = vectors[2 * D + CH :]
    turn = jnp.stack([jnp.cos(phases), jnp.sin(phases)])
    axes = ("dp", "rep")
    full_in = lax.all_gather(w_in.astype(low), axes, axis=0, tiled=True)
    full_out = lax.all_gather(w_out.astype(low), axes, axis=0, tiled=True)
    normed, scaling_one = normalize(inputs, gains_one)
    normed_low = normed.astype(low)
    pre_mix = jnp.dot(normed_low, full_in[:, :mixer_cols], preferred_element_type=wide)
    forget = jax.nn.sigmoid(-(pre_mix[:, :CH] + biases))
    driver_pre = pre_mix[:, CH : CH + D]
    driver = jax.nn.silu(driver_pre)
    gate_pre = pre_mix[:, CH + D :]
    forget_both = jnp.concatenate([forget, forget], axis=1)
    decay = jnp.where(starting, 1.0, forget).astype(low).astype(wide)
    retain = 1.0 - decay
    drive = (forget_both * driver).astype(low).astype(wide)
    drive_re, drive_im = drive[:, :CH], drive[:, CH:]
    summary = local_call(local_forward, [(32, CH)], retain, drive_re, drive_im, turn)[0]
    start = carry_in(summary, turn, length, False)
    states = local_call(
        whole_forward, [(2, length + 8, CH)], retain, drive_re, drive_im, turn, summary, start
    )[0]
    recurrent = jnp.concatenate([states[0, LANES:], states[1, LANES:]], axis=1)
    recurrent = recurrent.astype(low).astype(wide)
    gate_act = jax.nn.silu(gate_pre)
    masked = recurrent * filled
    gated_rows = (masked * gate_act).astype(low)
    middle = inputs + jnp.dot(gated_rows, full_out[:D], preferred_element_type=wide)
    normed_two, scaling_two = normalize(middle, gains_two)
    normed_two_low = normed_two.astype(low)
    glu_pre = jnp.dot(normed_two_low, full_in[:, mixer_cols:], preferred_element_type=wide)
    gate_glu = glu_pre[:, :FF]
    up_glu = glu_pre[:, FF:]
    hidden = (jax.nn.silu(gate_glu) * up_glu).astype(low)
    block_out = middle + jnp.dot(hidden, full_out[D:], preferred_element_type=wide)
    upstream = stripe(cotangent[0]).astype(wide) * filled
    upstream_low = upstream.astype(low)
    grad_down = jnp.einsum("tf,te->fe", hidden, upstream_low, preferred_element_type=wide)
    d_hidden = jnp.einsum("te,fe->tf", upstream_low, full_out[D:], preferred_element_type=wide)
    d_glu = jnp.concatenate(
        [d_hidden * up_glu * silu_slope(gate_glu), d_hidden * jax.nn.silu(gate_glu)], axis=1
    ).astype(low)
    grad_glu = jnp.einsum("td,tc->dc", normed_two_low, d_glu, preferred_element_type=wide)
    d_normed_two = jnp.einsum(
        "tc,dc->td", d_glu, full_in[:, mixer_cols:], preferred_element_type=wide
    )
    grad_gains_two = jnp.sum(d_normed_two * middle * scaling_two, axis=0)
    d_middle = upstream + normalize_back(middle, scaling_two, gains_two, d_normed_two)
    d_mixed_low = d_middle.astype(low)
    grad_mixer_out = jnp.einsum("td,te->de", gated_rows, d_mixed_low, preferred_element_type=wide)
    d_gated = jnp.einsum("te,de->td", d_mixed_low, full_out[:D], preferred_element_type=wide)
    d_recurrent = (d_gated * gate_act * filled).astype(low).astype(wide)
    d_gate_pre = d_gated * masked * silu_slope(gate_pre)
    grad_re, grad_im = d_recurrent[:, :CH], d_recurrent[:, CH:]
    summary_back = local_call(local_backward, [(32, CH)], retain, grad_re, grad_im, turn)[0]
    start_back = carry_in(summary_back, turn, length, True)
    d_decay, d_in_re, d_in_im, d_phase = local_call(
        whole_backward,
        [(length, CH)] * 3 + [(1, CH)],
        retain,
        grad_re,
        grad_im,
        turn,
        summary_back,
        start_back,
        states,
    )
    d_decay = d_decay.astype(low).astype(wide)
    d_input = jnp.concatenate([d_in_re, d_in_im], axis=1).astype(low).astype(wide)
    pulled = d_input * driver
    d_forget = jnp.where(starting, 0.0, d_decay) + pulled[:, :CH] + pulled[:, CH:]
    d_forget_pre = -forget * (1.0 - forget) * d_forget
    d_driver_pre = d_input * forget_both * silu_slope(driver_pre)
    d_mix = jnp.concatenate([d_forget_pre, d_driver_pre, d_gate_pre], axis=1).astype(low)
    grad_mixer_in = jnp.einsum("td,tc->dc", normed_low, d_mix, preferred_element_type=wide)
    d_normed = jnp.einsum(
        "tc,dc->td", d_mix, full_in[:, :mixer_cols], preferred_element_type=wide
    )
    grad_gains_one = jnp.sum(d_normed * inputs * scaling_one, axis=0)
    d_tokens = d_middle + normalize_back(inputs, scaling_one, gains_one, d_normed)
    grad_biases = jnp.sum(d_forget_pre, axis=0)
    grad_vectors = jnp.concatenate([grad_gains_one, grad_gains_two, d_phase[0], grad_biases])
    grad_in_all = jnp.concatenate([grad_mixer_in, grad_glu], axis=1)
    grad_out_all = jnp.concatenate([grad_mixer_out, grad_down], axis=0)
    summed_in = lax.psum_scatter(grad_in_all, axes, scatter_dimension=0, tiled=True)
    summed_out = lax.psum_scatter(grad_out_all, axes, scatter_dimension=0, tiled=True)
    summed_vec, total = lax.psum((grad_vectors, jnp.sum(filled)), axes)
    return unstripe(block_out.astype(low)), unstripe(d_tokens), summed_in, summed_out, summed_vec, total


def body(
    tokens,
    cotangent,
    padding,
    opening,
    w_in,
    w_out,
    vectors,
    m_in,
    v_in,
    m_out,
    v_out,
    m_vec,
    v_vec,
    counter,
):
    if routed(tokens, w_in, w_out):
        block_out, d_tokens, sum_in, sum_out, planes = block_routed(
            tokens, cotangent, padding, opening, w_in, w_out, vectors
        )
        sums, masters = (sum_in, sum_out), (w_in, w_out)
        moments = ((m_in, v_in), (m_out, v_out))
        lines = [x.reshape(VEC_COUNT, TILE) for x in (vectors, m_vec, v_vec)]
        results = update(
            counter, planes, block_out, d_tokens, sums, masters, moments, lines
        )
        block_out, d_tokens = results[:2]
        grad_vec, update_vec, first_vec, second_vec, grad_bias = results[12:]
        return (
            block_out[None],
            d_tokens[None],
            *results[2:12],
            grad_vec,
            grad_bias,
            update_vec,
            first_vec,
            second_vec,
        )
    block_out, d_tokens, summed_in, summed_out, summed_vec, total = block_anywhere(
        tokens, cotangent, padding, opening, w_in, w_out, vectors
    )
    steps = counter[0].astype(jnp.float32)
    grad_in = summed_in / total
    grad_out = summed_out / total
    grad_vec = summed_vec / total
    new_in, first_in, second_in, change_in = adam_update(
        w_in, grad_in, m_in, v_in, steps, WEIGHT_DECAY
    )
    new_out, first_out, second_out, change_out = adam_update(
        w_out, grad_out, m_out, v_out, steps, WEIGHT_DECAY
    )
    new_vec, first_vec, second_vec, update_vec = adam_update(
        vectors, grad_vec, m_vec, v_vec, steps, 0.0
    )
    return (
        block_out[None],
        d_tokens[None],
        grad_in,
        new_in,
        first_in,
        second_in,
        new_in.astype(jnp.bfloat16),
        grad_out,
        new_out,
        first_out,
        second_out,
        new_out.astype(jnp.bfloat16),
        grad_vec,
        grad_vec[2 * D + CH :],
        update_vec,
        first_vec,
        second_vec,
    )


def solution(mesh):
    in_specs = (
        P("rep", "dp", None),
        P("rep", "dp", None),
        P("rep", "dp"),
        P("rep", "dp"),
        P(("dp", "rep"), None),
        P(("dp", "rep"), None),
        P(),
        P(("dp", "rep"), None),
        P(("dp", "rep"), None),
        P(("dp", "rep"), None),
        P(("dp", "rep"), None),
        P(),
        P(),
        P(),
    )
    out_specs = (
        P("rep", "dp", None),
        P("rep", "dp", None),
        P(("dp", "rep"), None),
        P(("dp", "rep"), None),
        P(("dp", "rep"), None),
        P(("dp", "rep"), None),
        P(("dp", "rep"), None),
        P(("dp", "rep"), None),
        P(("dp", "rep"), None),
        P(("dp", "rep"), None),
        P(("dp", "rep"), None),
        P(("dp", "rep"), None),
        P(),
        P(),
        P(),
        P(),
        P(),
    )
    return jax.shard_map(body, mesh=mesh, in_specs=in_specs, out_specs=out_specs, check_vma=False)
```

```python
import functools

import jax
import jax.numpy as jnp
from jax import lax
from jax.experimental import pallas as pl
from jax.experimental.pallas import tpu as pltpu
from jax.sharding import PartitionSpec as P

D = 768
CH = 384
FF = 1536


NORM_EPSILON = 1e-06
LEARN_RATE = 0.05
BETA_ONE = 0.9
BETA_TWO = 0.999
ADAM_EPSILON = 1e-08
WEIGHT_DECAY = 0.1


LANES = 8


def rotate(real, imag, cosine, sine):
    return cosine * real - sine * imag, sine * real + cosine * imag


def turn_power(cosine, sine, doublings):
    for _ in range(doublings):
        cosine, sine = cosine * cosine - sine * sine, 2.0 * cosine * sine
    return cosine, sine


def local_forward(retain, drive_re, drive_im, turn, summary):
    steps = retain.shape[0] // LANES
    cosine, sine = turn[0:1], turn[1:2]
    zero = jnp.zeros((LANES, retain.shape[1]), jnp.float32)

    def step(i, carry):
        real, imag, product = carry
        rows = pl.ds(pl.multiple_of(LANES * i, LANES), LANES)
        r = retain[rows, :]
        turned_re, turned_im = rotate(real, imag, cosine, sine)
        return r * turned_re + drive_re[rows, :], r * turned_im + drive_im[rows, :], r * product

    real, imag, product = lax.fori_loop(0, steps, step, (zero, zero, zero + 1.0), unroll=4)
    cos_sub, sin_sub = turn_power(cosine, sine, steps.bit_length() - 1)
    total_re, total_im, total = real[0:1], imag[0:1], product[0:1]
    for j in range(1, LANES):
        turned_re, turned_im = rotate(total_re, total_im, cos_sub, sin_sub)
        total_re = product[j : j + 1] * turned_re + real[j : j + 1]
        total_im = product[j : j + 1] * turned_im + imag[j : j + 1]
        total = product[j : j + 1] * total
    summary[0:LANES] = real
    summary[LANES : 2 * LANES] = imag
    summary[2 * LANES : 3 * LANES] = product
    summary[24:32] = jnp.concatenate([total_re, total_im, total, zero[3:]], axis=0)


def whole_forward(retain, drive_re, drive_im, turn, summary, start, states):
    steps = retain.shape[0] // LANES
    cosine, sine = turn[0:1], turn[1:2]
    cos_sub, sin_sub = turn_power(cosine, sine, steps.bit_length() - 1)
    now_re, now_im = start[0:1], start[1:2]
    reals, imags = [now_re], [now_im]
    for j in range(LANES - 1):
        turned_re, turned_im = rotate(now_re, now_im, cos_sub, sin_sub)
        product = summary[2 * LANES + j : 2 * LANES + j + 1]
        now_re = product * turned_re + summary[j : j + 1]
        now_im = product * turned_im + summary[LANES + j : LANES + j + 1]
        reals.append(now_re)
        imags.append(now_im)
    carry = (jnp.concatenate(reals, axis=0), jnp.concatenate(imags, axis=0))

    def step(i, carry):
        real, imag = carry
        rows = pl.ds(pl.multiple_of(LANES * i, LANES), LANES)
        states[0, rows, :] = real
        states[1, rows, :] = imag
        r = retain[rows, :]
        turned_re, turned_im = rotate(real, imag, cosine, sine)
        return r * turned_re + drive_re[rows, :], r * turned_im + drive_im[rows, :]

    real, imag = lax.fori_loop(0, steps, step, carry, unroll=4)
    states[0, LANES * steps :, :] = real
    states[1, LANES * steps :, :] = imag


def local_backward(retain, grad_re, grad_im, turn, summary):
    steps = retain.shape[0] // LANES
    cosine, sine = turn[0:1], -turn[1:2]
    zero = jnp.zeros((LANES, retain.shape[1]), jnp.float32)

    def step(k, carry):
        real, imag, product = carry
        rows = pl.ds(pl.multiple_of(LANES * (steps - 1 - k), LANES), LANES)
        r = retain[rows, :]
        turned_re, turned_im = rotate(grad_re[rows, :] + real, grad_im[rows, :] + imag, cosine, sine)
        return r * turned_re, r * turned_im, r * product

    real, imag, product = lax.fori_loop(0, steps, step, (zero, zero, zero + 1.0), unroll=4)
    cos_sub, sin_sub = turn_power(cosine, sine, steps.bit_length() - 1)
    last = LANES - 1
    total_re, total_im, total = real[last:], imag[last:], product[last:]
    for j in range(LANES - 2, -1, -1):
        turned_re, turned_im = rotate(total_re, total_im, cos_sub, sin_sub)
        total_re = product[j : j + 1] * turned_re + real[j : j + 1]
        total_im = product[j : j + 1] * turned_im + imag[j : j + 1]
        total = product[j : j + 1] * total
    summary[0:LANES] = real
    summary[LANES : 2 * LANES] = imag
    summary[2 * LANES : 3 * LANES] = product
    summary[24:32] = jnp.concatenate([total_re, total_im, total, zero[3:]], axis=0)


def whole_backward(
    retain, grad_re, grad_im, turn, summary, start, states, d_decay, d_in_re, d_in_im, d_phase
):
    steps = retain.shape[0] // LANES
    cosine, sine = turn[0:1], turn[1:2]
    cos_sub, sin_sub = turn_power(cosine, -sine, steps.bit_length() - 1)
    now_re, now_im = start[0:1], start[1:2]
    reals, imags = [now_re], [now_im]
    for j in range(LANES - 1, 0, -1):
        turned_re, turned_im = rotate(now_re, now_im, cos_sub, sin_sub)
        product = summary[2 * LANES + j : 2 * LANES + j + 1]
        now_re = product * turned_re + summary[j : j + 1]
        now_im = product * turned_im + summary[LANES + j : LANES + j + 1]
        reals.append(now_re)
        imags.append(now_im)
    zero = jnp.zeros((LANES, retain.shape[1]), jnp.float32)
    carry = (jnp.concatenate(reals[::-1], axis=0), jnp.concatenate(imags[::-1], axis=0), zero)

    def step(k, carry):
        real, imag, phase = carry
        rows = pl.ds(pl.multiple_of(LANES * (steps - 1 - k), LANES), LANES)
        r = retain[rows, :]
        real = grad_re[rows, :] + real
        imag = grad_im[rows, :] + imag
        prior_re, prior_im = rotate(states[0, rows, :], states[1, rows, :], cosine, sine)
        d_decay[rows, :] = -(real * prior_re + imag * prior_im)
        d_in_re[rows, :] = real
        d_in_im[rows, :] = imag
        phase = phase + r * (imag * prior_re - real * prior_im)
        turned_re, turned_im = rotate(real, imag, cosine, -sine)
        return r * turned_re, r * turned_im, phase

    _, _, phase = lax.fori_loop(0, steps, step, carry, unroll=4)
    d_phase[...] = jnp.sum(phase, axis=0, keepdims=True)


def stripe(rows):
    count, columns = rows.shape
    return rows.reshape(LANES, count // LANES, columns).swapaxes(0, 1).reshape(count, columns)


def unstripe(rows):
    count, columns = rows.shape
    return rows.reshape(count // LANES, LANES, columns).swapaxes(0, 1).reshape(count, columns)


def local_call(kernel, outs, *args):
    return pl.pallas_call(
        kernel,
        out_shape=[jax.ShapeDtypeStruct(shape, jnp.float32) for shape in outs],
        compiler_params=pltpu.CompilerParams(vmem_limit_bytes=32 * 1024 * 1024),
    )(*args)


def carry_chain(every, turn, me, length, reverse):
    sine = -turn[1:2] if reverse else turn[1:2]
    cosine, sine = turn_power(turn[0:1], sine, length.bit_length() - 1)
    count = every.shape[0]
    real = jnp.zeros_like(cosine)
    imag = jnp.zeros_like(cosine)
    for j in range(count - 1, 0, -1) if reverse else range(count - 1):
        use = (j > me) if reverse else (j < me)
        turned_re, turned_im = rotate(real, imag, cosine, sine)
        real = jnp.where(use, every[j, 2:3] * turned_re + every[j, 0:1], real)
        imag = jnp.where(use, every[j, 2:3] * turned_im + every[j, 1:2], imag)
    return jnp.concatenate([real, imag], axis=0)


def carry_in(summary, turn, length, reverse):
    every = lax.all_gather(summary[24:32], "dp", axis=0)
    return carry_chain(every, turn, lax.axis_index("dp"), length, reverse)


def normalize(values, gains):
    scaling = lax.rsqrt(jnp.mean(values * values, axis=-1, keepdims=True) + NORM_EPSILON)
    return (values * scaling * gains, scaling)


def normalize_back(values, scaling, gains, gradient):
    scaled = gradient * gains
    return scaling * scaled - values * scaling**3 * jnp.mean(
        values * scaled, axis=-1, keepdims=True
    )


def silu_slope(values):
    logistic = jax.nn.sigmoid(values)
    return logistic * (1.0 + values * (1.0 - logistic))


def adam_update(master, gradient, first, second, steps, decay):
    first_new = BETA_ONE * first + (1.0 - BETA_ONE) * gradient
    second_new = BETA_TWO * second + (1.0 - BETA_TWO) * gradient * gradient
    corrected = (
        first_new
        / (1.0 - BETA_ONE**steps)
        / (jnp.sqrt(second_new / (1.0 - BETA_TWO**steps)) + ADAM_EPSILON)
    )
    change = -LEARN_RATE * (corrected + decay * master)
    return (master + change, first_new, second_new, change)


MESH = pl.DeviceIdType.MESH
LOW = jnp.bfloat16
WIDE = jnp.float32
PLANES = 4
SIDE = 2
IN_ROWS = 24
OUT_ROWS = 72
MIX = CH + 2 * D
CHUNK = 512
CHUNKS = FF // CHUNK
OUT = 2
TILE = 128
OUTS = D // 2 // TILE
GLU = OUT + OUTS
VMEM_BYTES = 63 * 1024 * 1024
SLOTS = 512
ROWS = 64
RUN = SLOTS // LANES


class Piece:
    def __init__(self, matrix, rows, columns, starts, overlap=0):
        self.matrix, self.rows, self.columns = matrix, rows, columns
        self.starts, self.overlap = starts, overlap

    def shape(self):
        return (2, PLANES, SIDE, SIDE, 2 * self.rows, self.columns)


def piece_list():
    drive = (CH + D) // 2 + TILE // 2
    mix = [
        Piece("in", IN_ROWS, drive, (0, CH + D - drive), TILE),
        Piece("in", IN_ROWS, D // 2, (CH + D, MIX - D // 2)),
    ]
    out = [Piece("out", OUT_ROWS, TILE, (TILE * k, D // 2 + TILE * k)) for k in range(OUTS)]
    glu = [
        Piece("in", IN_ROWS, CHUNK, (MIX + CHUNK * k, MIX + FF + CHUNK * k)) for k in range(CHUNKS)
    ]
    return mix + out + glu


PIECES = piece_list()


class Place:
    def __init__(self):
        dp, rep = lax.axis_index("dp"), lax.axis_index("rep")
        self.z, self.x = dp // SIDE, dp % SIDE
        self.y, self.core = rep // 2, rep % 2

    def at(self, z, x, y, core):
        return (z * SIDE + x, y * 2 + core)

    def sibling(self):
        return self.at(self.z, self.x, self.y, 1 - self.core)

    def plane(self, z):
        return self.at(z, self.x, self.y, self.core)

    def near(self, core):
        if core == 0:
            return self.at(self.z, 1 - self.x, self.y, self.core)
        return self.at(self.z, self.x, 1 - self.y, self.core)

    def far(self, core):
        return self.near(1 - core)

    def away(self):
        return self.z % 2 + 1, (3 * self.z + 2) % 5, 3 - 3 * (self.z // 2)

    def when_inner(self, run):
        pl.when((self.z + 1) // 2 == 1)(run)

    def when_end(self, run):
        pl.when((self.z + 1) // 2 != 1)(run)

    def turn(self, step):
        return lax.rem(self.z + step, PLANES)

    def sides(self, core):
        return (self.x, self.y) if core == 0 else (self.y, self.x)

    def by_core(self, run):
        for core in range(2):
            pl.when(self.core == core)(functools.partial(run, core))

    def greet(self):
        barrier = pltpu.get_barrier_semaphore()
        partners = [self.sibling(), self.near(0), self.near(1)]
        for step in (1, 2, 3):
            partners.append(self.plane(self.turn(step)))
            partners.append(self.at(self.turn(step), 1 - self.x, self.y, self.core))
        for partner in partners:
            pl.semaphore_signal(barrier, inc=1, device_id=partner, device_id_type=MESH)
        return lambda: pl.semaphore_wait(barrier, len(partners))


def always(run):
    run()


def block_of(ref, core, z, near, far):
    return ref.at[core, z, near, far] if core == 0 else ref.at[core, z, far, near]


def pair_of(ref, core, z, far):
    return ref.at[core, z, :, far] if core == 0 else ref.at[core, z, far]


def remote(source, target, sent, received, device):
    return pltpu.make_async_remote_copy(
        src_ref=source,
        dst_ref=target,
        send_sem=sent,
        recv_sem=received,
        device_id=device,
        device_id_type=MESH,
    )


GATHER_NEAR_FIRST = (4, 6, 7)
REDUCE_NEAR_LAST = (2, 3, 6, 7)
GATHER_RELAYED = (0, 1, 2, 3, 4, 5)
REDUCE_RELAYED = (0, 1, 3, 4, 5, 6, 7)


class Gather:
    def __init__(self, place, masters, buffers, staging, sems):
        self.place, self.masters, self.buffers, self.staging = place, masters, buffers, staging
        self.local, self.sent0, self.got0 = sems[:3]
        self.z_sent, self.near_sent, self.far_sent, self.chip_sent, self.chip_got = sems[3:8]
        self.z_got, self.near_got, self.far_got = sems[8:]

    @staticmethod
    def scratch():
        n = len(PIECES)
        dma = pltpu.SemaphoreType.DMA
        return (
            [pltpu.VMEM(p.shape(), LOW) for p in PIECES]
            + [pltpu.VMEM((2 * p.rows, p.columns), WIDE) for p in PIECES]
            + [dma((n,))] * 8
            + [dma((n, PLANES))] * 3
        )

    def part(self, p, half):
        piece = PIECES[p]
        start = piece.starts[0] + half * (piece.starts[1] - piece.starts[0])
        return self.masters[piece.matrix].at[:, pl.ds(pl.multiple_of(start, TILE), piece.columns)]

    def own_rows(self, p):
        rows = PIECES[p].rows
        return self.staging[p].at[pl.ds(pl.multiple_of(self.place.core * rows, 8), rows)]

    def to_sibling(self, p):
        return remote(
            self.part(p, 1 - self.place.core),
            self.own_rows(p),
            self.sent0.at[p],
            self.got0.at[p],
            self.place.sibling(),
        )

    def to_self(self, p):
        return pltpu.make_async_copy(
            self.part(p, self.place.core), self.own_rows(p), self.local.at[p]
        )

    def along_z(self, p, z, target, core):
        place = self.place
        near, far = place.sides(core)
        if p in GATHER_NEAR_FIRST:
            part = pair_of(self.buffers[p], core, z, far)
        else:
            part = block_of(self.buffers[p], core, z, near, far)
        sems = self.z_sent.at[p], self.z_got.at[p, z]
        return remote(part, part, *sems, place.plane(target))

    def relay(self, p, core):
        place = self.place
        last = place.away()[2]
        return self.along_z(p, last, 3 - last, core)

    def along_near(self, p, z, core):
        block = block_of(self.buffers[p], core, z, *self.place.sides(core))
        return remote(
            block, block, self.near_sent.at[p], self.near_got.at[p, z], self.place.near(core)
        )

    def along_far(self, p, z, core):
        pair = pair_of(self.buffers[p], core, z, self.place.sides(core)[1])
        return remote(
            pair, pair, self.far_sent.at[p], self.far_got.at[p, z], self.place.far(core)
        )

    def in_chip(self, p, planes, core):
        part = self.buffers[p].at[core, planes]
        return remote(
            part, part, self.chip_sent.at[p], self.chip_got.at[p], self.place.sibling()
        )

    def begin(self):
        for p in range(len(PIECES)):
            self.to_sibling(p).start()
            self.to_self(p).start()


    def near_own(self, p):
        place = self.place
        self.to_self(p).wait()
        self.to_sibling(p).wait_recv()
        self.buffers[p][place.core, place.z, place.x, place.y] = self.staging[p][...].astype(LOW)
        place.by_core(lambda core: self.along_near(p, place.z, core).start())

    def z_targets(self, p):
        first, second, third = self.place.away()
        relayed = self.place.when_inner if p in GATHER_RELAYED else always
        return (first, always), (second, always), (third, relayed)

    def z_own(self, p):
        place = self.place

        def run(core):
            for z, when in self.z_targets(p):
                when(lambda: self.along_z(p, place.z, z, core).start())

        place.by_core(run)

    def from_z(self, p, index, core):
        place = self.place
        z = place.away()[index]
        self.along_z(p, z, place.z, core).wait_recv()
        if index == 2 and p in GATHER_RELAYED:
            place.when_inner(lambda: self.relay(p, core).start())
        return z

    def far_own(self, p):
        place = self.place

        def run(core):
            self.along_near(p, place.z, core).wait_recv()
            self.along_far(p, place.z, core).start()

        place.by_core(run)

    def near(self, p, *indices):
        place = self.place

        def run(core):
            for index in indices or range(3):
                z = self.from_z(p, index, core)
                self.along_near(p, z, core).start()

        if p not in GATHER_NEAR_FIRST:
            place.by_core(run)

    def far(self, p, *indices):
        place = self.place

        def run(core):
            for index in indices or range(3):
                z = place.away()[index]
                if p in GATHER_NEAR_FIRST:
                    self.from_z(p, index, core)
                else:
                    self.along_near(p, z, core).wait_recv()
                self.along_far(p, z, core).start()

        place.by_core(run)

    def chip(self, p, *indices):
        def run(core):
            for index in indices or range(4):
                z = (self.place.z, *self.place.away())[index]
                self.along_far(p, z, core).wait_recv()
                self.in_chip(p, z, core).start()

        self.place.by_core(run)

    def arrive(self, p):
        self.in_chip(p, pl.ds(0, PLANES), 1 - self.place.core).wait_recv()

    def drain(self, p):
        place, ref = self.place, self.buffers[p]
        self.to_sibling(p).wait_send()

        def sent(part, sem):
            remote(part, part, sem.at[p], sem.at[p], place.sibling()).wait_send()

        def run(core):
            def sent_z(count):
                planes = pl.ds(0, count)
                near_first = p in GATHER_NEAR_FIRST
                part = ref.at[core, planes, :, 0] if near_first else ref.at[core, planes, 0, 0]
                sent(part, self.z_sent)

            if p in GATHER_RELAYED:
                place.when_inner(lambda: sent_z(4))
                place.when_end(lambda: sent_z(2))
            else:
                sent_z(3)
            sent(ref.at[core, pl.ds(0, 1 if p in GATHER_NEAR_FIRST else 4), 0, 0], self.near_sent)
            sent(ref.at[core, :, :, 0], self.far_sent)
            sent(ref.at[core], self.chip_sent)

        place.by_core(run)


class Reduce:
    def __init__(self, place, grads, refs, results):
        n = len(PIECES)
        self.place, self.grads, self.results = place, grads, results
        self.far_got, self.near_got, self.planes, self.final = (refs[k * n : (k + 1) * n] for k in range(4))
        self.far_sem, self.near_sem, self.z_sem = refs[4 * n : 4 * n + 3]
        self.far_sent, self.near_sent, self.z_sent = refs[4 * n + 3 : 4 * n + 6]
        self.chip_sent, self.chip_got = refs[4 * n + 6 :]

    @staticmethod
    def scratch():
        n = len(PIECES)
        dma = pltpu.SemaphoreType.DMA
        blocks = [p.shape()[4:] for p in PIECES]
        return (
            [pltpu.VMEM((PLANES, SIDE) + s, LOW) for s in blocks]
            + [pltpu.VMEM((PLANES,) + s, LOW) for s in blocks]
            + [
                pltpu.VMEM((PLANES,) + (SIDE,) * (p in REDUCE_NEAR_LAST) + s, LOW)
                for p, s in enumerate(blocks)
            ]
            + [pltpu.VMEM(s, WIDE) for s in blocks]
            + [dma((n, PLANES))] * 3
            + [dma((n,))] * 5
        )

    def block(self, p, z, near, far, core):
        return self.grads[p].at[z, near, far] if core == 0 else self.grads[p].at[z, far, near]

    def pair(self, p, z, far, core):
        return self.grads[p].at[z, :, far] if core == 0 else self.grads[p].at[z, far]

    def along_far(self, p, z, core):
        return remote(
            self.pair(p, z, 1 - self.place.sides(core)[1], core),
            self.far_got[p].at[z],
            self.far_sent.at[p],
            self.far_sem.at[p, z],
            self.place.far(core),
        )

    def along_near(self, p, z, core):
        near, far = self.place.sides(core)
        return remote(
            self.block(p, z, 1 - near, far, core),
            self.near_got[p].at[z],
            self.near_sent.at[p],
            self.near_sem.at[p, z],
            self.place.near(core),
        )

    def order(self):
        first, second, third = self.place.away()
        inner = (self.place.z + 1) // 2 % 2
        return (
            inner * first + (1 - inner) * third,
            second,
            inner * third + (1 - inner) * first,
            self.place.z,
        )

    def z_part(self, p, z, core):
        near, far = self.place.sides(core)
        if p in REDUCE_NEAR_LAST:
            return self.pair(p, z, far, core)
        return self.block(p, z, near, far, core)

    def along_z(self, p, z, sender, core):
        sems = self.z_sent.at[p], self.z_sem.at[p, sender]
        target = self.planes[p].at[sender]
        return remote(self.z_part(p, z, core), target, *sems, self.place.plane(z))

    def to_relay(self, p, core, slot):
        first, _, third = self.place.away()
        sems = self.z_sent.at[p], self.z_sem.at[p, slot]
        target = self.planes[p].at[slot]
        return remote(self.z_part(p, third, core), target, *sems, self.place.plane(first))

    def send_z(self, p, core, index):
        place = self.place
        z = self.order()[index]
        if index == 1:
            self.along_z(p, z, place.z, core).start()
        elif p not in REDUCE_RELAYED:
            if index != 3:
                self.along_z(p, z, place.z, core).start()
        elif index == 0:
            place.when_inner(lambda: self.along_z(p, z, place.z, core).start())
            place.when_end(lambda: self.to_relay(p, core, place.away()[0]).start())
        elif index == 2:

            def pass_on():
                self.to_relay(p, core, place.z).wait_recv()
                self.add(self.z_part(p, z, core), self.planes[p].at[place.z])

            place.when_inner(pass_on)
            self.along_z(p, z, place.z, core).start()

    def sum_planes(self, p, core, result):
        place = self.place
        first, second, third = place.away()
        for z in (first, second):
            self.along_z(p, place.z, z, core).wait_recv()
        total = self.z_part(p, place.z, core)[...].astype(WIDE)
        total = total + self.planes[p][first].astype(WIDE) + self.planes[p][second].astype(WIDE)

        def inner():
            self.along_z(p, place.z, third, core).wait_recv()
            result[...] = (total + self.planes[p][third].astype(WIDE)).astype(result.dtype)

        def end():
            result[...] = total.astype(result.dtype)

        if p in REDUCE_RELAYED:
            place.when_inner(inner)
            place.when_end(end)
        else:
            inner()

    def result(self, p, core):
        piece = PIECES[p]
        skip = piece.overlap * core
        start, width = piece.starts[core] + skip, piece.columns - skip
        return self.results[piece.matrix].at[:, pl.ds(start, width)], pl.ds(skip, width)

    def to_sibling(self, p, core):
        rows = PIECES[p].rows
        target, columns = self.result(p, core)
        return remote(
            self.final[p].at[pl.ds(rows * (1 - core), rows), columns],
            target,
            self.chip_sent.at[p],
            self.chip_got.at[p],
            self.place.sibling(),
        )

    @staticmethod
    def add(target, source):
        target[...] = target[...] + source[...]

    def far(self, p):
        def run(core):
            for z in self.order():
                self.along_far(p, z, core).start()

        self.place.by_core(run)

    def after_far(self, p, *indices):
        def run(core):
            for index in indices or range(4):
                z = self.order()[index]
                self.along_far(p, z, core).wait_recv()
                self.add(self.pair(p, z, self.place.sides(core)[1], core), self.far_got[p].at[z])
                if p in REDUCE_NEAR_LAST:
                    self.send_z(p, core, index)
                else:
                    self.along_near(p, z, core).start()

        self.place.by_core(run)

    def after_near(self, p, *indices):
        place = self.place

        def run(core):
            near, far = place.sides(core)
            if p in REDUCE_NEAR_LAST:
                self.sum_planes(p, core, self.pair(p, place.z, far, core))
                self.along_near(p, place.z, core).start()
                return
            for index in indices or range(4):
                z = self.order()[index]
                self.along_near(p, z, core).wait_recv()
                self.add(self.block(p, z, near, far, core), self.near_got[p].at[z])
                self.send_z(p, core, index)

        place.by_core(run)

    def finish(self, p):
        rows, place = PIECES[p].rows, self.place

        def run(core):
            near, far = place.sides(core)
            if p in REDUCE_NEAR_LAST:
                self.along_near(p, place.z, core).wait_recv()
                own = self.block(p, place.z, near, far, core)[...].astype(WIDE)
                self.final[p][...] = own + self.near_got[p][place.z].astype(WIDE)
            else:
                self.sum_planes(p, core, self.final[p])
            self.to_sibling(p, core).start()
            target, columns = self.result(p, core)
            target[...] = self.final[p][pl.ds(rows * core, rows), columns]

        place.by_core(run)

    def drain(self, p):
        place = self.place

        def sent(part, sem):
            remote(part, part, sem.at[p], sem.at[p], place.sibling()).wait_send()

        def run(core):
            self.to_sibling(p, 1 - core).wait_recv()
            self.to_sibling(p, core).wait_send()

        place.by_core(run)
        sent(self.far_got[p], self.far_sent)
        sent(self.near_got[p].at[pl.ds(0, 1 if p in REDUCE_NEAR_LAST else 4)], self.near_sent)
        sent(self.planes[p].at[pl.ds(0, 3)], self.z_sent)


def tiled(column, count):
    return jnp.concatenate([column] * count, axis=1)


def each_block(run, size=ROWS):
    def block(i, carry):
        run(pl.ds(pl.multiple_of(i * size, size), size))
        return carry

    lax.fori_loop(0, SLOTS // size, block, 0)


def inner(left, right, dims=((1,), (0,))):
    return lax.dot_general(left, right, (dims, ((), ())), preferred_element_type=WIDE)


def across(left, right):
    return inner(left, right, ((1,), (1,)))


def along(left, right):
    return inner(left, right, ((0,), (0,)))


def out_segments(start, count):
    size, runs, stop = 2 * OUT_ROWS, [], start + count
    while start < stop:
        chip, first = divmod(start, size)
        last = min(size, first + stop - start)
        runs.append((chip // 4, chip // 2 % 2, chip % 2, first, last))
        start += last - first
    return runs


def row_norm(values):
    return lax.rsqrt(jnp.mean(values * values, axis=1, keepdims=True) + NORM_EPSILON)


def eights(values):
    return jnp.sum(values.reshape(values.shape[0] // 8, 8, values.shape[1]), axis=0)


def block_scratch():
    vmem, dma = pltpu.VMEM, pltpu.SemaphoreType.DMA
    rows = (SLOTS, D)
    both = (2 * SLOTS, D)
    return dict(
        arrivals=dma((2,)),
        departures=dma((2,)),
        perm=vmem((SLOTS, SLOTS), LOW),
        live=vmem((SLOTS, TILE), WIDE),
        opens=vmem((SLOTS, TILE), WIDE),
        params=vmem((8, D), WIDE),
        tokens=vmem(rows, LOW),
        upstream=vmem((2, SLOTS, D // 2), LOW),
        upstream_got=vmem((SLOTS, D // 2), LOW),
        normed=vmem(both, LOW),
        normed_two=vmem(both, LOW),
        gated=vmem(both, LOW),
        hidden=vmem((CHUNKS, 2 * SLOTS, CHUNK), LOW),
        d_glu=vmem((CHUNKS, 2, SLOTS, CHUNK), LOW),
        d_glu_got=vmem((CHUNKS, SLOTS, CHUNK), LOW),
        d_out=vmem((2, SLOTS, D // 2), LOW),
        d_out_got=vmem((SLOTS, D // 2), LOW),
        d_drive=vmem((2, SLOTS, PIECES[0].columns), LOW),
        d_drive_got=vmem((SLOTS, PIECES[0].columns), LOW),
        d_gate=vmem((2, SLOTS, PIECES[1].columns), LOW),
        d_gate_got=vmem((SLOTS, PIECES[1].columns), LOW),
        pre_mix=vmem((SLOTS, MIX), WIDE),
        retain=vmem((SLOTS, CH), WIDE),
        drive=vmem(rows, WIDE),
        states=vmem((2, SLOTS + LANES, CH), WIDE),
        summaries=vmem((2, 32, CH), WIDE),
        every=vmem((2, PLANES * SIDE, 8, CH), WIDE),
        middle=vmem(rows, WIDE),
        d_normed=vmem(rows, WIDE),
        total=vmem(rows, WIDE),
        block_out=vmem(rows, LOW),
        sums=vmem((3, 8, D), WIDE),
        vector=vmem((8, VEC_ROWS, TILE), WIDE),
        pair_sent=dma((PAIRS,)),
        pair_got=dma((PAIRS,)),
        carry_sent=dma((2,)),
        carry_got=dma((2,)),
        vector_sent=dma((6,)),
        vector_got=dma((6,)),
    )


VEC_ROWS = 24
VEC_COUNT = 18
PAIRS = 13


class Block:
    def __init__(self, place, buffers, grads, refs):
        self.place, self.weights, self.grads = place, buffers, grads
        for name, ref in refs.items():
            setattr(self, name, ref)
        self.me = place.z * SIDE + place.x


    def swaps(self):
        own, got = pl.ds(0, SLOTS), pl.ds(SLOTS, SLOTS)
        other = 1 - self.place.core
        pairs = dict(
            normed=(self.normed.at[own], self.normed.at[got]),
            normed_two=(self.normed_two.at[own], self.normed_two.at[got]),
            gated=(self.gated.at[own], self.gated.at[got]),
            upstream=(self.upstream.at[other], self.upstream_got),
            d_out=(self.d_out.at[other], self.d_out_got),
            d_drive=(self.d_drive.at[other], self.d_drive_got),
            d_gate=(self.d_gate.at[other], self.d_gate_got),
        )
        for k in range(CHUNKS):
            pairs["hidden", k] = (self.hidden.at[k, own], self.hidden.at[k, got])
            pairs["d_glu", k] = (self.d_glu.at[k, other], self.d_glu_got.at[k])
        return pairs

    def swap(self, name):
        pairs = self.swaps()
        slot = list(pairs).index(name)
        sems = self.pair_sent.at[slot], self.pair_got.at[slot]
        return remote(*pairs[name], *sems, self.place.sibling())

    def give(self, *names):
        for name in names:
            self.swap(name).start()

    def take(self, *names):
        for name in names:
            self.swap(name).wait_recv()

    def settle(self):
        for name in self.swaps():
            self.swap(name).wait_send()


    def mix_weight(self, half, m):
        return self.weights[m][half].reshape(D, PIECES[m].columns)

    def glu_weight(self, k):
        parts = [self.weights[GLU + k][half].reshape(D, CHUNK) for half in range(2)]
        return jnp.concatenate(parts, axis=1)

    def out_weight(self, start, count):
        columns = []
        for half in range(2):
            for p in range(OUT, GLU):
                ref = self.weights[p]
                runs = out_segments(start, count)
                parts = [ref[half, z, x, y, first:last] for z, x, y, first, last in runs]
                columns.append(jnp.concatenate(parts, axis=0))
        return jnp.concatenate(columns, axis=1)

    def put_in(self, p, value):
        self.grads[p][...] = value.astype(LOW).reshape(self.grads[p].shape)

    def put_out(self, start, value):
        value, done = value.astype(LOW), 0
        for z, x, y, first, last in out_segments(start, value.shape[0]):
            count = last - first
            for k in range(OUTS):
                part = value[done : done + count, k * TILE : (k + 1) * TILE]
                self.grads[OUT + k][z, x, y, first:last] = part
            done += count


    def prepare(self, padding, opening, vectors):
        row = lax.broadcasted_iota(jnp.int32, (SLOTS, SLOTS), 0)
        column = lax.broadcasted_iota(jnp.int32, (SLOTS, SLOTS), 1)
        perm = (column == row % LANES * RUN + row // LANES).astype(WIDE)
        self.perm[...] = perm.astype(LOW)
        ones = jnp.ones((SLOTS, TILE), LOW)
        self.live[...] = inner((perm * padding[...].astype(WIDE)).astype(LOW), ones)
        self.opens[...] = inner((perm * opening[...].astype(WIDE)).astype(LOW), ones)

        def line(first, count):
            return jnp.concatenate([vectors[first + i : first + i + 1] for i in range(count)], axis=1)

        phase = line(12, 3)
        self.params[0:1] = line(0, 6)
        self.params[1:2] = line(6, 6)
        self.params[2:3] = jnp.concatenate([jnp.cos(phase), jnp.sin(phase)], axis=1)
        self.params[3:4] = jnp.concatenate([line(15, 3)] * 2, axis=1)
        self.sums[...] = jnp.zeros_like(self.sums)

    def turn(self):
        return jnp.concatenate([self.params[2:3, :CH], self.params[2:3, CH:]], axis=0)

    def first_norm(self, raw):
        values = inner(self.perm[...], raw[...])
        self.tokens[...] = values.astype(LOW)
        self.normed[0:SLOTS] = (values * row_norm(values) * self.params[0:1]).astype(LOW)

    def mask_upstream(self, raw):
        striped = inner(self.perm[...], raw[...]) * tiled(self.live[...], D // TILE)
        self.upstream[0] = striped[:, : D // 2].astype(LOW)
        self.upstream[1] = striped[:, D // 2 :].astype(LOW)

    def mix(self, m):
        piece = PIECES[m]
        weight = (self.mix_weight(0, m), self.mix_weight(1, m)[:, piece.overlap :])
        weight = jnp.concatenate(weight, axis=1)
        start = piece.starts[0]
        self.pre_mix[:, start : start + weight.shape[1]] = inner(self.normed[0:SLOTS], weight)

    def drives(self):
        forget = jax.nn.sigmoid(-(self.pre_mix[:, :CH] + self.params[3:4, :CH]))
        pre = self.pre_mix[:, CH : CH + D]
        driver = pre * jax.nn.sigmoid(pre)
        opens = tiled(self.opens[...], CH // TILE)
        decay = jnp.where(opens > 0.5, 1.0, forget).astype(LOW).astype(WIDE)
        self.retain[...] = 1.0 - decay
        drive = jnp.concatenate([forget, forget], axis=1) * driver
        self.drive[...] = drive.astype(LOW).astype(WIDE)

    def parts(self):
        return self.drive.at[:, pl.ds(0, CH)], self.drive.at[:, pl.ds(CH, CH)]

    def others(self):
        place = self.place
        for step in range(PLANES):
            for flip in range(SIDE):
                if step or flip:
                    z = place.turn(step)
                    x = 1 - place.x if flip else place.x
                    yield place.at(z, x, place.y, place.core)

    def carry_copy(self, way, device):
        return remote(
            self.summaries.at[way, pl.ds(24, 8)],
            self.every.at[way, self.me],
            self.carry_sent.at[way],
            self.carry_got.at[way],
            device,
        )

    def all_carries(self, way):
        part = self.every.at[way, pl.ds(0, PLANES * SIDE - 1)]
        sems = self.carry_sent.at[way], self.carry_got.at[way]
        return remote(part, part, *sems, self.place.sibling())

    def scan_own(self, way):
        run = local_backward if way else local_forward
        run(self.retain, *self.parts(), self.turn(), self.summaries.at[way])
        self.every[way, self.me] = self.summaries[way, 24:32]
        for device in self.others():
            self.carry_copy(way, device).start()

    def carried(self, way):
        self.all_carries(way).wait_recv()
        turn = self.turn()
        return carry_chain(self.every.at[way], turn, self.me, SLOTS, way == 1)

    def scan_states(self):
        start = self.carried(0)
        run = whole_forward
        run(self.retain, *self.parts(), self.turn(), self.summaries.at[0], start, self.states)

    def recurrent(self):
        both = jnp.concatenate([self.states[0, LANES:], self.states[1, LANES:]], axis=1)
        return both.astype(LOW).astype(WIDE)

    def gate_rows(self):
        pre = self.pre_mix[:, CH + D :]
        masked = self.recurrent() * tiled(self.live[...], D // TILE)
        self.gated[0:SLOTS] = (masked * (pre * jax.nn.sigmoid(pre))).astype(LOW)

    def second_norm(self):
        mixed = inner(self.gated[0:SLOTS], self.out_weight(0, D))
        middle = self.tokens[...].astype(WIDE) + mixed
        self.middle[...] = middle
        self.total[...] = middle
        self.normed_two[0:SLOTS] = (middle * row_norm(middle) * self.params[1:2]).astype(LOW)

    def whole_upstream(self):
        return jnp.concatenate([self.upstream[0], self.upstream[1]], axis=1)

    def glu_forward(self, k):
        pre = inner(self.normed_two[0:SLOTS], self.glu_weight(k))
        gate, up = pre[:, :CHUNK], pre[:, CHUNK:]
        d_hidden = across(self.whole_upstream(), self.out_weight(D + CHUNK * k, CHUNK))
        logistic = jax.nn.sigmoid(gate)
        active = gate * logistic
        slope = logistic * (1.0 + gate * (1.0 - logistic))
        self.hidden[k, 0:SLOTS] = (active * up).astype(LOW)
        self.d_glu[k, 0] = (d_hidden * up * slope).astype(LOW)
        self.d_glu[k, 1] = (d_hidden * active).astype(LOW)

    def glu_back(self, k):
        d_glu = jnp.concatenate([self.d_glu[k, 0], self.d_glu[k, 1]], axis=1)
        d_share = across(d_glu, self.glu_weight(k))
        self.d_normed[...] = d_share if k == 0 else self.d_normed[...] + d_share

    def own_half(self, ref, got):
        return jnp.concatenate([ref[self.place.core], got], axis=0)

    def glu_grads(self, k):
        d_glu = jnp.concatenate([self.d_glu[k, self.place.core], self.d_glu_got[k]], axis=0)
        self.put_in(GLU + k, along(self.normed_two[...], d_glu))
        upstream = self.own_half(self.upstream, self.upstream_got[...])
        self.put_out(D + CHUNK * k, along(self.hidden[k], upstream))

    def add_sum(self, index, values):
        self.sums[index] += eights(values)

    def middle_back(self):
        middle, d_normed = self.middle[...], self.d_normed[...]
        scaling = row_norm(middle)
        self.add_sum(1, d_normed * middle * scaling)
        scaled = d_normed * self.params[1:2]
        mean = jnp.mean(middle * scaled, axis=1, keepdims=True)
        upstream = self.whole_upstream().astype(WIDE)
        d_middle = upstream + scaling * scaled - middle * (scaling**3 * mean)
        self.middle[...] = d_middle
        self.d_out[0] = d_middle[:, : D // 2].astype(LOW)
        self.d_out[1] = d_middle[:, D // 2 :].astype(LOW)

    def gate_back(self):
        d_out = jnp.concatenate([self.d_out[0], self.d_out[1]], axis=1)
        d_gated = across(d_out, self.out_weight(0, D))
        pre = self.pre_mix[:, CH + D :]
        logistic = jax.nn.sigmoid(pre)
        d_live = d_gated * tiled(self.live[...], D // TILE)
        self.drive[...] = (d_live * (pre * logistic)).astype(LOW).astype(WIDE)
        slope = logistic * (1.0 + pre * (1.0 - logistic))
        d_gate = (d_live * self.recurrent() * slope).astype(LOW)
        self.d_gate[0] = d_gate[:, : D // 2]
        self.d_gate[1] = d_gate[:, D // 2 :]

    def mixer_out_grad(self):
        d_out = self.own_half(self.d_out, self.d_out_got[...])
        self.put_out(0, along(self.gated[...], d_out))

    def scan_back(self):
        start = self.carried(1)
        real, imag = self.parts()
        whole_backward(
            self.retain,
            real,
            imag,
            self.turn(),
            self.summaries.at[1],
            start,
            self.states,
            self.retain,
            real,
            imag,
            self.sums.at[2, pl.ds(0, 1), pl.ds(0, CH)],
        )

    def drives_back(self):
        def run(rows):
            forget = jax.nn.sigmoid(-(self.pre_mix[rows, :CH] + self.params[3:4, :CH]))
            pre = self.pre_mix[rows, CH : CH + D]
            logistic = jax.nn.sigmoid(pre)
            d_decay = self.retain[rows, :].astype(LOW).astype(WIDE)
            d_input = self.drive[rows, :].astype(LOW).astype(WIDE)
            pulled = d_input * (pre * logistic)
            opens = tiled(self.opens[rows, :], CH // TILE)
            d_forget = jnp.where(opens > 0.5, 0.0, d_decay) + pulled[:, :CH] + pulled[:, CH:]
            d_first = -forget * (1.0 - forget) * d_forget
            self.sums[2, :, CH:] += eights(d_first)
            slope = logistic * (1.0 + pre * (1.0 - logistic))
            d_driver = d_input * jnp.concatenate([forget, forget], axis=1) * slope
            d_pre = jnp.concatenate([d_first, d_driver], axis=1).astype(LOW)
            piece = PIECES[0]
            for half, start in enumerate(piece.starts):
                self.d_drive[half, rows, :] = d_pre[:, start : start + piece.columns]

        each_block(run)

    def mix_grads(self, m):
        own, got = ((self.d_drive, self.d_drive_got), (self.d_gate, self.d_gate_got))[m]
        self.put_in(m, along(self.normed[...], self.own_half(own, got[...])))

    def gate_normed(self):
        left = jnp.concatenate([self.d_gate[0], self.d_gate[1]], axis=1)
        right = jnp.concatenate([self.mix_weight(0, 1), self.mix_weight(1, 1)], axis=1)
        self.d_normed[...] = across(left, right)

    def first_back(self):
        skip = PIECES[0].overlap
        left = jnp.concatenate([self.d_drive[0], self.d_drive[1][:, skip:]], axis=1)
        right = jnp.concatenate([self.mix_weight(0, 0), self.mix_weight(1, 0)[:, skip:]], axis=1)
        d_normed = self.d_normed[...] + across(left, right)
        values = self.tokens[...].astype(WIDE)
        scaling = row_norm(values)
        self.add_sum(0, d_normed * values * scaling)
        scaled = d_normed * self.params[0:1]
        mean = jnp.mean(values * scaled, axis=1, keepdims=True)
        self.middle[...] += scaling * scaled - values * (scaling**3 * mean)

    def natural_out(self):
        hidden = jnp.concatenate([self.hidden[k, 0:SLOTS] for k in range(CHUNKS)], axis=1)
        total = self.total[...] + inner(hidden, self.out_weight(D, FF))
        self.block_out[...] = along(self.perm[...], total.astype(LOW)).astype(LOW)

    def natural_tokens(self):
        rest = self.middle[...]
        total = jnp.zeros_like(rest)
        for _ in range(3):
            part = rest.astype(LOW)
            total = total + along(self.perm[...], part)
            rest = rest - part.astype(WIDE)
        self.d_normed[...] = total


    def gather_vector(self):
        lines = [
            jnp.sum(self.sums[0], axis=0, keepdims=True),
            jnp.sum(self.sums[1], axis=0, keepdims=True),
            jnp.concatenate(
                [self.sums[2, 0:1, :CH], jnp.sum(self.sums[2, :, CH:], axis=0, keepdims=True)], axis=1
            ),
        ]
        for i, line in enumerate(lines):
            for j in range(D // TILE):
                row = i * (D // TILE) + j
                self.vector[0, row : row + 1] = line[:, j * TILE : (j + 1) * TILE]
        filled = jnp.sum(self.live[...], axis=0, keepdims=True)
        rest = jnp.zeros((VEC_ROWS - VEC_COUNT - 1, TILE), WIDE)
        self.vector[0, VEC_COUNT:] = jnp.concatenate([filled, rest], axis=0)

    def vector_copy(self, stage):
        place = self.place
        device = (place.sibling(), place.near(0), place.near(1))[stage]
        source = self.vector.at[stage]
        target = self.vector.at[4 + stage]
        return remote(source, target, self.vector_sent.at[stage], self.vector_got.at[stage], device)

    def vector_step(self, stage):
        if stage:
            self.vector_copy(stage - 1).wait_recv()
            self.vector[stage] = self.vector[stage - 1] + self.vector[3 + stage]
        if stage < 3:
            self.vector_copy(stage).start()

    def vector_plane(self, planes, step, sender):
        place = self.place
        return remote(
            self.vector.at[3],
            planes.at[sender],
            self.vector_sent.at[2 + step],
            self.vector_got.at[2 + step],
            place.plane(place.turn(step)),
        )


def block_kernel(tokens, cotangent, padding, opening, w_in, w_out, vectors, *refs):
    n = len(PIECES)
    block_out, d_tokens, sum_in, sum_out, planes = refs[:5]
    refs = refs[5:]
    count = len(Gather.scratch())
    gather_refs, refs = refs[:count], refs[count:]
    buffers, staging, gather_sems = gather_refs[:n], gather_refs[n : 2 * n], gather_refs[2 * n :]
    grads, refs = refs[:n], refs[n:]
    count = len(Reduce.scratch())
    reduce_refs, refs = refs[:count], refs[count:]
    place = Place()
    gather = Gather(place, {"in": w_in, "out": w_out}, buffers, staging, gather_sems)
    reduce = Reduce(place, grads, reduce_refs, {"in": sum_in, "out": sum_out})
    block = Block(place, buffers, grads, dict(zip(block_scratch(), refs, strict=True)))

    entered = place.greet()
    raw_tokens, raw_upstream = block.gated.at[pl.ds(0, SLOTS)], block.block_out
    loads = [
        pltpu.make_async_copy(tokens.at[0], raw_tokens, block.arrivals.at[0]),
        pltpu.make_async_copy(cotangent.at[0], raw_upstream, block.arrivals.at[1]),
    ]
    leave_out = pltpu.make_async_copy(block.block_out, block_out, block.departures.at[0])
    leave_tokens = pltpu.make_async_copy(block.d_normed, d_tokens, block.departures.at[1])
    for load in loads:
        load.start()
    block.prepare(padding, opening, vectors)
    entered()
    gather.begin()
    gather.near_own(0)
    gather.z_own(0)
    gather.near_own(3)
    gather.near_own(1)
    gather.near_own(2)
    gather.near_own(6)
    gather.near_own(4)
    gather.z_own(1)
    gather.z_own(2)
    loads[0].wait()
    block.first_norm(raw_tokens)
    gather.near_own(7)
    gather.near_own(5)
    gather.far_own(0)
    gather.far_own(3)
    gather.z_own(3)
    gather.far_own(2)
    gather.near(0, 1)
    gather.z_own(5)
    loads[1].wait()
    block.mask_upstream(raw_upstream)
    gather.near(1, 0)
    gather.near(0, 0)
    block.give("normed")
    gather.far_own(7)
    gather.far_own(5)
    gather.far_own(4)
    gather.far_own(6)
    gather.near(0, 2)
    gather.far(0, 1)
    gather.near(1, 2)
    gather.near(2, 0)
    gather.z_own(4)
    gather.near(3, 0)
    gather.far(0, 0)
    gather.far(1, 0)
    gather.near(3, 1)
    gather.near(5, 0)
    gather.near(2, 1)
    gather.chip(2, 0)
    gather.far(0, 2)
    gather.far(1, 2)
    gather.near(3, 2)
    gather.z_own(6)
    gather.chip(6, 0)
    gather.far(5, 0)
    gather.near(1, 1)
    gather.near(2, 2)
    gather.far(3, 2)
    gather.chip(0, 0)
    gather.far_own(1)
    gather.far(2, 0)
    gather.near(5, 2)
    gather.far(4, 1)
    gather.far(1, 1)
    gather.far(4, 2)
    gather.chip(7, 0)
    gather.chip(0, 3)
    gather.z_own(7)
    gather.chip(1, 0)
    gather.near(5, 1)
    gather.chip(0, 1)
    gather.far(3, 0)
    gather.chip(4, 0)
    gather.far(2, 1)
    gather.chip(0, 2)
    gather.far(3, 1)
    gather.chip(1, 3)
    gather.far(6, 1)
    gather.arrive(0)
    gather.far(2, 2)
    gather.chip(4, 2)
    gather.chip(1, 2)
    block.take("normed")
    block.give("upstream")
    gather.far(5, 1, 2)
    block.mix(0)
    gather.chip(5, 1)
    gather.chip(3, 2)
    gather.chip(2, 1)
    gather.chip(3, 0, 1)
    gather.far(4, 0)
    gather.chip(2, 2)
    block.drives()
    gather.chip(1, 1)
    block.scan_own(0)
    gather.chip(2, 3)
    gather.chip(4, 3)
    gather.far(6, 2)
    gather.chip(3, 3)
    gather.far(6, 0)
    gather.chip(5, 0, 2)
    gather.chip(4, 1)
    gather.far(7, 1, 2)
    gather.arrive(3)
    gather.chip(5, 3)
    gather.far(7, 0)
    gather.arrive(1)
    block.mix(1)
    gather.chip(6, 2)
    block.take("upstream")
    gather.arrive(2)
    gather.arrive(4)
    block.scan_states()
    gather.arrive(5)
    block.gate_rows()
    block.second_norm()
    gather.chip(6, 1, 3)
    block.give("normed_two")
    block.glu_forward(0)
    gather.chip(7, 3)
    gather.arrive(6)
    gather.chip(7, 2)
    block.glu_forward(1)
    gather.chip(7, 1)
    block.give(("d_glu", 1), ("hidden", 1))
    block.glu_back(0)
    block.give(("hidden", 0))
    gather.arrive(7)
    block.glu_forward(2)
    block.give(("hidden", 2))
    block.take(("d_glu", 1))
    block.give(("d_glu", 2), ("d_glu", 0))
    block.take(("hidden", 1), "normed_two")
    block.glu_grads(1)
    reduce.far(6)
    block.glu_back(1)
    block.take(("hidden", 2), ("d_glu", 2))
    block.glu_grads(2)
    block.take(("hidden", 0))
    reduce.far(7)
    block.glu_back(2)
    reduce.after_far(6, 0)
    block.take(("d_glu", 0))
    block.middle_back()
    block.gate_back()
    block.scan_own(1)
    block.give("gated")
    block.glu_grads(0)
    reduce.far(5)
    block.give("d_out")
    reduce.after_far(6, 1)
    block.give("d_gate")
    block.take("gated")
    block.gate_normed()
    block.take("d_out")
    reduce.after_far(7, 1)
    block.mixer_out_grad()
    block.scan_back()
    reduce.after_far(7, 3)
    reduce.after_far(5, 0)
    reduce.far(3)
    reduce.far(2)
    reduce.after_far(7, 0)
    block.drives_back()
    block.take("d_gate")
    reduce.after_far(6, 2)
    block.first_back()
    block.mix_grads(1)
    reduce.after_far(3, 0)
    reduce.after_far(7, 2)
    reduce.after_far(5, 1)
    block.give("d_drive")
    block.natural_tokens()
    leave_tokens.start()
    block.gather_vector()
    block.vector_step(0)
    reduce.far(1)
    block.take("d_drive")
    reduce.after_far(5, 2)
    reduce.after_far(2, 0)
    reduce.after_near(5, 0)
    block.mix_grads(0)
    reduce.far(4)
    reduce.after_far(2, 2)
    reduce.after_far(3, 2, 1)
    reduce.far(0)
    block.natural_out()
    leave_out.start()
    reduce.after_far(1, 1)
    block.vector_step(1)
    reduce.after_far(1, 0)
    reduce.after_near(1, 0)
    reduce.after_far(1, 2)
    reduce.after_near(5, 1)
    reduce.after_far(2, 1, 3)
    reduce.after_near(1, 1)
    reduce.after_far(6, 3)
    reduce.after_far(4, 0)
    reduce.after_far(5, 3)
    reduce.after_far(0, 0)
    reduce.after_far(4, 1)
    reduce.after_near(4, 0)
    reduce.after_far(0, 1)
    reduce.after_far(3, 3)
    reduce.after_near(5, 2)
    reduce.after_near(1, 2)
    reduce.after_near(0, 0)
    reduce.after_far(4, 2)
    reduce.after_far(1, 3)
    reduce.after_near(4, 1)
    reduce.after_far(0, 2)
    reduce.after_near(2)
    reduce.after_near(0, 1)
    reduce.after_near(5, 3)
    reduce.finish(5)
    reduce.after_near(6)
    reduce.after_far(4, 3)
    block.vector_step(2)
    reduce.after_near(3)
    reduce.after_near(1, 3)
    reduce.after_far(0, 3)
    reduce.after_near(4, 2)
    reduce.after_near(0, 2)
    reduce.after_near(7)
    reduce.finish(6)
    block.vector_step(3)
    for step in (1, 2, 3):
        block.vector_plane(planes, step, place.z).start()
    planes[place.z] = block.vector[3]
    reduce.finish(1)
    reduce.finish(2)
    reduce.after_near(0, 3)
    reduce.after_near(4, 3)
    reduce.finish(4)
    reduce.finish(7)
    reduce.finish(3)
    reduce.finish(0)

    for step in (1, 2, 3):
        block.vector_plane(planes, step, place.z).wait_send()
        block.vector_plane(planes, step, place.turn(4 - step)).wait_recv()
    for stage in range(3):
        block.vector_copy(stage).wait_send()
    for way in range(2):
        block.all_carries(way).wait_send()
    block.settle()
    for p in range(n):
        gather.drain(p)
        reduce.drain(p)
    leave_out.wait()
    leave_tokens.wait()


def block_routed(tokens, cotangent, padding, opening, w_in, w_out, vectors):
    vmem = pl.BlockSpec(memory_space=pltpu.VMEM)
    anywhere = pl.BlockSpec(memory_space=pl.ANY)
    out_shape = [
        jax.ShapeDtypeStruct((SLOTS, D), LOW),
        jax.ShapeDtypeStruct((SLOTS, D), WIDE),
        jax.ShapeDtypeStruct(w_in.shape, WIDE),
        jax.ShapeDtypeStruct(w_out.shape, WIDE),
        jax.ShapeDtypeStruct((PLANES, VEC_ROWS, TILE), WIDE),
    ]
    grads = [pltpu.VMEM(p.shape()[1:], LOW) for p in PIECES]
    block_out, d_tokens, sum_in, sum_out, planes = pl.pallas_call(
        block_kernel,
        out_shape=out_shape,
        in_specs=[anywhere, anywhere, vmem, vmem, anywhere, anywhere, vmem],
        out_specs=[anywhere, anywhere, vmem, vmem, vmem],
        scratch_shapes=Gather.scratch()
        + grads
        + Reduce.scratch()
        + list(block_scratch().values()),
        compiler_params=pltpu.CompilerParams(
            collective_id=0, has_side_effects=True, vmem_limit_bytes=VMEM_BYTES
        ),
    )(tokens, cotangent, padding, opening, w_in, w_out, vectors.reshape(VEC_COUNT, TILE))
    return block_out, d_tokens, sum_in, sum_out, planes


def power(base, count):
    return lax.fori_loop(0, count, lambda _, value: value * base, jnp.float32(1.0))


def update_kernel(counter, planes, block_from, tokens_from, *refs):
    ins, outs = refs[:11], refs[11:]
    outs[0][...] = block_from[...]
    outs[1][...] = tokens_from[...]
    first_scale = 1.0 - power(BETA_ONE, counter[0])
    second_scale = 1.0 - power(BETA_TWO, counter[0])
    vectors = (planes[0] + planes[1]) + (planes[2] + planes[3])
    total = vectors[VEC_COUNT : VEC_COUNT + 1, 0:1]

    def step(summed, master, first, second, decay):
        gradient = summed / total
        first = BETA_ONE * first + (1.0 - BETA_ONE) * gradient
        second = BETA_TWO * second + (1.0 - BETA_TWO) * gradient * gradient
        corrected = first / first_scale / (jnp.sqrt(second / second_scale) + ADAM_EPSILON)
        return gradient, -LEARN_RATE * (corrected + decay * master), first, second

    for k in range(2):
        summed, master, first, second = (ref[...] for ref in ins[4 * k : 4 * k + 4])
        gradient, change, first, second = step(summed, master, first, second, WEIGHT_DECAY)
        new = master + change
        results = (gradient, new, first, second, new.astype(LOW))
        for ref, value in zip(outs[2 + 5 * k : 7 + 5 * k], results, strict=True):
            ref[...] = value
    master, first, second = (ref[...] for ref in ins[8:])
    results = step(vectors[:VEC_COUNT], master, first, second, 0.0)
    for ref, value in zip(outs[12:16], results, strict=True):
        for i in range(VEC_COUNT):
            ref[pl.ds(i * TILE, TILE)] = value[i]
    for i in range(CH // TILE):
        outs[16][pl.ds(i * TILE, TILE)] = results[0][VEC_COUNT - CH // TILE + i]


UPDATE_BLOCKS = 1


def update(counter, planes, block_out, d_tokens, sums, masters, moments, vector_state):
    shapes = [x.shape for x in sums]

    def by_columns(shape):
        return pl.BlockSpec((shape[0], shape[1] // UPDATE_BLOCKS), lambda i: (0, i))

    def whole(shape):
        return pl.BlockSpec(shape, lambda i: (0,) * len(shape))

    vector = whole((VEC_COUNT, TILE))
    columns = [by_columns(shape) for shape in shapes]
    types = (WIDE, WIDE, WIDE, WIDE, LOW)
    out_shape = [
        jax.ShapeDtypeStruct(block_out.shape, block_out.dtype),
        jax.ShapeDtypeStruct(d_tokens.shape, d_tokens.dtype),
    ]
    out_shape += [jax.ShapeDtypeStruct(shape, kind) for shape in shapes for kind in types]
    lines = [(VEC_COUNT * TILE,)] * 4 + [(CH,)]
    out_shape += [jax.ShapeDtypeStruct(line, WIDE) for line in lines]
    operands = []
    for k in range(2):
        operands += [sums[k], masters[k], *moments[k]]
    return pl.pallas_call(
        update_kernel,
        grid=(UPDATE_BLOCKS,),
        out_shape=out_shape,
        in_specs=[pl.BlockSpec(memory_space=pltpu.SMEM), whole(planes.shape)]
        + [by_columns(block_out.shape)] * 2
        + [columns[0]] * 4
        + [columns[1]] * 4
        + [vector] * 3,
        out_specs=[by_columns(block_out.shape)] * 2 + [columns[0]] * 5 + [columns[1]] * 5 + [whole(line) for line in lines],
        compiler_params=pltpu.CompilerParams(vmem_limit_bytes=VMEM_BYTES),
    )(counter, planes, block_out, d_tokens, *operands, *vector_state)


def routed(tokens, w_in, w_out):
    sizes = (lax.axis_size("dp"), lax.axis_size("rep"))
    shards = (tokens.shape[1], w_in.shape[0], w_out.shape[0])
    return sizes == (PLANES * SIDE, SIDE * 2) and shards == (SLOTS, IN_ROWS, OUT_ROWS)


def block_anywhere(tokens, cotangent, padding, opening, w_in, w_out, vectors):
    low = jnp.bfloat16
    wide = jnp.float32
    mixer_cols = CH + 2 * D
    length = tokens.shape[1]
    inputs = stripe(tokens[0]).astype(wide)
    filled = stripe(padding[0][:, None]).astype(wide)
    starting = stripe(opening[0][:, None]) == 1
    gains_one = vectors[:D]
    gains_two = vectors[D : 2 * D]
    phases = vectors[2 * D : 2 * D + CH]
    biases = vectors[2 * D + CH :]
    turn = jnp.stack([jnp.cos(phases), jnp.sin(phases)])
    axes = ("dp", "rep")
    full_in = lax.all_gather(w_in.astype(low), axes, axis=0, tiled=True)
    full_out = lax.all_gather(w_out.astype(low), axes, axis=0, tiled=True)
    normed, scaling_one = normalize(inputs, gains_one)
    normed_low = normed.astype(low)
    pre_mix = jnp.dot(normed_low, full_in[:, :mixer_cols], preferred_element_type=wide)
    forget = jax.nn.sigmoid(-(pre_mix[:, :CH] + biases))
    driver_pre = pre_mix[:, CH : CH + D]
    driver = jax.nn.silu(driver_pre)
    gate_pre = pre_mix[:, CH + D :]
    forget_both = jnp.concatenate([forget, forget], axis=1)
    decay = jnp.where(starting, 1.0, forget).astype(low).astype(wide)
    retain = 1.0 - decay
    drive = (forget_both * driver).astype(low).astype(wide)
    drive_re, drive_im = drive[:, :CH], drive[:, CH:]
    summary = local_call(local_forward, [(32, CH)], retain, drive_re, drive_im, turn)[0]
    start = carry_in(summary, turn, length, False)
    states = local_call(
        whole_forward, [(2, length + 8, CH)], retain, drive_re, drive_im, turn, summary, start
    )[0]
    recurrent = jnp.concatenate([states[0, LANES:], states[1, LANES:]], axis=1)
    recurrent = recurrent.astype(low).astype(wide)
    gate_act = jax.nn.silu(gate_pre)
    masked = recurrent * filled
    gated_rows = (masked * gate_act).astype(low)
    middle = inputs + jnp.dot(gated_rows, full_out[:D], preferred_element_type=wide)
    normed_two, scaling_two = normalize(middle, gains_two)
    normed_two_low = normed_two.astype(low)
    glu_pre = jnp.dot(normed_two_low, full_in[:, mixer_cols:], preferred_element_type=wide)
    gate_glu = glu_pre[:, :FF]
    up_glu = glu_pre[:, FF:]
    hidden = (jax.nn.silu(gate_glu) * up_glu).astype(low)
    block_out = middle + jnp.dot(hidden, full_out[D:], preferred_element_type=wide)
    upstream = stripe(cotangent[0]).astype(wide) * filled
    upstream_low = upstream.astype(low)
    grad_down = jnp.einsum("tf,te->fe", hidden, upstream_low, preferred_element_type=wide)
    d_hidden = jnp.einsum("te,fe->tf", upstream_low, full_out[D:], preferred_element_type=wide)
    d_glu = jnp.concatenate(
        [d_hidden * up_glu * silu_slope(gate_glu), d_hidden * jax.nn.silu(gate_glu)], axis=1
    ).astype(low)
    grad_glu = jnp.einsum("td,tc->dc", normed_two_low, d_glu, preferred_element_type=wide)
    d_normed_two = jnp.einsum(
        "tc,dc->td", d_glu, full_in[:, mixer_cols:], preferred_element_type=wide
    )
    grad_gains_two = jnp.sum(d_normed_two * middle * scaling_two, axis=0)
    d_middle = upstream + normalize_back(middle, scaling_two, gains_two, d_normed_two)
    d_mixed_low = d_middle.astype(low)
    grad_mixer_out = jnp.einsum("td,te->de", gated_rows, d_mixed_low, preferred_element_type=wide)
    d_gated = jnp.einsum("te,de->td", d_mixed_low, full_out[:D], preferred_element_type=wide)
    d_recurrent = (d_gated * gate_act * filled).astype(low).astype(wide)
    d_gate_pre = d_gated * masked * silu_slope(gate_pre)
    grad_re, grad_im = d_recurrent[:, :CH], d_recurrent[:, CH:]
    summary_back = local_call(local_backward, [(32, CH)], retain, grad_re, grad_im, turn)[0]
    start_back = carry_in(summary_back, turn, length, True)
    d_decay, d_in_re, d_in_im, d_phase = local_call(
        whole_backward,
        [(length, CH)] * 3 + [(1, CH)],
        retain,
        grad_re,
        grad_im,
        turn,
        summary_back,
        start_back,
        states,
    )
    d_decay = d_decay.astype(low).astype(wide)
    d_input = jnp.concatenate([d_in_re, d_in_im], axis=1).astype(low).astype(wide)
    pulled = d_input * driver
    d_forget = jnp.where(starting, 0.0, d_decay) + pulled[:, :CH] + pulled[:, CH:]
    d_forget_pre = -forget * (1.0 - forget) * d_forget
    d_driver_pre = d_input * forget_both * silu_slope(driver_pre)
    d_mix = jnp.concatenate([d_forget_pre, d_driver_pre, d_gate_pre], axis=1).astype(low)
    grad_mixer_in = jnp.einsum("td,tc->dc", normed_low, d_mix, preferred_element_type=wide)
    d_normed = jnp.einsum(
        "tc,dc->td", d_mix, full_in[:, :mixer_cols], preferred_element_type=wide
    )
    grad_gains_one = jnp.sum(d_normed * inputs * scaling_one, axis=0)
    d_tokens = d_middle + normalize_back(inputs, scaling_one, gains_one, d_normed)
    grad_biases = jnp.sum(d_forget_pre, axis=0)
    grad_vectors = jnp.concatenate([grad_gains_one, grad_gains_two, d_phase[0], grad_biases])
    grad_in_all = jnp.concatenate([grad_mixer_in, grad_glu], axis=1)
    grad_out_all = jnp.concatenate([grad_mixer_out, grad_down], axis=0)
    summed_in = lax.psum_scatter(grad_in_all, axes, scatter_dimension=0, tiled=True)
    summed_out = lax.psum_scatter(grad_out_all, axes, scatter_dimension=0, tiled=True)
    summed_vec, total = lax.psum((grad_vectors, jnp.sum(filled)), axes)
    return unstripe(block_out.astype(low)), unstripe(d_tokens), summed_in, summed_out, summed_vec, total


def body(
    tokens,
    cotangent,
    padding,
    opening,
    w_in,
    w_out,
    vectors,
    m_in,
    v_in,
    m_out,
    v_out,
    m_vec,
    v_vec,
    counter,
):
    if routed(tokens, w_in, w_out):
        block_out, d_tokens, sum_in, sum_out, planes = block_routed(
            tokens, cotangent, padding, opening, w_in, w_out, vectors
        )
        sums, masters = (sum_in, sum_out), (w_in, w_out)
        moments = ((m_in, v_in), (m_out, v_out))
        lines = [x.reshape(VEC_COUNT, TILE) for x in (vectors, m_vec, v_vec)]
        results = update(
            counter, planes, block_out, d_tokens, sums, masters, moments, lines
        )
        block_out, d_tokens = results[:2]
        grad_vec, update_vec, first_vec, second_vec, grad_bias = results[12:]
        return (
            block_out[None],
            d_tokens[None],
            *results[2:12],
            grad_vec,
            grad_bias,
            update_vec,
            first_vec,
            second_vec,
        )
    block_out, d_tokens, summed_in, summed_out, summed_vec, total = block_anywhere(
        tokens, cotangent, padding, opening, w_in, w_out, vectors
    )
    steps = counter[0].astype(jnp.float32)
    grad_in = summed_in / total
    grad_out = summed_out / total
    grad_vec = summed_vec / total
    new_in, first_in, second_in, change_in = adam_update(
        w_in, grad_in, m_in, v_in, steps, WEIGHT_DECAY
    )
    new_out, first_out, second_out, change_out = adam_update(
        w_out, grad_out, m_out, v_out, steps, WEIGHT_DECAY
    )
    new_vec, first_vec, second_vec, update_vec = adam_update(
        vectors, grad_vec, m_vec, v_vec, steps, 0.0
    )
    return (
        block_out[None],
        d_tokens[None],
        grad_in,
        new_in,
        first_in,
        second_in,
        new_in.astype(jnp.bfloat16),
        grad_out,
        new_out,
        first_out,
        second_out,
        new_out.astype(jnp.bfloat16),
        grad_vec,
        grad_vec[2 * D + CH :],
        update_vec,
        first_vec,
        second_vec,
    )


def solution(mesh):
    in_specs = (
        P("rep", "dp", None),
        P("rep", "dp", None),
        P("rep", "dp"),
        P("rep", "dp"),
        P(("dp", "rep"), None),
        P(("dp", "rep"), None),
        P(),
        P(("dp", "rep"), None),
        P(("dp", "rep"), None),
        P(("dp", "rep"), None),
        P(("dp", "rep"), None),
        P(),
        P(),
        P(),
    )
    out_specs = (
        P("rep", "dp", None),
        P("rep", "dp", None),
        P(("dp", "rep"), None),
        P(("dp", "rep"), None),
        P(("dp", "rep"), None),
        P(("dp", "rep"), None),
        P(("dp", "rep"), None),
        P(("dp", "rep"), None),
        P(("dp", "rep"), None),
        P(("dp", "rep"), None),
        P(("dp", "rep"), None),
        P(("dp", "rep"), None),
        P(),
        P(),
        P(),
        P(),
        P(),
    )
    return jax.shard_map(body, mesh=mesh, in_specs=in_specs, out_specs=out_specs, check_vma=False)
```
